32 devices in a mesh: cp: 8 (over z, x), tp: 4 (over y, core).
Axes of the slice: x: 2, y: 2, z: 4, core: 2. Of those that a mesh axis runs over, the one named last changes fastest.
Arguments:
- layer_input: bfloat16 [4096, 1536], P('cp'), may hold values from -6 to 6
- norm1_gain: float32 [1536], replicated, may hold values from 0.1 to 1.9
- w_query: bfloat16 [1536, 1536], P(None, 'tp'), may hold values from -0.15625 to 0.15625
- b_query: float32 [1536], P('tp'), may hold values from -3 to 3
- w_key: bfloat16 [1536, 256], replicated, may hold values from -0.15625 to 0.15625
- b_key: float32 [256], replicated, may hold values from -3 to 3
- w_value: bfloat16 [1536, 256], replicated, may hold values from -0.15625 to 0.15625
- b_value: float32 [256], replicated, may hold values from -3 to 3
- w_out: bfloat16 [1536, 1536], P('tp'), may hold values from -0.4375 to 0.4375
- norm2_gain: float32 [1536], replicated, may hold values from 0.1 to 1.9
- w_gate: bfloat16 [1536, 8960], P(None, 'tp'), may hold values from -0.15625 to 0.15625
- w_up: bfloat16 [1536, 8960], P(None, 'tp'), may hold values from -0.15625 to 0.15625
- w_down: bfloat16 [8960, 1536], P('tp'), may hold values from -0.125 to 0.125
- doc_ids: int32 [4096], replicated, may hold values from 0 to 2, as said below
- positions: int32 [4096], replicated, may hold values from 0 to 2047, as said below
- cotangent: bfloat16 [4096, 1536], P('cp'), may hold values from -6 to 6
Outputs:
- output: bfloat16 [4096, 1536], P('cp')
- grad_x: bfloat16 [4096, 1536], P('cp')
- grad_norm1_gain: float32 [1536], replicated
- grad_w_query: float32 [1536, 1536], P('cp', 'tp')
- grad_b_query: float32 [1536], P('tp')
- grad_w_key: float32 [1536, 256], P('cp')
- grad_b_key: float32 [256], replicated
- grad_w_value: float32 [1536, 256], P('cp')
- grad_b_value: float32 [256], replicated
- grad_w_out: float32 [1536, 1536], P('tp', 'cp')
- grad_norm2_gain: float32 [1536], replicated
- grad_w_gate: float32 [1536, 8960], P('cp', 'tp')
- grad_w_up: float32 [1536, 8960], P('cp', 'tp')
- grad_w_down: float32 [8960, 1536], P('tp', 'cp')
The draws below stay inside these ranges and needn't reach their ends.
Inputs may be any that keep to these rules, and one draw needn't show every extreme that they name: `doc_ids`: document 0 has 2048 tokens in 16 blocks of 128; index i of cp holds block i as its first 128 tokens and block 15 - i as its last. Between them each index i holds 256 tokens of document 1 if i is below a cut c (1 <= c < 8, drawn), else of document 2; documents 1 and 2 run in order over the indices, index i holding their block i, resp. i - c. `positions`: each token's place in its document; documents are laid out as doc_ids states, every document's places starting at 0.
All inputs are finite; a program needn't handle non-finite values.
Results may differ from the reference program's by a relative error of at most 0.025.
Values may be sent and summed in bfloat16 or wider, within the bound.
A program may use at most 192 MiB of HBM per device.

```python
import math
from functools import partial
import jax
import jax.numpy as jnp
from jax import lax

D = 1536
H = 12
KVH = 2
HD = 128
FF = 8960
TOK_DEV = 512
ZIG = 256
TOKENS = 4096


def shared_plan(key):
    devices = TOKENS // TOK_DEV
    half = ZIG // 2
    rest = TOK_DEV - ZIG
    cut = jax.random.randint(key, (), 1, devices).astype(jnp.int32)
    device_rows = jnp.arange(devices, dtype=jnp.int32)[:, None]
    half_lanes = jnp.arange(half, dtype=jnp.int32)[None, :]
    rest_lanes = jnp.arange(rest, dtype=jnp.int32)[None, :]
    before = device_rows < cut
    middle_docs = jnp.where(before, 1, 2) * jnp.ones((1, rest), jnp.int32)
    middle_pos = jnp.where(before, device_rows, device_rows - cut) * rest + rest_lanes
    zeros_half = jnp.zeros((devices, half), jnp.int32)
    doc_plan = jnp.concatenate([zeros_half, middle_docs, zeros_half], 1).reshape(-1)
    first_pos = device_rows * half + half_lanes
    last_pos = (2 * devices - 1 - device_rows) * half + half_lanes
    pos_plan = jnp.concatenate([first_pos, middle_pos, last_pos], 1).reshape(-1)
    return (doc_plan.astype(jnp.int32), pos_plan.astype(jnp.int32))


def draw_doc_ids(key, part):
    doc_plan, pos_plan = shared_plan(key)
    return doc_plan


def draw_positions(key, part):
    doc_plan, pos_plan = shared_plan(key)
    return pos_plan


def level_of(stream_key, extent, cuts, low, high):
    def one(position, blocks):
        draws = jax.random.uniform(jax.random.fold_in(jax.random.fold_in(stream_key, 6), position), (blocks,), jnp.float32, low / len(cuts), high / len(cuts))
        return jnp.repeat(jnp.exp(draws), extent[position] // blocks).reshape((-1,) + (1,) * (len(extent) - position - 1))

    loudness = one(*cuts[0])
    for cut in cuts[1:]:
        loudness = loudness * one(*cut)
    return loudness


def centred(stream_key, extent, scale, limit, cuts=(), held_as=jnp.bfloat16):
    level = level_of(stream_key, extent, cuts, -0.22, 0.18) if cuts else 1.0
    values = jax.random.normal(stream_key, extent, jnp.float32) * scale * level
    return jnp.minimum(jnp.maximum(values, -limit), limit).astype(held_as)


def setup_inputs(seed: int = 0) -> dict:
    key_list = jax.random.split(jax.random.key(seed), 17)
    return {
        "layer_input": centred(key_list[0], (TOKENS, D), 1.0, 6.0, ((0, 8),)),
        "norm1_gain": jnp.clip(1.0 + 0.18 * jax.random.normal(key_list[1], (D,), jnp.float32), 0.1, 1.9),
        "w_query": centred(key_list[2], (D, H * HD), D ** -0.5, 0.15625, ((1, 4),)),
        "b_query": centred(key_list[3], (H * HD,), 0.5, 3.0, ((0, 4),), jnp.float32),
        "w_key": centred(key_list[4], (D, KVH * HD), D ** -0.5, 0.15625),
        "b_key": centred(key_list[5], (KVH * HD,), 0.5, 3.0, (), jnp.float32),
        "w_value": centred(key_list[6], (D, KVH * HD), D ** -0.5, 0.15625),
        "b_value": centred(key_list[7], (KVH * HD,), 0.5, 3.0, (), jnp.float32),
        "w_out": centred(key_list[8], (H * HD, D), (H * HD // 8) ** -0.5, 0.4375, ((0, 4),)),
        "norm2_gain": jnp.clip(1.0 + 0.18 * jax.random.normal(key_list[9], (D,), jnp.float32), 0.1, 1.9),
        "w_gate": centred(key_list[10], (D, FF), D ** -0.5, 0.15625, ((1, 4),)),
        "w_up": centred(key_list[11], (D, FF), D ** -0.5, 0.15625, ((1, 4),)),
        "w_down": centred(key_list[12], (FF, D), (FF // 4) ** -0.5, 0.125, ((0, 4),)),
        "doc_ids": draw_doc_ids(jax.random.fold_in(key_list[16], 71), 0),
        "positions": draw_positions(jax.random.fold_in(key_list[16], 71), 0),
        "cotangent": centred(key_list[15], (TOKENS, D), 1.0, 6.0, ((0, 8),)),
    }


EPSILON = 1e-06
ROPE_BASE = 10000.0
MASKED = -1e+30

@jax.custom_vjp
def low(v):
    return lax.optimization_barrier(v.astype(jnp.bfloat16)).astype(jnp.float32)

@jax.custom_vjp
def low_back(v):
    return v

def low_keep(v):
    return (low(v), None)

def low_pass(kept, grad):
    return (grad,)

def back_keep(v):
    return (v, None)

def back_low(kept, grad):
    return (low(grad),)
low.defvjp(low_keep, low_pass)
low_back.defvjp(back_keep, back_low)

def product(left, right):
    return jnp.dot(left, right, precision=lax.Precision.HIGHEST)

def normed(values, gain):
    return values * lax.rsqrt(lax.optimization_barrier(jnp.mean(values * values, axis=-1, keepdims=True)) + EPSILON) * gain

def rope_tables(tok_pos):
    half = HD // 2
    freq = ROPE_BASE ** (-(jnp.arange(half, dtype=jnp.float32) * 2.0 / HD))
    angle = tok_pos.astype(jnp.float32)[:, None] * freq[None, :]
    cosine = jnp.concatenate([jnp.cos(angle), jnp.cos(angle)], -1)[:, None, :]
    sine = jnp.concatenate([jnp.sin(angle), jnp.sin(angle)], -1)[:, None, :]
    return (cosine, sine)

def rotary(values, cosine, sine):
    half = values.shape[-1] // 2
    return values * cosine + jnp.concatenate([-values[..., half:], values[..., :half]], -1) * sine

def layer(doc_ids, positions, layer_input, norm1_gain, w_query, b_query, w_key, b_key, w_value, b_value, w_out, norm2_gain, w_gate, w_up, w_down):
    count = layer_input.shape[0]
    cosine, sine = rope_tables(positions)
    normed1 = low(normed(layer_input, norm1_gain))
    query = low(rotary(low_back(product(normed1, w_query) + b_query).reshape(count, H, HD), cosine, sine))
    key = low(rotary(low_back(product(normed1, w_key) + b_key).reshape(count, KVH, HD), cosine, sine))
    value = low_back(low(product(normed1, w_value) + b_value)).reshape(count, KVH, HD)
    key_wide = jnp.repeat(key, H // KVH, axis=1)
    value_wide = jnp.repeat(value, H // KVH, axis=1)
    scale = HD ** (-0.5)
    block = math.gcd(count, 512)

    def attend_block(item):
        query_block, query_doc, query_pos = item
        scores = jnp.einsum('qhd,khd->hqk', query_block, key_wide, precision=lax.Precision.HIGHEST) * scale
        allowed = (query_doc[:, None] == doc_ids[None, :]) & (positions[None, :] <= query_pos[:, None])
        scores = low_back(jnp.where(allowed[None], scores, MASKED))
        probs = low(jax.nn.softmax(scores, axis=-1))
        return jnp.einsum('hqk,khd->qhd', probs, value_wide, precision=lax.Precision.HIGHEST)
    blocks = lax.map(jax.checkpoint(attend_block), (query.reshape(count // block, block, H, HD), doc_ids.reshape(count // block, block), positions.reshape(count // block, block)))
    attn = low_back(low(blocks.reshape(count, H * HD)))
    middle = layer_input + low_back(product(attn, w_out))
    normed2 = low(normed(middle, norm2_gain))
    gate = low_back(product(normed2, w_gate))
    up_part = low_back(product(normed2, w_up))
    hidden = low(jax.nn.silu(gate) * up_part)
    return middle + low_back(product(hidden, w_down))

def reference(layer_input, norm1_gain, w_query, b_query, w_key, b_key, w_value, b_value, w_out, norm2_gain, w_gate, w_up, w_down, doc_ids, positions, cotangent):
    params = [argument.astype(jnp.float32) for argument in (layer_input, norm1_gain, w_query, b_query, w_key, b_key, w_value, b_value, w_out, norm2_gain, w_gate, w_up, w_down)]
    output, pull = jax.vjp(partial(layer, doc_ids, positions), *params)
    grads = pull(cotangent.astype(jnp.float32))
    return (output.astype(jnp.bfloat16), grads[0].astype(jnp.bfloat16), grads[1], grads[2], grads[3], grads[4], grads[5], grads[6], grads[7], grads[8], grads[9], grads[10], grads[11], grads[12])
```

```python
import functools
import math

import jax
import jax.numpy as jnp
from jax import lax
from jax.experimental import pallas as pl
from jax.experimental.pallas import tpu as pltpu
from jax.sharding import PartitionSpec as P

H = 12
HD = 128
HALF = 128
EPSILON = 1e-06
ROPE_BASE = 10000.0
MASKED = -1e30
LOG2E = 1.4426950408889634
TILE = 256
CHUNK_TILES = 3
VMEM_LIMIT = 56 * 1024 * 1024
TP_ORDER = (0, 2, 1, 3)


def matmul(left, right):
    return jnp.dot(left, right, preferred_element_type=jnp.float32)


def contract_rows(left, right):
    return lax.dot_general(
        left, right, (((0,), (0,)), ((), ())), preferred_element_type=jnp.float32
    )


def contract_cols(left, right):
    return lax.dot_general(
        left, right, (((1,), (1,)), ((), ())), preferred_element_type=jnp.float32
    )


def rope_tables(tok_pos, width):
    half = width // 2
    freq = ROPE_BASE ** (-(jnp.arange(half, dtype=jnp.float32) * 2.0 / width))
    angle = tok_pos.astype(jnp.float32)[:, None] * freq[None, :]
    cosine = jnp.concatenate([jnp.cos(angle), jnp.cos(angle)], -1)
    sine = jnp.concatenate([jnp.sin(angle), jnp.sin(angle)], -1)
    return (cosine, sine)


def rotary(values, cosine, sine):
    half = values.shape[-1] // 2
    return values * cosine + jnp.concatenate([-values[..., half:], values[..., :half]], -1) * sine


def rotary_back(grads, cosine, sine):
    half = grads.shape[-1] // 2
    scaled = grads * sine
    return grads * cosine + jnp.concatenate([scaled[..., half:], -scaled[..., :half]], -1)


def swap(value, axis, bit):
    size = lax.axis_size(axis)
    return lax.ppermute(value, axis, [(i, i ^ bit) for i in range(size)])


def after(value, *earlier):
    return lax.optimization_barrier((value, *earlier))[0]


def bits_of(size):
    return size.bit_length() - 1


def reverse_bits(index, bits):
    out = 0
    for i in range(bits):
        out = out | (((index >> i) & 1) << (bits - 1 - i))
    return out


def params(**more):
    return pltpu.CompilerParams(vmem_limit_bytes=VMEM_LIMIT, **more)


SMEM = pl.BlockSpec(memory_space=pltpu.SMEM)
VMEM = pl.BlockSpec(memory_space=pltpu.VMEM)


def spread_kernel(shards, place_ref, rows_ref, own_ref, send_ref, turned):
    me, core = place_ref[0], place_ref[1]
    turned[...] = rows_ref[...].T
    width = turned.shape[0] // shards
    bits = bits_of(shards)
    for i in range(shards // 2):
        far = reverse_bits(i, bits)
        block = pl.multiple_of((me ^ far) * width, 16)
        own_ref[i * width : (i + 1) * width, :] = turned[pl.ds(block, width), :]
    for i in range(shards // 4):
        far = reverse_bits(core * (shards // 4) + i, bits) | 1
        block = pl.multiple_of((me ^ far) * width, 16)
        send_ref[i * width : (i + 1) * width, :] = turned[pl.ds(block, width), :]


def spread(place, rows, shards):
    count, width = rows.shape
    return pl.pallas_call(
        functools.partial(spread_kernel, shards),
        out_shape=(
            jax.ShapeDtypeStruct((width // 2, count), rows.dtype),
            jax.ShapeDtypeStruct((width // 4, count), rows.dtype),
        ),
        in_specs=[SMEM, VMEM],
        out_specs=(VMEM, VMEM),
        scratch_shapes=[pltpu.VMEM((width, count), rows.dtype)],
        compiler_params=params(),
        cost_estimate=pl.CostEstimate(flops=0, bytes_accessed=4 * rows.size, transcendentals=0),
    )(place, rows)


def share(place, rows, shards):
    own, send = spread(place, rows, shards)
    near = swap(send, "cp", 1)
    return own, near, swap(near, "tp", 1)


def weigh_kernel(place_ref, own_ref, near_ref, far_ref, mine_ref, theirs_ref, send_ref, keep_ref, joined):
    core = place_ref[1]

    @pl.when(pl.program_id(0) == 0)
    def _():
        joined[core] = near_ref[...]
        joined[1 - core] = far_ref[...]

    half = send_ref.shape[0]
    mine, theirs = mine_ref[...], theirs_ref[...]
    send_ref[...] = (
        matmul(own_ref[half:, :], mine) + matmul(joined[1], theirs)
    ).astype(send_ref.dtype)
    keep_ref[...] = (
        matmul(own_ref[:half, :], mine) + matmul(joined[0], theirs)
    ).astype(keep_ref.dtype)


def weigh(place, shared, mine, theirs):
    own, near, far = shared
    half, count = near.shape
    width = mine.shape[1]
    tile = min(width, 512)
    whole = lambda j: (0, 0)
    column = lambda j: (0, j)
    return pl.pallas_call(
        weigh_kernel,
        grid=(pl.cdiv(width, tile),),
        out_shape=(jax.ShapeDtypeStruct((half, width), jnp.bfloat16),) * 2,
        in_specs=[
            SMEM,
            pl.BlockSpec((2 * half, count), whole),
            pl.BlockSpec((half, count), whole),
            pl.BlockSpec((half, count), whole),
            pl.BlockSpec((count, tile), column),
            pl.BlockSpec((count, tile), column),
        ],
        out_specs=(pl.BlockSpec((half, tile), column),) * 2,
        scratch_shapes=[pltpu.VMEM((2, half, count), jnp.bfloat16)],
        compiler_params=params(),
        cost_estimate=pl.CostEstimate(
            flops=8 * half * count * width,
            bytes_accessed=4 * (2 * half * count + count * width + half * width),
            transcendentals=0,
        ),
    )(place, own, near, far, mine, theirs)


def weight_grad(place, shared, mine, shards):
    theirs = swap(mine, "cp", 1)
    send, keep = weigh(place, shared, mine, theirs)
    terms = [keep]
    bit = 2
    while bit < shards:
        terms.append(swap(send, "cp", bit))
        bit *= 2
        if bit < shards:
            rows = terms[0].shape[0] // 2
            send = sum(t[rows:].astype(jnp.float32) for t in terms).astype(jnp.bfloat16)
            terms = [t[:rows] for t in terms]
    return sum(t.astype(jnp.float32) for t in terms)


def hidden_kernel(first, last, offset, units, *refs):
    place_ref, rows_ref, cot_ref, gate_ref, up_ref, down_ref = refs[:6]
    refs = refs[6:]
    if not first:
        before_ref, refs = refs[0], refs[1:]
    hidden_ref, grads_ref, sum_ref, total = refs
    step = pl.program_id(0)

    @pl.when(step == 0)
    def _():
        total[...] = jnp.zeros_like(total) if first else before_ref[...]

    rows = rows_ref[...]
    w_gate, w_up, w_down = gate_ref[...], up_ref[...], down_ref[...]
    if last:
        left = units - (offset + step) * TILE
        inside = lax.broadcasted_iota(jnp.int32, w_gate.shape, 1) < left
        w_gate = jnp.where(inside, w_gate, 0)
        w_up = jnp.where(inside, w_up, 0)
        inside = lax.broadcasted_iota(jnp.int32, w_down.shape, 0) < left
        w_down = jnp.where(inside, w_down, 0)
    gate = matmul(rows, w_gate)
    up_part = matmul(rows, w_up)
    grad_hidden = contract_cols(cot_ref[...], w_down)
    sigma = jax.nn.sigmoid(gate)
    swish = gate * sigma
    hidden_ref[...] = (swish * up_part).astype(jnp.bfloat16)
    grad_gate = (grad_hidden * up_part * sigma * (1.0 + gate * (1.0 - sigma))).astype(jnp.bfloat16)
    grad_up = (grad_hidden * swish).astype(jnp.bfloat16)
    grads_ref[:, :TILE] = grad_gate
    grads_ref[:, TILE:] = grad_up
    total[...] += contract_cols(grad_gate, w_gate) + contract_cols(grad_up, w_up)

    @pl.when(step == pl.num_programs(0) - 1)
    def _():
        if last:
            part = total.shape[0] // len(TP_ORDER)
            for i, far in enumerate(TP_ORDER):
                block = pl.multiple_of((place_ref[2] ^ far) * part, part)
                sum_ref[i * part : (i + 1) * part, :] = total[pl.ds(block, part), :].astype(
                    sum_ref.dtype
                )
        else:
            sum_ref[...] = total[...]


def hidden_chunk(place, rows, cotangent, w_gate, w_up, w_down, before, index):
    count, width = rows.shape
    units = w_gate.shape[1]
    tiles = pl.cdiv(units, TILE)
    offset = index * CHUNK_TILES
    steps = min(CHUNK_TILES, tiles - offset)
    first, last = index == 0, offset + steps == tiles
    inner = min(steps * TILE, units - offset * TILE)
    outer = (steps - 1) * 2 * TILE + TILE + inner - (steps - 1) * TILE
    whole = lambda j: (0, 0)
    column = lambda j: (0, j)
    in_specs = [
        SMEM,
        pl.BlockSpec((count, width), whole),
        pl.BlockSpec((count, width), whole),
        pl.BlockSpec((width, TILE), lambda j: (0, offset + j)),
        pl.BlockSpec((width, TILE), lambda j: (0, offset + j)),
        pl.BlockSpec((TILE, width), lambda j: (offset + j, 0)),
    ]
    operands = [place, rows, cotangent, w_gate, w_up, w_down]
    if not first:
        in_specs.append(pl.BlockSpec((count, width), whole))
        operands.append(before)
    return pl.pallas_call(
        functools.partial(hidden_kernel, first, last, offset, units),
        grid=(steps,),
        out_shape=(
            jax.ShapeDtypeStruct((count, inner), jnp.bfloat16),
            jax.ShapeDtypeStruct((count, outer), jnp.bfloat16),
            jax.ShapeDtypeStruct((count, width), jnp.bfloat16 if last else jnp.float32),
        ),
        in_specs=in_specs,
        out_specs=(
            pl.BlockSpec((count, TILE), column),
            pl.BlockSpec((count, 2 * TILE), column),
            pl.BlockSpec((count, width), whole),
        ),
        scratch_shapes=[pltpu.VMEM((count, width), jnp.float32)],
        compiler_params=params(),
        cost_estimate=pl.CostEstimate(
            flops=10 * count * width * inner,
            bytes_accessed=6 * width * inner + 12 * count * width,
            transcendentals=count * inner,
        ),
    )(*operands)


def region_rows(ref, start, count):
    return ref[:, start : start + count, :].reshape(-1, HD)


def triangle(rows, keys):
    row = lax.broadcasted_iota(jnp.int32, (rows, keys), 0) & (keys - 1)
    return row >= lax.broadcasted_iota(jnp.int32, (rows, keys), 1)


def regions(place_ref, shards, tok_rows):
    me, start = place_ref[0], place_ref[3]
    bits = bits_of(shards)

    def of_first(block):
        low = block < shards
        device = jnp.where(low, block, 2 * shards - 1 - block)
        return reverse_bits(device ^ me, bits), jnp.where(low, 0, tok_rows - HALF)

    def of_middle(block):
        return reverse_bits((start + block) ^ me, bits), HALF

    return (
        (0, HALF, me, of_first),
        (tok_rows - HALF, HALF, 2 * shards - 1 - me, of_first),
        (HALF, tok_rows - 2 * HALF, me - start, of_middle),
    )


def attend_kernel(shards, place_ref, q_ref, mine_ref, other_ref, low_ref, full_ref, log_ref, pair):
    core = place_ref[1]
    pair[core] = mine_ref[...]
    pair[1 - core] = other_ref[...]
    heads, tok_rows = q_ref.shape[0], q_ref.shape[1]
    factor = HD**-0.5 * LOG2E
    for begin, count, blocks, locate in regions(place_ref, shards, tok_rows):
        query = region_rows(q_ref, begin, count)
        rows = heads * count

        def read(which, block):
            slot, offset = locate(block)
            return pair[which, slot, pl.ds(pl.multiple_of(offset, HALF), count), :]

        mask = triangle(rows, count)
        last = jnp.where(mask, contract_cols(query, read(0, blocks)), MASKED)
        peak = lax.fori_loop(
            0, blocks, lambda t, top: jnp.maximum(top, contract_cols(query, read(0, t))), last
        )
        peak = jnp.max(peak, axis=1, keepdims=True) * factor

        def add(block, carry, scores):
            total, accum = carry
            weights = jnp.exp2(scores * factor - peak)
            return total + weights, accum + matmul(weights.astype(jnp.bfloat16), read(1, block))

        carry = add(blocks, (jnp.zeros((rows, count), jnp.float32), jnp.zeros((rows, HD), jnp.float32)), last)
        total, accum = lax.fori_loop(
            0, blocks, lambda t, held: add(t, held, contract_cols(query, read(0, t))), carry
        )
        total = jnp.sum(total, axis=1, keepdims=True)
        full = accum / total
        log_total = jnp.broadcast_to(peak + jnp.log2(total), (rows, HD))
        for head in range(heads):
            part = slice(head * count, (head + 1) * count)
            lanes = slice(head * HD, (head + 1) * HD)
            low_ref[begin : begin + count, lanes] = full[part].astype(jnp.bfloat16)
            full_ref[head, begin : begin + count, :] = full[part]
            log_ref[head, begin : begin + count, :] = log_total[part]


def attend(place, query, mine, other):
    heads, tok_rows, _ = query.shape
    shards = mine.shape[0]
    pairs = heads * tok_rows * tok_rows * shards // 4
    return pl.pallas_call(
        functools.partial(attend_kernel, shards),
        out_shape=(
            jax.ShapeDtypeStruct((tok_rows, heads * HD), jnp.bfloat16),
            jax.ShapeDtypeStruct((heads, tok_rows, HD), jnp.float32),
            jax.ShapeDtypeStruct((heads, tok_rows, HD), jnp.float32),
        ),
        in_specs=[SMEM, VMEM, VMEM, VMEM],
        out_specs=(VMEM, VMEM, VMEM),
        scratch_shapes=[pltpu.VMEM((2,) + mine.shape, jnp.bfloat16)],
        compiler_params=params(),
        cost_estimate=pl.CostEstimate(
            flops=6 * pairs * HD, bytes_accessed=4 * mine.size, transcendentals=pairs
        ),
    )(place, query, mine, other)


def attend_back_kernel(
    shards, place_ref, q_ref, mine_ref, other_ref, low_ref, full_ref, log_ref, cos_ref, sin_ref,
    query_ref, keep_ref, send_ref, pair, grads,
):
    core = place_ref[1]
    pair[core] = mine_ref[...]
    pair[1 - core] = other_ref[...]
    grads[...] = jnp.zeros_like(grads)
    heads, tok_rows = q_ref.shape[0], q_ref.shape[1]
    scale = HD**-0.5
    factor = scale * LOG2E
    sign = jnp.where(lax.broadcasted_iota(jnp.int32, (1, HD), 1) < HD // 2, 1.0, -1.0)
    for begin, count, blocks, locate in regions(place_ref, shards, tok_rows):
        query = region_rows(q_ref, begin, count)
        rows = heads * count
        incoming = jnp.concatenate(
            [low_ref[begin : begin + count, h * HD : (h + 1) * HD] for h in range(heads)], 0
        )
        full = region_rows(full_ref, begin, count)
        log_total = region_rows(log_ref, begin, count)[:, :1]
        delta = jnp.sum(incoming.astype(jnp.float32) * full, axis=1, keepdims=True)

        def add(block, grad_query, mask=None):
            slot, offset = locate(block)
            place = pl.ds(pl.multiple_of(offset, HALF), count)
            keys, values = pair[0, slot, place, :], pair[1, slot, place, :]
            probs = jnp.exp2(contract_cols(query, keys) * factor - log_total)
            if mask is not None:
                probs = jnp.where(mask, probs, 0.0)
            grad_scores = (probs * (contract_cols(incoming, values) - delta)).astype(jnp.bfloat16)
            grads[0, slot, place, :] += contract_rows(grad_scores, query)
            grads[1, slot, place, :] += contract_rows(probs.astype(jnp.bfloat16), incoming)
            return grad_query + matmul(grad_scores, keys)

        grad_query = add(blocks, jnp.zeros((rows, HD), jnp.float32), triangle(rows, count))
        grad_query = lax.fori_loop(0, blocks, add, grad_query) * scale
        cosine, sine = cos_ref[begin : begin + count, :], sin_ref[begin : begin + count, :]
        for head in range(heads):
            part = grad_query[head * count : (head + 1) * count]
            turned = part * cosine + pltpu.roll(part * sine, HD // 2, 1) * sign
            query_ref[begin : begin + count, head * HD : (head + 1) * HD] = turned.astype(
                jnp.bfloat16
            )
    is_key = core == 0
    keep_ref[...] = (grads[core] * jnp.where(is_key, scale, 1.0)).astype(jnp.bfloat16)
    send_ref[...] = (grads[1 - core] * jnp.where(is_key, 1.0, scale)).astype(jnp.bfloat16)


def attend_back(place, query, mine, other, low, full, log_total, cosine, sine):
    heads, tok_rows, _ = query.shape
    shards = mine.shape[0]
    pairs = heads * tok_rows * tok_rows * shards // 4
    return pl.pallas_call(
        functools.partial(attend_back_kernel, shards),
        out_shape=(
            jax.ShapeDtypeStruct((tok_rows, heads * HD), jnp.bfloat16),
            jax.ShapeDtypeStruct(mine.shape, jnp.bfloat16),
            jax.ShapeDtypeStruct(mine.shape, jnp.bfloat16),
        ),
        in_specs=[SMEM] + [VMEM] * 8,
        out_specs=(VMEM, VMEM, VMEM),
        scratch_shapes=[
            pltpu.VMEM((2,) + mine.shape, jnp.bfloat16),
            pltpu.VMEM((2,) + mine.shape, jnp.float32),
        ],
        compiler_params=params(),
        cost_estimate=pl.CostEstimate(
            flops=10 * pairs * HD, bytes_accessed=8 * mine.size, transcendentals=pairs
        ),
    )(place, query, mine, other, low, full, log_total, cosine, sine)


def gather_tp(value, axis):
    value = jnp.concatenate([value, swap(value, "tp", 2)], axis)
    return jnp.concatenate([value, swap(value, "tp", 1)], axis)


def scatter_tp(value):
    half, part = value.shape[0] // 2, value.shape[0] // 4
    other = swap(value[half:], "tp", 1)
    send = (value[part:half].astype(jnp.float32) + other[part:].astype(jnp.float32)).astype(
        jnp.bfloat16
    )
    last = swap(send, "tp", 2)
    return (
        value[:part].astype(jnp.float32)
        + other[:part].astype(jnp.float32)
        + last.astype(jnp.float32)
    )


def in_order(value, me):
    part = value.shape[0] // 4
    return jnp.concatenate(
        [
            lax.dynamic_slice_in_dim(value, reverse_bits(me ^ i, 2) * part, part, 0)
            for i in range(4)
        ],
        0,
    )


def on_device(
    layer_input,
    norm1_gain,
    w_query,
    b_query,
    w_key,
    b_key,
    w_value,
    b_value,
    w_out,
    norm2_gain,
    w_gate,
    w_up,
    w_down,
    doc_ids,
    positions,
    cotangent,
):
    tok_rows, width = layer_input.shape
    shards = lax.axis_size("cp")
    heads = w_query.shape[1] // HD
    kv_heads = w_key.shape[1] // HD
    me = lax.axis_index("cp")
    lane = lax.axis_index("tp")
    core = lane % 2
    kv_index = lane * heads // (H // kv_heads)
    is_key = core == 0

    middle_docs = doc_ids.reshape(shards, tok_rows)[:, HALF]
    my_doc = middle_docs[me]
    start = jnp.sum((middle_docs < my_doc).astype(jnp.int32))
    place = jnp.stack([me, core, lane, start]).astype(jnp.int32)
    my_pos = lax.dynamic_slice_in_dim(positions, me * tok_rows, tok_rows)
    cosine, sine = rope_tables(my_pos, HD)

    inputs = layer_input.astype(jnp.float32)
    scale1 = lax.rsqrt(jnp.mean(inputs * inputs, axis=-1, keepdims=True) + EPSILON)
    normed1 = (inputs * scale1 * norm1_gain).astype(jnp.bfloat16)

    def pair_weight(index):
        head = index * heads // (H // kv_heads)
        source = jnp.where(index % 2 == 0, w_key, w_value)
        return lax.dynamic_slice_in_dim(source, head * HD, HD, 1)

    pair_bias = lax.dynamic_slice_in_dim(jnp.where(is_key, b_key, b_value), kv_index * HD, HD)
    pair_cos = jnp.where(is_key, cosine, 1.0)
    pair_sin = jnp.where(is_key, sine, 0.0)
    pair_pre = matmul(normed1, pair_weight(lane)) + pair_bias
    pair = rotary(pair_pre, pair_cos, pair_sin).astype(jnp.bfloat16)[None]
    bit = shards // 2
    while bit:
        pair = jnp.concatenate([pair, swap(pair, "cp", bit)], 0)
        bit //= 2
    other = swap(pair, "tp", 1)

    q_pre = matmul(normed1, w_query) + b_query
    query = rotary(
        q_pre.reshape(tok_rows, heads, HD), cosine[:, None, :], sine[:, None, :]
    ).astype(jnp.bfloat16)
    query = query.transpose(1, 0, 2)

    attn, attn_full, log_total = attend(place, query, pair, other)
    w_out_all = gather_tp(w_out, 0)
    w_query_all = gather_tp(after(w_query, w_out_all), 1)
    cot_shared = share(place, after(cotangent, other), shards)
    normed1_shared = share(place, after(normed1, other), shards)

    middle = inputs + matmul(gather_tp(attn, 1), w_out_all)
    scale2 = lax.rsqrt(jnp.mean(middle * middle, axis=-1, keepdims=True) + EPSILON)
    normed2 = (middle * scale2 * norm2_gain).astype(jnp.bfloat16)

    units = w_gate.shape[1]
    chunks = pl.cdiv(pl.cdiv(units, TILE), CHUNK_TILES)
    hiddens, grads, total = [], [], None
    for index in range(chunks):
        hidden, grad, total = hidden_chunk(
            place, normed2, cotangent, w_gate, w_up, w_down, total, index
        )
        hiddens.append(hidden)
        grads.append(grad)
    normed2_shared = share(place, normed2, shards)

    downs, gates, ups = [], [], []
    for hidden, grad in zip(hiddens, grads):
        downs.append(weight_grad(place, cot_shared, hidden, shards).T)
        both = weight_grad(place, normed2_shared, grad, shards)
        span = hidden.shape[1]
        for at in range(0, span, TILE):
            size = min(TILE, span - at)
            gates.append(both[:, 2 * at : 2 * at + size])
            ups.append(both[:, 2 * at + TILE : 2 * at + TILE + size])
    grad_w_down = jnp.concatenate(downs, 0)
    grad_w_gate = jnp.concatenate(gates, 1)
    grad_w_up = jnp.concatenate(ups, 1)

    grad_normed2 = in_order(gather_tp(scatter_tp(total).astype(jnp.bfloat16), 0), lane).astype(
        jnp.float32
    )
    weighted2 = grad_normed2 * norm2_gain
    gain2_part = jnp.sum(grad_normed2 * middle * scale2, axis=0)
    grad_middle = (
        cotangent.astype(jnp.float32)
        + scale2 * weighted2
        - middle * scale2**3 * jnp.mean(weighted2 * middle, axis=-1, keepdims=True)
    )
    grad_branch = grad_middle.astype(jnp.bfloat16)
    grad_attn = contract_cols(grad_branch, w_out).astype(jnp.bfloat16)
    grad_query, keep, send = attend_back(
        place, query, pair, other, grad_attn, attn_full, log_total, cosine, sine
    )

    part = tok_rows // 4
    ffn = sum(matmul(h, lax.slice_in_dim(w_down, i * CHUNK_TILES * TILE, i * CHUNK_TILES * TILE + h.shape[1])) for i, h in enumerate(hiddens))
    ffn = after(ffn.astype(jnp.bfloat16), grad_middle)
    ffn_rel = jnp.concatenate(
        [lax.dynamic_slice_in_dim(ffn, (lane ^ far) * part, part, 0) for far in TP_ORDER], 0
    )
    out_part = scatter_tp(ffn_rel) + lax.dynamic_slice_in_dim(middle, lane * part, part, 0)
    output = in_order(gather_tp(out_part.astype(jnp.bfloat16), 0), lane)

    summed = keep.astype(jnp.float32) + swap(send, "tp", 1).astype(jnp.float32)
    bit = 1
    while bit < shards:
        count = summed.shape[0] // 2
        summed = summed[:count] + swap(summed[count:].astype(jnp.bfloat16), "cp", bit).astype(
            jnp.float32
        )
        bit *= 2
    grad_pair = rotary_back(summed[0], pair_cos, pair_sin).astype(jnp.bfloat16)

    branch_shared = share(place, grad_branch, shards)
    grad_w_out = weight_grad(place, branch_shared, attn, shards).T
    grad_w_query = weight_grad(place, normed1_shared, grad_query, shards)
    grad_w_pair = weight_grad(place, normed1_shared, grad_pair, shards)

    pairs_all = gather_tp(grad_pair, 1)
    grad_normed1 = contract_cols(gather_tp(grad_query, 1), w_query_all)
    for i, far in enumerate(TP_ORDER):
        grad_normed1 = grad_normed1 + contract_cols(
            pairs_all[:, i * HD : (i + 1) * HD], pair_weight(lane ^ far)
        )
    weighted1 = grad_normed1 * norm1_gain
    gain1_part = jnp.sum(grad_normed1 * inputs * scale1, axis=0)
    grad_input = (
        grad_middle
        + scale1 * weighted1
        - inputs * scale1**3 * jnp.mean(weighted1 * inputs, axis=-1, keepdims=True)
    ).astype(jnp.bfloat16)

    small = jnp.concatenate(
        [
            gain1_part,
            gain2_part,
            jnp.sum(grad_query.astype(jnp.float32), axis=0),
            jnp.sum(grad_pair.astype(jnp.float32), axis=0),
        ]
    ).reshape(-1, HD)
    bit = 1
    while bit < shards:
        small = small + swap(small, "cp", bit)
        bit *= 2
    wide = width // HD
    gain1_sum = small[:wide].reshape(-1)
    gain2_sum = small[wide : 2 * wide].reshape(-1)
    bias_query = small[2 * wide : 2 * wide + heads].reshape(-1)

    def assemble(parts, axis):
        at = lambda index: lax.dynamic_index_in_dim(parts, reverse_bits(lane ^ index, 2), 0, keepdims=False)
        return (
            jnp.concatenate([at(0), at(2)], axis),
            jnp.concatenate([at(1), at(3)], axis),
        )

    bias_key, bias_value = assemble(gather_tp(small[None, 2 * wide + heads], 0), 0)
    grad_w_key, grad_w_value = assemble(gather_tp(grad_w_pair[None], 0), 1)
    return (
        output,
        grad_input,
        gain1_sum,
        grad_w_query,
        bias_query,
        grad_w_key,
        bias_key,
        grad_w_value,
        bias_value,
        grad_w_out,
        gain2_sum,
        grad_w_gate,
        grad_w_up,
        grad_w_down,
    )


def solution(mesh):
    return jax.shard_map(
        on_device,
        mesh=mesh,
        in_specs=(
            P("cp", None),
            P(),
            P(None, "tp"),
            P("tp"),
            P(),
            P(),
            P(),
            P(),
            P("tp", None),
            P(),
            P(None, "tp"),
            P(None, "tp"),
            P("tp", None),
            P(),
            P(),
            P("cp", None),
        ),
        out_specs=(
            P("cp", None),
            P("cp", None),
            P(),
            P("cp", "tp"),
            P("tp"),
            P("cp", None),
            P(),
            P("cp", None),
            P(),
            P("tp", "cp"),
            P(),
            P("cp", "tp"),
            P("cp", "tp"),
            P("tp", "cp"),
        ),
        check_vma=False,
    )
```

```python
import functools
import math

import jax
import jax.numpy as jnp
from jax import lax
from jax.experimental import pallas as pl
from jax.experimental.pallas import tpu as pltpu
from jax.sharding import PartitionSpec as P

H = 12
HD = 128
HALF = 128
EPSILON = 1e-06
ROPE_BASE = 10000.0
MASKED = -1e30
LOG2E = 1.4426950408889634
TILE = 256
CHUNK_TILES = 3
VMEM_LIMIT = 56 * 1024 * 1024
TP_ORDER = (0, 2, 1, 3)


def matmul(left, right):
    return jnp.dot(left, right, preferred_element_type=jnp.float32)


def contract_rows(left, right):
    return lax.dot_general(
        left, right, (((0,), (0,)), ((), ())), preferred_element_type=jnp.float32
    )


def contract_cols(left, right):
    return lax.dot_general(
        left, right, (((1,), (1,)), ((), ())), preferred_element_type=jnp.float32
    )


def rope_tables(tok_pos, width):
    half = width // 2
    freq = ROPE_BASE ** (-(jnp.arange(half, dtype=jnp.float32) * 2.0 / width))
    angle = tok_pos.astype(jnp.float32)[:, None] * freq[None, :]
    cosine = jnp.concatenate([jnp.cos(angle), jnp.cos(angle)], -1)
    sine = jnp.concatenate([jnp.sin(angle), jnp.sin(angle)], -1)
    return (cosine, sine)


def rotary(values, cosine, sine):
    half = values.shape[-1] // 2
    return values * cosine + jnp.concatenate([-values[..., half:], values[..., :half]], -1) * sine


def rotary_back(grads, cosine, sine):
    half = grads.shape[-1] // 2
    scaled = grads * sine
    return grads * cosine + jnp.concatenate([scaled[..., half:], -scaled[..., :half]], -1)


def swap(value, axis, bit):
    size = lax.axis_size(axis)
    return lax.ppermute(value, axis, [(i, i ^ bit) for i in range(size)])


def after(value, *earlier):
    return lax.optimization_barrier((value, *earlier))[0]


def bits_of(size):
    return size.bit_length() - 1


def reverse_bits(index, bits):
    out = 0
    for i in range(bits):
        out = out | (((index >> i) & 1) << (bits - 1 - i))
    return out


def params(**more):
    return pltpu.CompilerParams(vmem_limit_bytes=VMEM_LIMIT, **more)


SMEM = pl.BlockSpec(memory_space=pltpu.SMEM)
VMEM = pl.BlockSpec(memory_space=pltpu.VMEM)


def spread_kernel(shards, place_ref, rows_ref, own_ref, send_ref, turned):
    me, core = place_ref[0], place_ref[1]
    turned[...] = rows_ref[...].T
    width = turned.shape[0] // shards
    bits = bits_of(shards)
    for i in range(shards // 2):
        far = reverse_bits(i, bits)
        block = pl.multiple_of((me ^ far) * width, 16)
        own_ref[i * width : (i + 1) * width, :] = turned[pl.ds(block, width), :]
    for i in range(shards // 4):
        far = reverse_bits(core * (shards // 4) + i, bits) | 1
        block = pl.multiple_of((me ^ far) * width, 16)
        send_ref[i * width : (i + 1) * width, :] = turned[pl.ds(block, width), :]


def spread(place, rows, shards):
    count, width = rows.shape
    return pl.pallas_call(
        functools.partial(spread_kernel, shards),
        out_shape=(
            jax.ShapeDtypeStruct((width // 2, count), rows.dtype),
            jax.ShapeDtypeStruct((width // 4, count), rows.dtype),
        ),
        in_specs=[SMEM, VMEM],
        out_specs=(VMEM, VMEM),
        scratch_shapes=[pltpu.VMEM((width, count), rows.dtype)],
        compiler_params=params(),
        cost_estimate=pl.CostEstimate(flops=0, bytes_accessed=4 * rows.size, transcendentals=0),
    )(place, rows)


def share(place, rows, shards):
    own, send = spread(place, rows, shards)
    near = swap(send, "cp", 1)
    return own, near, swap(near, "tp", 1)


def weigh_kernel(place_ref, own_ref, near_ref, far_ref, mine_ref, theirs_ref, send_ref, keep_ref, joined):
    core = place_ref[1]

    @pl.when(pl.program_id(0) == 0)
    def _():
        joined[core] = near_ref[...]
        joined[1 - core] = far_ref[...]

    half = send_ref.shape[0]
    mine, theirs = mine_ref[...], theirs_ref[...]
    send_ref[...] = (
        matmul(own_ref[half:, :], mine) + matmul(joined[1], theirs)
    ).astype(send_ref.dtype)
    keep_ref[...] = (
        matmul(own_ref[:half, :], mine) + matmul(joined[0], theirs)
    ).astype(keep_ref.dtype)


def weigh(place, shared, mine, theirs):
    own, near, far = shared
    half, count = near.shape
    width = mine.shape[1]
    tile = min(width, 512)
    whole = lambda j: (0, 0)
    column = lambda j: (0, j)
    return pl.pallas_call(
        weigh_kernel,
        grid=(pl.cdiv(width, tile),),
        out_shape=(jax.ShapeDtypeStruct((half, width), jnp.bfloat16),) * 2,
        in_specs=[
            SMEM,
            pl.BlockSpec((2 * half, count), whole),
            pl.BlockSpec((half, count), whole),
            pl.BlockSpec((half, count), whole),
            pl.BlockSpec((count, tile), column),
            pl.BlockSpec((count, tile), column),
        ],
        out_specs=(pl.BlockSpec((half, tile), column),) * 2,
        scratch_shapes=[pltpu.VMEM((2, half, count), jnp.bfloat16)],
        compiler_params=params(),
        cost_estimate=pl.CostEstimate(
            flops=8 * half * count * width,
            bytes_accessed=4 * (2 * half * count + count * width + half * width),
            transcendentals=0,
        ),
    )(place, own, near, far, mine, theirs)


def weight_grad(place, shared, mine, shards):
    theirs = swap(mine, "cp", 1)
    send, keep = weigh(place, shared, mine, theirs)
    terms = [keep]
    bit = 2
    while bit < shards:
        terms.append(swap(send, "cp", bit))
        bit *= 2
        if bit < shards:
            rows = terms[0].shape[0] // 2
            send = sum(t[rows:].astype(jnp.float32) for t in terms).astype(jnp.bfloat16)
            terms = [t[:rows] for t in terms]
    return sum(t.astype(jnp.float32) for t in terms)


def hidden_kernel(first, last, offset, units, *refs):
    place_ref, rows_ref, cot_ref, gate_ref, up_ref, down_ref = refs[:6]
    refs = refs[6:]
    if not first:
        before_ref, refs = refs[0], refs[1:]
    hidden_ref, grads_ref, sum_ref, total = refs
    step = pl.program_id(0)

    @pl.when(step == 0)
    def _():
        total[...] = jnp.zeros_like(total) if first else before_ref[...]

    rows = rows_ref[...]
    w_gate, w_up, w_down = gate_ref[...], up_ref[...], down_ref[...]
    if last:
        left = units - (offset + step) * TILE
        inside = lax.broadcasted_iota(jnp.int32, w_gate.shape, 1) < left
        w_gate = jnp.where(inside, w_gate, 0)
        w_up = jnp.where(inside, w_up, 0)
        inside = lax.broadcasted_iota(jnp.int32, w_down.shape, 0) < left
        w_down = jnp.where(inside, w_down, 0)
    gate = matmul(rows, w_gate)
    up_part = matmul(rows, w_up)
    grad_hidden = contract_cols(cot_ref[...], w_down)
    sigma = jax.nn.sigmoid(gate)
    swish = gate * sigma
    hidden_ref[...] = (swish * up_part).astype(jnp.bfloat16)
    grad_gate = (grad_hidden * up_part * sigma * (1.0 + gate * (1.0 - sigma))).astype(jnp.bfloat16)
    grad_up = (grad_hidden * swish).astype(jnp.bfloat16)
    grads_ref[:, :TILE] = grad_gate
    grads_ref[:, TILE:] = grad_up
    total[...] += contract_cols(grad_gate, w_gate) + contract_cols(grad_up, w_up)

    @pl.when(step == pl.num_programs(0) - 1)
    def _():
        if last:
            part = total.shape[0] // len(TP_ORDER)
            for i, far in enumerate(TP_ORDER):
                block = pl.multiple_of((place_ref[2] ^ far) * part, part)
                sum_ref[i * part : (i + 1) * part, :] = total[pl.ds(block, part), :].astype(
                    sum_ref.dtype
                )
        else:
            sum_ref[...] = total[...]


def hidden_chunk(place, rows, cotangent, w_gate, w_up, w_down, before, index):
    count, width = rows.shape
    units = w_gate.shape[1]
    tiles = pl.cdiv(units, TILE)
    offset = index * CHUNK_TILES
    steps = min(CHUNK_TILES, tiles - offset)
    first, last = index == 0, offset + steps == tiles
    inner = min(steps * TILE, units - offset * TILE)
    outer = (steps - 1) * 2 * TILE + TILE + inner - (steps - 1) * TILE
    whole = lambda j: (0, 0)
    column = lambda j: (0, j)
    in_specs = [
        SMEM,
        pl.BlockSpec((count, width), whole),
        pl.BlockSpec((count, width), whole),
        pl.BlockSpec((width, TILE), lambda j: (0, offset + j)),
        pl.BlockSpec((width, TILE), lambda j: (0, offset + j)),
        pl.BlockSpec((TILE, width), lambda j: (offset + j, 0)),
    ]
    operands = [place, rows, cotangent, w_gate, w_up, w_down]
    if not first:
        in_specs.append(pl.BlockSpec((count, width), whole))
        operands.append(before)
    return pl.pallas_call(
        functools.partial(hidden_kernel, first, last, offset, units),
        grid=(steps,),
        out_shape=(
            jax.ShapeDtypeStruct((count, inner), jnp.bfloat16),
            jax.ShapeDtypeStruct((count, outer), jnp.bfloat16),
            jax.ShapeDtypeStruct((count, width), jnp.bfloat16 if last else jnp.float32),
        ),
        in_specs=in_specs,
        out_specs=(
            pl.BlockSpec((count, TILE), column),
            pl.BlockSpec((count, 2 * TILE), column),
            pl.BlockSpec((count, width), whole),
        ),
        scratch_shapes=[pltpu.VMEM((count, width), jnp.float32)],
        compiler_params=params(),
        cost_estimate=pl.CostEstimate(
            flops=10 * count * width * inner,
            bytes_accessed=6 * width * inner + 12 * count * width,
            transcendentals=count * inner,
        ),
    )(*operands)


def region_rows(ref, start, count):
    return ref[:, start : start + count, :].reshape(-1, HD)


def triangle(rows, keys):
    row = lax.broadcasted_iota(jnp.int32, (rows, keys), 0) & (keys - 1)
    return row >= lax.broadcasted_iota(jnp.int32, (rows, keys), 1)


def regions(place_ref, shards, tok_rows):
    me, start = place_ref[0], place_ref[3]
    bits = bits_of(shards)

    def of_first(block):
        low = block < shards
        device = jnp.where(low, block, 2 * shards - 1 - block)
        return reverse_bits(device ^ me, bits), jnp.where(low, 0, tok_rows - HALF)

    def of_middle(block):
        return reverse_bits((start + block) ^ me, bits), HALF

    return (
        (0, HALF, me, of_first),
        (tok_rows - HALF, HALF, 2 * shards - 1 - me, of_first),
        (HALF, tok_rows - 2 * HALF, me - start, of_middle),
    )


def attend_kernel(shards, place_ref, q_ref, mine_ref, other_ref, low_ref, full_ref, log_ref, pair):
    core = place_ref[1]
    pair[core] = mine_ref[...]
    pair[1 - core] = other_ref[...]
    heads, tok_rows = q_ref.shape[0], q_ref.shape[1]
    factor = HD**-0.5 * LOG2E
    for begin, count, blocks, locate in regions(place_ref, shards, tok_rows):
        query = region_rows(q_ref, begin, count)
        rows = heads * count

        def read(which, block):
            slot, offset = locate(block)
            return pair[which, slot, pl.ds(pl.multiple_of(offset, HALF), count), :]

        mask = triangle(rows, count)
        last = jnp.where(mask, contract_cols(query, read(0, blocks)), MASKED)
        peak = lax.fori_loop(
            0, blocks, lambda t, top: jnp.maximum(top, contract_cols(query, read(0, t))), last
        )
        peak = jnp.max(peak, axis=1, keepdims=True) * factor

        def add(block, carry, scores):
            total, accum = carry
            weights = jnp.exp2(scores * factor - peak)
            return total + weights, accum + matmul(weights.astype(jnp.bfloat16), read(1, block))

        carry = add(blocks, (jnp.zeros((rows, count), jnp.float32), jnp.zeros((rows, HD), jnp.float32)), last)
        total, accum = lax.fori_loop(
            0, blocks, lambda t, held: add(t, held, contract_cols(query, read(0, t))), carry
        )
        total = jnp.sum(total, axis=1, keepdims=True)
        full = accum / total
        log_total = jnp.broadcast_to(peak + jnp.log2(total), (rows, HD))
        for head in range(heads):
            part = slice(head * count, (head + 1) * count)
            lanes = slice(head * HD, (head + 1) * HD)
            low_ref[begin : begin + count, lanes] = full[part].astype(jnp.bfloat16)
            full_ref[head, begin : begin + count, :] = full[part]
            log_ref[head, begin : begin + count, :] = log_total[part]


def attend(place, query, mine, other):
    heads, tok_rows, _ = query.shape
    shards = mine.shape[0]
    pairs = heads * tok_rows * tok_rows * shards // 4
    return pl.pallas_call(
        functools.partial(attend_kernel, shards),
        out_shape=(
            jax.ShapeDtypeStruct((tok_rows, heads * HD), jnp.bfloat16),
            jax.ShapeDtypeStruct((heads, tok_rows, HD), jnp.float32),
            jax.ShapeDtypeStruct((heads, tok_rows, HD), jnp.float32),
            jax.ShapeDtypeStruct((2,) + mine.shape, jnp.bfloat16),
        ),
        in_specs=[SMEM, VMEM, VMEM, VMEM],
        out_specs=(VMEM, VMEM, VMEM, VMEM),
        compiler_params=params(),
        cost_estimate=pl.CostEstimate(
            flops=6 * pairs * HD, bytes_accessed=4 * mine.size, transcendentals=pairs
        ),
    )(place, query, mine, other)


def attend_back_kernel(
    shards, place_ref, q_ref, pair, low_ref, full_ref, log_ref, cos_ref, sin_ref,
    query_ref, keep_ref, send_ref, grads,
):
    core = place_ref[1]
    grads[...] = jnp.zeros_like(grads)
    heads, tok_rows = q_ref.shape[0], q_ref.shape[1]
    scale = HD**-0.5
    factor = scale * LOG2E
    sign = jnp.where(lax.broadcasted_iota(jnp.int32, (1, HD), 1) < HD // 2, 1.0, -1.0)
    for begin, count, blocks, locate in regions(place_ref, shards, tok_rows):
        query = region_rows(q_ref, begin, count)
        rows = heads * count
        incoming = jnp.concatenate(
            [low_ref[begin : begin + count, h * HD : (h + 1) * HD] for h in range(heads)], 0
        )
        full = region_rows(full_ref, begin, count)
        log_total = region_rows(log_ref, begin, count)[:, :1]
        delta = jnp.sum(incoming.astype(jnp.float32) * full, axis=1, keepdims=True)

        def add(block, grad_query, mask=None):
            slot, offset = locate(block)
            place = pl.ds(pl.multiple_of(offset, HALF), count)
            keys, values = pair[0, slot, place, :], pair[1, slot, place, :]
            probs = jnp.exp2(contract_cols(query, keys) * factor - log_total)
            if mask is not None:
                probs = jnp.where(mask, probs, 0.0)
            grad_scores = (probs * (contract_cols(incoming, values) - delta)).astype(jnp.bfloat16)
            grads[0, slot, place, :] += contract_rows(grad_scores, query)
            grads[1, slot, place, :] += contract_rows(probs.astype(jnp.bfloat16), incoming)
            return grad_query + matmul(grad_scores, keys)

        grad_query = add(blocks, jnp.zeros((rows, HD), jnp.float32), triangle(rows, count))
        grad_query = lax.fori_loop(0, blocks, add, grad_query) * scale
        cosine, sine = cos_ref[begin : begin + count, :], sin_ref[begin : begin + count, :]
        for head in range(heads):
            part = grad_query[head * count : (head + 1) * count]
            turned = part * cosine + pltpu.roll(part * sine, HD // 2, 1) * sign
            query_ref[begin : begin + count, head * HD : (head + 1) * HD] = turned.astype(
                jnp.bfloat16
            )
    is_key = core == 0
    keep_ref[...] = (grads[core] * jnp.where(is_key, scale, 1.0)).astype(jnp.bfloat16)
    send_ref[...] = (grads[1 - core] * jnp.where(is_key, 1.0, scale)).astype(jnp.bfloat16)


def attend_back(place, query, pair, low, full, log_total, cosine, sine):
    heads, tok_rows, _ = query.shape
    shards = pair.shape[1]
    pairs = heads * tok_rows * tok_rows * shards // 4
    return pl.pallas_call(
        functools.partial(attend_back_kernel, shards),
        out_shape=(
            jax.ShapeDtypeStruct((tok_rows, heads * HD), jnp.bfloat16),
            jax.ShapeDtypeStruct(pair.shape[1:], jnp.bfloat16),
            jax.ShapeDtypeStruct(pair.shape[1:], jnp.bfloat16),
        ),
        in_specs=[SMEM] + [VMEM] * 7,
        out_specs=(VMEM, VMEM, VMEM),
        scratch_shapes=[pltpu.VMEM(pair.shape, jnp.float32)],
        compiler_params=params(),
        cost_estimate=pl.CostEstimate(
            flops=10 * pairs * HD, bytes_accessed=4 * pair.size, transcendentals=pairs
        ),
    )(place, query, pair, low, full, log_total, cosine, sine)


def gather_tp(value, axis):
    value = jnp.concatenate([value, swap(value, "tp", 2)], axis)
    return jnp.concatenate([value, swap(value, "tp", 1)], axis)


def scatter_tp(value):
    half, part = value.shape[0] // 2, value.shape[0] // 4
    other = swap(value[half:], "tp", 1)
    send = (value[part:half].astype(jnp.float32) + other[part:].astype(jnp.float32)).astype(
        jnp.bfloat16
    )
    last = swap(send, "tp", 2)
    return (
        value[:part].astype(jnp.float32)
        + other[:part].astype(jnp.float32)
        + last.astype(jnp.float32)
    )


def in_order(value, me):
    part = value.shape[0] // 4
    return jnp.concatenate(
        [
            lax.dynamic_slice_in_dim(value, reverse_bits(me ^ i, 2) * part, part, 0)
            for i in range(4)
        ],
        0,
    )


UNITS = 256
TOK = 512


def back_kernel(width, units, *refs):
    (
        docs_ref, gain_ref, attn_hbm, full_hbm, log_hbm, q_hbm, pair_hbm, x_hbm, cot_hbm,
        cot_turned_hbm, n1_turned_hbm, cos_hbm, sin_hbm, wo_hbm, wg_hbm, wu_hbm, wd_hbm,
        tiles_out, wo_out, wq_out, wp_out, gain_out, output_out, middle_out, query_out, pair_out,
        own_hbm, far_hbm, near1_hbm, near2_hbm,
        attn_all, attn_far, query_far, pair_far, middle, acc, turned,
        own_a, far_a, stage, far_stage, part_s, part_k, part_f, near1, part_s2, near2, final,
        rel, core_in, lane_send, lane_in, grad_full, out_core_in, out_lane_in,
        kv_send, kv_in, grad_query, grad_pair, small_s, small_in, small_s2, small_in2,
        send_sem, recv_sem, local_sem, weight_sem,
    ) = refs
    me = lax.axis_index("cp")
    lane = lax.axis_index("tp")
    b0, b1, b2 = me % 2, (me // 2) % 2, me // 4
    core, high = lane % 2, lane // 2
    x_to = {"cp": me + 1 - 2 * b0}
    z1_to = {"cp": me + 2 - 4 * b1}
    z2_to = {"cp": me + 4 - 8 * b2}
    c_to = {"tp": lane + 1 - 2 * core}
    y_to = {"tp": lane + 2 - 4 * high}
    lane_c, lane_y = lane + 1 - 2 * core, lane + 2 - 4 * high
    lane_cy = 3 - lane
    tiles = pl.cdiv(units, UNITS)
    rest = units - (tiles - 1) * UNITS
    block = width // 8
    half = width // 4
    quarter = TOK // 4
    scale = HD**-0.5
    factor = scale * LOG2E
    used = {"remote": 0, "local": 0}

    def remote(src, dst, to, count=1):
        index = used["remote"]
        used["remote"] += 1
        return pltpu.make_async_remote_copy(
            src_ref=src, dst_ref=dst, send_sem=send_sem.at[index], recv_sem=recv_sem.at[index],
            device_id=to, device_id_type=pl.DeviceIdType.MESH,
        )

    def local(src, dst):
        index = used["local"]
        used["local"] += 1
        return pltpu.make_async_copy(src, dst, local_sem.at[index])

    def started(*copies):
        for copy in copies:
            copy.start()
        return copies[0] if len(copies) == 1 else copies

    def row_block(side, h, i):
        mine = (b0 + side) % 2 + 2 * ((b1 + h) % 2) + 4 * ((b2 + i) % 2)
        return pl.ds(pl.multiple_of(mine * block, 16), block)

    def rows_of(index):
        return pl.ds(pl.multiple_of(index * quarter, quarter), quarter)

    base = used["remote"]
    used["remote"] += 3 * tiles

    def tile_copy(kind, src, dst, t, to):
        index = base + kind * tiles + t
        return pltpu.make_async_remote_copy(
            src_ref=src, dst_ref=dst, send_sem=send_sem.at[index], recv_sem=recv_sem.at[index],
            device_id=to, device_id_type=pl.DeviceIdType.MESH,
        )

    def x_tile(t):
        return tile_copy(0, own_hbm.at[t], far_hbm.at[t], t, x_to)

    def z1_tile(t):
        return tile_copy(1, part_s.at[t % 2], near1_hbm.at[t], t, z1_to)

    def z2_tile(t):
        return tile_copy(2, part_s2.at[t % 2], near2_hbm.at[t], t, z2_to)

    barrier = pltpu.get_barrier_semaphore()
    for to in (x_to, z1_to, z2_to, c_to, y_to):
        pl.semaphore_signal(barrier, inc=1, device_id=to, device_id_type=pl.DeviceIdType.MESH)
    pl.semaphore_wait(barrier, 5)

    def share(source, index):
        return [
            remote(
                source.at[row_block(1, core, i)],
                far_a.at[index, core, pl.ds(i * block, block)],
                x_to,
            )
            for i in range(2)
        ]

    def forward(index):
        return remote(far_a.at[index, core], far_a.at[index, core], c_to)

    COT, N2, GB, N1 = range(4)
    attn_y = remote(attn_hbm, attn_all.at[1], y_to)
    attn_c = remote(attn_hbm, attn_all.at[2], c_to)
    attn_cy = remote(attn_all.at[1], attn_all.at[3], c_to)
    attn_x = remote(attn_hbm, attn_far, x_to)
    attn_own = local(attn_hbm, attn_all.at[0])
    started(attn_y, attn_c, attn_own)
    cot_x = share(cot_turned_hbm, COT)
    started(*cot_x)
    started(attn_x)
    n1_x = share(n1_turned_hbm, N1)
    started(*n1_x)
    own_loads = []
    for index, source in ((COT, cot_turned_hbm), (N1, n1_turned_hbm)):
        for p in range(4):
            own_loads.append(
                local(
                    source.at[row_block(0, p // 2, p % 2)],
                    own_a.at[index, pl.ds(p * block, block)],
                )
            )
    started(*own_loads)

    def norm_scale(rows):
        return lax.rsqrt(jnp.mean(rows * rows, axis=-1, keepdims=True) + EPSILON)

    gain = gain_ref[...]
    n2_x = share(turned, N2)

    def front(weights, cot_turned, ring, wo, x_rows):
        def fetch(t, slot, rows):
            return [
                pltpu.make_async_copy(
                    source.at[pl.ds(t * UNITS, rows)],
                    weights.at[slot, k, pl.ds(0, rows)],
                    weight_sem.at[slot, k],
                )
                for k, source in enumerate((wg_hbm, wu_hbm, wd_hbm))
            ]

        loads = [local(wo_hbm, wo), local(x_hbm, x_rows), local(cot_turned_hbm, cot_turned)]
        started(*loads)
        started(*fetch(0, 0, UNITS))
        loads[0].wait()
        loads[1].wait()

        def add_part(p, first=False):
            def body(n, carry):
                cols = pl.ds(pl.multiple_of(n * 512, 512), 512)
                held = x_rows[:, cols].astype(jnp.float32) if first else middle[:, cols]
                middle[:, cols] = held + matmul(attn_all[p], wo[p, :, cols])
                return carry

            lax.fori_loop(0, width // 512, body, 0)

        attn_own.wait()
        add_part(0, True)
        attn_c.wait_recv()
        add_part(2)
        attn_y.wait_recv()
        started(attn_cy)
        add_part(1)
        attn_cy.wait_recv()
        add_part(3)

        def norm(a, carry):
            rows = middle[rows_of(a), :]
            turned[:, rows_of(a)] = (rows * norm_scale(rows) * gain).astype(jnp.bfloat16).T
            return carry

        lax.fori_loop(0, 4, norm, 0)
        started(*n2_x)
        for p in range(4):
            own_a[N2, p * block : (p + 1) * block, :] = turned[row_block(0, p // 2, p % 2), :]
        loads[2].wait()
        acc[...] = jnp.zeros_like(acc)

        def keep_tile(t):
            return pltpu.make_async_copy(ring.at[t % 2], own_hbm.at[t], weight_sem.at[2, t % 2])

        def tile(t, carry):
            slot = t % 2

            @pl.when(t < tiles - 1)
            def _():
                for copy in fetch(t, slot, UNITS):
                    copy.wait()

            @pl.when(t == tiles - 1)
            def _():
                for copy in fetch(t, slot, rest):
                    copy.wait()

            @pl.when(t + 1 < tiles - 1)
            def _():
                started(*fetch(t + 1, 1 - slot, UNITS))

            @pl.when(t + 1 == tiles - 1)
            def _():
                weights[1 - slot, :, rest:, :] = jnp.zeros(
                    (3, UNITS - rest, width), weights.dtype
                )
                started(*fetch(t + 1, 1 - slot, rest))

            gate = matmul(weights[slot, 0], turned[...])
            up_part = matmul(weights[slot, 1], turned[...])
            grad_hidden = matmul(weights[slot, 2], cot_turned[...])
            sigma = jax.nn.sigmoid(gate)
            swish = gate * sigma
            ring[slot, :, :UNITS] = (swish * up_part).astype(jnp.bfloat16).T
            ring[slot, :, UNITS : 2 * UNITS] = (
                (grad_hidden * up_part * sigma * (1.0 + gate * (1.0 - sigma)))
                .astype(jnp.bfloat16)
                .T
            )
            ring[slot, :, 2 * UNITS :] = (grad_hidden * swish).astype(jnp.bfloat16).T

            def body(n, carry):
                cols = pl.ds(pl.multiple_of(n * 512, 512), 512)
                acc[:, cols] += matmul(
                    ring[slot, :, UNITS : 2 * UNITS], weights[slot, 0, :, cols]
                ) + matmul(ring[slot, :, 2 * UNITS :], weights[slot, 1, :, cols])
                return carry

            lax.fori_loop(0, width // 512, body, 0)

            @pl.when(t > 0)
            def _():
                keep_tile(t - 1).wait()

            @pl.when((t > 0) & (t <= AHEAD))
            def _():
                x_tile(t - 1).start()

            keep_tile(t).start()
            return carry

        lax.fori_loop(0, tiles, tile, 0)
        keep_tile(tiles - 1).wait()
        for copy in n2_x:
            copy.wait_send()

    pl.run_scoped(
        front,
        pltpu.VMEM((2, 3, UNITS, width), jnp.bfloat16),
        pltpu.VMEM((width, TOK), jnp.bfloat16),
        pltpu.VMEM((2, TOK, 3 * UNITS), jnp.bfloat16),
        pltpu.VMEM((4, width // 4, width), jnp.bfloat16),
        pltpu.VMEM((TOK, width), jnp.bfloat16),
    )

    def reduce_start(total, sent, core_to):
        sent[...] = total[...].astype(jnp.bfloat16)
        copies = [
            remote(sent.at[rows_of(lane_c)], core_to.at[0], c_to),
            remote(sent.at[rows_of(lane_cy)], core_to.at[1], c_to),
        ]
        started(*copies)
        return copies

    def reduce_middle(total, copies, core_to, lane_to):
        for copy in copies:
            copy.wait()
        lane_send[...] = (
            total[rows_of(lane_y), :] + core_to[1].astype(jnp.float32)
        ).astype(jnp.bfloat16)
        copy = remote(lane_send, lane_to, y_to)
        copy.start()
        return copy

    def reduce_end(total, copy, core_to, lane_to):
        copy.wait()
        return (
            total[rows_of(lane), :]
            + core_to[0].astype(jnp.float32)
            + lane_to[...].astype(jnp.float32)
        )

    def spread_start(full):
        mine, theirs = full.at[rows_of(lane)], full.at[rows_of(lane_y)]
        copies = [
            remote(mine, mine, y_to),
            remote(mine, mine, c_to),
            remote(theirs, theirs, c_to),
        ]
        started(*copies[:2])
        return copies

    def spread_end(copies):
        copies[0].wait_recv()
        copies[2].start()
        copies[0].wait_send()
        copies[1].wait()
        copies[2].wait()

    def first_product(a, b_own, b_far, h, index):
        return matmul(own_a[index, h * half : (h + 1) * half, :], b_own) + matmul(
            far_a[index, h], b_far
        )

    tile_loads = {}

    def load_own(t):
        tile_loads[t] = started(local(own_hbm.at[t], stage.at[t % 2]))

    def first_step(t):
        slot = t % 2
        if t not in tile_loads:
            load_own(t)
        x_tile(t).wait_recv()
        far_load = started(local(far_hbm.at[t], far_stage))
        if t + AHEAD < tiles:
            x_tile(t + AHEAD).start()
        tile_loads[t].wait()
        far_load.wait()
        if t >= 2:
            z1_tile(t - 2).wait_send()

        def body(n, h):
            cols = pl.ds(pl.multiple_of(n * UNITS, UNITS), UNITS)
            index = (n + 1) // 2
            return cols, matmul(
                own_a[index, h * half : (h + 1) * half, :], stage[slot, :, cols]
            ) + matmul(far_a[index, h], far_stage[:, cols])

        def sent(n, carry):
            cols, value = body(n, 1)
            part_s[slot, :, cols] = value.astype(jnp.bfloat16)
            return carry

        def kept(n, carry):
            cols, value = body(n, 0)
            part_k[slot, :, cols] = value.astype(jnp.bfloat16)
            return carry

        lax.fori_loop(0, 3, sent, 0)
        z1_tile(t).start()
        lax.fori_loop(0, 3, kept, 0)
        if t + 1 < tiles:
            load_own(t + 1)

    def second_step(t):
        slot = t % 2
        z1_tile(t).wait_recv()
        load = started(local(near1_hbm.at[t], near1))
        load.wait()
        if t >= 2:
            z2_tile(t - 2).wait_send()
        part_s2[slot] = (
            part_k[slot, block:, :].astype(jnp.float32) + near1[block:, :].astype(jnp.float32)
        ).astype(jnp.bfloat16)
        z2_tile(t).start()
        part_f[slot] = part_k[slot, :block, :].astype(jnp.float32) + near1[:block, :].astype(
            jnp.float32
        )

    final_copies = {}

    def third_step(t):
        slot = t % 2
        z2_tile(t).wait_recv()
        load = started(local(near2_hbm.at[t], near2))
        load.wait()
        if t >= 2:
            final_copies[t - 2].wait()
        final[slot] = part_f[slot] + near2[...].astype(jnp.float32)
        final_copies[t] = started(local(final.at[slot], tiles_out.at[t]))

    def step(t):
        if t < tiles:
            first_step(t)
        if 0 <= t - 1 < tiles:
            second_step(t - 1)
        if 0 <= t - 2 < tiles:
            third_step(t - 2)

    SMALL = {"out": (0, 384, GB), "query": (384, 384, N1), "pair": (768, 128, N1)}
    small_copies = {}

    def small_first(name, b_own, b_far):
        begin, wide, index = SMALL[name]
        cols = slice(begin, begin + wide)
        small_s[half:, cols] = (
            matmul(own_a[index, half:, :], b_own) + matmul(far_a[index, 1], b_far)
        ).astype(jnp.bfloat16)
        copy = remote(small_s.at[pl.ds(half, half), pl.ds(begin, wide)], small_in.at[:, pl.ds(begin, wide)], z1_to)
        copy.start()
        small_copies[name] = copy
        small_s[:half, cols] = (
            matmul(own_a[index, :half, :], b_own) + matmul(far_a[index, 0], b_far)
        ).astype(jnp.bfloat16)

    def small_second(name):
        begin, wide, _ = SMALL[name]
        cols = slice(begin, begin + wide)
        small_copies[name].wait_recv()
        small_s2[:, cols] = (
            small_s[block:half, cols].astype(jnp.float32)
            + small_in[block:, cols].astype(jnp.float32)
        ).astype(jnp.bfloat16)
        copy = remote(small_s2.at[:, pl.ds(begin, wide)], small_in2.at[:, pl.ds(begin, wide)], z2_to)
        copy.start()
        small_copies[name].wait_send()
        small_copies[name] = copy

    def small_third(name, out_ref):
        begin, wide, _ = SMALL[name]
        cols = slice(begin, begin + wide)
        small_copies[name].wait()
        out_ref[...] = (
            small_s[:block, cols].astype(jnp.float32)
            + small_in[:block, cols].astype(jnp.float32)
            + small_in2[:, cols].astype(jnp.float32)
        )

    def rest_of(cot, query, pair, full, log_total, cosine, sine, grads, incoming, wo_own):
        loads = [
            local(cot_hbm, cot),
            local(q_hbm, query),
            local(pair_hbm, pair),
            local(full_hbm, full),
            local(log_hbm, log_total),
            local(cos_hbm, cosine),
            local(sin_hbm, sine),
            local(wo_hbm.at[0], wo_own),
        ]
        started(*loads)
        copies = reduce_start(acc, rel, core_in)
        forwards = []
        for index, parts in ((COT, cot_x), (N1, n1_x), (N2, n2_x)):
            for copy in parts:
                copy.wait_recv()
            forwards.append(started(forward(index)))
        lane_copy = reduce_middle(acc, copies, core_in, lane_in)
        for load in own_loads:
            load.wait()
        for copy in forwards:
            copy.wait()
        step(0)
        grad_full[rows_of(lane), :] = reduce_end(acc, lane_copy, core_in, lane_in).astype(
            jnp.bfloat16
        )
        spread = spread_start(grad_full)
        for copy in cot_x + n1_x:
            copy.wait_send()
        grads[...] = jnp.zeros_like(grads)
        spread_end(spread)
        for load in loads:
            load.wait()

        def middle_back(a, total):
            grad = grad_full[rows_of(a), :].astype(jnp.float32)
            rows = middle[rows_of(a), :]
            factor2 = norm_scale(rows)
            weighted = grad * gain
            result = (
                cot[rows_of(a), :].astype(jnp.float32)
                + factor2 * weighted
                - rows * factor2**3 * jnp.mean(weighted * rows, axis=-1, keepdims=True)
            )
            acc[rows_of(a), :] = result
            turned[:, rows_of(a)] = result.astype(jnp.bfloat16).T
            return total + jnp.sum(grad * rows * factor2, axis=0, keepdims=True)

        gain_out[...] = lax.fori_loop(0, 4, middle_back, jnp.zeros((1, width), jnp.float32))
        middle_copy = started(local(acc, middle_out))
        branch_x = share(turned, GB)
        started(*branch_x)
        incoming[...] = matmul(wo_own[...], turned[...]).astype(jnp.bfloat16).T
        for p in range(4):
            own_a[GB, p * block : (p + 1) * block, :] = turned[row_block(0, p // 2, p % 2), :]
        step(1)

        sign = jnp.where(lax.broadcasted_iota(jnp.int32, (1, HD), 1) < HD // 2, 1.0, -1.0)

        def of_first(t):
            late = t // 8
            device = t * (1 - late) + (15 - t) * late
            return device, late * (TOK - HALF)

        def of_middle(t):
            return t, HALF

        def region(begin, count, blocks, locate, shared):
            heads = query.shape[0]
            rows = heads * count
            q_rows = region_rows(query, begin, count)
            grad_rows = jnp.concatenate(
                [incoming[begin : begin + count, h * HD : (h + 1) * HD] for h in range(heads)], 0
            )
            logs = region_rows(log_total, begin, count)[:, :1]
            delta = jnp.sum(
                grad_rows.astype(jnp.float32) * region_rows(full, begin, count),
                axis=1,
                keepdims=True,
            )

            def add(t, carry, diagonal=False):
                device, offset = locate(t)
                slot = (
                    4 * ((device % 2 + b0) % 2)
                    + 2 * (((device // 2) % 2 + b1) % 2)
                    + (device // 4 + b2) % 2
                )
                place = pl.ds(pl.multiple_of(offset, HALF), count)
                keys, values = pair[0, slot, place, :], pair[1, slot, place, :]
                probs = jnp.exp2(contract_cols(q_rows, keys) * factor - logs)
                if diagonal:
                    probs = jnp.where(triangle(rows, count), probs, 0.0)
                elif shared:
                    same = docs_ref[pl.ds(device, 1), :] == docs_ref[pl.ds(me, 1), :]
                    probs = jnp.where(same, probs, 0.0)
                grad_scores = (probs * (contract_cols(grad_rows, values) - delta)).astype(
                    jnp.bfloat16
                )
                grads[0, slot, place, :] += contract_rows(grad_scores, q_rows)
                grads[1, slot, place, :] += contract_rows(probs.astype(jnp.bfloat16), grad_rows)
                return carry + matmul(grad_scores, keys)

            total = add(blocks, jnp.zeros((rows, HD), jnp.float32), True)
            total = lax.fori_loop(0, blocks, add, total) * scale
            cosines, sines = cosine[begin : begin + count, :], sine[begin : begin + count, :]
            for h in range(heads):
                part = total[h * count : (h + 1) * count]
                grad_query[begin : begin + count, h * HD : (h + 1) * HD] = (
                    part * cosines + pltpu.roll(part * sines, HD // 2, 1) * sign
                ).astype(jnp.bfloat16)

        region(0, HALF, me, of_first, False)
        region(TOK - HALF, HALF, 15 - me, of_first, False)
        step(2)
        region(HALF, TOK - 2 * HALF, me, of_middle, True)

        is_key = jnp.where(core == 0, 1.0, 0.0)
        keep_by = is_key * scale + (1.0 - is_key)
        send_by = (1.0 - is_key) * scale + is_key

        def to_core(s, carry):
            kv_send[s] = (grads[1 - core, s] * send_by).astype(jnp.bfloat16)
            return carry

        lax.fori_loop(0, 8, to_core, 0)
        kv_c = remote(kv_send.at[pl.ds(0, 8)], kv_in.at[pl.ds(0, 8)], c_to)
        kv_x = remote(kv_send.at[pl.ds(8, 4)], kv_in.at[pl.ds(8, 4)], x_to)
        kv_1 = remote(kv_send.at[pl.ds(12, 2)], kv_in.at[pl.ds(12, 2)], z1_to)
        kv_2 = remote(kv_send.at[pl.ds(14, 1)], kv_in.at[pl.ds(14, 1)], z2_to)
        kv_c.start()
        query_x = remote(grad_query, query_far, x_to)
        query_y = remote(grad_query, query_out.at[1], y_to)
        query_c = remote(grad_query, query_out.at[2], c_to)
        query_cy = remote(query_out.at[1], query_out.at[3], c_to)
        query_own = local(grad_query, query_out.at[0])
        started(query_x, query_y, query_c, query_own)
        for copy in branch_x:
            copy.wait()
        branch_c = started(forward(GB))
        kv_c.wait()

        def from_core(s, carry):
            grads[core, s] = grads[core, s] * keep_by + kv_in[s].astype(jnp.float32)
            return carry

        lax.fori_loop(0, 8, from_core, 0)

        def pass_on(copy, first, count):
            def cast(s, carry):
                kv_send[first + s] = grads[core, count + s].astype(jnp.bfloat16)
                return carry

            lax.fori_loop(0, count, cast, 0)
            copy.start()

        def take(copy, first, count):
            copy.wait()

            def add(s, carry):
                grads[core, s] += kv_in[first + s].astype(jnp.float32)
                return carry

            lax.fori_loop(0, count, add, 0)

        pass_on(kv_x, 8, 4)
        step(3)
        attn_x.wait()
        branch_c.wait()
        small_first("out", attn_all[0], attn_far[...])
        query_y.wait_recv()
        query_cy.start()
        take(kv_x, 8, 4)
        pass_on(kv_1, 12, 2)

        def down(weights, hidden):
            def fetch(t, slot, rows):
                return [
                    pltpu.make_async_copy(
                        wd_hbm.at[pl.ds(t * UNITS, rows)],
                        weights.at[slot, pl.ds(0, rows)],
                        weight_sem.at[slot, 0],
                    ),
                    pltpu.make_async_copy(
                        own_hbm.at[t, :, pl.ds(0, UNITS)], hidden.at[slot], weight_sem.at[slot, 1]
                    ),
                ]

            started(*fetch(0, 0, UNITS))

            def tile(t, carry):
                slot = t % 2

                @pl.when(t < tiles - 1)
                def _():
                    for copy in fetch(t, slot, UNITS):
                        copy.wait()

                @pl.when(t == tiles - 1)
                def _():
                    for copy in fetch(t, slot, rest):
                        copy.wait()

                @pl.when(t + 1 < tiles - 1)
                def _():
                    started(*fetch(t + 1, 1 - slot, UNITS))

                @pl.when(t + 1 == tiles - 1)
                def _():
                    weights[1 - slot, rest:, :] = jnp.zeros((UNITS - rest, width), weights.dtype)
                    started(*fetch(t + 1, 1 - slot, rest))

                def body(n, carry):
                    cols = pl.ds(pl.multiple_of(n * 512, 512), 512)
                    product = matmul(hidden[slot], weights[slot, :, cols])
                    acc[:, cols] = jnp.where(t == 0, product, acc[:, cols] + product)
                    return carry

                lax.fori_loop(0, width // 512, body, 0)
                return carry

            lax.fori_loop(0, tiles, tile, 0)

        middle_copy.wait()
        pl.run_scoped(
            down,
            pltpu.VMEM((2, UNITS, width), jnp.bfloat16),
            pltpu.VMEM((2, TOK, UNITS), jnp.bfloat16),
        )
        out_copies = reduce_start(acc, rel, out_core_in)
        step(4)
        small_second("out")
        take(kv_1, 12, 2)
        pass_on(kv_2, 14, 1)
        out_lane = reduce_middle(acc, out_copies, out_core_in, out_lane_in)
        query_x.wait()
        small_first("query", grad_query[...], query_far[...])
        step(5)
        small_third("out", wo_out)
        kv_2.wait()
        f_cos = cosine[...] * is_key + (1.0 - is_key)
        f_sin = sine[...] * is_key
        total = grads[core, 0] + kv_in[14].astype(jnp.float32)
        grad_pair[...] = (total * f_cos + pltpu.roll(total * f_sin, HD // 2, 1) * sign).astype(
            jnp.bfloat16
        )
        pair_x = remote(grad_pair, pair_far, x_to)
        pair_y = remote(grad_pair, pair_out.at[1], y_to)
        pair_c = remote(grad_pair, pair_out.at[2], c_to)
        pair_cy = remote(pair_out.at[1], pair_out.at[3], c_to)
        pair_own = local(grad_pair, pair_out.at[0])
        started(pair_x, pair_y, pair_c, pair_own)
        out_rows = reduce_end(acc, out_lane, out_core_in, out_lane_in) + middle[rows_of(lane), :]
        grad_full[rows_of(lane), :] = out_rows.astype(jnp.bfloat16)
        here = output_out.at[rows_of(lane)]
        there = output_out.at[rows_of(lane_y)]
        out_spread = [
            remote(grad_full.at[rows_of(lane)], here, y_to),
            remote(grad_full.at[rows_of(lane)], here, c_to),
            remote(there, there, c_to),
        ]
        out_own = local(grad_full.at[rows_of(lane)], here)
        started(out_spread[0], out_spread[1], out_own)
        small_second("query")
        step(6)
        pair_x.wait()
        small_first("pair", grad_pair[...], pair_far[...])
        pair_y.wait_recv()
        pair_cy.start()
        small_third("query", wq_out)
        out_spread[0].wait_recv()
        out_spread[2].start()
        step(7)
        small_second("pair")
        step(8)
        small_third("pair", wp_out)
        step(9)
        step(10)
        for t in (tiles - 2, tiles - 1):
            z1_tile(t).wait_send()
            z2_tile(t).wait_send()
            final_copies[t].wait()
        for t in range(tiles):
            x_tile(t).wait_send()
        for copy in (attn_y, attn_c, attn_cy, query_y, pair_y, out_spread[0]):
            copy.wait_send()
        for copy in (query_c, query_cy, pair_c, pair_cy, out_spread[1], out_spread[2]):
            copy.wait()
        for copy in (query_own, pair_own, out_own):
            copy.wait()

    pl.run_scoped(
        rest_of,
        pltpu.VMEM((TOK, width), jnp.bfloat16),
        pltpu.VMEM((3, TOK, HD), jnp.bfloat16),
        pltpu.VMEM((2, 8, TOK, HD), jnp.bfloat16),
        pltpu.VMEM((3, TOK, HD), jnp.float32),
        pltpu.VMEM((3, TOK, HD), jnp.float32),
        pltpu.VMEM((TOK, HD), jnp.float32),
        pltpu.VMEM((TOK, HD), jnp.float32),
        pltpu.VMEM((2, 8, TOK, HD), jnp.float32),
        pltpu.VMEM((TOK, 3 * HD), jnp.bfloat16),
        pltpu.VMEM((width // 4, width), jnp.bfloat16),
    )
    assert used["remote"] <= REMOTE and used["local"] <= LOCAL, used


AHEAD = 3
REMOTE = 96
LOCAL = 96


def back(docs, gain, attn, full, log_total, query, pair, x, cot, normed1, cosine, sine, wo, wg, wu, wd):
    tok_rows, width = x.shape
    units = wg.shape[0]
    tiles = pl.cdiv(units, UNITS)
    half, block, quarter = width // 4, width // 8, tok_rows // 4
    low, wide = jnp.bfloat16, jnp.float32
    shape = jax.ShapeDtypeStruct
    any_ = pl.BlockSpec(memory_space=pl.ANY)
    outs = (
        shape((tiles, block, 3 * UNITS), wide),
        shape((block, 384), wide),
        shape((block, 384), wide),
        shape((block, HD), wide),
        shape((1, width), wide),
        shape((tok_rows, width), low),
        shape((tok_rows, width), wide),
        shape((4, tok_rows, 384), low),
        shape((4, tok_rows, HD), low),
        shape((tiles, tok_rows, 3 * UNITS), low),
        shape((tiles, tok_rows, 3 * UNITS), low),
        shape((tiles, half, 3 * UNITS), low),
        shape((tiles, block, 3 * UNITS), low),
    )
    vmem = pltpu.VMEM
    scratch = [
        vmem((4, tok_rows, 384), low),
        vmem((tok_rows, 384), low),
        vmem((tok_rows, 384), low),
        vmem((tok_rows, HD), low),
        vmem((tok_rows, width), wide),
        vmem((tok_rows, width), wide),
        vmem((width, tok_rows), low),
        vmem((4, width // 2, tok_rows), low),
        vmem((4, 2, half, tok_rows), low),
        vmem((2, tok_rows, 3 * UNITS), low),
        vmem((tok_rows, 3 * UNITS), low),
        vmem((2, half, 3 * UNITS), low),
        vmem((2, half, 3 * UNITS), low),
        vmem((2, block, 3 * UNITS), wide),
        vmem((half, 3 * UNITS), low),
        vmem((2, block, 3 * UNITS), low),
        vmem((block, 3 * UNITS), low),
        vmem((2, block, 3 * UNITS), wide),
        vmem((tok_rows, width), low),
        vmem((2, quarter, width), low),
        vmem((quarter, width), low),
        vmem((quarter, width), low),
        vmem((tok_rows, width), low),
        vmem((2, quarter, width), low),
        vmem((quarter, width), low),
        vmem((15, tok_rows, HD), low),
        vmem((15, tok_rows, HD), low),
        vmem((tok_rows, 384), low),
        vmem((tok_rows, HD), low),
        vmem((2 * half, 896), low),
        vmem((half, 896), low),
        vmem((block, 896), low),
        vmem((block, 896), low),
        pltpu.SemaphoreType.DMA((REMOTE,)),
        pltpu.SemaphoreType.DMA((REMOTE,)),
        pltpu.SemaphoreType.DMA((LOCAL,)),
        pltpu.SemaphoreType.DMA((3, 3)),
    ]
    return pl.pallas_call(
        functools.partial(back_kernel, width, units),
        out_shape=outs,
        in_specs=[VMEM, VMEM] + [any_] * 15,
        out_specs=(any_, VMEM, VMEM, VMEM, VMEM) + (any_,) * 8,
        scratch_shapes=scratch,
        compiler_params=pltpu.CompilerParams(
            vmem_limit_bytes=64 * 1024 * 1024, collective_id=0, has_side_effects=True
        ),
        cost_estimate=pl.CostEstimate(
            flops=20 * tok_rows * width * units, bytes_accessed=10 * width * units, transcendentals=0
        ),
    )(docs, gain, attn, full, log_total, query, pair, x, cot, cot.T, normed1.T, cosine, sine, wo, wg, wu, wd)


def on_device(
    layer_input,
    norm1_gain,
    w_query,
    b_query,
    w_key,
    b_key,
    w_value,
    b_value,
    w_out,
    norm2_gain,
    w_gate,
    w_up,
    w_down,
    doc_ids,
    positions,
    cotangent,
):
    tok_rows, width = layer_input.shape
    shards = lax.axis_size("cp")
    heads = w_query.shape[1] // HD
    kv_heads = w_key.shape[1] // HD
    me = lax.axis_index("cp")
    lane = lax.axis_index("tp")
    core = lane % 2
    kv_index = lane * heads // (H // kv_heads)
    is_key = core == 0

    def finish(
        output, grad_middle, grad_normed1, grad_query, grad_pair, gain2_part,
        grad_w_query, grad_w_pair, grad_w_out, grad_w_gate, grad_w_up, grad_w_down,
    ):
        weighted1 = grad_normed1 * norm1_gain
        gain1_part = jnp.sum(grad_normed1 * inputs * scale1, axis=0)
        grad_input = (
            grad_middle
            + scale1 * weighted1
            - inputs * scale1**3 * jnp.mean(weighted1 * inputs, axis=-1, keepdims=True)
        ).astype(jnp.bfloat16)

        small = jnp.concatenate(
            [
                gain1_part,
                gain2_part,
                jnp.sum(grad_query.astype(jnp.float32), axis=0),
                jnp.sum(grad_pair.astype(jnp.float32), axis=0),
            ]
        ).reshape(-1, HD)
        bit = 1
        while bit < shards:
            small = small + swap(small, "cp", bit)
            bit *= 2
        wide = width // HD
        gain1_sum = small[:wide].reshape(-1)
        gain2_sum = small[wide : 2 * wide].reshape(-1)
        bias_query = small[2 * wide : 2 * wide + heads].reshape(-1)

        def assemble(parts, axis):
            at = lambda index: lax.dynamic_index_in_dim(parts, reverse_bits(lane ^ index, 2), 0, keepdims=False)
            return (
                jnp.concatenate([at(0), at(2)], axis),
                jnp.concatenate([at(1), at(3)], axis),
            )

        bias_key, bias_value = assemble(gather_tp(small[None, 2 * wide + heads], 0), 0)
        grad_w_key, grad_w_value = assemble(gather_tp(grad_w_pair[None], 0), 1)
        return (
            output,
            grad_input,
            gain1_sum,
            grad_w_query,
            bias_query,
            grad_w_key,
            bias_key,
            grad_w_value,
            bias_value,
            grad_w_out,
            gain2_sum,
            grad_w_gate,
            grad_w_up,
            grad_w_down,
        )

    middle_docs = doc_ids.reshape(shards, tok_rows)[:, HALF]
    my_doc = middle_docs[me]
    start = jnp.sum((middle_docs < my_doc).astype(jnp.int32))
    place = jnp.stack([me, core, lane, start]).astype(jnp.int32)
    my_pos = lax.dynamic_slice_in_dim(positions, me * tok_rows, tok_rows)
    cosine, sine = rope_tables(my_pos, HD)

    inputs = layer_input.astype(jnp.float32)
    scale1 = lax.rsqrt(jnp.mean(inputs * inputs, axis=-1, keepdims=True) + EPSILON)
    normed1 = (inputs * scale1 * norm1_gain).astype(jnp.bfloat16)

    def pair_weight(index):
        head = index * heads // (H // kv_heads)
        source = jnp.where(index % 2 == 0, w_key, w_value)
        return lax.dynamic_slice_in_dim(source, head * HD, HD, 1)

    pair_bias = lax.dynamic_slice_in_dim(jnp.where(is_key, b_key, b_value), kv_index * HD, HD)
    pair_cos = jnp.where(is_key, cosine, 1.0)
    pair_sin = jnp.where(is_key, sine, 0.0)
    pair_pre = matmul(normed1, pair_weight(lane)) + pair_bias
    pair = rotary(pair_pre, pair_cos, pair_sin).astype(jnp.bfloat16)[None]
    bit = shards // 2
    while bit:
        pair = jnp.concatenate([pair, swap(pair, "cp", bit)], 0)
        bit //= 2
    other = swap(pair, "tp", 1)

    q_pre = matmul(normed1, w_query) + b_query
    query = rotary(
        q_pre.reshape(tok_rows, heads, HD), cosine[:, None, :], sine[:, None, :]
    ).astype(jnp.bfloat16)
    query = query.transpose(1, 0, 2)

    attn, attn_full, log_total, pair = attend(place, query, pair, other)
    w_out_all = gather_tp(w_out, 0)
    w_query_all = gather_tp(w_query, 1)
    if shards == 8 and tok_rows == TOK:
        (
            tiles, grad_w_out, grad_w_query, grad_w_pair, gain2_part, output, grad_middle,
            queries_all, pairs_all, *_,
        ) = back(
            jnp.broadcast_to(middle_docs[:, None], (shards, 2 * HALF)),
            norm2_gain[None],
            attn, attn_full, log_total, query, pair, layer_input, cotangent, normed1,
            cosine, sine, w_out_all.reshape(4, -1, width), w_gate.T, w_up.T, w_down,
        )
        grad_w_out = grad_w_out.T
        gain2_part = gain2_part[0]
        grad_query, grad_pair = queries_all[0], pairs_all[0]
        units = w_gate.shape[1]

        def columns(kind):
            part = tiles[:, :, kind * UNITS : (kind + 1) * UNITS]
            return part.transpose(1, 0, 2).reshape(part.shape[1], -1)[:, :units]

        grad_w_down, grad_w_gate, grad_w_up = columns(0).T, columns(1), columns(2)
        grad_normed1 = sum(
            contract_cols(queries_all[i], w_query_all[:, i * heads * HD : (i + 1) * heads * HD])
            for i in range(4)
        )
        for i, far in enumerate(TP_ORDER):
            grad_normed1 = grad_normed1 + contract_cols(pairs_all[i], pair_weight(lane ^ far))
        return finish(
            output, grad_middle, grad_normed1, grad_query, grad_pair, gain2_part,
            grad_w_query, grad_w_pair, grad_w_out, grad_w_gate, grad_w_up, grad_w_down,
        )
    cot_shared = share(place, cotangent, shards)
    normed1_shared = share(place, normed1, shards)

    middle = inputs + matmul(gather_tp(attn, 1), w_out_all)
    scale2 = lax.rsqrt(jnp.mean(middle * middle, axis=-1, keepdims=True) + EPSILON)
    normed2 = (middle * scale2 * norm2_gain).astype(jnp.bfloat16)

    units = w_gate.shape[1]
    chunks = pl.cdiv(pl.cdiv(units, TILE), CHUNK_TILES)
    hiddens, grads, total = [], [], None
    for index in range(chunks):
        hidden, grad, total = hidden_chunk(
            place, normed2, cotangent, w_gate, w_up, w_down, total, index
        )
        hiddens.append(hidden)
        grads.append(grad)
    normed2_shared = share(place, normed2, shards)

    downs, gates, ups = [], [], []
    for hidden, grad in zip(hiddens, grads):
        downs.append(weight_grad(place, cot_shared, hidden, shards).T)
        both = weight_grad(place, normed2_shared, grad, shards)
        span = hidden.shape[1]
        for at in range(0, span, TILE):
            size = min(TILE, span - at)
            gates.append(both[:, 2 * at : 2 * at + size])
            ups.append(both[:, 2 * at + TILE : 2 * at + TILE + size])
    grad_w_down = jnp.concatenate(downs, 0)
    grad_w_gate = jnp.concatenate(gates, 1)
    grad_w_up = jnp.concatenate(ups, 1)

    grad_normed2 = in_order(gather_tp(scatter_tp(total).astype(jnp.bfloat16), 0), lane).astype(
        jnp.float32
    )
    weighted2 = grad_normed2 * norm2_gain
    gain2_part = jnp.sum(grad_normed2 * middle * scale2, axis=0)
    grad_middle = (
        cotangent.astype(jnp.float32)
        + scale2 * weighted2
        - middle * scale2**3 * jnp.mean(weighted2 * middle, axis=-1, keepdims=True)
    )
    grad_branch = grad_middle.astype(jnp.bfloat16)
    grad_attn = contract_cols(grad_branch, w_out).astype(jnp.bfloat16)
    grad_query, keep, send = attend_back(
        place, query, pair, grad_attn, attn_full, log_total, cosine, sine
    )

    part = tok_rows // 4
    ffn = sum(matmul(h, lax.slice_in_dim(w_down, i * CHUNK_TILES * TILE, i * CHUNK_TILES * TILE + h.shape[1])) for i, h in enumerate(hiddens))
    ffn = after(ffn.astype(jnp.bfloat16), grad_middle)
    ffn_rel = jnp.concatenate(
        [lax.dynamic_slice_in_dim(ffn, (lane ^ far) * part, part, 0) for far in TP_ORDER], 0
    )
    out_part = scatter_tp(ffn_rel) + lax.dynamic_slice_in_dim(middle, lane * part, part, 0)
    output = in_order(gather_tp(out_part.astype(jnp.bfloat16), 0), lane)

    summed = keep.astype(jnp.float32) + swap(send, "tp", 1).astype(jnp.float32)
    bit = 1
    while bit < shards:
        count = summed.shape[0] // 2
        summed = summed[:count] + swap(summed[count:].astype(jnp.bfloat16), "cp", bit).astype(
            jnp.float32
        )
        bit *= 2
    grad_pair = rotary_back(summed[0], pair_cos, pair_sin).astype(jnp.bfloat16)

    branch_shared = share(place, grad_branch, shards)
    grad_w_out = weight_grad(place, branch_shared, attn, shards).T
    grad_w_query = weight_grad(place, normed1_shared, grad_query, shards)
    grad_w_pair = weight_grad(place, normed1_shared, grad_pair, shards)

    pairs_all = gather_tp(grad_pair, 1)
    grad_normed1 = contract_cols(gather_tp(grad_query, 1), w_query_all)
    for i, far in enumerate(TP_ORDER):
        grad_normed1 = grad_normed1 + contract_cols(
            pairs_all[:, i * HD : (i + 1) * HD], pair_weight(lane ^ far)
        )
    return finish(
        output, grad_middle, grad_normed1, grad_query, grad_pair, gain2_part,
        grad_w_query, grad_w_pair, grad_w_out, grad_w_gate, grad_w_up, grad_w_down,
    )


def solution(mesh):
    return jax.shard_map(
        on_device,
        mesh=mesh,
        in_specs=(
            P("cp", None),
            P(),
            P(None, "tp"),
            P("tp"),
            P(),
            P(),
            P(),
            P(),
            P("tp", None),
            P(),
            P(None, "tp"),
            P(None, "tp"),
            P("tp", None),
            P(),
            P(),
            P("cp", None),
        ),
        out_specs=(
            P("cp", None),
            P("cp", None),
            P(),
            P("cp", "tp"),
            P("tp"),
            P("cp", None),
            P(),
            P("cp", None),
            P(),
            P("tp", "cp"),
            P(),
            P("cp", "tp"),
            P("cp", "tp"),
            P("tp", "cp"),
        ),
        check_vma=False,
    )
```

```python
import functools
import math

import jax
import jax.numpy as jnp
from jax import lax
from jax.experimental import pallas as pl
from jax.experimental.pallas import tpu as pltpu
from jax.sharding import PartitionSpec as P

H = 12
HD = 128
HALF = 128
EPSILON = 1e-06
ROPE_BASE = 10000.0
MASKED = -1e30
LOG2E = 1.4426950408889634
TILE = 256
CHUNK_TILES = 3
VMEM_LIMIT = 56 * 1024 * 1024
TP_ORDER = (0, 2, 1, 3)


def matmul(left, right):
    return jnp.dot(left, right, preferred_element_type=jnp.float32)


def contract_rows(left, right):
    return lax.dot_general(
        left, right, (((0,), (0,)), ((), ())), preferred_element_type=jnp.float32
    )


def contract_cols(left, right):
    return lax.dot_general(
        left, right, (((1,), (1,)), ((), ())), preferred_element_type=jnp.float32
    )


def rope_tables(tok_pos, width):
    half = width // 2
    freq = ROPE_BASE ** (-(jnp.arange(half, dtype=jnp.float32) * 2.0 / width))
    angle = tok_pos.astype(jnp.float32)[:, None] * freq[None, :]
    cosine = jnp.concatenate([jnp.cos(angle), jnp.cos(angle)], -1)
    sine = jnp.concatenate([jnp.sin(angle), jnp.sin(angle)], -1)
    return (cosine, sine)


def rotary(values, cosine, sine):
    half = values.shape[-1] // 2
    return values * cosine + jnp.concatenate([-values[..., half:], values[..., :half]], -1) * sine


def rotary_back(grads, cosine, sine):
    half = grads.shape[-1] // 2
    scaled = grads * sine
    return grads * cosine + jnp.concatenate([scaled[..., half:], -scaled[..., :half]], -1)


def swap(value, axis, bit):
    size = lax.axis_size(axis)
    return lax.ppermute(value, axis, [(i, i ^ bit) for i in range(size)])


def after(value, *earlier):
    return lax.optimization_barrier((value, *earlier))[0]


def bits_of(size):
    return size.bit_length() - 1


def reverse_bits(index, bits):
    out = 0
    for i in range(bits):
        out = out | (((index >> i) & 1) << (bits - 1 - i))
    return out


def params(**more):
    return pltpu.CompilerParams(vmem_limit_bytes=VMEM_LIMIT, **more)


SMEM = pl.BlockSpec(memory_space=pltpu.SMEM)
VMEM = pl.BlockSpec(memory_space=pltpu.VMEM)


def spread_kernel(shards, place_ref, rows_ref, own_ref, send_ref, turned):
    me, core = place_ref[0], place_ref[1]
    turned[...] = rows_ref[...].T
    width = turned.shape[0] // shards
    bits = bits_of(shards)
    for i in range(shards // 2):
        far = reverse_bits(i, bits)
        block = pl.multiple_of((me ^ far) * width, 16)
        own_ref[i * width : (i + 1) * width, :] = turned[pl.ds(block, width), :]
    for i in range(shards // 4):
        far = reverse_bits(core * (shards // 4) + i, bits) | 1
        block = pl.multiple_of((me ^ far) * width, 16)
        send_ref[i * width : (i + 1) * width, :] = turned[pl.ds(block, width), :]


def spread(place, rows, shards):
    count, width = rows.shape
    return pl.pallas_call(
        functools.partial(spread_kernel, shards),
        out_shape=(
            jax.ShapeDtypeStruct((width // 2, count), rows.dtype),
            jax.ShapeDtypeStruct((width // 4, count), rows.dtype),
        ),
        in_specs=[SMEM, VMEM],
        out_specs=(VMEM, VMEM),
        scratch_shapes=[pltpu.VMEM((width, count), rows.dtype)],
        compiler_params=params(),
        cost_estimate=pl.CostEstimate(flops=0, bytes_accessed=4 * rows.size, transcendentals=0),
    )(place, rows)


def share(place, rows, shards):
    own, send = spread(place, rows, shards)
    near = swap(send, "cp", 1)
    return own, near, swap(near, "tp", 1)


def weigh_kernel(place_ref, own_ref, near_ref, far_ref, mine_ref, theirs_ref, send_ref, keep_ref, joined):
    core = place_ref[1]

    @pl.when(pl.program_id(0) == 0)
    def _():
        joined[core] = near_ref[...]
        joined[1 - core] = far_ref[...]

    half = send_ref.shape[0]
    mine, theirs = mine_ref[...], theirs_ref[...]
    send_ref[...] = (
        matmul(own_ref[half:, :], mine) + matmul(joined[1], theirs)
    ).astype(send_ref.dtype)
    keep_ref[...] = (
        matmul(own_ref[:half, :], mine) + matmul(joined[0], theirs)
    ).astype(keep_ref.dtype)


def weigh(place, shared, mine, theirs):
    own, near, far = shared
    half, count = near.shape
    width = mine.shape[1]
    tile = min(width, 512)
    whole = lambda j: (0, 0)
    column = lambda j: (0, j)
    return pl.pallas_call(
        weigh_kernel,
        grid=(pl.cdiv(width, tile),),
        out_shape=(jax.ShapeDtypeStruct((half, width), jnp.bfloat16),) * 2,
        in_specs=[
            SMEM,
            pl.BlockSpec((2 * half, count), whole),
            pl.BlockSpec((half, count), whole),
            pl.BlockSpec((half, count), whole),
            pl.BlockSpec((count, tile), column),
            pl.BlockSpec((count, tile), column),
        ],
        out_specs=(pl.BlockSpec((half, tile), column),) * 2,
        scratch_shapes=[pltpu.VMEM((2, half, count), jnp.bfloat16)],
        compiler_params=params(),
        cost_estimate=pl.CostEstimate(
            flops=8 * half * count * width,
            bytes_accessed=4 * (2 * half * count + count * width + half * width),
            transcendentals=0,
        ),
    )(place, own, near, far, mine, theirs)


def weight_grad(place, shared, mine, shards):
    theirs = swap(mine, "cp", 1)
    send, keep = weigh(place, shared, mine, theirs)
    terms = [keep]
    bit = 2
    while bit < shards:
        terms.append(swap(send, "cp", bit))
        bit *= 2
        if bit < shards:
            rows = terms[0].shape[0] // 2
            send = sum(t[rows:].astype(jnp.float32) for t in terms).astype(jnp.bfloat16)
            terms = [t[:rows] for t in terms]
    return sum(t.astype(jnp.float32) for t in terms)


def hidden_kernel(first, last, offset, units, *refs):
    place_ref, rows_ref, cot_ref, gate_ref, up_ref, down_ref = refs[:6]
    refs = refs[6:]
    if not first:
        before_ref, refs = refs[0], refs[1:]
    hidden_ref, grads_ref, sum_ref, total = refs
    step = pl.program_id(0)

    @pl.when(step == 0)
    def _():
        total[...] = jnp.zeros_like(total) if first else before_ref[...]

    rows = rows_ref[...]
    w_gate, w_up, w_down = gate_ref[...], up_ref[...], down_ref[...]
    if last:
        left = units - (offset + step) * TILE
        inside = lax.broadcasted_iota(jnp.int32, w_gate.shape, 1) < left
        w_gate = jnp.where(inside, w_gate, 0)
        w_up = jnp.where(inside, w_up, 0)
        inside = lax.broadcasted_iota(jnp.int32, w_down.shape, 0) < left
        w_down = jnp.where(inside, w_down, 0)
    gate = matmul(rows, w_gate)
    up_part = matmul(rows, w_up)
    grad_hidden = contract_cols(cot_ref[...], w_down)
    sigma = jax.nn.sigmoid(gate)
    swish = gate * sigma
    hidden_ref[...] = (swish * up_part).astype(jnp.bfloat16)
    grad_gate = (grad_hidden * up_part * sigma * (1.0 + gate * (1.0 - sigma))).astype(jnp.bfloat16)
    grad_up = (grad_hidden * swish).astype(jnp.bfloat16)
    grads_ref[:, :TILE] = grad_gate
    grads_ref[:, TILE:] = grad_up
    total[...] += contract_cols(grad_gate, w_gate) + contract_cols(grad_up, w_up)

    @pl.when(step == pl.num_programs(0) - 1)
    def _():
        if last:
            part = total.shape[0] // len(TP_ORDER)
            for i, far in enumerate(TP_ORDER):
                block = pl.multiple_of((place_ref[2] ^ far) * part, part)
                sum_ref[i * part : (i + 1) * part, :] = total[pl.ds(block, part), :].astype(
                    sum_ref.dtype
                )
        else:
            sum_ref[...] = total[...]


def hidden_chunk(place, rows, cotangent, w_gate, w_up, w_down, before, index):
    count, width = rows.shape
    units = w_gate.shape[1]
    tiles = pl.cdiv(units, TILE)
    offset = index * CHUNK_TILES
    steps = min(CHUNK_TILES, tiles - offset)
    first, last = index == 0, offset + steps == tiles
    inner = min(steps * TILE, units - offset * TILE)
    outer = (steps - 1) * 2 * TILE + TILE + inner - (steps - 1) * TILE
    whole = lambda j: (0, 0)
    column = lambda j: (0, j)
    in_specs = [
        SMEM,
        pl.BlockSpec((count, width), whole),
        pl.BlockSpec((count, width), whole),
        pl.BlockSpec((width, TILE), lambda j: (0, offset + j)),
        pl.BlockSpec((width, TILE), lambda j: (0, offset + j)),
        pl.BlockSpec((TILE, width), lambda j: (offset + j, 0)),
    ]
    operands = [place, rows, cotangent, w_gate, w_up, w_down]
    if not first:
        in_specs.append(pl.BlockSpec((count, width), whole))
        operands.append(before)
    return pl.pallas_call(
        functools.partial(hidden_kernel, first, last, offset, units),
        grid=(steps,),
        out_shape=(
            jax.ShapeDtypeStruct((count, inner), jnp.bfloat16),
            jax.ShapeDtypeStruct((count, outer), jnp.bfloat16),
            jax.ShapeDtypeStruct((count, width), jnp.bfloat16 if last else jnp.float32),
        ),
        in_specs=in_specs,
        out_specs=(
            pl.BlockSpec((count, TILE), column),
            pl.BlockSpec((count, 2 * TILE), column),
            pl.BlockSpec((count, width), whole),
        ),
        scratch_shapes=[pltpu.VMEM((count, width), jnp.float32)],
        compiler_params=params(),
        cost_estimate=pl.CostEstimate(
            flops=10 * count * width * inner,
            bytes_accessed=6 * width * inner + 12 * count * width,
            transcendentals=count * inner,
        ),
    )(*operands)


def region_rows(ref, start, count):
    return ref[:, start : start + count, :].reshape(-1, HD)


def triangle(rows, keys):
    row = lax.broadcasted_iota(jnp.int32, (rows, keys), 0) & (keys - 1)
    return row >= lax.broadcasted_iota(jnp.int32, (rows, keys), 1)


def regions(place_ref, shards, tok_rows):
    me, start = place_ref[0], place_ref[3]
    bits = bits_of(shards)

    def of_first(block):
        low = block < shards
        device = jnp.where(low, block, 2 * shards - 1 - block)
        return reverse_bits(device ^ me, bits), jnp.where(low, 0, tok_rows - HALF)

    def of_middle(block):
        return reverse_bits((start + block) ^ me, bits), HALF

    return (
        (0, HALF, me, of_first),
        (tok_rows - HALF, HALF, 2 * shards - 1 - me, of_first),
        (HALF, tok_rows - 2 * HALF, me - start, of_middle),
    )


def attend_kernel(shards, place_ref, q_ref, mine_ref, other_ref, low_ref, full_ref, log_ref, pair):
    core = place_ref[1]
    pair[core] = mine_ref[...]
    pair[1 - core] = other_ref[...]
    heads, tok_rows = q_ref.shape[0], q_ref.shape[1]
    factor = HD**-0.5 * LOG2E
    for begin, count, blocks, locate in regions(place_ref, shards, tok_rows):
        query = region_rows(q_ref, begin, count)
        rows = heads * count

        def read(which, block):
            slot, offset = locate(block)
            return pair[which, slot, pl.ds(pl.multiple_of(offset, HALF), count), :]

        mask = triangle(rows, count)
        last = jnp.where(mask, contract_cols(query, read(0, blocks)), MASKED)
        peak = lax.fori_loop(
            0, blocks, lambda t, top: jnp.maximum(top, contract_cols(query, read(0, t))), last
        )
        peak = jnp.max(peak, axis=1, keepdims=True) * factor

        def add(block, carry, scores):
            total, accum = carry
            weights = jnp.exp2(scores * factor - peak)
            return total + weights, accum + matmul(weights.astype(jnp.bfloat16), read(1, block))

        carry = add(blocks, (jnp.zeros((rows, count), jnp.float32), jnp.zeros((rows, HD), jnp.float32)), last)
        total, accum = lax.fori_loop(
            0, blocks, lambda t, held: add(t, held, contract_cols(query, read(0, t))), carry
        )
        total = jnp.sum(total, axis=1, keepdims=True)
        full = accum / total
        log_total = jnp.broadcast_to(peak + jnp.log2(total), (rows, HD))
        for head in range(heads):
            part = slice(head * count, (head + 1) * count)
            lanes = slice(head * HD, (head + 1) * HD)
            low_ref[begin : begin + count, lanes] = full[part].astype(jnp.bfloat16)
            full_ref[head, begin : begin + count, :] = full[part]
            log_ref[head, begin : begin + count, :] = log_total[part]


def attend(place, query, mine, other):
    heads, tok_rows, _ = query.shape
    shards = mine.shape[0]
    pairs = heads * tok_rows * tok_rows * shards // 4
    return pl.pallas_call(
        functools.partial(attend_kernel, shards),
        out_shape=(
            jax.ShapeDtypeStruct((tok_rows, heads * HD), jnp.bfloat16),
            jax.ShapeDtypeStruct((heads, tok_rows, HD), jnp.float32),
            jax.ShapeDtypeStruct((heads, tok_rows, HD), jnp.float32),
            jax.ShapeDtypeStruct((2,) + mine.shape, jnp.bfloat16),
        ),
        in_specs=[SMEM, VMEM, VMEM, VMEM],
        out_specs=(VMEM, VMEM, VMEM, VMEM),
        compiler_params=params(),
        cost_estimate=pl.CostEstimate(
            flops=6 * pairs * HD, bytes_accessed=4 * mine.size, transcendentals=pairs
        ),
    )(place, query, mine, other)


def attend_back_kernel(
    shards, place_ref, q_ref, pair, low_ref, full_ref, log_ref, cos_ref, sin_ref,
    query_ref, keep_ref, send_ref, grads,
):
    core = place_ref[1]
    grads[...] = jnp.zeros_like(grads)
    heads, tok_rows = q_ref.shape[0], q_ref.shape[1]
    scale = HD**-0.5
    factor = scale * LOG2E
    sign = jnp.where(lax.broadcasted_iota(jnp.int32, (1, HD), 1) < HD // 2, 1.0, -1.0)
    for begin, count, blocks, locate in regions(place_ref, shards, tok_rows):
        query = region_rows(q_ref, begin, count)
        rows = heads * count
        incoming = jnp.concatenate(
            [low_ref[begin : begin + count, h * HD : (h + 1) * HD] for h in range(heads)], 0
        )
        full = region_rows(full_ref, begin, count)
        log_total = region_rows(log_ref, begin, count)[:, :1]
        delta = jnp.sum(incoming.astype(jnp.float32) * full, axis=1, keepdims=True)

        def add(block, grad_query, mask=None):
            slot, offset = locate(block)
            place = pl.ds(pl.multiple_of(offset, HALF), count)
            keys, values = pair[0, slot, place, :], pair[1, slot, place, :]
            probs = jnp.exp2(contract_cols(query, keys) * factor - log_total)
            if mask is not None:
                probs = jnp.where(mask, probs, 0.0)
            grad_scores = (probs * (contract_cols(incoming, values) - delta)).astype(jnp.bfloat16)
            grads[0, slot, place, :] += contract_rows(grad_scores, query)
            grads[1, slot, place, :] += contract_rows(probs.astype(jnp.bfloat16), incoming)
            return grad_query + matmul(grad_scores, keys)

        grad_query = add(blocks, jnp.zeros((rows, HD), jnp.float32), triangle(rows, count))
        grad_query = lax.fori_loop(0, blocks, add, grad_query) * scale
        cosine, sine = cos_ref[begin : begin + count, :], sin_ref[begin : begin + count, :]
        for head in range(heads):
            part = grad_query[head * count : (head + 1) * count]
            turned = part * cosine + pltpu.roll(part * sine, HD // 2, 1) * sign
            query_ref[begin : begin + count, head * HD : (head + 1) * HD] = turned.astype(
                jnp.bfloat16
            )
    is_key = core == 0
    keep_ref[...] = (grads[core] * jnp.where(is_key, scale, 1.0)).astype(jnp.bfloat16)
    send_ref[...] = (grads[1 - core] * jnp.where(is_key, 1.0, scale)).astype(jnp.bfloat16)


def attend_back(place, query, pair, low, full, log_total, cosine, sine):
    heads, tok_rows, _ = query.shape
    shards = pair.shape[1]
    pairs = heads * tok_rows * tok_rows * shards // 4
    return pl.pallas_call(
        functools.partial(attend_back_kernel, shards),
        out_shape=(
            jax.ShapeDtypeStruct((tok_rows, heads * HD), jnp.bfloat16),
            jax.ShapeDtypeStruct(pair.shape[1:], jnp.bfloat16),
            jax.ShapeDtypeStruct(pair.shape[1:], jnp.bfloat16),
        ),
        in_specs=[SMEM] + [VMEM] * 7,
        out_specs=(VMEM, VMEM, VMEM),
        scratch_shapes=[pltpu.VMEM(pair.shape, jnp.float32)],
        compiler_params=params(),
        cost_estimate=pl.CostEstimate(
            flops=10 * pairs * HD, bytes_accessed=4 * pair.size, transcendentals=pairs
        ),
    )(place, query, pair, low, full, log_total, cosine, sine)


def gather_tp(value, axis):
    value = jnp.concatenate([value, swap(value, "tp", 2)], axis)
    return jnp.concatenate([value, swap(value, "tp", 1)], axis)


def scatter_tp(value):
    half, part = value.shape[0] // 2, value.shape[0] // 4
    other = swap(value[half:], "tp", 1)
    send = (value[part:half].astype(jnp.float32) + other[part:].astype(jnp.float32)).astype(
        jnp.bfloat16
    )
    last = swap(send, "tp", 2)
    return (
        value[:part].astype(jnp.float32)
        + other[:part].astype(jnp.float32)
        + last.astype(jnp.float32)
    )


def in_order(value, me):
    part = value.shape[0] // 4
    return jnp.concatenate(
        [
            lax.dynamic_slice_in_dim(value, reverse_bits(me ^ i, 2) * part, part, 0)
            for i in range(4)
        ],
        0,
    )


UNITS = 256
TOK = 512


def back_kernel(width, units, *refs):
    (
        docs_ref, gain_ref, bias_ref, cosine, sine, x_hbm, cot_hbm, wq_hbm, wk_hbm, wv_hbm, wo_hbm,
        wg_hbm, wu_hbm, wd_hbm,
        tiles_out, wo_out, wq_out, wp_out, sums_out, output_out, input_out,
        middle_hbm, query_hbm, pair_hbm, own_hbm, far_hbm, near_hbm, wo_all, wq_all, all_hbm, n1_hbm,
        query, pair, full, log_total, sums, sums_in,
        attn_all, attn_far, query_far, pair_far, middle, acc, turned,
        own_a, far_a, part_s, part_k, near1, part_s2, near2, near_stage, final, sent_tile,
        rel, core_in, lane_send, lane_in, grad_full,
        kv_send, kv_in, grad_query, grad_pair, small_s, small_in, small_s2, small_in2,
        send_sem, recv_sem, local_sem, weight_sem,
    ) = refs
    me = lax.axis_index("cp")
    lane = lax.axis_index("tp")
    b0, b1, b2 = me % 2, (me // 2) % 2, me // 4
    core, high = lane % 2, lane // 2
    x_to = {"cp": me + 1 - 2 * b0}
    z1_to = {"cp": me + 2 - 4 * b1}
    z2_to = {"cp": me + 4 - 8 * b2}
    z3_to = {"cp": me + 6 - 4 * b1 - 8 * b2}
    inner = (b1 + b2) % 2
    peers = [
        me + (r % 2) * (1 - 2 * b0) + (r // 2 % 2) * (2 - 4 * b1) + (r // 4) * (4 - 8 * b2)
        for r in range(8)
    ]
    c_to = {"tp": lane + 1 - 2 * core}
    y_to = {"tp": lane + 2 - 4 * high}
    lane_c, lane_y = lane + 1 - 2 * core, lane + 2 - 4 * high
    lane_cy = 3 - lane
    tiles = pl.cdiv(units, UNITS)
    rest = units - (tiles - 1) * UNITS
    block = width // 8
    half = width // 4
    quarter = TOK // 4
    scale = HD**-0.5
    factor = scale * LOG2E
    used = {"remote": 0, "local": 0}

    def remote(src, dst, to, count=1):
        index = used["remote"]
        used["remote"] += 1
        return pltpu.make_async_remote_copy(
            src_ref=src, dst_ref=dst, send_sem=send_sem.at[index], recv_sem=recv_sem.at[index],
            device_id=to, device_id_type=pl.DeviceIdType.MESH,
        )

    def local(src, dst):
        index = used["local"]
        used["local"] += 1
        return pltpu.make_async_copy(src, dst, local_sem.at[index])

    def started(*copies):
        for copy in copies:
            copy.start()
        return copies[0] if len(copies) == 1 else copies

    def row_block(side, h, i):
        mine = (b0 + side) % 2 + 2 * ((b1 + h) % 2) + 4 * ((b2 + i) % 2)
        return pl.ds(pl.multiple_of(mine * block, 16), block)

    def rows_of_block(index):
        return pl.ds(pl.multiple_of(index * block, 16), block)

    def rows_of(index):
        return pl.ds(pl.multiple_of(index * quarter, quarter), quarter)

    x_tile = remote(own_hbm.at[tiles - 1], far_hbm, x_to)
    z1_tile = remote(part_s, near1, z1_to)
    z2_tile = remote(part_s2, near2, z2_to)

    spread_base = used["remote"]
    used["remote"] += 2 * 20
    wide_half, wide_quarter = width // 2, width // 4

    def block_of(j, side):
        z = (b1 + 2 * b2, 1 - b1 + 2 * b2, 2 - b2, 3 - 3 * b2)[j]
        return 2 * z + (b0 + side) % 2

    def spread_part(k, j, side, c, y=None):
        if y is None:
            rows = pl.ds(pl.multiple_of(c * wide_half, wide_half), wide_half)
        else:
            rows = pl.ds(
                pl.multiple_of(c * wide_half + y * wide_quarter, wide_quarter), wide_quarter
            )
        return all_hbm.at[k, block_of(j, side), rows]

    def spread_copy(k, part, send, recv, to):
        index = spread_base + 20 * k
        return pltpu.make_async_remote_copy(
            src_ref=part, dst_ref=part, send_sem=send_sem.at[index + send],
            recv_sem=recv_sem.at[index + recv], device_id=to, device_id_type=pl.DeviceIdType.MESH,
        )

    def z_copy(k, m):
        j, recv, to = ((0, 1, z1_to), (0, 2, z3_to), (1, 3, z3_to), (2, 2, z1_to), (3, 3, z1_to))[m]
        return spread_copy(k, spread_part(k, j, 0, core), m, recv, to)

    def z_arrival(k, j):
        return spread_copy(k, spread_part(k, j, 0, core), 0, j, z1_to)

    def c_copy(k, j, c=None):
        return spread_copy(k, spread_part(k, j, 0, core if c is None else c), 4 + j, 4 + j, c_to)

    def x_copy(k, j, side=0):
        part = spread_part(k, j, side, core, None if (k, j) in WHOLE_HALVES else high)
        return spread_copy(k, part, 8 + j, 8 + j, x_to)

    def y_copy(k, j, y=None):
        return spread_copy(
            k, spread_part(k, j, 1, core, high if y is None else y), 12 + j, 12 + j, y_to
        )

    def d_copy(k, j, c=None):
        return spread_copy(k, spread_part(k, j, 1, core if c is None else c), 16 + j, 16 + j, c_to)

    def when(condition):
        return pl.when(condition == 1)

    def begin_spread(k):
        z_copy(k, 0).start()

        @when(inner)
        def _():
            z_copy(k, 1).start()

    def arrive(k, j):
        z_arrival(k, j).wait_recv()

        @when(inner)
        def _():
            z_copy(k, j + 1).start()

        started(c_copy(k, j), x_copy(k, j))

    def arrive_inner(k, j):
        @when(inner)
        def _():
            arrive(k, j)

    def arrive_outer(k, j):
        @when(1 - inner)
        def _():
            arrive(k, j)

    def pass_y(k, j):
        assert (k, j) not in WHOLE_HALVES
        x_copy(k, j, 1).wait_recv()
        y_copy(k, j).start()

    def pass_core(k, j):
        if (k, j) in WHOLE_HALVES:
            x_copy(k, j, 1).wait_recv()
        else:
            y_copy(k, j, 1 - high).wait_recv()
        d_copy(k, j).start()

    barrier = pltpu.get_barrier_semaphore()
    for to in (*({"cp": peers[r]} for r in (1, 2, 3, 4, 6)), c_to, y_to):
        pl.semaphore_signal(barrier, inc=1, device_id=to, device_id_type=pl.DeviceIdType.MESH)
    pl.semaphore_wait(barrier, 7)

    def share(source, index):
        return [
            remote(
                source.at[row_block(1, core, i)],
                far_a.at[index, core, pl.ds(i * block, block)],
                x_to,
            )
            for i in range(2)
        ]

    def forward(index):
        return remote(far_a.at[index, core], far_a.at[index, core], c_to)

    COT, N2, GB, N1 = range(4)
    own_blocks = [local(turned, all_hbm.at[k, me]) for k in range(2)]
    wo_y = remote(wo_hbm, wo_all.at[1], y_to)
    wo_c = remote(wo_hbm, wo_all.at[2], c_to)
    wo_cy = remote(wo_all.at[1], wo_all.at[3], c_to)
    wq_y = remote(wq_hbm, wq_all.at[1], y_to)
    wq_c = remote(wq_hbm, wq_all.at[2], c_to)
    wq_cy = remote(wq_all.at[1], wq_all.at[3], c_to)
    attn_y = remote(attn_all.at[0], attn_all.at[1], y_to)
    attn_c = remote(attn_all.at[0], attn_all.at[2], c_to)
    attn_cy = remote(attn_all.at[1], attn_all.at[3], c_to)
    attn_x = remote(attn_all.at[0], attn_far, x_to)
    n1_x = share(n1_hbm, N1)
    n1_keep = local(turned, n1_hbm)
    pair_1 = remote(pair.at[core, 0], pair.at[core, 2], z1_to)
    pair_2 = remote(pair.at[core, 0], pair.at[core, 1], z2_to)
    pair_3 = remote(pair.at[core, 0], pair.at[core, 3], z3_to)
    pair_near = [remote(pair.at[core, i], pair.at[core, 4 + i], x_to) for i in range(4)]
    pair_core = [remote(pair.at[core, i], pair.at[core, i], c_to) for i in range(8)]
    started(wo_y, wo_c)

    def norm_scale(rows):
        return lax.rsqrt(jnp.mean(rows * rows, axis=-1, keepdims=True) + EPSILON)

    gain1, gain2 = gain_ref[0:1, :], gain_ref[1:2, :]
    sign = jnp.where(lax.broadcasted_iota(jnp.int32, (1, HD), 1) < HD // 2, 1.0, -1.0)
    is_key = jnp.where(core == 0, 1.0, 0.0)

    def turn(rows, cosines, sines):
        return rows * cosines + pltpu.roll(rows * sign, HD // 2, 1) * sines

    def turn_back(rows, cosines, sines):
        return rows * cosines + pltpu.roll(rows * sines, HD // 2, 1) * sign

    def opening(x_rows, cot_rows, normed, w_query, w_pair):
        loads = [
            local(x_hbm, x_rows),
            local(wq_hbm, w_query),
            local(cot_hbm, cot_rows),
        ]
        started(*loads)
        index = used["local"]
        used["local"] += 1
        columns = pl.ds(pl.multiple_of(high * HD, HD), HD)
        key_load = pltpu.make_async_copy(wk_hbm.at[:, columns], w_pair, local_sem.at[index])
        value_load = pltpu.make_async_copy(wv_hbm.at[:, columns], w_pair, local_sem.at[index])

        @pl.when(core == 0)
        def _():
            key_load.start()

        @pl.when(core == 1)
        def _():
            value_load.start()

        loads[0].wait()

        def norm(a, carry):
            rows = x_rows[rows_of(a), :].astype(jnp.float32)
            normed[rows_of(a), :] = (rows * norm_scale(rows) * gain1).astype(jnp.bfloat16)
            return carry

        lax.fori_loop(0, 4, norm, 0)
        key_load.wait()
        rows = matmul(normed[...], w_pair[...]) + bias_ref[0:1, 3 * HD :]
        pair[core, 0] = turn(
            rows, cosine[...] * is_key + (1.0 - is_key), sine[...] * is_key
        ).astype(jnp.bfloat16)
        started(pair_1, pair_2, pair_3, pair_near[0], pair_core[0])
        loads[2].wait()

        def flip_cot(a, carry):
            turned[:, rows_of(a)] = cot_rows[rows_of(a), :].T
            return carry

        lax.fori_loop(0, 4, flip_cot, 0)
        own_blocks[0].start()
        loads[1].wait()
        rows = matmul(normed[...], w_query[...]) + bias_ref[0:1, : 3 * HD]
        for h in range(3):
            query[h] = turn(rows[:, h * HD : (h + 1) * HD], cosine[...], sine[...]).astype(
                jnp.bfloat16
            )
        own_blocks[0].wait()
        begin_spread(0)
        for copy, i in ((pair_1, 2), (pair_2, 1), (pair_3, 3)):
            copy.wait_recv()
            started(pair_near[i], pair_core[i])

        def flip(a, carry):
            turned[:, rows_of(a)] = normed[rows_of(a), :].T
            return carry

        lax.fori_loop(0, 4, flip, 0)
        for p in range(4):
            own_a[N1, p * block : (p + 1) * block, :] = turned[row_block(0, p // 2, p % 2), :]
        for i in (0, 2, 1, 3):
            pair_near[i].wait_recv()
            pair_core[4 + i].start()
        x_copy(0, 0).start()
        n1_keep.start()
        n1_keep.wait()
        started(*n1_x)
        for copy in pair_core:
            copy.wait_recv()

    pl.run_scoped(
        opening,
        pltpu.VMEM((TOK, width), jnp.bfloat16),
        pltpu.VMEM((TOK, width), jnp.bfloat16),
        pltpu.VMEM((TOK, width), jnp.bfloat16),
        pltpu.VMEM((width, 3 * HD), jnp.bfloat16),
        pltpu.VMEM((width, HD), jnp.bfloat16),
    )

    def of_first(t):
        late = t // 8
        device = t * (1 - late) + (15 - t) * late
        return device, late * (TOK - HALF)

    def of_middle(t):
        return t, HALF

    def rows_at(t, locate, count):
        device, offset = locate(t)
        slot = (
            4 * ((device % 2 + b0) % 2)
            + 2 * (((device // 2) % 2 + b1) % 2)
            + (device // 4 + b2) % 2
        )
        return device, slot, pl.ds(pl.multiple_of(offset, HALF), count)

    def same_document(device):
        return docs_ref[pl.ds(device, 1), :] == docs_ref[pl.ds(me, 1), :]

    def attend_region(begin, count, blocks, locate, shared):
        rows = 3 * count
        q_rows = region_rows(query, begin, count)

        def score(t, diagonal=False):
            device, slot, place = rows_at(t, locate, count)
            scores = contract_cols(q_rows, pair[0, slot, place, :])
            if diagonal:
                return jnp.where(triangle(rows, count), scores, MASKED)
            if shared:
                return jnp.where(same_document(device), scores, MASKED)
            return scores

        def add(t, carry, scores):
            _, slot, place = rows_at(t, locate, count)
            total, accum = carry
            weights = jnp.exp2(scores * factor - peak)
            return total + weights, accum + matmul(
                weights.astype(jnp.bfloat16), pair[1, slot, place, :]
            )

        last = score(blocks, True)
        peak = lax.fori_loop(0, blocks, lambda t, top: jnp.maximum(top, score(t)), last)
        peak = jnp.max(peak, axis=1, keepdims=True) * factor
        carry = add(
            blocks, (jnp.zeros((rows, count), jnp.float32), jnp.zeros((rows, HD), jnp.float32)), last
        )
        total, accum = lax.fori_loop(0, blocks, lambda t, held: add(t, held, score(t)), carry)
        total = jnp.sum(total, axis=1, keepdims=True)
        result = accum / total
        logs = jnp.broadcast_to(peak + jnp.log2(total), (rows, HD))
        for h in range(3):
            part = slice(h * count, (h + 1) * count)
            attn_all[0, begin : begin + count, h * HD : (h + 1) * HD] = result[part].astype(
                jnp.bfloat16
            )
            full[h, begin : begin + count, :] = result[part]
            log_total[h, begin : begin + count, :] = logs[part]

    def front(weights, ring, wo, x_rows, cot_turned):
        def fetch(t, slot, rows):
            return [
                pltpu.make_async_copy(
                    source.at[pl.ds(t * UNITS, rows)],
                    weights.at[slot, k, pl.ds(0, rows)],
                    weight_sem.at[slot, k],
                )
                for k, source in enumerate((wg_hbm, wu_hbm, wd_hbm))
            ]

        loads = [
            local(wo_hbm, wo.at[0]),
            local(x_hbm, x_rows),
            local(wo_all.at[2], wo.at[2]),
            local(wo_all.at[1], wo.at[1]),
            local(wo_all.at[3], wo.at[3]),
            local(all_hbm.at[0, me], cot_turned),
        ]
        wo_c.wait_recv()
        started(*loads[:3], loads[5])
        started(*fetch(0, 0, UNITS))
        attend_region(0, HALF, me, of_first, False)
        attend_region(TOK - HALF, HALF, 15 - me, of_first, False)
        wo_y.wait_recv()
        wo_cy.start()
        loads[3].start()
        attend_region(HALF, TOK - 2 * HALF, me, of_middle, True)
        started(attn_y, attn_c)
        wo_cy.wait_recv()
        loads[4].start()
        arrive(0, 1)
        arrive_inner(0, 2)
        started(attn_x)
        pass_y(0, 0)
        for load in loads[:4]:
            load.wait()
        for copy in (pair_1, pair_2, pair_3, *pair_near, *pair_core):
            copy.wait_send()
        def add_part(p, first=False):
            def body(n, carry):
                cols = pl.ds(pl.multiple_of(n * 512, 512), 512)
                held = x_rows[:, cols].astype(jnp.float32) if first else middle[:, cols]
                middle[:, cols] = held + matmul(attn_all[p], wo[p, :, cols])
                return carry

            lax.fori_loop(0, width // 512, body, 0)

        add_part(0, True)
        attn_c.wait_recv()
        add_part(2)
        attn_y.wait_recv()
        started(attn_cy)
        add_part(1)
        attn_cy.wait_recv()
        loads[4].wait()
        add_part(3)

        def norm(a, carry):
            rows = middle[rows_of(a), :]
            turned[:, rows_of(a)] = (rows * norm_scale(rows) * gain2).astype(jnp.bfloat16).T
            return carry

        lax.fori_loop(0, 4, norm, 0)
        own_blocks[1].start()
        own_blocks[1].wait()
        begin_spread(1)
        x_copy(1, 0).start()
        loads[5].wait()
        acc[...] = jnp.zeros_like(acc)

        def keep_tile(t):
            return pltpu.make_async_copy(ring.at[t % 2], own_hbm.at[t], weight_sem.at[2, t % 2])

        def tile(t, carry):
            slot = t % 2

            @pl.when(t < tiles - 1)
            def _():
                for copy in fetch(t, slot, UNITS):
                    copy.wait()

            @pl.when(t == tiles - 1)
            def _():
                for copy in fetch(t, slot, rest):
                    copy.wait()

            @pl.when(t + 1 < tiles - 1)
            def _():
                started(*fetch(t + 1, 1 - slot, UNITS))

            @pl.when(t + 1 == tiles - 1)
            def _():
                weights[1 - slot, :, rest:, :] = jnp.zeros(
                    (3, UNITS - rest, width), weights.dtype
                )
                started(*fetch(t + 1, 1 - slot, rest))

            gate = matmul(weights[slot, 0], turned[...])
            up_part = matmul(weights[slot, 1], turned[...])
            grad_hidden = matmul(weights[slot, 2], cot_turned[...])
            sigma = jax.nn.sigmoid(gate)
            swish = gate * sigma
            ring[slot, :, :UNITS] = (swish * up_part).astype(jnp.bfloat16).T
            ring[slot, :, UNITS : 2 * UNITS] = (
                (grad_hidden * up_part * sigma * (1.0 + gate * (1.0 - sigma)))
                .astype(jnp.bfloat16)
                .T
            )
            ring[slot, :, 2 * UNITS :] = (grad_hidden * swish).astype(jnp.bfloat16).T

            def body(n, carry):
                cols = pl.ds(pl.multiple_of(n * 512, 512), 512)
                acc[:, cols] += matmul(
                    ring[slot, :, UNITS : 2 * UNITS], weights[slot, 0, :, cols]
                ) + matmul(ring[slot, :, 2 * UNITS :], weights[slot, 1, :, cols])
                return carry

            lax.fori_loop(0, width // 512, body, 0)

            @pl.when(t > 0)
            def _():
                keep_tile(t - 1).wait()

            @pl.when(t == 3)
            def _():
                arrive_outer(0, 2)
                arrive_inner(0, 3)
                pass_core(0, 0)
                pass_y(0, 1)

            @pl.when(t == 7)
            def _():
                arrive(1, 1)
                arrive_inner(1, 2)
                pass_y(1, 0)
                pass_core(0, 1)

            keep_tile(t).start()
            return carry

        lax.fori_loop(0, tiles, tile, 0)
        keep_tile(tiles - 1).wait()
        x_tile.start()

    pl.run_scoped(
        front,
        pltpu.VMEM((2, 3, UNITS, width), jnp.bfloat16),
        pltpu.VMEM((2, TOK, 3 * UNITS), jnp.bfloat16),
        pltpu.VMEM((4, width // 4, width), jnp.bfloat16),
        pltpu.VMEM((TOK, width), jnp.bfloat16),
        pltpu.VMEM((width, TOK), jnp.bfloat16),
    )

    def reduce_start(total, sent, core_to):
        sent[...] = total[...].astype(jnp.bfloat16)
        copies = [
            remote(sent.at[rows_of(lane_c)], core_to.at[0], c_to),
            remote(sent.at[rows_of(lane_cy)], core_to.at[1], c_to),
        ]
        started(*copies)
        return copies

    def reduce_middle(total, copies, core_to, lane_to):
        for copy in copies:
            copy.wait()
        lane_send[...] = (
            total[rows_of(lane_y), :] + core_to[1].astype(jnp.float32)
        ).astype(jnp.bfloat16)
        copy = remote(lane_send, lane_to, y_to)
        copy.start()
        return copy

    def reduce_end(total, copy, core_to, lane_to):
        copy.wait()
        return (
            total[rows_of(lane), :]
            + core_to[0].astype(jnp.float32)
            + lane_to[...].astype(jnp.float32)
        )

    def spread_start(full):
        mine, theirs = full.at[rows_of(lane)], full.at[rows_of(lane_y)]
        copies = [
            remote(mine, mine, y_to),
            remote(mine, mine, c_to),
            remote(theirs, theirs, c_to),
        ]
        started(*copies[:2])
        return copies

    def spread_end(copies):
        copies[0].wait_recv()
        copies[2].start()
        copies[0].wait_send()
        copies[1].wait()
        copies[2].wait()

    near_base = used["remote"]
    used["remote"] += 4
    near_loads = [local(near_hbm.at[r], near_stage) for r in range(4)]

    def near_copy(r):
        index = near_base + r
        return pltpu.make_async_remote_copy(
            src_ref=sent_tile.at[rows_of_block(peers[r] - 4 * b2)], dst_ref=near_hbm.at[r],
            send_sem=send_sem.at[index], recv_sem=recv_sem.at[index],
            device_id={"cp": peers[r]}, device_id_type=pl.DeviceIdType.MESH,
        )

    final_base = used["local"]
    used["local"] += 3

    def final_copies(t):
        return [
            pltpu.make_async_copy(
                final.at[:, pl.ds(k * UNITS, UNITS)],
                tiles_out.at[k, :, pl.ds(pl.multiple_of(t * UNITS, UNITS), UNITS)],
                local_sem.at[final_base + k],
            )
            for k in range(3)
        ]

    def finish_tile(t, value):
        final[...] = value
        started(*final_copies(t))
        for copy in final_copies(t):
            copy.wait()

    SMALL = {"out": (0, 384, GB), "query": (384, 384, N1), "pair": (768, 128, N1)}
    small_base = used["remote"]
    used["remote"] += 6

    def small_copy(name, second):
        begin, wide, _ = SMALL[name]
        index = small_base + 2 * list(SMALL).index(name) + second
        cols = pl.ds(begin, wide)
        if second:
            src, dst, to = small_s2.at[:, cols], small_in2.at[:, cols], z2_to
        else:
            src, dst, to = small_s.at[pl.ds(half, half), cols], small_in.at[:, cols], z1_to
        return pltpu.make_async_remote_copy(
            src_ref=src, dst_ref=dst, send_sem=send_sem.at[index], recv_sem=recv_sem.at[index],
            device_id=to, device_id_type=pl.DeviceIdType.MESH,
        )

    def small_first(name, b_own, b_far):
        begin, wide, index = SMALL[name]
        cols = slice(begin, begin + wide)
        small_s[half:, cols] = (
            matmul(own_a[index, half:, :], b_own) + matmul(far_a[index, 1], b_far)
        ).astype(jnp.bfloat16)
        small_copy(name, 0).start()
        small_s[:half, cols] = (
            matmul(own_a[index, :half, :], b_own) + matmul(far_a[index, 0], b_far)
        ).astype(jnp.bfloat16)

    def small_second(name):
        begin, wide, _ = SMALL[name]
        cols = slice(begin, begin + wide)
        small_copy(name, 0).wait_recv()
        small_s2[:, cols] = (
            small_s[block:half, cols].astype(jnp.float32)
            + small_in[block:, cols].astype(jnp.float32)
        ).astype(jnp.bfloat16)
        small_copy(name, 1).start()
        small_copy(name, 0).wait_send()

    def small_third(name, out_ref):
        begin, wide, _ = SMALL[name]
        cols = slice(begin, begin + wide)
        small_copy(name, 1).wait()
        out_ref[...] = (
            small_s[:block, cols].astype(jnp.float32)
            + small_in[:block, cols].astype(jnp.float32)
            + small_in2[:, cols].astype(jnp.float32)
        )

    query_x = remote(grad_query, query_far, x_to)
    query_y = remote(grad_query, query_hbm.at[1], y_to)
    query_c = remote(grad_query, query_hbm.at[2], c_to)
    query_cy = remote(query_hbm.at[1], query_hbm.at[3], c_to)
    query_own = local(grad_query, query_hbm.at[0])
    pair_x = remote(grad_pair, pair_far, x_to)
    pair_y = remote(grad_pair, pair_hbm.at[1], y_to)
    pair_c = remote(grad_pair, pair_hbm.at[2], c_to)
    pair_cy = remote(pair_hbm.at[1], pair_hbm.at[3], c_to)
    pair_own = local(grad_pair, pair_hbm.at[0])
    here = output_out.at[rows_of(lane)]
    there = output_out.at[rows_of(lane_y)]
    out_spread = [
        remote(grad_full.at[rows_of(lane)], here, y_to),
        remote(grad_full.at[rows_of(lane)], here, c_to),
        remote(there, there, c_to),
    ]
    out_own = local(grad_full.at[rows_of(lane)], here)

    def rest_of(grads, wo_own, second, cots, weights, ring, total_tile):
        mine = [b0 + 2 * b1 + 4 * i for i in range(2)]
        weight_loads = [
            local(source.at[pl.ds(pl.multiple_of(tile * UNITS, UNITS), UNITS)], weights.at[i, k])
            for i, tile in enumerate(mine)
            for k, source in enumerate((wg_hbm, wu_hbm, wd_hbm))
        ]
        wo_load = local(wo_hbm, wo_own)
        started(*weight_loads, wo_load)
        block_base = used["local"]
        used["local"] += 4
        own_tiles = [local(own_hbm.at[tile], ring) for tile in mine]
        own_rows = pl.ds(pl.multiple_of(b2 * wide_half, wide_half), wide_half)

        def block_loads(j, side):
            slot = (2 * j + side) % 2
            return [
                pltpu.make_async_copy(
                    all_hbm.at[k, block_of(j, side)], ref.at[slot], local_sem.at[block_base + 2 * slot + k]
                )
                for k, ref in ((0, cots), (1, second))
            ]

        def prefetch(j, side):
            if side:
                d_copy(0, j, 1 - core).wait_recv()
                d_copy(1, j, 1 - core).wait_recv()
            elif j:
                c_copy(0, j, 1 - core).wait_recv()
                c_copy(1, j, 1 - core).wait_recv()
            started(*block_loads(j, side))

        def product(j, side):
            slot = (2 * j + side) % 2
            loads = block_loads(j, side)
            first = j == 0 and side == 0
            loads[1].wait()
            for i in range(2):
                if first:
                    own_tiles[i].start()
                    own_tiles[i].wait()
                    if i == 0:
                        loads[0].wait()
                else:
                    gate = matmul(weights[i, 0], second[slot])
                    up_part = matmul(weights[i, 1], second[slot])
                    sigma = jax.nn.sigmoid(gate)
                    swish = gate * sigma
                    ring[:, :UNITS] = (swish * up_part).astype(jnp.bfloat16).T
                    if i == 0:
                        loads[0].wait()
                    grad_hidden = matmul(weights[i, 2], cots[slot])
                    ring[:, UNITS : 2 * UNITS] = (
                        (grad_hidden * up_part * sigma * (1.0 + gate * (1.0 - sigma)))
                        .astype(jnp.bfloat16)
                        .T
                    )
                    ring[:, 2 * UNITS :] = (grad_hidden * swish).astype(jnp.bfloat16).T
                for n, rows in enumerate((cots, second, second)):
                    cols = slice(n * UNITS, (n + 1) * UNITS)
                    total_cols = slice((3 * i + n) * UNITS, (3 * i + n + 1) * UNITS)
                    value = matmul(rows[slot, own_rows, :], ring[:, cols])
                    if first:
                        total_tile[:, total_cols] = value
                    else:
                        total_tile[:, total_cols] += value

        far_loads = [
            local(
                all_hbm.at[k, block_of(0, side), row_block(0, p // 2, p % 2)],
                (far_a.at[k, p // 2, pl.ds((p % 2) * block, block)] if side else own_a.at[k, pl.ds(p * block, block)]),
            )
            for k in range(2)
            for side in range(2)
            for p in range(4)
        ]
        stage, far_stage = sent_tile.at[:TOK, : 3 * UNITS], sent_tile.at[:TOK, 3 * UNITS :]
        last_loads = [local(own_hbm.at[tiles - 1], stage), local(far_hbm, far_stage)]

        def last_first():
            x_tile.wait_recv()
            started(*far_loads, *last_loads)
            for load in (*far_loads, *last_loads):
                load.wait()

            def body(n, h):
                cols = pl.ds(pl.multiple_of(n * UNITS, UNITS), UNITS)
                far_cols = pl.ds(pl.multiple_of((3 + n) * UNITS, UNITS), UNITS)
                index = (n + 1) // 2
                return cols, matmul(
                    own_a[index, h * half : (h + 1) * half, :], sent_tile[:TOK, cols]
                ) + matmul(far_a[index, h], sent_tile[:TOK, far_cols])

            def sent(n, carry):
                cols, value = body(n, 1)
                part_s[:, cols] = value.astype(jnp.bfloat16)
                return carry

            def kept(n, carry):
                cols, value = body(n, 0)
                part_k[:, cols] = value
                return carry

            lax.fori_loop(0, 3, sent, 0)
            z1_tile.start()
            lax.fori_loop(0, 3, kept, 0)

        copies = reduce_start(acc, rel, core_in)
        prefetch(0, 0)
        for load in weight_loads:
            load.wait()
        lane_copy = reduce_middle(acc, copies, core_in, lane_in)
        product(0, 0)
        pass_core(1, 0)
        arrive_outer(0, 3)
        grad_full[rows_of(lane), :] = reduce_end(acc, lane_copy, core_in, lane_in).astype(
            jnp.bfloat16
        )
        spread = spread_start(grad_full)
        cot_load = started(local(cot_hbm, rel))
        prefetch(0, 1)
        pass_y(0, 2)
        pass_y(1, 1)
        product(0, 1)
        arrive_inner(1, 3)
        grads[...] = jnp.zeros_like(grads)
        spread_end(spread)
        cot_load.wait()
        wo_load.wait()

        def middle_back(a, total):
            grad = grad_full[rows_of(a), :].astype(jnp.float32)
            rows = middle[rows_of(a), :]
            factor2 = norm_scale(rows)
            weighted = grad * gain2
            result = (
                rel[rows_of(a), :].astype(jnp.float32)
                + factor2 * weighted
                - rows * factor2**3 * jnp.mean(weighted * rows, axis=-1, keepdims=True)
            )
            acc[rows_of(a), :] = result
            turned[:, rows_of(a)] = result.astype(jnp.bfloat16).T
            return total + jnp.sum(grad * rows * factor2, axis=0, keepdims=True)

        sums[...] = jnp.zeros_like(sums)
        sums[0, 1:2, :] = lax.fori_loop(
            0, 4, middle_back, jnp.zeros((1, width), jnp.float32)
        )
        middle_copy = started(local(acc, middle_hbm))
        branch_x = share(turned, GB)
        pass_core(0, 2)
        attn_cy.wait_send()
        attn_all[1] = matmul(wo_own[...], turned[...]).astype(jnp.bfloat16).T
        for p in range(4):
            own_a[GB, p * block : (p + 1) * block, :] = turned[row_block(0, p // 2, p % 2), :]
        arrive_outer(1, 2)
        prefetch(1, 0)
        product(1, 0)
        pass_core(1, 1)
        pass_core(0, 3)
        last_first()

        def region(begin, count, blocks, locate, shared):
            heads = query.shape[0]
            rows = heads * count
            q_rows = region_rows(query, begin, count)
            grad_rows = jnp.concatenate(
                [attn_all[1, begin : begin + count, h * HD : (h + 1) * HD] for h in range(heads)], 0
            )
            logs = region_rows(log_total, begin, count)[:, :1]
            delta = jnp.sum(
                grad_rows.astype(jnp.float32) * region_rows(full, begin, count),
                axis=1,
                keepdims=True,
            )

            def add(t, carry, diagonal=False):
                device, slot, place = rows_at(t, locate, count)
                keys, values = pair[0, slot, place, :], pair[1, slot, place, :]
                probs = jnp.exp2(contract_cols(q_rows, keys) * factor - logs)
                if diagonal:
                    probs = jnp.where(triangle(rows, count), probs, 0.0)
                elif shared:
                    probs = jnp.where(same_document(device), probs, 0.0)
                grad_scores = (probs * (contract_cols(grad_rows, values) - delta)).astype(
                    jnp.bfloat16
                )
                grads[0, slot, place, :] += contract_rows(grad_scores, q_rows)
                grads[1, slot, place, :] += contract_rows(probs.astype(jnp.bfloat16), grad_rows)
                return carry + matmul(grad_scores, keys)

            total = add(blocks, jnp.zeros((rows, HD), jnp.float32), True)
            total = lax.fori_loop(0, blocks, add, total) * scale
            cosines, sines = cosine[begin : begin + count, :], sine[begin : begin + count, :]
            for h in range(heads):
                part = total[h * count : (h + 1) * count]
                grad_query[begin : begin + count, h * HD : (h + 1) * HD] = (
                    turn_back(part, cosines, sines)
                ).astype(jnp.bfloat16)

        region(0, HALF, me, of_first, False)
        region(TOK - HALF, HALF, 15 - me, of_first, False)
        prefetch(1, 1)
        product(1, 1)
        prefetch(2, 0)
        arrive_outer(1, 3)
        pass_core(1, 2)
        region(HALF, TOK - 2 * HALF, me, of_middle, True)

        keep_by = is_key * scale + (1.0 - is_key)
        send_by = (1.0 - is_key) * scale + is_key

        def to_core(s, carry):
            kv_send[s] = (grads[1 - core, s] * send_by).astype(jnp.bfloat16)
            return carry

        lax.fori_loop(0, 8, to_core, 0)
        kv_c = remote(kv_send.at[pl.ds(0, 8)], kv_in.at[pl.ds(0, 8)], c_to)
        kv_x = remote(kv_send.at[pl.ds(0, 4)], kv_in.at[pl.ds(8, 4)], x_to)
        kv_1 = remote(kv_send.at[pl.ds(4, 2)], kv_in.at[pl.ds(12, 2)], z1_to)
        kv_2 = remote(kv_send.at[pl.ds(6, 1)], kv_in.at[pl.ds(14, 1)], z2_to)
        kv_c.start()
        started(query_y, query_c, query_own)
        product(2, 0)
        prefetch(2, 1)
        kv_c.wait()

        def from_core(s, carry):
            grads[core, s] = grads[core, s] * keep_by + kv_in[s].astype(jnp.float32)
            return carry

        lax.fori_loop(0, 8, from_core, 0)

        def pass_on(copy, first, count):
            def cast(s, carry):
                kv_send[first - 8 + s] = grads[core, count + s].astype(jnp.bfloat16)
                return carry

            lax.fori_loop(0, count, cast, 0)
            copy.start()

        def take(copy, first, count):
            copy.wait()

            def add(s, carry):
                grads[core, s] += kv_in[first + s].astype(jnp.float32)
                return carry

            lax.fori_loop(0, count, add, 0)

        pass_on(kv_x, 8, 4)
        started(query_x, *branch_x, wq_y, wq_c)
        product(2, 1)
        prefetch(3, 0)
        z1_tile.wait_recv()
        part_s2[...] = (
            part_k[block:, :] + near1[block:, :].astype(jnp.float32)
        ).astype(jnp.bfloat16)
        z2_tile.start()
        product(3, 0)
        take(kv_x, 8, 4)
        pass_on(kv_1, 12, 2)
        pass_core(1, 3)
        prefetch(3, 1)
        n1_forward = forward(N1)
        for copy in n1_x:
            copy.wait()
        n1_forward.start()
        product(3, 1)
        sent_tile[...] = total_tile[...].astype(jnp.bfloat16)
        take(kv_1, 12, 2)
        pass_on(kv_2, 14, 1)
        for r in (3, 1, 2):
            near_copy(r).start()
        query_y.wait_recv()
        query_cy.start()
        for copy in branch_x:
            copy.wait()
        branch_c = started(forward(GB))
        for i, tile in enumerate(mine):
            finish_tile(
                tile,
                total_tile[
                    rows_of_block(me - 4 * b2), i * 3 * UNITS : (i + 1) * 3 * UNITS
                ],
            )
        attn_x.wait()
        branch_c.wait()
        small_first("out", attn_all[0], attn_far[...])
        query_x.wait()
        n1_forward.wait()
        small_first("query", grad_query[...], query_far[...])
        kv_2.wait()
        f_cos = cosine[...] * is_key + (1.0 - is_key)
        f_sin = sine[...] * is_key
        total = grads[core, 0] + kv_in[14].astype(jnp.float32)
        grad_pair[...] = turn_back(total, f_cos, f_sin).astype(jnp.bfloat16)
        started(pair_x, pair_y, pair_c, pair_own)
        wq_y.wait_recv()
        wq_cy.start()

        def down(weights, hidden):
            def fetch(t, slot, rows):
                return [
                    pltpu.make_async_copy(
                        wd_hbm.at[pl.ds(t * UNITS, rows)],
                        weights.at[slot, pl.ds(0, rows)],
                        weight_sem.at[slot, 0],
                    ),
                    pltpu.make_async_copy(
                        own_hbm.at[t, :, pl.ds(0, UNITS)], hidden.at[slot], weight_sem.at[slot, 1]
                    ),
                ]

            started(*fetch(0, 0, UNITS))

            def tile(t, carry):
                slot = t % 2

                @pl.when(t < tiles - 1)
                def _():
                    for copy in fetch(t, slot, UNITS):
                        copy.wait()

                @pl.when(t == tiles - 1)
                def _():
                    for copy in fetch(t, slot, rest):
                        copy.wait()

                @pl.when(t + 1 < tiles - 1)
                def _():
                    started(*fetch(t + 1, 1 - slot, UNITS))

                @pl.when(t + 1 == tiles - 1)
                def _():
                    weights[1 - slot, rest:, :] = jnp.zeros((UNITS - rest, width), weights.dtype)
                    started(*fetch(t + 1, 1 - slot, rest))

                def body(n, carry):
                    cols = pl.ds(pl.multiple_of(n * 512, 512), 512)
                    product = matmul(hidden[slot], weights[slot, :, cols])
                    acc[:, cols] = jnp.where(t == 0, product, acc[:, cols] + product)
                    return carry

                lax.fori_loop(0, width // 512, body, 0)
                return carry

            lax.fori_loop(0, tiles, tile, 0)

        middle_copy.wait()
        pl.run_scoped(
            down,
            pltpu.VMEM((2, UNITS, width), jnp.bfloat16),
            pltpu.VMEM((2, TOK, UNITS), jnp.bfloat16),
        )
        out_copies = reduce_start(acc, rel, core_in)
        small_second("out")
        out_lane = reduce_middle(acc, out_copies, core_in, lane_in)
        small_second("query")
        z2_tile.wait_recv()
        finish_tile(
            tiles - 1,
            part_k[:block, :]
            + near1[:block, :].astype(jnp.float32)
            + near2[...].astype(jnp.float32),
        )
        out_rows = reduce_end(acc, out_lane, core_in, lane_in) + middle[rows_of(lane), :]
        grad_full[rows_of(lane), :] = out_rows.astype(jnp.bfloat16)
        started(out_spread[0], out_spread[1], out_own)

    pl.run_scoped(
        rest_of,
        pltpu.VMEM((2, 8, TOK, HD), jnp.float32),
        pltpu.VMEM((width // 4, width), jnp.bfloat16),
        pltpu.VMEM((2, width, TOK), jnp.bfloat16),
        pltpu.VMEM((2, width, TOK), jnp.bfloat16),
        pltpu.VMEM((2, 3, UNITS, width), jnp.bfloat16),
        pltpu.VMEM((TOK, 3 * UNITS), jnp.bfloat16),
        pltpu.VMEM((width // 2, 6 * UNITS), jnp.float32),
    )
    pair_x.wait()
    small_first("pair", grad_pair[...], pair_far[...])
    pair_y.wait_recv()
    pair_cy.start()
    out_spread[0].wait_recv()
    out_spread[2].start()
    small_third("out", wo_out)
    pair_cy.wait_recv()
    pair_c.wait_recv()
    query_own.wait()
    pair_own.wait()
    query_c.wait_recv()
    query_cy.wait_recv()
    wq_c.wait_recv()
    wq_cy.wait_recv()

    def closing(x_rows, queries, pairs, w_queries, w_pairs):
        loads = [
            local(query_hbm, queries),
            local(wq_all.at[pl.ds(1, 3)], w_queries.at[pl.ds(1, 3)]),
            local(wq_hbm, w_queries.at[0]),
            local(pair_hbm, pairs),
            local(wk_hbm, w_pairs.at[0]),
            local(wv_hbm, w_pairs.at[1]),
            local(x_hbm, x_rows),
            local(middle_hbm, middle),
        ]
        started(*loads)
        for load in loads:
            load.wait()

        def part_of(n, carry):
            cols = pl.ds(pl.multiple_of(n * 512, 512), 512)
            total = jnp.zeros((TOK, 512), jnp.float32)
            for p, far in enumerate(TP_ORDER):
                kind = (core + far % 2) % 2
                head = (high + far // 2) % 2
                lanes = pl.ds(pl.multiple_of(head * HD, HD), HD)
                total += contract_cols(queries[p], w_queries[p, cols, :])
                total += contract_cols(pairs[p], w_pairs[kind, cols, lanes])
            acc[:, cols] = total
            return carry

        lax.fori_loop(0, width // 512, part_of, 0)

        def last(a, total):
            grad = acc[rows_of(a), :]
            rows = x_rows[rows_of(a), :].astype(jnp.float32)
            scale1 = norm_scale(rows)
            weighted = grad * gain1
            rel[rows_of(a), :] = (
                middle[rows_of(a), :]
                + scale1 * weighted
                - rows * scale1**3 * jnp.mean(weighted * rows, axis=-1, keepdims=True)
            ).astype(jnp.bfloat16)
            return total + jnp.sum(grad * rows * scale1, axis=0, keepdims=True)

        gain1_part = lax.fori_loop(0, 4, last, jnp.zeros((1, width), jnp.float32))
        copy = started(local(rel, input_out))
        sums[0, 0:1, :] = gain1_part
        sums[0, 2:3, : 3 * HD] = jnp.sum(
            grad_query[...].astype(jnp.float32), axis=0, keepdims=True
        )
        sums[0, 2:3, 3 * HD : 4 * HD] = jnp.sum(
            grad_pair[...].astype(jnp.float32), axis=0, keepdims=True
        )
        sums_copies[0].start()
        copy.wait()

    sums_copies = [
        remote(sums.at[i], sums_in.at[i], to) for i, to in enumerate((x_to, z1_to, z2_to))
    ]
    pl.run_scoped(
        closing,
        pltpu.VMEM((TOK, width), jnp.bfloat16),
        pltpu.VMEM((4, TOK, 3 * HD), jnp.bfloat16),
        pltpu.VMEM((4, TOK, HD), jnp.bfloat16),
        pltpu.VMEM((4, width, 3 * HD), jnp.bfloat16),
        pltpu.VMEM((2, width, 2 * HD), jnp.bfloat16),
    )
    sums_copies[0].wait()
    sums[1] = sums[0] + sums_in[0]
    sums_copies[1].start()
    small_second("pair")
    small_third("query", wq_out)

    def take_near(r):
        near_copy(r).wait_recv()
        near_loads[r].start()
        near_loads[r].wait()
        for i in range(2):
            finish_tile(
                peers[r] - 4 * b2 + 4 * i,
                near_stage[:, i * 3 * UNITS : (i + 1) * 3 * UNITS].astype(jnp.float32),
            )

    take_near(1)
    take_near(2)
    sums_copies[1].wait()
    sums[2] = sums[1] + sums_in[1]
    sums_copies[2].start()
    take_near(3)
    small_third("pair", wp_out)
    sums_copies[2].wait()
    sums_out[...] = sums[2] + sums_in[2]
    x_tile.wait_send()
    z1_tile.wait_send()
    z2_tile.wait_send()
    for r in (1, 2, 3):
        near_copy(r).wait_send()
    for k in range(2):
        z_copy(k, 0).wait_send()

        @when(inner)
        def _():
            for m in (1, 2, 3, 4):
                z_copy(k, m).wait_send()

        for j in range(4):
            if j:
                c_copy(k, j).wait_send()
            x_copy(k, j).wait_send()
            if (k, j) not in WHOLE_HALVES:
                y_copy(k, j).wait_send()
            d_copy(k, j).wait_send()
    for copy in (
        attn_y, attn_c, query_y, query_c, query_cy, pair_y, pair_c, pair_cy,
        out_spread[0], wo_y, wo_c, wo_cy, wq_y, wq_c, wq_cy,
    ):
        copy.wait_send()
    for copy in (out_spread[1], out_spread[2]):
        copy.wait()
    out_own.wait()
    assert used["remote"] <= REMOTE and used["local"] <= LOCAL, used


WHOLE_HALVES = ((0, 3), (1, 2), (1, 3))
REMOTE = 134
LOCAL = 130


def whole_layer(
    docs, gains, biases, cosine, sine, x, cot, w_query, w_key, w_value, w_out, w_gate, w_up, w_down
):
    tok_rows, width = x.shape
    units = w_gate.shape[0]
    tiles = pl.cdiv(units, UNITS)
    half, block, quarter = width // 4, width // 8, tok_rows // 4
    low, wide = jnp.bfloat16, jnp.float32
    shape = jax.ShapeDtypeStruct
    any_ = pl.BlockSpec(memory_space=pl.ANY)
    outs = (
        shape((3, block, tiles * UNITS), wide),
        shape((block, 384), wide),
        shape((block, 384), wide),
        shape((block, HD), wide),
        shape((8, width), wide),
        shape((tok_rows, width), low),
        shape((tok_rows, width), low),
        shape((tok_rows, width), wide),
        shape((4, tok_rows, 384), low),
        shape((4, tok_rows, HD), low),
        shape((tiles, tok_rows, 3 * UNITS), low),
        shape((tok_rows, 3 * UNITS), low),
        shape((4, block, 6 * UNITS), low),
        shape((4,) + w_out.shape, low),
        shape((4,) + w_query.shape, low),
        shape((2, 8, width, tok_rows), low),
        shape((width, tok_rows), low),
    )
    vmem = pltpu.VMEM
    scratch = [
        vmem((3, tok_rows, HD), low),
        vmem((2, 8, tok_rows, HD), low),
        vmem((3, tok_rows, HD), wide),
        vmem((3, tok_rows, HD), wide),
        vmem((3, 8, width), wide),
        vmem((3, 8, width), wide),
        vmem((4, tok_rows, 384), low),
        vmem((tok_rows, 384), low),
        vmem((tok_rows, 384), low),
        vmem((tok_rows, HD), low),
        vmem((tok_rows, width), wide),
        vmem((tok_rows, width), wide),
        vmem((width, tok_rows), low),
        vmem((4, width // 2, tok_rows), low),
        vmem((4, 2, half, tok_rows), low),
        vmem((half, 3 * UNITS), low),
        vmem((half, 3 * UNITS), wide),
        vmem((half, 3 * UNITS), low),
        vmem((block, 3 * UNITS), low),
        vmem((block, 3 * UNITS), low),
        vmem((block, 6 * UNITS), low),
        vmem((block, 3 * UNITS), wide),
        vmem((width // 2, 6 * UNITS), low),
        vmem((tok_rows, width), low),
        vmem((2, quarter, width), low),
        vmem((quarter, width), low),
        vmem((quarter, width), low),
        vmem((tok_rows, width), low),
        vmem((8, tok_rows, HD), low),
        vmem((15, tok_rows, HD), low),
        vmem((tok_rows, 384), low),
        vmem((tok_rows, HD), low),
        vmem((2 * half, 896), low),
        vmem((half, 896), low),
        vmem((block, 896), low),
        vmem((block, 896), low),
        pltpu.SemaphoreType.DMA((REMOTE,)),
        pltpu.SemaphoreType.DMA((REMOTE,)),
        pltpu.SemaphoreType.DMA((LOCAL,)),
        pltpu.SemaphoreType.DMA((3, 3)),
    ]
    return pl.pallas_call(
        functools.partial(back_kernel, width, units),
        out_shape=outs,
        in_specs=[VMEM] * 5 + [any_] * 9,
        out_specs=(any_, VMEM, VMEM, VMEM, VMEM) + (any_,) * 12,
        scratch_shapes=scratch,
        compiler_params=pltpu.CompilerParams(
            vmem_limit_bytes=64 * 1024 * 1024, collective_id=0, has_side_effects=True
        ),
        cost_estimate=pl.CostEstimate(
            flops=20 * tok_rows * width * units, bytes_accessed=10 * width * units, transcendentals=0
        ),
    )(docs, gains, biases, cosine, sine, x, cot, w_query, w_key, w_value, w_out, w_gate, w_up, w_down)


def on_device(
    layer_input,
    norm1_gain,
    w_query,
    b_query,
    w_key,
    b_key,
    w_value,
    b_value,
    w_out,
    norm2_gain,
    w_gate,
    w_up,
    w_down,
    doc_ids,
    positions,
    cotangent,
):
    tok_rows, width = layer_input.shape
    shards = lax.axis_size("cp")
    heads = w_query.shape[1] // HD
    kv_heads = w_key.shape[1] // HD
    me = lax.axis_index("cp")
    lane = lax.axis_index("tp")
    core = lane % 2
    kv_index = lane * heads // (H // kv_heads)
    is_key = core == 0

    def assemble(parts, axis):
        at = lambda index: lax.dynamic_index_in_dim(parts, reverse_bits(lane ^ index, 2), 0, keepdims=False)
        return (
            jnp.concatenate([at(0), at(2)], axis),
            jnp.concatenate([at(1), at(3)], axis),
        )

    def finish(
        output, grad_middle, grad_normed1, grad_query, grad_pair, gain2_part,
        grad_w_query, grad_w_pair, grad_w_out, grad_w_gate, grad_w_up, grad_w_down,
    ):
        weighted1 = grad_normed1 * norm1_gain
        gain1_part = jnp.sum(grad_normed1 * inputs * scale1, axis=0)
        grad_input = (
            grad_middle
            + scale1 * weighted1
            - inputs * scale1**3 * jnp.mean(weighted1 * inputs, axis=-1, keepdims=True)
        ).astype(jnp.bfloat16)

        small = jnp.concatenate(
            [
                gain1_part,
                gain2_part,
                jnp.sum(grad_query.astype(jnp.float32), axis=0),
                jnp.sum(grad_pair.astype(jnp.float32), axis=0),
            ]
        ).reshape(-1, HD)
        bit = 1
        while bit < shards:
            small = small + swap(small, "cp", bit)
            bit *= 2
        wide = width // HD
        gain1_sum = small[:wide].reshape(-1)
        gain2_sum = small[wide : 2 * wide].reshape(-1)
        bias_query = small[2 * wide : 2 * wide + heads].reshape(-1)

        bias_key, bias_value = assemble(gather_tp(small[None, 2 * wide + heads], 0), 0)
        grad_w_key, grad_w_value = assemble(gather_tp(grad_w_pair[None], 0), 1)
        return (
            output,
            grad_input,
            gain1_sum,
            grad_w_query,
            bias_query,
            grad_w_key,
            bias_key,
            grad_w_value,
            bias_value,
            grad_w_out,
            gain2_sum,
            grad_w_gate,
            grad_w_up,
            grad_w_down,
        )

    middle_docs = doc_ids.reshape(shards, tok_rows)[:, HALF]
    my_doc = middle_docs[me]
    start = jnp.sum((middle_docs < my_doc).astype(jnp.int32))
    place = jnp.stack([me, core, lane, start]).astype(jnp.int32)
    my_pos = lax.dynamic_slice_in_dim(positions, me * tok_rows, tok_rows)
    cosine, sine = rope_tables(my_pos, HD)

    pair_bias = lax.dynamic_slice_in_dim(jnp.where(is_key, b_key, b_value), kv_index * HD, HD)

    if shards == 8 and tok_rows == TOK:
        tiles, grad_w_out, grad_w_query, grad_w_pair, sums, output, grad_input, *_ = whole_layer(
            jnp.broadcast_to(middle_docs[:, None], (shards, 2 * HALF)),
            jnp.stack([norm1_gain, norm2_gain]),
            jnp.concatenate([b_query, pair_bias])[None],
            cosine, sine, layer_input, cotangent, w_query, w_key, w_value, w_out,
            w_gate.T, w_up.T, w_down,
        )
        units = w_gate.shape[1]
        bias_query, bias_pair = sums[2, : heads * HD], sums[2, heads * HD : (heads + 1) * HD]
        bias_key, bias_value = assemble(gather_tp(bias_pair[None], 0), 0)
        grad_w_key, grad_w_value = assemble(gather_tp(grad_w_pair[None], 0), 1)
        return (
            output,
            grad_input,
            sums[0],
            grad_w_query,
            bias_query,
            grad_w_key,
            bias_key,
            grad_w_value,
            bias_value,
            grad_w_out.T,
            sums[1],
            tiles[1, :, :units],
            tiles[2, :, :units],
            tiles[0, :, :units].T,
        )

    inputs = layer_input.astype(jnp.float32)
    scale1 = lax.rsqrt(jnp.mean(inputs * inputs, axis=-1, keepdims=True) + EPSILON)
    normed1 = (inputs * scale1 * norm1_gain).astype(jnp.bfloat16)

    def pair_weight(index):
        head = index * heads // (H // kv_heads)
        source = jnp.where(index % 2 == 0, w_key, w_value)
        return lax.dynamic_slice_in_dim(source, head * HD, HD, 1)

    pair_cos = jnp.where(is_key, cosine, 1.0)
    pair_sin = jnp.where(is_key, sine, 0.0)
    pair_pre = matmul(normed1, pair_weight(lane)) + pair_bias
    pair = rotary(pair_pre, pair_cos, pair_sin).astype(jnp.bfloat16)[None]
    bit = shards // 2
    while bit:
        pair = jnp.concatenate([pair, swap(pair, "cp", bit)], 0)
        bit //= 2
    other = swap(pair, "tp", 1)

    q_pre = matmul(normed1, w_query) + b_query
    query = rotary(
        q_pre.reshape(tok_rows, heads, HD), cosine[:, None, :], sine[:, None, :]
    ).astype(jnp.bfloat16)
    query = query.transpose(1, 0, 2)

    attn, attn_full, log_total, pair = attend(place, query, pair, other)
    w_out_all = gather_tp(w_out, 0)
    w_query_all = gather_tp(w_query, 1)
    cot_shared = share(place, cotangent, shards)
    normed1_shared = share(place, normed1, shards)

    middle = inputs + matmul(gather_tp(attn, 1), w_out_all)
    scale2 = lax.rsqrt(jnp.mean(middle * middle, axis=-1, keepdims=True) + EPSILON)
    normed2 = (middle * scale2 * norm2_gain).astype(jnp.bfloat16)

    units = w_gate.shape[1]
    chunks = pl.cdiv(pl.cdiv(units, TILE), CHUNK_TILES)
    hiddens, grads, total = [], [], None
    for index in range(chunks):
        hidden, grad, total = hidden_chunk(
            place, normed2, cotangent, w_gate, w_up, w_down, total, index
        )
        hiddens.append(hidden)
        grads.append(grad)
    normed2_shared = share(place, normed2, shards)

    downs, gates, ups = [], [], []
    for hidden, grad in zip(hiddens, grads):
        downs.append(weight_grad(place, cot_shared, hidden, shards).T)
        both = weight_grad(place, normed2_shared, grad, shards)
        span = hidden.shape[1]
        for at in range(0, span, TILE):
            size = min(TILE, span - at)
            gates.append(both[:, 2 * at : 2 * at + size])
            ups.append(both[:, 2 * at + TILE : 2 * at + TILE + size])
    grad_w_down = jnp.concatenate(downs, 0)
    grad_w_gate = jnp.concatenate(gates, 1)
    grad_w_up = jnp.concatenate(ups, 1)

    grad_normed2 = in_order(gather_tp(scatter_tp(total).astype(jnp.bfloat16), 0), lane).astype(
        jnp.float32
    )
    weighted2 = grad_normed2 * norm2_gain
    gain2_part = jnp.sum(grad_normed2 * middle * scale2, axis=0)
    grad_middle = (
        cotangent.astype(jnp.float32)
        + scale2 * weighted2
        - middle * scale2**3 * jnp.mean(weighted2 * middle, axis=-1, keepdims=True)
    )
    grad_branch = grad_middle.astype(jnp.bfloat16)
    grad_attn = contract_cols(grad_branch, w_out).astype(jnp.bfloat16)
    grad_query, keep, send = attend_back(
        place, query, pair, grad_attn, attn_full, log_total, cosine, sine
    )

    part = tok_rows // 4
    ffn = sum(matmul(h, lax.slice_in_dim(w_down, i * CHUNK_TILES * TILE, i * CHUNK_TILES * TILE + h.shape[1])) for i, h in enumerate(hiddens))
    ffn = after(ffn.astype(jnp.bfloat16), grad_middle)
    ffn_rel = jnp.concatenate(
        [lax.dynamic_slice_in_dim(ffn, (lane ^ far) * part, part, 0) for far in TP_ORDER], 0
    )
    out_part = scatter_tp(ffn_rel) + lax.dynamic_slice_in_dim(middle, lane * part, part, 0)
    output = in_order(gather_tp(out_part.astype(jnp.bfloat16), 0), lane)

    summed = keep.astype(jnp.float32) + swap(send, "tp", 1).astype(jnp.float32)
    bit = 1
    while bit < shards:
        count = summed.shape[0] // 2
        summed = summed[:count] + swap(summed[count:].astype(jnp.bfloat16), "cp", bit).astype(
            jnp.float32
        )
        bit *= 2
    grad_pair = rotary_back(summed[0], pair_cos, pair_sin).astype(jnp.bfloat16)

    branch_shared = share(place, grad_branch, shards)
    grad_w_out = weight_grad(place, branch_shared, attn, shards).T
    grad_w_query = weight_grad(place, normed1_shared, grad_query, shards)
    grad_w_pair = weight_grad(place, normed1_shared, grad_pair, shards)

    pairs_all = gather_tp(grad_pair, 1)
    grad_normed1 = contract_cols(gather_tp(grad_query, 1), w_query_all)
    for i, far in enumerate(TP_ORDER):
        grad_normed1 = grad_normed1 + contract_cols(
            pairs_all[:, i * HD : (i + 1) * HD], pair_weight(lane ^ far)
        )
    return finish(
        output, grad_middle, grad_normed1, grad_query, grad_pair, gain2_part,
        grad_w_query, grad_w_pair, grad_w_out, grad_w_gate, grad_w_up, grad_w_down,
    )


def solution(mesh):
    return jax.shard_map(
        on_device,
        mesh=mesh,
        in_specs=(
            P("cp", None),
            P(),
            P(None, "tp"),
            P("tp"),
            P(),
            P(),
            P(),
            P(),
            P("tp", None),
            P(),
            P(None, "tp"),
            P(None, "tp"),
            P("tp", None),
            P(),
            P(),
            P("cp", None),
        ),
        out_specs=(
            P("cp", None),
            P("cp", None),
            P(),
            P("cp", "tp"),
            P("tp"),
            P("cp", None),
            P(),
            P("cp", None),
            P(),
            P("tp", "cp"),
            P(),
            P("cp", "tp"),
            P("cp", "tp"),
            P("tp", "cp"),
        ),
        check_vma=False,
    )
```

```python
import functools
import math

import jax
import jax.numpy as jnp
from jax import lax
from jax.experimental import pallas as pl
from jax.experimental.pallas import tpu as pltpu
from jax.sharding import PartitionSpec as P

H = 12
HD = 128
HALF = 128
EPSILON = 1e-06
ROPE_BASE = 10000.0
MASKED = -1e30
LOG2E = 1.4426950408889634
TILE = 256
CHUNK_TILES = 3
VMEM_LIMIT = 56 * 1024 * 1024
TP_ORDER = (0, 2, 1, 3)


def matmul(left, right):
    return jnp.dot(left, right, preferred_element_type=jnp.float32)


def contract_rows(left, right):
    return lax.dot_general(
        left, right, (((0,), (0,)), ((), ())), preferred_element_type=jnp.float32
    )


def contract_cols(left, right):
    return lax.dot_general(
        left, right, (((1,), (1,)), ((), ())), preferred_element_type=jnp.float32
    )


def rope_tables(tok_pos, width):
    half = width // 2
    freq = ROPE_BASE ** (-(jnp.arange(half, dtype=jnp.float32) * 2.0 / width))
    angle = tok_pos.astype(jnp.float32)[:, None] * freq[None, :]
    cosine = jnp.concatenate([jnp.cos(angle), jnp.cos(angle)], -1)
    sine = jnp.concatenate([jnp.sin(angle), jnp.sin(angle)], -1)
    return (cosine, sine)


def rotary(values, cosine, sine):
    half = values.shape[-1] // 2
    return values * cosine + jnp.concatenate([-values[..., half:], values[..., :half]], -1) * sine


def rotary_back(grads, cosine, sine):
    half = grads.shape[-1] // 2
    scaled = grads * sine
    return grads * cosine + jnp.concatenate([scaled[..., half:], -scaled[..., :half]], -1)


def swap(value, axis, bit):
    size = lax.axis_size(axis)
    return lax.ppermute(value, axis, [(i, i ^ bit) for i in range(size)])


def after(value, *earlier):
    return lax.optimization_barrier((value, *earlier))[0]


def bits_of(size):
    return size.bit_length() - 1


def reverse_bits(index, bits):
    out = 0
    for i in range(bits):
        out = out | (((index >> i) & 1) << (bits - 1 - i))
    return out


def params(**more):
    return pltpu.CompilerParams(vmem_limit_bytes=VMEM_LIMIT, **more)


SMEM = pl.BlockSpec(memory_space=pltpu.SMEM)
VMEM = pl.BlockSpec(memory_space=pltpu.VMEM)


def spread_kernel(shards, place_ref, rows_ref, own_ref, send_ref, turned):
    me, core = place_ref[0], place_ref[1]
    turned[...] = rows_ref[...].T
    width = turned.shape[0] // shards
    bits = bits_of(shards)
    for i in range(shards // 2):
        far = reverse_bits(i, bits)
        block = pl.multiple_of((me ^ far) * width, 16)
        own_ref[i * width : (i + 1) * width, :] = turned[pl.ds(block, width), :]
    for i in range(shards // 4):
        far = reverse_bits(core * (shards // 4) + i, bits) | 1
        block = pl.multiple_of((me ^ far) * width, 16)
        send_ref[i * width : (i + 1) * width, :] = turned[pl.ds(block, width), :]


def spread(place, rows, shards):
    count, width = rows.shape
    return pl.pallas_call(
        functools.partial(spread_kernel, shards),
        out_shape=(
            jax.ShapeDtypeStruct((width // 2, count), rows.dtype),
            jax.ShapeDtypeStruct((width // 4, count), rows.dtype),
        ),
        in_specs=[SMEM, VMEM],
        out_specs=(VMEM, VMEM),
        scratch_shapes=[pltpu.VMEM((width, count), rows.dtype)],
        compiler_params=params(),
        cost_estimate=pl.CostEstimate(flops=0, bytes_accessed=4 * rows.size, transcendentals=0),
    )(place, rows)


def share(place, rows, shards):
    own, send = spread(place, rows, shards)
    near = swap(send, "cp", 1)
    return own, near, swap(near, "tp", 1)


def weigh_kernel(place_ref, own_ref, near_ref, far_ref, mine_ref, theirs_ref, send_ref, keep_ref, joined):
    core = place_ref[1]

    @pl.when(pl.program_id(0) == 0)
    def _():
        joined[core] = near_ref[...]
        joined[1 - core] = far_ref[...]

    half = send_ref.shape[0]
    mine, theirs = mine_ref[...], theirs_ref[...]
    send_ref[...] = (
        matmul(own_ref[half:, :], mine) + matmul(joined[1], theirs)
    ).astype(send_ref.dtype)
    keep_ref[...] = (
        matmul(own_ref[:half, :], mine) + matmul(joined[0], theirs)
    ).astype(keep_ref.dtype)


def weigh(place, shared, mine, theirs):
    own, near, far = shared
    half, count = near.shape
    width = mine.shape[1]
    tile = min(width, 512)
    whole = lambda j: (0, 0)
    column = lambda j: (0, j)
    return pl.pallas_call(
        weigh_kernel,
        grid=(pl.cdiv(width, tile),),
        out_shape=(jax.ShapeDtypeStruct((half, width), jnp.bfloat16),) * 2,
        in_specs=[
            SMEM,
            pl.BlockSpec((2 * half, count), whole),
            pl.BlockSpec((half, count), whole),
            pl.BlockSpec((half, count), whole),
            pl.BlockSpec((count, tile), column),
            pl.BlockSpec((count, tile), column),
        ],
        out_specs=(pl.BlockSpec((half, tile), column),) * 2,
        scratch_shapes=[pltpu.VMEM((2, half, count), jnp.bfloat16)],
        compiler_params=params(),
        cost_estimate=pl.CostEstimate(
            flops=8 * half * count * width,
            bytes_accessed=4 * (2 * half * count + count * width + half * width),
            transcendentals=0,
        ),
    )(place, own, near, far, mine, theirs)


def weight_grad(place, shared, mine, shards):
    theirs = swap(mine, "cp", 1)
    send, keep = weigh(place, shared, mine, theirs)
    terms = [keep]
    bit = 2
    while bit < shards:
        terms.append(swap(send, "cp", bit))
        bit *= 2
        if bit < shards:
            rows = terms[0].shape[0] // 2
            send = sum(t[rows:].astype(jnp.float32) for t in terms).astype(jnp.bfloat16)
            terms = [t[:rows] for t in terms]
    return sum(t.astype(jnp.float32) for t in terms)


def hidden_kernel(first, last, offset, units, *refs):
    place_ref, rows_ref, cot_ref, gate_ref, up_ref, down_ref = refs[:6]
    refs = refs[6:]
    if not first:
        before_ref, refs = refs[0], refs[1:]
    hidden_ref, grads_ref, sum_ref, total = refs
    step = pl.program_id(0)

    @pl.when(step == 0)
    def _():
        total[...] = jnp.zeros_like(total) if first else before_ref[...]

    rows = rows_ref[...]
    w_gate, w_up, w_down = gate_ref[...], up_ref[...], down_ref[...]
    if last:
        left = units - (offset + step) * TILE
        inside = lax.broadcasted_iota(jnp.int32, w_gate.shape, 1) < left
        w_gate = jnp.where(inside, w_gate, 0)
        w_up = jnp.where(inside, w_up, 0)
        inside = lax.broadcasted_iota(jnp.int32, w_down.shape, 0) < left
        w_down = jnp.where(inside, w_down, 0)
    gate = matmul(rows, w_gate)
    up_part = matmul(rows, w_up)
    grad_hidden = contract_cols(cot_ref[...], w_down)
    sigma = jax.nn.sigmoid(gate)
    swish = gate * sigma
    hidden_ref[...] = (swish * up_part).astype(jnp.bfloat16)
    grad_gate = (grad_hidden * up_part * sigma * (1.0 + gate * (1.0 - sigma))).astype(jnp.bfloat16)
    grad_up = (grad_hidden * swish).astype(jnp.bfloat16)
    grads_ref[:, :TILE] = grad_gate
    grads_ref[:, TILE:] = grad_up
    total[...] += contract_cols(grad_gate, w_gate) + contract_cols(grad_up, w_up)

    @pl.when(step == pl.num_programs(0) - 1)
    def _():
        if last:
            part = total.shape[0] // len(TP_ORDER)
            for i, far in enumerate(TP_ORDER):
                block = pl.multiple_of((place_ref[2] ^ far) * part, part)
                sum_ref[i * part : (i + 1) * part, :] = total[pl.ds(block, part), :].astype(
                    sum_ref.dtype
                )
        else:
            sum_ref[...] = total[...]


def hidden_chunk(place, rows, cotangent, w_gate, w_up, w_down, before, index):
    count, width = rows.shape
    units = w_gate.shape[1]
    tiles = pl.cdiv(units, TILE)
    offset = index * CHUNK_TILES
    steps = min(CHUNK_TILES, tiles - offset)
    first, last = index == 0, offset + steps == tiles
    inner = min(steps * TILE, units - offset * TILE)
    outer = (steps - 1) * 2 * TILE + TILE + inner - (steps - 1) * TILE
    whole = lambda j: (0, 0)
    column = lambda j: (0, j)
    in_specs = [
        SMEM,
        pl.BlockSpec((count, width), whole),
        pl.BlockSpec((count, width), whole),
        pl.BlockSpec((width, TILE), lambda j: (0, offset + j)),
        pl.BlockSpec((width, TILE), lambda j: (0, offset + j)),
        pl.BlockSpec((TILE, width), lambda j: (offset + j, 0)),
    ]
    operands = [place, rows, cotangent, w_gate, w_up, w_down]
    if not first:
        in_specs.append(pl.BlockSpec((count, width), whole))
        operands.append(before)
    return pl.pallas_call(
        functools.partial(hidden_kernel, first, last, offset, units),
        grid=(steps,),
        out_shape=(
            jax.ShapeDtypeStruct((count, inner), jnp.bfloat16),
            jax.ShapeDtypeStruct((count, outer), jnp.bfloat16),
            jax.ShapeDtypeStruct((count, width), jnp.bfloat16 if last else jnp.float32),
        ),
        in_specs=in_specs,
        out_specs=(
            pl.BlockSpec((count, TILE), column),
            pl.BlockSpec((count, 2 * TILE), column),
            pl.BlockSpec((count, width), whole),
        ),
        scratch_shapes=[pltpu.VMEM((count, width), jnp.float32)],
        compiler_params=params(),
        cost_estimate=pl.CostEstimate(
            flops=10 * count * width * inner,
            bytes_accessed=6 * width * inner + 12 * count * width,
            transcendentals=count * inner,
        ),
    )(*operands)


def region_rows(ref, start, count):
    return ref[:, start : start + count, :].reshape(-1, HD)


def triangle(rows, keys):
    row = lax.broadcasted_iota(jnp.int32, (rows, keys), 0) & (keys - 1)
    return row >= lax.broadcasted_iota(jnp.int32, (rows, keys), 1)


def regions(place_ref, shards, tok_rows):
    me, start = place_ref[0], place_ref[3]
    bits = bits_of(shards)

    def of_first(block):
        low = block < shards
        device = jnp.where(low, block, 2 * shards - 1 - block)
        return reverse_bits(device ^ me, bits), jnp.where(low, 0, tok_rows - HALF)

    def of_middle(block):
        return reverse_bits((start + block) ^ me, bits), HALF

    return (
        (0, HALF, me, of_first),
        (tok_rows - HALF, HALF, 2 * shards - 1 - me, of_first),
        (HALF, tok_rows - 2 * HALF, me - start, of_middle),
    )


def attend_kernel(shards, place_ref, q_ref, mine_ref, other_ref, low_ref, full_ref, log_ref, pair):
    core = place_ref[1]
    pair[core] = mine_ref[...]
    pair[1 - core] = other_ref[...]
    heads, tok_rows = q_ref.shape[0], q_ref.shape[1]
    factor = HD**-0.5 * LOG2E
    for begin, count, blocks, locate in regions(place_ref, shards, tok_rows):
        query = region_rows(q_ref, begin, count)
        rows = heads * count

        def read(which, block):
            slot, offset = locate(block)
            return pair[which, slot, pl.ds(pl.multiple_of(offset, HALF), count), :]

        mask = triangle(rows, count)
        last = jnp.where(mask, contract_cols(query, read(0, blocks)), MASKED)
        peak = lax.fori_loop(
            0, blocks, lambda t, top: jnp.maximum(top, contract_cols(query, read(0, t))), last
        )
        peak = jnp.max(peak, axis=1, keepdims=True) * factor

        def add(block, carry, scores):
            total, accum = carry
            weights = jnp.exp2(scores * factor - peak)
            return total + weights, accum + matmul(weights.astype(jnp.bfloat16), read(1, block))

        carry = add(blocks, (jnp.zeros((rows, count), jnp.float32), jnp.zeros((rows, HD), jnp.float32)), last)
        total, accum = lax.fori_loop(
            0, blocks, lambda t, held: add(t, held, contract_cols(query, read(0, t))), carry
        )
        total = jnp.sum(total, axis=1, keepdims=True)
        full = accum / total
        log_total = jnp.broadcast_to(peak + jnp.log2(total), (rows, HD))
        for head in range(heads):
            part = slice(head * count, (head + 1) * count)
            lanes = slice(head * HD, (head + 1) * HD)
            low_ref[begin : begin + count, lanes] = full[part].astype(jnp.bfloat16)
            full_ref[head, begin : begin + count, :] = full[part]
            log_ref[head, begin : begin + count, :] = log_total[part]


def attend(place, query, mine, other):
    heads, tok_rows, _ = query.shape
    shards = mine.shape[0]
    pairs = heads * tok_rows * tok_rows * shards // 4
    return pl.pallas_call(
        functools.partial(attend_kernel, shards),
        out_shape=(
            jax.ShapeDtypeStruct((tok_rows, heads * HD), jnp.bfloat16),
            jax.ShapeDtypeStruct((heads, tok_rows, HD), jnp.float32),
            jax.ShapeDtypeStruct((heads, tok_rows, HD), jnp.float32),
            jax.ShapeDtypeStruct((2,) + mine.shape, jnp.bfloat16),
        ),
        in_specs=[SMEM, VMEM, VMEM, VMEM],
        out_specs=(VMEM, VMEM, VMEM, VMEM),
        compiler_params=params(),
        cost_estimate=pl.CostEstimate(
            flops=6 * pairs * HD, bytes_accessed=4 * mine.size, transcendentals=pairs
        ),
    )(place, query, mine, other)


def attend_back_kernel(
    shards, place_ref, q_ref, pair, low_ref, full_ref, log_ref, cos_ref, sin_ref,
    query_ref, keep_ref, send_ref, grads,
):
    core = place_ref[1]
    grads[...] = jnp.zeros_like(grads)
    heads, tok_rows = q_ref.shape[0], q_ref.shape[1]
    scale = HD**-0.5
    factor = scale * LOG2E
    sign = jnp.where(lax.broadcasted_iota(jnp.int32, (1, HD), 1) < HD // 2, 1.0, -1.0)
    for begin, count, blocks, locate in regions(place_ref, shards, tok_rows):
        query = region_rows(q_ref, begin, count)
        rows = heads * count
        incoming = jnp.concatenate(
            [low_ref[begin : begin + count, h * HD : (h + 1) * HD] for h in range(heads)], 0
        )
        full = region_rows(full_ref, begin, count)
        log_total = region_rows(log_ref, begin, count)[:, :1]
        delta = jnp.sum(incoming.astype(jnp.float32) * full, axis=1, keepdims=True)

        def add(block, grad_query, mask=None):
            slot, offset = locate(block)
            place = pl.ds(pl.multiple_of(offset, HALF), count)
            keys, values = pair[0, slot, place, :], pair[1, slot, place, :]
            probs = jnp.exp2(contract_cols(query, keys) * factor - log_total)
            if mask is not None:
                probs = jnp.where(mask, probs, 0.0)
            grad_scores = (probs * (contract_cols(incoming, values) - delta)).astype(jnp.bfloat16)
            grads[0, slot, place, :] += contract_rows(grad_scores, query)
            grads[1, slot, place, :] += contract_rows(probs.astype(jnp.bfloat16), incoming)
            return grad_query + matmul(grad_scores, keys)

        grad_query = add(blocks, jnp.zeros((rows, HD), jnp.float32), triangle(rows, count))
        grad_query = lax.fori_loop(0, blocks, add, grad_query) * scale
        cosine, sine = cos_ref[begin : begin + count, :], sin_ref[begin : begin + count, :]
        for head in range(heads):
            part = grad_query[head * count : (head + 1) * count]
            turned = part * cosine + pltpu.roll(part * sine, HD // 2, 1) * sign
            query_ref[begin : begin + count, head * HD : (head + 1) * HD] = turned.astype(
                jnp.bfloat16
            )
    is_key = core == 0
    keep_ref[...] = (grads[core] * jnp.where(is_key, scale, 1.0)).astype(jnp.bfloat16)
    send_ref[...] = (grads[1 - core] * jnp.where(is_key, 1.0, scale)).astype(jnp.bfloat16)


def attend_back(place, query, pair, low, full, log_total, cosine, sine):
    heads, tok_rows, _ = query.shape
    shards = pair.shape[1]
    pairs = heads * tok_rows * tok_rows * shards // 4
    return pl.pallas_call(
        functools.partial(attend_back_kernel, shards),
        out_shape=(
            jax.ShapeDtypeStruct((tok_rows, heads * HD), jnp.bfloat16),
            jax.ShapeDtypeStruct(pair.shape[1:], jnp.bfloat16),
            jax.ShapeDtypeStruct(pair.shape[1:], jnp.bfloat16),
        ),
        in_specs=[SMEM] + [VMEM] * 7,
        out_specs=(VMEM, VMEM, VMEM),
        scratch_shapes=[pltpu.VMEM(pair.shape, jnp.float32)],
        compiler_params=params(),
        cost_estimate=pl.CostEstimate(
            flops=10 * pairs * HD, bytes_accessed=4 * pair.size, transcendentals=pairs
        ),
    )(place, query, pair, low, full, log_total, cosine, sine)


def gather_tp(value, axis):
    value = jnp.concatenate([value, swap(value, "tp", 2)], axis)
    return jnp.concatenate([value, swap(value, "tp", 1)], axis)


def scatter_tp(value):
    half, part = value.shape[0] // 2, value.shape[0] // 4
    other = swap(value[half:], "tp", 1)
    send = (value[part:half].astype(jnp.float32) + other[part:].astype(jnp.float32)).astype(
        jnp.bfloat16
    )
    last = swap(send, "tp", 2)
    return (
        value[:part].astype(jnp.float32)
        + other[:part].astype(jnp.float32)
        + last.astype(jnp.float32)
    )


def in_order(value, me):
    part = value.shape[0] // 4
    return jnp.concatenate(
        [
            lax.dynamic_slice_in_dim(value, reverse_bits(me ^ i, 2) * part, part, 0)
            for i in range(4)
        ],
        0,
    )


UNITS = 256
TOK = 512


def back_kernel(width, units, *refs):
    (
        docs_ref, pos_ref, freq_ref, gain1_ref, gain2_ref, bq_ref, bk_ref, bv_ref, x_hbm, cot_hbm, wq_hbm, wk_hbm, wv_hbm, wo_hbm,
        wg_hbm, wu_hbm, wd_hbm,
        tiles_out, wo_out, wq_out, wkv_out, sums_out, output_out, input_out,
        middle_hbm, pair_hbm, own_hbm, near_hbm, wo_all, wq_turned_hbm, all_hbm, n1_hbm, via_hbm,
        cosine, sine, gains, w_pair_grad, query, pair, full, log_total, sums, sums_in,
        attn_all, attn_far, query_far, pair_far, middle, acc, turned,
        own_a, far_a, part_s, part_k, near1, part_s2, near2, sent_tile,
        rel, core_in, lane_send, lane_in, grad_full,
        held_query, kv_send, kv_in, grad_query, grad_pair, small_s, small_in, small_s2, small_in2, pair_terms,
        send_sem, recv_sem, local_sem, weight_sem,
    ) = refs
    me = lax.axis_index("cp")
    lane = lax.axis_index("tp")
    b0, b1, b2 = me % 2, (me // 2) % 2, me // 4
    core, high = lane % 2, lane // 2
    x_to = {"cp": me + 1 - 2 * b0}
    z1_to = {"cp": me + 2 - 4 * b1}
    z2_to = {"cp": me + 4 - 8 * b2}
    z3_to = {"cp": me + 6 - 4 * b1 - 8 * b2}
    inner = (b1 + b2) % 2
    peers = [
        me + (r % 2) * (1 - 2 * b0) + (r // 2 % 2) * (2 - 4 * b1) + (r // 4) * (4 - 8 * b2)
        for r in range(8)
    ]
    c_to = {"tp": lane + 1 - 2 * core}
    y_to = {"tp": lane + 2 - 4 * high}
    lane_c, lane_y = lane + 1 - 2 * core, lane + 2 - 4 * high
    lane_cy = 3 - lane
    cy_to = {"tp": lane_cy}
    tiles = pl.cdiv(units, UNITS)
    rest = units - (tiles - 1) * UNITS
    block = width // 8
    half = width // 4
    quarter = TOK // 4
    scale = HD**-0.5
    factor = scale * LOG2E
    used = {"remote": 0, "local": 0}

    def remote(src, dst, to, count=1):
        index = used["remote"]
        used["remote"] += 1
        return pltpu.make_async_remote_copy(
            src_ref=src, dst_ref=dst, send_sem=send_sem.at[index], recv_sem=recv_sem.at[index],
            device_id=to, device_id_type=pl.DeviceIdType.MESH,
        )

    def local(src, dst):
        index = used["local"]
        used["local"] += 1
        return pltpu.make_async_copy(src, dst, local_sem.at[index])

    def started(*copies):
        for copy in copies:
            copy.start()
        return copies[0] if len(copies) == 1 else copies

    def row_block(side, h, i):
        mine = (b0 + side) % 2 + 2 * ((b1 + h) % 2) + 4 * ((b2 + i) % 2)
        return pl.ds(pl.multiple_of(mine * block, 16), block)

    def rows_of_block(index):
        return pl.ds(pl.multiple_of(index * block, 16), block)

    def rows_of(index):
        return pl.ds(pl.multiple_of(index * quarter, quarter), quarter)

    z1_tile = remote(part_s, near1, z1_to)
    z2_tile = remote(part_s2, near2, z2_to)

    spread_base = used["remote"]
    used["remote"] += 2 * 20
    wide_half, wide_quarter = width // 2, width // 4

    def block_of(j, side):
        z = (b1 + 2 * b2, 1 - b1 + 2 * b2, 2 - b2, 3 - 3 * b2)[j]
        return 2 * z + (b0 + side) % 2

    def spread_part(k, j, side, c, y=None):
        rows = half_of(c, y)
        return all_hbm.at[k, block_of(j, side), rows]

    def half_of(c, y=None):
        if y is None:
            return pl.ds(pl.multiple_of(c * wide_half, wide_half), wide_half)
        return pl.ds(pl.multiple_of(c * wide_half + y * wide_quarter, wide_quarter), wide_quarter)

    def spread_copy(k, part, send, recv, to, source=None):
        index = spread_base + 20 * k
        return pltpu.make_async_remote_copy(
            src_ref=part if source is None else source, dst_ref=part,
            send_sem=send_sem.at[index + send],
            recv_sem=recv_sem.at[index + recv], device_id=to, device_id_type=pl.DeviceIdType.MESH,
        )

    def z_copy(k, m):
        j, recv, to = ((0, 1, z1_to), (0, 2, z3_to), (1, 3, z3_to), (2, 2, z1_to), (3, 3, z1_to))[m]
        own = turned.at[half_of(core)] if (k, j) == (1, 0) else None
        return spread_copy(k, spread_part(k, j, 0, core), m, recv, to, own)

    def z_arrival(k, j):
        return spread_copy(k, spread_part(k, j, 0, core), 0, j, z1_to)

    def c_copy(k, j, c=None):
        return spread_copy(k, spread_part(k, j, 0, core if c is None else c), 4 + j, 4 + j, c_to)

    def x_copy(k, j, side=0):
        y = None if (k, j) in WHOLE_HALVES else high
        own = turned.at[half_of(core, y)] if (k, j, side) == (1, 0, 0) else None
        return spread_copy(k, spread_part(k, j, side, core, y), 8 + j, 8 + j, x_to, own)

    def y_copy(k, j, y=None):
        return spread_copy(
            k, spread_part(k, j, 1, core, high if y is None else y), 12 + j, 12 + j, y_to
        )

    def d_copy(k, j, c=None):
        return spread_copy(k, spread_part(k, j, 1, core if c is None else c), 16 + j, 16 + j, c_to)

    def when(condition):
        return pl.when(condition == 1)

    def begin_spread(k):
        z_copy(k, 0).start()

        @when(inner)
        def _():
            z_copy(k, 1).start()

    def arrive(k, j):
        z_arrival(k, j).wait_recv()

        @when(inner)
        def _():
            z_copy(k, j + 1).start()

        started(c_copy(k, j), x_copy(k, j))

    def arrive_inner(k, j):
        @when(inner)
        def _():
            arrive(k, j)

    def arrive_outer(k, j):
        @when(1 - inner)
        def _():
            arrive(k, j)

    def pass_y(k, j):
        assert (k, j) not in WHOLE_HALVES
        x_copy(k, j, 1).wait_recv()
        y_copy(k, j).start()

    def pass_core(k, j):
        if (k, j) in WHOLE_HALVES:
            x_copy(k, j, 1).wait_recv()
        else:
            y_copy(k, j, 1 - high).wait_recv()
        d_copy(k, j).start()

    barrier = pltpu.get_barrier_semaphore()
    for to in (*({"cp": peer} for peer in peers[1:]), c_to, y_to, cy_to):
        pl.semaphore_signal(barrier, inc=1, device_id=to, device_id_type=pl.DeviceIdType.MESH)

    def share(source, index):
        return [
            remote(
                source.at[row_block(1, core, i)],
                far_a.at[index, core, pl.ds(i * block, block)],
                x_to,
            )
            for i in range(2)
        ]

    def forward(index):
        return remote(far_a.at[index, core], far_a.at[index, core], c_to)

    COT, N2, GB, N1 = range(4)
    own_blocks = [local(turned, all_hbm.at[k, me]) for k in range(2)]
    wo_y = remote(wo_hbm, wo_all.at[1], y_to)
    wo_c = remote(wo_hbm, wo_all.at[2], c_to)
    wo_cy = remote(wo_all.at[1], wo_all.at[3], c_to)
    attn_y, attn_c, attn_cy = [
        [
            remote(
                attn_all.at[src, pl.ds(begin, count)], attn_all.at[dst, pl.ds(begin, count)], to
            )
            for begin, count in ((0, HALF), (TOK - HALF, HALF), (HALF, TOK - 2 * HALF))
        ]
        for src, dst, to in ((0, 1, y_to), (0, 2, c_to), (1, 3, c_to))
    ]
    attn_x = remote(attn_all.at[0], attn_far, x_to)
    n1_x = share(n1_hbm, N1)
    n1_keep = local(turned, n1_hbm)
    pair_1 = remote(pair.at[core, 0], pair.at[core, 2], z1_to)
    pair_2 = remote(pair.at[core, 0], pair.at[core, 1], z2_to)
    pair_3 = remote(pair.at[core, 0], pair.at[core, 3], z3_to)
    pair_near = [remote(pair.at[core, i], pair.at[core, 4 + i], x_to) for i in range(4)]
    pair_core = [remote(pair.at[core, i], pair.at[core, i], c_to) for i in range(8)]
    def norm_scale(rows):
        return lax.rsqrt(jnp.mean(rows * rows, axis=-1, keepdims=True) + EPSILON)

    sign = jnp.where(lax.broadcasted_iota(jnp.int32, (1, HD), 1) < HD // 2, 1.0, -1.0)
    is_key = jnp.where(core == 0, 1.0, 0.0)

    def turn(rows, cosines, sines):
        return rows * cosines + pltpu.roll(rows * sign, HD // 2, 1) * sines

    def turn_back(rows, cosines, sines):
        return rows * cosines + pltpu.roll(rows * sines, HD // 2, 1) * sign

    def opening(x_rows, cot_rows, normed, w_query, w_pair, w_turned):
        loads = [
            local(x_hbm, x_rows),
            local(wq_hbm, w_query),
            local(cot_hbm, cot_rows),
        ]
        started(*loads)
        index = used["local"]
        used["local"] += 1
        columns = pl.ds(pl.multiple_of(high * HD, HD), HD)
        key_load = pltpu.make_async_copy(wk_hbm.at[:, columns], w_pair, local_sem.at[index])
        value_load = pltpu.make_async_copy(wv_hbm.at[:, columns], w_pair, local_sem.at[index])

        @pl.when(core == 0)
        def _():
            key_load.start()

        @pl.when(core == 1)
        def _():
            value_load.start()

        lanes_of = [slice(i * HD, (i + 1) * HD) for i in range(width // HD)]
        for i, lanes in enumerate(lanes_of):
            gains[0:1, lanes] = gain1_ref[i : i + 1, :]
            gains[1:2, lanes] = gain2_ref[i : i + 1, :]
        places = pos_ref[pl.ds(me * 4, 4), :].astype(jnp.float32)
        places = jnp.concatenate([places, places], 0).T
        for i in range(4):
            angle = places[:, i : i + 1] * freq_ref[...]
            cosine[i * HD : (i + 1) * HD, :] = jnp.cos(angle)
            sine[i * HD : (i + 1) * HD, :] = jnp.sin(angle)
        loads[0].wait()

        def norm(a, carry):
            rows = x_rows[rows_of(a), :].astype(jnp.float32)
            normed[rows_of(a), :] = (rows * norm_scale(rows) * gains[0:1, :]).astype(
                jnp.bfloat16
            )
            return carry

        lax.fori_loop(0, 4, norm, 0)
        key_load.wait()
        rows = (
            matmul(normed[...], w_pair[...])
            + bk_ref[pl.ds(high, 1), :] * is_key
            + bv_ref[pl.ds(high, 1), :] * (1.0 - is_key)
        )
        pair[core, 0] = turn(
            rows, cosine[...] * is_key + (1.0 - is_key), sine[...] * is_key
        ).astype(jnp.bfloat16)
        pl.semaphore_wait(barrier, 10)
        started(pair_1, pair_2, pair_3, pair_near[0], pair_core[0], wo_y, wo_c)
        loads[2].wait()

        def flip_cot(a, carry):
            turned[:, rows_of(a)] = cot_rows[rows_of(a), :].T
            return carry

        lax.fori_loop(0, 4, flip_cot, 0)
        own_blocks[0].start()
        loads[1].wait()
        rows = matmul(normed[...], w_query[...])
        for h in range(3):
            query[h] = turn(
                rows[:, h * HD : (h + 1) * HD] + bq_ref[h : h + 1, :], cosine[...], sine[...]
            ).astype(jnp.bfloat16)
        own_blocks[0].wait()
        begin_spread(0)
        w_turned[...] = w_query[...].T
        turned_copy = started(local(w_turned, wq_turned_hbm))
        for copy, i in ((pair_1, 2), (pair_2, 1), (pair_3, 3)):
            copy.wait_recv()
            started(pair_near[i], pair_core[i])

        def flip(a, carry):
            turned[:, rows_of(a)] = normed[rows_of(a), :].T
            return carry

        lax.fori_loop(0, 4, flip, 0)
        for p in range(4):
            own_a[N1, p * block : (p + 1) * block, :] = turned[row_block(0, p // 2, p % 2), :]
        for i in (0, 2, 1, 3):
            pair_near[i].wait_recv()
            pair_core[4 + i].start()
        x_copy(0, 0).start()
        n1_keep.start()
        for copy in pair_core:
            copy.wait_recv()
        turned_copy.wait()

    pl.run_scoped(
        opening,
        pltpu.VMEM((TOK, width), jnp.bfloat16),
        pltpu.VMEM((TOK, width), jnp.bfloat16),
        pltpu.VMEM((TOK, width), jnp.bfloat16),
        pltpu.VMEM((width, 3 * HD), jnp.bfloat16),
        pltpu.VMEM((width, HD), jnp.bfloat16),
        pltpu.VMEM((3 * HD, width), jnp.bfloat16),
    )

    def of_first(t):
        t = t - t // 16
        late = t // 8
        device = t * (1 - late) + (15 - t) * late
        return device, late * (TOK - HALF)

    def same_document(device):
        ids = [docs_ref[pl.ds(4 * at + 1, 1), :] for at in (device, me)]
        return jnp.concatenate([ids[0], ids[0]], 1) == jnp.concatenate([ids[1], ids[1]], 1)

    def slot_of(device):
        return (
            4 * ((device % 2 + b0) % 2)
            + 2 * (((device // 2) % 2 + b1) % 2)
            + (device // 4 + b2) % 2
        )

    def places_of(step, wide):
        if wide:
            return [(slot_of(step), pl.ds(HALF, TOK - 2 * HALF))]
        places = []
        for block in (2 * step, 2 * step + 1):
            device, offset = of_first(block)
            places.append((slot_of(device), pl.ds(pl.multiple_of(offset, HALF), HALF)))
        return places

    def keys_of(which, step, wide):
        parts = [pair[which, slot, rows, :] for slot, rows in places_of(step, wide)]
        return parts[0] if wide else jnp.concatenate(parts, 0)

    def seen(begin, count, blocks, wide):
        shape = (3 * count, 2 * HALF)
        row = lax.broadcasted_iota(jnp.int32, shape, 0) & (count - 1)
        if not wide:
            row = row + blocks % 2 * HALF
        return row >= lax.broadcasted_iota(jnp.int32, shape, 1)

    def regions():
        return (
            (0, HALF, me, False, me // 2),
            (TOK - HALF, HALF, 15 - me, False, (15 - me) // 2),
            (HALF, TOK - 2 * HALF, me, True, me),
        )

    def attend_region(begin, count, blocks, wide, steps):
        rows = 3 * count
        q_rows = region_rows(query, begin, count)

        def score(step):
            scores = contract_cols(q_rows, keys_of(0, step, wide))
            return jnp.where(same_document(step), scores, MASKED) if wide else scores

        def add(step, carry, scores):
            total, accum = carry
            weights = jnp.exp2(scores * factor - peak)
            return total + weights, accum + matmul(
                weights.astype(jnp.bfloat16), keys_of(1, step, wide)
            )

        last = jnp.where(
            seen(begin, count, blocks, wide),
            contract_cols(q_rows, keys_of(0, steps, wide)),
            MASKED,
        )
        peak = lax.fori_loop(0, steps, lambda t, top: jnp.maximum(top, score(t)), last)
        peak = jnp.max(peak, axis=1, keepdims=True) * factor
        carry = add(
            steps,
            (jnp.zeros((rows, 2 * HALF), jnp.float32), jnp.zeros((rows, HD), jnp.float32)),
            last,
        )
        total, accum = lax.fori_loop(0, steps, lambda t, held: add(t, held, score(t)), carry)
        total = jnp.sum(total, axis=1, keepdims=True)
        result = accum / total
        logs = jnp.broadcast_to(peak + jnp.log2(total), (rows, HD))
        for h in range(3):
            part = slice(h * count, (h + 1) * count)
            attn_all[0, begin : begin + count, h * HD : (h + 1) * HD] = result[part].astype(
                jnp.bfloat16
            )
            full[h, begin : begin + count, :] = result[part]
            log_total[h, begin : begin + count, :] = logs[part]

    def front(weights, ring, wo, x_rows, cot_turned):
        def fetch(t, slot, rows):
            return [
                pltpu.make_async_copy(
                    source.at[pl.ds(t * UNITS, rows)],
                    weights.at[slot, k, pl.ds(0, rows)],
                    weight_sem.at[slot, k],
                )
                for k, source in enumerate((wg_hbm, wu_hbm, wd_hbm))
            ]

        loads = [
            local(wo_hbm, wo.at[0]),
            local(x_hbm, x_rows),
            local(wo_all.at[2], wo.at[2]),
            local(wo_all.at[1], wo.at[1]),
            local(wo_all.at[3], wo.at[3]),
            local(all_hbm.at[0, me], cot_turned),
        ]
        wo_c.wait_recv()
        started(*loads[:3], loads[5])
        started(*fetch(0, 0, UNITS))
        attend_region(*regions()[0])
        attend_region(*regions()[1])
        started(*attn_y[:2], *attn_c[:2])
        n1_keep.wait()
        started(*n1_x)
        arrive(0, 1)
        arrive_inner(0, 2)
        attend_region(*regions()[2])
        started(attn_y[2], attn_c[2])
        wo_y.wait_recv()
        wo_cy.start()
        loads[3].start()
        pass_y(0, 0)
        for load in loads[:3]:
            load.wait()
        for copy in (pair_1, pair_2, pair_3, *pair_near, *pair_core):
            copy.wait_send()
        def add_part(p, first=False):
            def body(n, carry):
                cols = pl.ds(pl.multiple_of(n * 512, 512), 512)
                held = x_rows[:, cols].astype(jnp.float32) if first else middle[:, cols]
                middle[:, cols] = held + matmul(attn_all[p], wo[p, :, cols])
                return carry

            lax.fori_loop(0, width // 512, body, 0)

        add_part(0, True)
        for copy in attn_c:
            copy.wait_recv()
        add_part(2)
        for copy, forward_copy in zip(attn_y, attn_cy):
            copy.wait_recv()
            forward_copy.start()
        loads[3].wait()
        wo_cy.wait_recv()
        loads[4].start()
        add_part(1)
        for copy in attn_cy:
            copy.wait_recv()
        loads[4].wait()
        add_part(3)

        def norm(a, carry):
            rows = middle[rows_of(a), :]
            turned[:, rows_of(a)] = (rows * norm_scale(rows) * gains[1:2, :]).astype(jnp.bfloat16).T
            return carry

        lax.fori_loop(0, 4, norm, 0)
        begin_spread(1)
        x_copy(1, 0).start()
        own_blocks[1].start()
        loads[5].wait()
        acc[...] = jnp.zeros_like(acc)

        def keep_tile(t):
            return pltpu.make_async_copy(ring.at[t % 2], own_hbm.at[t], weight_sem.at[2, t % 2])

        def tile(t, carry):
            slot = t % 2

            @pl.when(t < tiles - 1)
            def _():
                for copy in fetch(t, slot, UNITS):
                    copy.wait()

            @pl.when(t == tiles - 1)
            def _():
                for copy in fetch(t, slot, rest):
                    copy.wait()

            @pl.when(t + 1 < tiles - 1)
            def _():
                started(*fetch(t + 1, 1 - slot, UNITS))

            @pl.when(t + 1 == tiles - 1)
            def _():
                weights[1 - slot, :, rest:, :] = jnp.zeros(
                    (3, UNITS - rest, width), weights.dtype
                )
                started(*fetch(t + 1, 1 - slot, rest))

            for part in (slice(0, TOK // 2), slice(TOK // 2, TOK)):
                gate = matmul(weights[slot, 0], turned[:, part])
                up_part = matmul(weights[slot, 1], turned[:, part])
                grad_hidden = matmul(weights[slot, 2], cot_turned[:, part])
                sigma = jax.nn.sigmoid(gate)
                swish = gate * sigma
                ring[slot, part, :UNITS] = (swish * up_part).astype(jnp.bfloat16).T
                ring[slot, part, UNITS : 2 * UNITS] = (
                    (grad_hidden * up_part * sigma * (1.0 + gate * (1.0 - sigma)))
                    .astype(jnp.bfloat16)
                    .T
                )
                ring[slot, part, 2 * UNITS :] = (grad_hidden * swish).astype(jnp.bfloat16).T
            for part in (slice(0, TOK // 2), slice(TOK // 2, TOK)):
                acc[part, :] += matmul(
                    ring[slot, part, UNITS:], weights[slot, 0:2].reshape(2 * UNITS, width)
                )

            @pl.when(t > 0)
            def _():
                keep_tile(t - 1).wait()

            @pl.when(t == 3)
            def _():
                arrive_outer(0, 2)
                arrive_inner(0, 3)
                pass_core(0, 0)
                pass_y(0, 1)

            @pl.when(t == 6)
            def _():
                pass_y(1, 0)

            @pl.when(t == 7)
            def _():
                arrive(1, 1)
                arrive_inner(1, 2)

            keep_tile(t).start()
            return carry

        lax.fori_loop(0, tiles, tile, 0)
        keep_tile(tiles - 1).wait()
        own_blocks[1].wait()

    pl.run_scoped(
        front,
        pltpu.VMEM((2, 3, UNITS, width), jnp.bfloat16),
        pltpu.VMEM((2, TOK, 3 * UNITS), jnp.bfloat16),
        pltpu.VMEM((4, width // 4, width), jnp.bfloat16),
        pltpu.VMEM((TOK, width), jnp.bfloat16),
        pltpu.VMEM((width, TOK), jnp.bfloat16),
    )

    def reduce_copies():
        return (
            remote(rel.at[rows_of(lane_c)], core_in.at[0], c_to),
            remote(rel.at[rows_of(lane_cy)], core_in.at[1], c_to),
            remote(lane_send, lane_in, y_to),
        )

    def reduce_start(copies):
        rel[...] = acc[...].astype(jnp.bfloat16)
        started(*copies[:2])

    def reduce_middle(copies):
        copies[0].wait()
        copies[1].wait()
        lane_send[...] = (
            acc[rows_of(lane_y), :] + core_in[1].astype(jnp.float32)
        ).astype(jnp.bfloat16)
        copies[2].start()

    def reduce_end(copies, held):
        copies[2].wait()
        return held + core_in[0].astype(jnp.float32) + lane_in[...].astype(jnp.float32)

    def spread_copies(full):
        mine, theirs = full.at[rows_of(lane)], full.at[rows_of(lane_y)]
        return [
            remote(mine, mine, y_to),
            remote(mine, mine, c_to),
            remote(theirs, theirs, c_to),
        ]

    def spread_end(copies):
        copies[0].wait_recv()
        copies[2].start()
        copies[0].wait_send()
        copies[1].wait()
        copies[2].wait()

    near_base = used["remote"]
    used["remote"] += 4

    def near_copy(r):
        index = near_base + r
        return pltpu.make_async_remote_copy(
            src_ref=sent_tile.at[rows_of_block(peers[r] - 4 * b2)],
            dst_ref=via_hbm if r == 3 else near_hbm.at[r],
            send_sem=send_sem.at[index], recv_sem=recv_sem.at[index],
            device_id={"cp": peers[1 if r == 3 else r]}, device_id_type=pl.DeviceIdType.MESH,
        )

    via_copy = remote(via_hbm, near_hbm.at[3], z1_to)

    final_base = used["local"]
    used["local"] += 24

    SMALL = {"out": (0, 384, GB), "query": (384, 384, N1), "pair": (768, 128, N1)}
    small_base = used["remote"]
    used["remote"] += 6
    pair_hops = [
        remote(
            small_s.at[pl.ds(p * block, block), pl.ds(768, HD)], pair_terms.at[p - 1], to
        )
        for p, to in ((1, z2_to), (2, z1_to), (3, z3_to))
    ]

    def small_copy(name, second):
        begin, wide, _ = SMALL[name]
        index = small_base + 2 * list(SMALL).index(name) + second
        cols = pl.ds(begin, wide)
        if second:
            src, dst, to = small_s2.at[:, cols], small_in2.at[:, cols], z2_to
        else:
            src, dst, to = small_s.at[pl.ds(half, half), cols], small_in.at[:, cols], z1_to
        return pltpu.make_async_remote_copy(
            src_ref=src, dst_ref=dst, send_sem=send_sem.at[index], recv_sem=recv_sem.at[index],
            device_id=to, device_id_type=pl.DeviceIdType.MESH,
        )

    def small_first(name, b_own, b_far):
        begin, wide, index = SMALL[name]
        cols = slice(begin, begin + wide)
        small_s[half:, cols] = (
            matmul(own_a[index, half:, :], b_own) + matmul(far_a[index, 1], b_far)
        ).astype(jnp.bfloat16)
        if name != "pair":
            small_copy(name, 0).start()
        small_s[:half, cols] = (
            matmul(own_a[index, :half, :], b_own) + matmul(far_a[index, 0], b_far)
        ).astype(jnp.bfloat16)
        if name == "pair":
            started(*pair_hops)

    def small_second(name):
        begin, wide, _ = SMALL[name]
        cols = slice(begin, begin + wide)
        small_copy(name, 0).wait_recv()
        small_s2[:, cols] = (
            small_s[block:half, cols].astype(jnp.float32)
            + small_in[block:, cols].astype(jnp.float32)
        ).astype(jnp.bfloat16)
        small_copy(name, 1).start()
        small_copy(name, 0).wait_send()

    def small_third(name, out_ref):
        begin, wide, _ = SMALL[name]
        cols = slice(begin, begin + wide)
        small_copy(name, 1).wait()
        out_ref[...] = (
            small_s[:block, cols].astype(jnp.float32)
            + small_in[:block, cols].astype(jnp.float32)
            + small_in2[:, cols].astype(jnp.float32)
        )

    query_x = remote(grad_query, query_far, x_to)
    pair_x = remote(grad_pair, pair_far, x_to)
    pair_y = remote(grad_pair, pair_hbm.at[1], y_to)
    pair_c = remote(grad_pair, pair_hbm.at[2], c_to)
    pair_cy = remote(pair_hbm.at[1], pair_hbm.at[3], c_to)
    pair_own = local(grad_pair, pair_hbm.at[0])
    here = output_out.at[rows_of(lane)]
    there = output_out.at[rows_of(lane_y)]
    out_spread = [
        remote(lane_send, here, y_to),
        remote(lane_send, here, c_to),
        remote(there, there, c_to),
    ]
    out_own = local(lane_send, here)

    query_reduction = reduce_copies()

    def rest_of(grads, wo_own, second, cots, weights, w_last, ring, total_tile):
        mine = [b0 + 2 * b1 + 4 * i for i in range(2)]
        weight_loads = [
            local(
                source.at[pl.ds(pl.multiple_of(tile * UNITS, UNITS), UNITS)],
                weights.at[k, pl.ds(i * UNITS, UNITS)],
            )
            for i, tile in enumerate(mine)
            for k, source in enumerate((wg_hbm, wu_hbm, wd_hbm))
        ]
        wo_load = local(wo_hbm, wo_own)
        own_tiles = [
            local(
                own_hbm.at[tile, :, pl.ds(k * UNITS, UNITS)],
                ring.at[:, pl.ds((2 * k + i) * UNITS, UNITS)],
            )
            for i, tile in enumerate(mine)
            for k in range(3)
        ]
        block_base = used["local"]
        used["local"] += 3
        own_rows = pl.ds(pl.multiple_of(b2 * wide_half, wide_half), wide_half)
        order = ((0, 0), (1, 0), (0, 1), (1, 1), (2, 0), (3, 0), (2, 1), (3, 1))

        def load_second(j, side):
            slot = order.index((j, side)) % 2
            return pltpu.make_async_copy(
                all_hbm.at[1, block_of(j, side)], second.at[slot], local_sem.at[block_base + slot]
            )

        def load_cots(j, side):
            return pltpu.make_async_copy(
                all_hbm.at[0, block_of(j, side)], cots, local_sem.at[block_base + 2]
            )

        def prefetch(j, side):
            if side:
                d_copy(0, j, 1 - core).wait_recv()
                d_copy(1, j, 1 - core).wait_recv()
            elif j:
                c_copy(0, j, 1 - core).wait_recv()
                c_copy(1, j, 1 - core).wait_recv()
            load_second(j, side).start()

        def product(q):
            slot = q % 2
            pltpu.make_async_copy(
                all_hbm.at[1, 0], second.at[slot], local_sem.at[block_base + slot]
            ).wait()
            cots_load = pltpu.make_async_copy(
                all_hbm.at[0, 0], cots, local_sem.at[block_base + 2]
            )

            @pl.when(q == 0)
            def _():
                for load in own_tiles:
                    load.wait()
                cots_load.wait()

            @pl.when(q > 0)
            def _():
                for part in (slice(0, TOK // 2), slice(TOK // 2, TOK)):
                    gate = matmul(weights[0], second[slot, :, part])
                    up_part = matmul(weights[1], second[slot, :, part])
                    sigma = jax.nn.sigmoid(gate)
                    swish = gate * sigma
                    ring[part, : 2 * UNITS] = (swish * up_part).astype(jnp.bfloat16).T
                    if part.start == 0:
                        cots_load.wait()
                    grad_hidden = matmul(weights[2], cots[:, part])
                    ring[part, 2 * UNITS : 4 * UNITS] = (
                        (grad_hidden * up_part * sigma * (1.0 + gate * (1.0 - sigma)))
                        .astype(jnp.bfloat16)
                        .T
                    )
                    ring[part, 4 * UNITS :] = (grad_hidden * swish).astype(jnp.bfloat16).T

            for n in range(3):
                cols = slice(2 * n * UNITS, 2 * (n + 1) * UNITS)
                rows = second[slot, own_rows, :] if n else cots[own_rows, :]
                total_tile[:, cols] += matmul(rows, ring[:, cols])

        far_loads = [
            local(
                all_hbm.at[k, block_of(0, side), row_block(0, p // 2, p % 2)],
                (
                    far_a.at[k, p // 2, pl.ds((p % 2) * block, block)]
                    if side
                    else own_a.at[k, pl.ds(p * block, block)]
                ),
            )
            for k in range(2)
            for side in range(2)
            for p in range(4)
        ]
        last_loads = [local(own_hbm.at[tiles - 1], sent_tile.at[:TOK, : 3 * UNITS])]
        last_weights = [
            local(source.at[pl.ds((tiles - 1) * UNITS, rest)], w_last.at[k])
            for k, source in enumerate((wg_hbm, wu_hbm, wd_hbm))
        ]

        def last_far():
            slot = order.index((0, 1)) % 2
            for load in last_weights:
                load.wait()
            padding = jnp.zeros((TOK, UNITS - rest), jnp.bfloat16)
            gate = matmul(w_last[0], second[slot])
            up_part = matmul(w_last[1], second[slot])
            grad_hidden = matmul(w_last[2], cots[...])
            sigma = jax.nn.sigmoid(gate)
            swish = gate * sigma
            parts = (
                swish * up_part,
                grad_hidden * up_part * sigma * (1.0 + gate * (1.0 - sigma)),
                grad_hidden * swish,
            )
            for k, part in enumerate(parts):
                begin = (3 + k) * UNITS
                sent_tile[:TOK, begin : begin + UNITS] = jnp.concatenate(
                    [part.astype(jnp.bfloat16).T, padding], 1
                )

        def last_first():
            for load in (*far_loads, *last_loads):
                load.wait()

            def body(n, h):
                cols = pl.ds(pl.multiple_of(n * UNITS, UNITS), UNITS)
                far_cols = pl.ds(pl.multiple_of((3 + n) * UNITS, UNITS), UNITS)
                index = (n + 1) // 2
                return cols, matmul(
                    own_a[index, h * half : (h + 1) * half, :], sent_tile[:TOK, cols]
                ) + matmul(far_a[index, h], sent_tile[:TOK, far_cols])

            def sent(n, carry):
                cols, value = body(n, 1)
                part_s[:, cols] = value.astype(jnp.bfloat16)
                return carry

            def kept(n, carry):
                cols, value = body(n, 0)
                part_k[:, cols] = value.astype(jnp.bfloat16)
                return carry

            lax.fori_loop(0, 3, sent, 0)
            z1_tile.start()
            lax.fori_loop(0, 3, kept, 0)

        reduction = reduce_copies()
        wq_load = local(wq_turned_hbm, wo_own)
        spread = spread_copies(grad_full)
        cot_load = local(cot_hbm, rel)
        kv_c = remote(kv_send.at[pl.ds(0, 8)], kv_in.at[pl.ds(0, 8)], c_to)
        kv_x = remote(kv_send.at[pl.ds(0, 4)], kv_in.at[pl.ds(8, 4)], x_to)
        kv_1 = remote(kv_send.at[pl.ds(4, 2)], kv_in.at[pl.ds(12, 2)], z1_to)
        kv_2 = remote(kv_send.at[pl.ds(6, 1)], kv_in.at[pl.ds(14, 1)], z2_to)
        keep_by = is_key * scale + (1.0 - is_key)
        send_by = (1.0 - is_key) * scale + is_key

        def middle_back(a, total):
            grad = grad_full[rows_of(a), :].astype(jnp.float32)
            rows = middle[rows_of(a), :]
            factor2 = norm_scale(rows)
            weighted = grad * gains[1:2, :]
            result = (
                rel[rows_of(a), :].astype(jnp.float32)
                + factor2 * weighted
                - rows * factor2**3 * jnp.mean(weighted * rows, axis=-1, keepdims=True)
            )
            acc[rows_of(a), :] = result
            turned[:, rows_of(a)] = result.astype(jnp.bfloat16).T
            return total + jnp.sum(grad * rows * factor2, axis=0, keepdims=True)

        def region(begin, count, blocks, wide, steps):
            heads = query.shape[0]
            rows = heads * count
            q_rows = region_rows(query, begin, count)
            grad_rows = jnp.concatenate(
                [attn_all[1, begin : begin + count, h * HD : (h + 1) * HD] for h in range(heads)], 0
            )
            logs = region_rows(log_total, begin, count)[:, :1]
            delta = jnp.sum(
                grad_rows.astype(jnp.float32) * region_rows(full, begin, count),
                axis=1,
                keepdims=True,
            )

            def add(step, carry, last=False):
                keys, values = keys_of(0, step, wide), keys_of(1, step, wide)
                probs = jnp.exp2(contract_cols(q_rows, keys) * factor - logs)
                if last:
                    probs = jnp.where(seen(begin, count, blocks, wide), probs, 0.0)
                elif wide:
                    probs = jnp.where(same_document(step), probs, 0.0)
                grad_scores = (probs * (contract_cols(grad_rows, values) - delta)).astype(
                    jnp.bfloat16
                )
                key_part = contract_rows(grad_scores, q_rows)
                value_part = contract_rows(probs.astype(jnp.bfloat16), grad_rows)
                for i, (slot, place) in enumerate(places_of(step, wide)):
                    part = slice(None) if wide else slice(i * HALF, (i + 1) * HALF)
                    grads[0, slot, place, :] += key_part[part]
                    grads[1, slot, place, :] += value_part[part]
                return carry + matmul(grad_scores, keys)

            total = add(steps, jnp.zeros((rows, HD), jnp.float32), True)
            total = lax.fori_loop(0, steps, add, total) * scale
            cosines, sines = cosine[begin : begin + count, :], sine[begin : begin + count, :]
            for h in range(heads):
                part = total[h * count : (h + 1) * count]
                grad_query[begin : begin + count, h * HD : (h + 1) * HD] = (
                    turn_back(part, cosines, sines)
                ).astype(jnp.bfloat16)

        def to_core(s, carry):
            kv_send[s] = (grads[1 - core, s] * send_by).astype(jnp.bfloat16)
            return carry

        def from_core(s, carry):
            grads[core, s] = grads[core, s] * keep_by + kv_in[s].astype(jnp.float32)
            return carry

        def pass_on(copy, first, count):
            def cast(s, carry):
                kv_send[first - 8 + s] = grads[core, count + s].astype(jnp.bfloat16)
                return carry

            lax.fori_loop(0, count, cast, 0)
            copy.start()

        def take(copy, first, count):
            copy.wait()

            def add(s, carry):
                grads[core, s] += kv_in[first + s].astype(jnp.float32)
                return carry

            lax.fori_loop(0, count, add, 0)

        def stage_0():
            reduce_start(reduction)
            total_tile[...] = jnp.zeros_like(total_tile)
            reduce_middle(reduction)
            prefetch(1, 0)
            started(*weight_loads, wo_load)
            pass_core(1, 0)

        def stage_1():
            started(*last_weights, attn_x)
            for load in weight_loads:
                load.wait()

        def stage_2():
            arrive_inner(1, 3)
            prefetch(0, 1)
            grads[...] = jnp.zeros_like(grads)
            grad_full[rows_of(lane), :] = reduce_end(reduction, acc[rows_of(lane), :]).astype(
                jnp.bfloat16
            )
            started(*spread[:2])
            cot_load.start()
            pass_core(0, 1)

        def stage_3():
            last_far()
            spread_end(spread)
            pass_y(1, 1)
            cot_load.wait()
            wo_load.wait()
            z_copy(1, 0).wait_send()
            x_copy(1, 0).wait_send()

            @when(inner)
            def _():
                z_copy(1, 1).wait_send()

            sums[...] = jnp.zeros_like(sums)
            gain2_part = lax.fori_loop(0, 4, middle_back, jnp.zeros((1, width), jnp.float32))
            for i in range(width // HD):
                sums[12 + i : 13 + i, :] = gain2_part[:, i * HD : (i + 1) * HD]
            middle_copy.start()
            for copy in attn_cy:
                copy.wait_send()
            attn_all[1] = matmul(wo_own[...], turned[...]).astype(jnp.bfloat16).T
            wq_load.start()
            arrive_outer(1, 2)
            arrive_outer(0, 3)
            region(*regions()[0])
            pass_y(0, 2)
            region(*regions()[1])
            pass_core(1, 1)
            region(*regions()[2])
            lax.fori_loop(0, 8, to_core, 0)
            kv_c.start()
            arrive_outer(1, 3)
            prefetch(1, 1)
            prefetch(2, 0)

        def stage_4():
            started(*far_loads, *last_loads)
            kv_c.wait()
            lax.fori_loop(0, 8, from_core, 0)
            pass_on(kv_x, 8, 4)
            pass_y(1, 2)
            pass_y(0, 3)
            pass_core(0, 2)
            wq_load.wait()
            middle_copy.wait()
            acc[...] = matmul(grad_query[...], wo_own[...])
            reduce_start(query_reduction)

        def stage_5():
            prefetch(3, 0)
            last_first()
            started(*branch_x)
            pass_core(1, 2)

        def stage_6():
            prefetch(2, 1)
            take(kv_x, 8, 4)
            pass_on(kv_1, 12, 2)
            started(query_x)
            pass_y(1, 3)
            pass_core(0, 3)
            for p in range(4):
                own_a[GB, p * block : (p + 1) * block, :] = turned[
                    row_block(0, p // 2, p % 2), :
                ]
            for copy in n1_x:
                copy.wait()
            n1_forward.start()

        def stage_7():
            z1_tile.wait_recv()
            part_s2[...] = (
                part_k[block:, :].astype(jnp.float32) + near1[block:, :].astype(jnp.float32)
            ).astype(jnp.bfloat16)
            z2_tile.start()
            reduce_middle(query_reduction)
            held_query[...] = acc[rows_of(lane), :].astype(jnp.bfloat16)
            take(kv_1, 12, 2)
            pass_on(kv_2, 14, 1)
            pass_core(1, 3)
            n1_forward.wait()
            prefetch(3, 1)

        stages = (stage_0, stage_1, stage_2, stage_3, stage_4, stage_5, stage_6, stage_7)

        def body(q, carry):
            for at, (stage, of) in enumerate(zip(stages, order)):

                @pl.when(q == at)
                def _(stage=stage, of=of):
                    stage()
                    if of != order[0]:
                        load_cots(*of).start()

            product(q)
            return carry

        prefetch(0, 0)
        load_cots(0, 0).start()
        started(*own_tiles)
        lax.fori_loop(0, len(order), body, 0)
        sent_tile[...] = total_tile[...].astype(jnp.bfloat16)
        near_copy(2).start()
        for copy in branch_x:
            copy.wait()
        branch_forward.start()
        query_x.wait()
        small_first("query", grad_query[...], query_far[...])
        kv_2.wait()
        f_cos = cosine[...] * is_key + (1.0 - is_key)
        f_sin = sine[...] * is_key
        total = grads[core, 0] + kv_in[14].astype(jnp.float32)
        grad_pair[...] = turn_back(total, f_cos, f_sin).astype(jnp.bfloat16)
        started(pair_x, pair_y, pair_c, pair_own)
        near_copy(3).start()
        branch_forward.wait()
        attn_x.wait()
        small_first("out", attn_all[0], attn_far[...])

    n1_forward = forward(N1)
    branch_x = share(turned, GB)
    branch_forward = forward(GB)
    middle_copy = local(acc, middle_hbm)
    pl.run_scoped(
        rest_of,
        pltpu.VMEM((2, 8, TOK, HD), jnp.float32),
        pltpu.VMEM((width // 4, width), jnp.bfloat16),
        pltpu.VMEM((2, width, TOK), jnp.bfloat16),
        pltpu.VMEM((width, TOK), jnp.bfloat16),
        pltpu.VMEM((3, 2 * UNITS, width), jnp.bfloat16),
        pltpu.VMEM((3, rest, width), jnp.bfloat16),
        pltpu.VMEM((TOK, 6 * UNITS), jnp.bfloat16),
        pltpu.VMEM((width // 2, 6 * UNITS), jnp.float32),
    )

    def closing(
        x_rows, pres, w_pres, w_down, hidden, near_low, final, held
    ):
        gathered_pair = []
        loads = [local(x_hbm, x_rows)]
        pairs_load = [
            local(pair_hbm.at[p], pres.at[:, pl.ds(p * HD, HD)]) for p in range(4)
        ]
        for p, far in enumerate(TP_ORDER):
            head = (high + far // 2) % 2
            lanes = pl.ds(pl.multiple_of(head * HD, HD), HD)
            index = used["local"]
            used["local"] += 1
            key_load, value_load = [
                pltpu.make_async_copy(
                    source.at[:, lanes],
                    w_pres.at[:, pl.ds(p * HD, HD)],
                    local_sem.at[index],
                )
                for source in (wk_hbm, wv_hbm)
            ]
            kind = (core + far % 2) % 2

            @pl.when(kind == 0)
            def _(key_load=key_load):
                key_load.start()

            @pl.when(kind == 1)
            def _(value_load=value_load):
                value_load.start()

            gathered_pair.append(key_load)
        middle_load = local(middle_hbm, middle)
        wide_unit = 2 * UNITS
        steps = [
            (t, min(wide_unit, units - t * wide_unit)) for t in range(pl.cdiv(units, wide_unit))
        ]

        def fetch(t, rows):
            slot = t % 2
            copies = [
                pltpu.make_async_copy(
                    wd_hbm.at[pl.ds(t * wide_unit, rows)],
                    w_down.at[slot, pl.ds(0, rows)],
                    weight_sem.at[slot, 0],
                )
            ]
            for i in range(pl.cdiv(rows, UNITS)):
                copies.append(
                    pltpu.make_async_copy(
                        own_hbm.at[2 * t + i, :, pl.ds(0, UNITS)],
                        hidden.at[slot, :, pl.ds(i * UNITS, UNITS)],
                        weight_sem.at[slot, 1 + i],
                    )
                )
            return copies

        started(*fetch(*steps[0]), *loads)
        for t, rows in steps:
            slot = t % 2
            if t + 1 < len(steps):
                more = steps[t + 1][1]
                if more < wide_unit:
                    end = pl.cdiv(more, UNITS) * UNITS
                    w_down[1 - slot, more:end, :] = jnp.zeros((end - more, width), w_down.dtype)
                started(*fetch(*steps[t + 1]))
            for copy in fetch(t, rows):
                copy.wait()
            depth = pl.cdiv(rows, UNITS) * UNITS

            for part in (slice(0, TOK // 2), slice(TOK // 2, TOK)):
                value = matmul(hidden[slot, part, :depth], w_down[slot, :depth, :])
                if t == 0:
                    acc[part, :] = value
                else:
                    acc[part, :] += value
            if t == 0:
                pair_y.wait_recv()
                pair_cy.start()
                pair_c.wait_recv()
                pair_own.wait()
            if t == 1:
                pair_cy.wait_recv()
                started(*pairs_load)
                pair_x.wait()
                small_first("pair", grad_pair[...], pair_far[...])
                for load in (*pairs_load, *gathered_pair):
                    load.wait()
                grad_full[rows_of(lane), :] = (
                    reduce_end(query_reduction, held_query[...].astype(jnp.float32))
                    + contract_cols(pres[rows_of(lane), :], w_pres[...])
                ).astype(jnp.bfloat16)
                started(*normed_spread[:2])
        acc[rows_of(lane), :] += middle[rows_of(lane), :]
        middle_load.start()
        near_copy(3).wait_recv()
        via_copy.start()
        near_copy(1).start()
        spread_end(normed_spread)
        reduce_start(out_reduction)
        reduce_middle(out_reduction)
        held[...] = acc[rows_of(lane), :]
        for load in (*loads, middle_load):
            load.wait()

        def last(a, total):
            grad = grad_full[rows_of(a), :].astype(jnp.float32)
            rows = x_rows[rows_of(a), :].astype(jnp.float32)
            scale1 = norm_scale(rows)
            weighted = grad * gains[0:1, :]
            rel[rows_of(a), :] = (
                middle[rows_of(a), :]
                + scale1 * weighted
                - rows * scale1**3 * jnp.mean(weighted * rows, axis=-1, keepdims=True)
            ).astype(jnp.bfloat16)
            return total + jnp.sum(grad * rows * scale1, axis=0, keepdims=True)

        gain1_part = lax.fori_loop(0, 4, last, jnp.zeros((1, width), jnp.float32))
        input_copy = started(local(rel, input_out))
        for i in range(width // HD):
            sums[i : i + 1, :] = gain1_part[:, i * HD : (i + 1) * HD]
        bias_part = jnp.sum(grad_query[...].astype(jnp.float32), axis=0, keepdims=True)
        for h in range(3):
            sums[24 + h : 25 + h, :] = bias_part[:, h * HD : (h + 1) * HD]
        for p, far in enumerate(TP_ORDER):
            row = 27 + 2 * ((core + far % 2) % 2) + (high + far // 2) % 2
            lanes = slice(p * HD, (p + 1) * HD)
            sums[pl.ds(row, 1), :] = jnp.sum(
                pres[:, lanes].astype(jnp.float32), axis=0, keepdims=True
            )
        started(*sums_copies)
        small_second("query")
        lane_send[...] = reduce_end(out_reduction, held[...]).astype(jnp.bfloat16)
        started(out_spread[0], out_spread[1], out_own)
        for copy in pair_hops:
            copy.wait()
        w_pair_grad[...] = small_s[:block, 768 : 768 + HD].astype(jnp.float32) + sum(
            pair_terms[i].astype(jnp.float32) for i in range(3)
        )
        started(*w_pair_copies)

        mine_rows = rows_of_block(me - 4 * b2)

        def tile_copies(r):
            tile = peers[r] - 4 * b2
            return [
                pltpu.make_async_copy(
                    (near_low.at[r - 1] if r else sent_tile.at[mine_rows]).at[
                        :, pl.ds((2 * k + i) * UNITS, UNITS)
                    ],
                    tiles_out.at[
                        k, :, pl.ds(pl.multiple_of((tile + 4 * i) * UNITS, UNITS), UNITS)
                    ],
                    local_sem.at[final_base + 6 * r + 2 * k + i],
                )
                for k in range(3)
                for i in range(2)
            ]

        started(*tile_copies(0))
        near_loads = [None] + [local(near_hbm.at[r], near_low.at[r - 1]) for r in (1, 2, 3)]
        for r in (2, 1, 3):
            if r == 3:
                via_copy.wait_recv()
            else:
                near_copy(r).wait_recv()
            near_loads[r].start()
            if r == 1:
                small_second("out")
                out_spread[0].wait_recv()
                out_spread[2].start()
            near_loads[r].wait()
            started(*tile_copies(r))
        z2_tile.wait_recv()
        final[...] = (
            part_k[:block, :].astype(jnp.float32)
            + near1[:block, :].astype(jnp.float32)
            + near2[...].astype(jnp.float32)
        ).astype(jnp.bfloat16)
        last_copies = [
            local(
                final.at[:, pl.ds(k * UNITS, UNITS)],
                tiles_out.at[k, :, pl.ds((tiles - 1) * UNITS, UNITS)],
            )
            for k in range(3)
        ]
        started(*last_copies)
        small_third("out", wo_out)
        small_third("query", wq_out)
        input_copy.wait()
        for r in range(4):
            for copy in tile_copies(r):
                copy.wait()
        for copy in last_copies:
            copy.wait()

    out_reduction = reduce_copies()
    normed_spread = spread_copies(grad_full)
    sums_copies = [
        remote(sums, sums_in.at[r], {"cp": peers[r]}) for r in range(1, 8)
    ]
    w_pair_place = wkv_out.at[core, :, pl.ds(pl.multiple_of(high * HD, HD), HD)]
    w_pair_copies = [remote(w_pair_grad, w_pair_place, to) for to in (y_to, c_to, cy_to)]
    w_pair_copies.append(local(w_pair_grad, w_pair_place))
    pl.run_scoped(
        closing,
        pltpu.VMEM((TOK, width), jnp.bfloat16),
        pltpu.VMEM((TOK, 4 * HD), jnp.bfloat16),
        pltpu.VMEM((width, 4 * HD), jnp.bfloat16),
        pltpu.VMEM((2, 2 * UNITS, width), jnp.bfloat16),
        pltpu.VMEM((2, TOK, 2 * UNITS), jnp.bfloat16),
        pltpu.VMEM((3, block, 6 * UNITS), jnp.bfloat16),
        pltpu.VMEM((block, 3 * UNITS), jnp.bfloat16),
        pltpu.VMEM((quarter, width), jnp.float32),
    )
    for copy in sums_copies:
        copy.wait()
    sums_out[...] = sums[...] + sum(sums_in[r] for r in range(1, 8))
    for copy in w_pair_copies:
        copy.wait()
    z1_tile.wait_send()
    z2_tile.wait_send()
    for r in (1, 2, 3):
        near_copy(r).wait_send()
    via_copy.wait_send()
    z_copy(0, 0).wait_send()
    x_copy(0, 0).wait_send()

    @when(inner)
    def _():
        z_copy(0, 1).wait_send()
        for k in range(2):
            for m in (2, 3, 4):
                z_copy(k, m).wait_send()

    for k in range(2):
        for j in range(4):
            if j:
                c_copy(k, j).wait_send()
                x_copy(k, j).wait_send()
            if (k, j) not in WHOLE_HALVES:
                y_copy(k, j).wait_send()
            d_copy(k, j).wait_send()
    for copy in (
        *attn_y, *attn_c, pair_y, pair_c, pair_cy, out_spread[0], wo_y, wo_c, wo_cy,
    ):
        copy.wait_send()
    for copy in (out_spread[1], out_spread[2]):
        copy.wait()
    out_own.wait()
    assert used["remote"] <= REMOTE and used["local"] <= LOCAL, used


WHOLE_HALVES = ()
REMOTE = 134
LOCAL = 150


def whole_layer(
    docs, places, freq, gain1, gain2, b_query, b_key, b_value,
    x, cot, w_query, w_key, w_value, w_out, w_gate, w_up, w_down,
):
    tok_rows, width = x.shape
    units = w_gate.shape[0]
    tiles = pl.cdiv(units, UNITS)
    half, block, quarter = width // 4, width // 8, tok_rows // 4
    low, wide = jnp.bfloat16, jnp.float32
    shape = jax.ShapeDtypeStruct
    any_ = pl.BlockSpec(memory_space=pl.ANY)
    outs = (
        shape((3, block, tiles * UNITS), low),
        shape((block, 384), wide),
        shape((block, 384), wide),
        shape((2, block, 2 * HD), wide),
        shape((32, HD), wide),
        shape((tok_rows, width), low),
        shape((tok_rows, width), low),
        shape((tok_rows, width), wide),
        shape((4, tok_rows, HD), low),
        shape((tiles, tok_rows, 3 * UNITS), low),
        shape((4, block, 6 * UNITS), low),
        shape((4,) + w_out.shape, low),
        shape(w_query.shape[::-1], low),
        shape((2, 8, width, tok_rows), low),
        shape((width, tok_rows), low),
        shape((block, 6 * UNITS), low),
    )
    vmem = pltpu.VMEM
    scratch = [
        vmem((tok_rows, HD), wide),
        vmem((tok_rows, HD), wide),
        vmem((2, width), wide),
        vmem((block, HD), wide),
        vmem((3, tok_rows, HD), low),
        vmem((2, 8, tok_rows, HD), low),
        vmem((3, tok_rows, HD), wide),
        vmem((3, tok_rows, HD), wide),
        vmem((32, HD), wide),
        vmem((8, 32, HD), wide),
        vmem((4, tok_rows, 384), low),
        vmem((tok_rows, 384), low),
        vmem((tok_rows, 384), low),
        vmem((tok_rows, HD), low),
        vmem((tok_rows, width), wide),
        vmem((tok_rows, width), wide),
        vmem((width, tok_rows), low),
        vmem((4, width // 2, tok_rows), low),
        vmem((4, 2, half, tok_rows), low),
        vmem((half, 3 * UNITS), low),
        vmem((half, 3 * UNITS), low),
        vmem((half, 3 * UNITS), low),
        vmem((block, 3 * UNITS), low),
        vmem((block, 3 * UNITS), low),
        vmem((width // 2, 6 * UNITS), low),
        vmem((tok_rows, width), low),
        vmem((2, quarter, width), low),
        vmem((quarter, width), low),
        vmem((quarter, width), low),
        vmem((tok_rows, width), low),
        vmem((quarter, width), low),
        vmem((8, tok_rows, HD), low),
        vmem((15, tok_rows, HD), low),
        vmem((tok_rows, 384), low),
        vmem((tok_rows, HD), low),
        vmem((2 * half, 896), low),
        vmem((half, 896), low),
        vmem((block, 896), low),
        vmem((block, 896), low),
        vmem((3, block, HD), low),
        pltpu.SemaphoreType.DMA((REMOTE,)),
        pltpu.SemaphoreType.DMA((REMOTE,)),
        pltpu.SemaphoreType.DMA((LOCAL,)),
        pltpu.SemaphoreType.DMA((3, 3)),
    ]
    return pl.pallas_call(
        functools.partial(back_kernel, width, units),
        out_shape=outs,
        in_specs=[VMEM] * 8 + [any_] * 9,
        out_specs=(any_, VMEM, VMEM, any_, VMEM) + (any_,) * 11,
        scratch_shapes=scratch,
        compiler_params=pltpu.CompilerParams(
            vmem_limit_bytes=64 * 1024 * 1024, collective_id=0, has_side_effects=True
        ),
        cost_estimate=pl.CostEstimate(
            flops=20 * tok_rows * width * units, bytes_accessed=10 * width * units, transcendentals=0
        ),
    )(
        docs, places, freq, gain1, gain2, b_query, b_key, b_value,
        x, cot, w_query, w_key, w_value, w_out, w_gate, w_up, w_down,
    )


def on_device(
    layer_input,
    norm1_gain,
    w_query,
    b_query,
    w_key,
    b_key,
    w_value,
    b_value,
    w_out,
    norm2_gain,
    w_gate,
    w_up,
    w_down,
    doc_ids,
    positions,
    cotangent,
):
    tok_rows, width = layer_input.shape
    shards = lax.axis_size("cp")
    heads = w_query.shape[1] // HD
    kv_heads = w_key.shape[1] // HD
    me = lax.axis_index("cp")
    lane = lax.axis_index("tp")
    core = lane % 2
    kv_index = lane * heads // (H // kv_heads)
    is_key = core == 0

    if shards == 8 and tok_rows == TOK:
        half = HD // 2
        freq = ROPE_BASE ** (-(jnp.arange(half, dtype=jnp.float32) * 2.0 / HD))
        tiles, grad_w_out, grad_w_query, grad_w_pairs, sums, output, grad_input, *_ = whole_layer(
            doc_ids.reshape(-1, HD), positions.reshape(-1, HD),
            jnp.concatenate([freq, freq])[None],
            norm1_gain.reshape(-1, HD), norm2_gain.reshape(-1, HD),
            b_query.reshape(-1, HD), b_key.reshape(-1, HD), b_value.reshape(-1, HD),
            layer_input, cotangent, w_query, w_key, w_value, w_out,
            w_gate.T, w_up.T, w_down,
        )
        units = w_gate.shape[1]
        wide = width // HD
        return (
            output,
            grad_input,
            sums[:wide].reshape(-1),
            grad_w_query,
            sums[24 : 24 + heads].reshape(-1),
            grad_w_pairs[0],
            sums[27:29].reshape(-1),
            grad_w_pairs[1],
            sums[29:31].reshape(-1),
            grad_w_out.T,
            sums[wide : 2 * wide].reshape(-1),
            tiles[1, :, :units].astype(jnp.float32),
            tiles[2, :, :units].astype(jnp.float32),
            tiles[0, :, :units].astype(jnp.float32).T,
        )

    def assemble(parts, axis):
        at = lambda index: lax.dynamic_index_in_dim(parts, reverse_bits(lane ^ index, 2), 0, keepdims=False)
        return (
            jnp.concatenate([at(0), at(2)], axis),
            jnp.concatenate([at(1), at(3)], axis),
        )

    def finish(
        output, grad_middle, grad_normed1, grad_query, grad_pair, gain2_part,
        grad_w_query, grad_w_pair, grad_w_out, grad_w_gate, grad_w_up, grad_w_down,
    ):
        weighted1 = grad_normed1 * norm1_gain
        gain1_part = jnp.sum(grad_normed1 * inputs * scale1, axis=0)
        grad_input = (
            grad_middle
            + scale1 * weighted1
            - inputs * scale1**3 * jnp.mean(weighted1 * inputs, axis=-1, keepdims=True)
        ).astype(jnp.bfloat16)

        small = jnp.concatenate(
            [
                gain1_part,
                gain2_part,
                jnp.sum(grad_query.astype(jnp.float32), axis=0),
                jnp.sum(grad_pair.astype(jnp.float32), axis=0),
            ]
        ).reshape(-1, HD)
        bit = 1
        while bit < shards:
            small = small + swap(small, "cp", bit)
            bit *= 2
        wide = width // HD
        gain1_sum = small[:wide].reshape(-1)
        gain2_sum = small[wide : 2 * wide].reshape(-1)
        bias_query = small[2 * wide : 2 * wide + heads].reshape(-1)

        bias_key, bias_value = assemble(gather_tp(small[None, 2 * wide + heads], 0), 0)
        grad_w_key, grad_w_value = assemble(gather_tp(grad_w_pair[None], 0), 1)
        return (
            output,
            grad_input,
            gain1_sum,
            grad_w_query,
            bias_query,
            grad_w_key,
            bias_key,
            grad_w_value,
            bias_value,
            grad_w_out,
            gain2_sum,
            grad_w_gate,
            grad_w_up,
            grad_w_down,
        )

    middle_docs = doc_ids.reshape(shards, tok_rows)[:, HALF]
    my_doc = middle_docs[me]
    start = jnp.sum((middle_docs < my_doc).astype(jnp.int32))
    place = jnp.stack([me, core, lane, start]).astype(jnp.int32)
    my_pos = lax.dynamic_slice_in_dim(positions, me * tok_rows, tok_rows)
    cosine, sine = rope_tables(my_pos, HD)

    pair_bias = lax.dynamic_slice_in_dim(jnp.where(is_key, b_key, b_value), kv_index * HD, HD)

    inputs = layer_input.astype(jnp.float32)
    scale1 = lax.rsqrt(jnp.mean(inputs * inputs, axis=-1, keepdims=True) + EPSILON)
    normed1 = (inputs * scale1 * norm1_gain).astype(jnp.bfloat16)

    def pair_weight(index):
        head = index * heads // (H // kv_heads)
        source = jnp.where(index % 2 == 0, w_key, w_value)
        return lax.dynamic_slice_in_dim(source, head * HD, HD, 1)

    pair_cos = jnp.where(is_key, cosine, 1.0)
    pair_sin = jnp.where(is_key, sine, 0.0)
    pair_pre = matmul(normed1, pair_weight(lane)) + pair_bias
    pair = rotary(pair_pre, pair_cos, pair_sin).astype(jnp.bfloat16)[None]
    bit = shards // 2
    while bit:
        pair = jnp.concatenate([pair, swap(pair, "cp", bit)], 0)
        bit //= 2
    other = swap(pair, "tp", 1)

    q_pre = matmul(normed1, w_query) + b_query
    query = rotary(
        q_pre.reshape(tok_rows, heads, HD), cosine[:, None, :], sine[:, None, :]
    ).astype(jnp.bfloat16)
    query = query.transpose(1, 0, 2)

    attn, attn_full, log_total, pair = attend(place, query, pair, other)
    w_out_all = gather_tp(w_out, 0)
    w_query_all = gather_tp(w_query, 1)
    cot_shared = share(place, cotangent, shards)
    normed1_shared = share(place, normed1, shards)

    middle = inputs + matmul(gather_tp(attn, 1), w_out_all)
    scale2 = lax.rsqrt(jnp.mean(middle * middle, axis=-1, keepdims=True) + EPSILON)
    normed2 = (middle * scale2 * norm2_gain).astype(jnp.bfloat16)

    units = w_gate.shape[1]
    chunks = pl.cdiv(pl.cdiv(units, TILE), CHUNK_TILES)
    hiddens, grads, total = [], [], None
    for index in range(chunks):
        hidden, grad, total = hidden_chunk(
            place, normed2, cotangent, w_gate, w_up, w_down, total, index
        )
        hiddens.append(hidden)
        grads.append(grad)
    normed2_shared = share(place, normed2, shards)

    downs, gates, ups = [], [], []
    for hidden, grad in zip(hiddens, grads):
        downs.append(weight_grad(place, cot_shared, hidden, shards).T)
        both = weight_grad(place, normed2_shared, grad, shards)
        span = hidden.shape[1]
        for at in range(0, span, TILE):
            size = min(TILE, span - at)
            gates.append(both[:, 2 * at : 2 * at + size])
            ups.append(both[:, 2 * at + TILE : 2 * at + TILE + size])
    grad_w_down = jnp.concatenate(downs, 0)
    grad_w_gate = jnp.concatenate(gates, 1)
    grad_w_up = jnp.concatenate(ups, 1)

    grad_normed2 = in_order(gather_tp(scatter_tp(total).astype(jnp.bfloat16), 0), lane).astype(
        jnp.float32
    )
    weighted2 = grad_normed2 * norm2_gain
    gain2_part = jnp.sum(grad_normed2 * middle * scale2, axis=0)
    grad_middle = (
        cotangent.astype(jnp.float32)
        + scale2 * weighted2
        - middle * scale2**3 * jnp.mean(weighted2 * middle, axis=-1, keepdims=True)
    )
    grad_branch = grad_middle.astype(jnp.bfloat16)
    grad_attn = contract_cols(grad_branch, w_out).astype(jnp.bfloat16)
    grad_query, keep, send = attend_back(
        place, query, pair, grad_attn, attn_full, log_total, cosine, sine
    )

    part = tok_rows // 4
    ffn = sum(matmul(h, lax.slice_in_dim(w_down, i * CHUNK_TILES * TILE, i * CHUNK_TILES * TILE + h.shape[1])) for i, h in enumerate(hiddens))
    ffn = after(ffn.astype(jnp.bfloat16), grad_middle)
    ffn_rel = jnp.concatenate(
        [lax.dynamic_slice_in_dim(ffn, (lane ^ far) * part, part, 0) for far in TP_ORDER], 0
    )
    out_part = scatter_tp(ffn_rel) + lax.dynamic_slice_in_dim(middle, lane * part, part, 0)
    output = in_order(gather_tp(out_part.astype(jnp.bfloat16), 0), lane)

    summed = keep.astype(jnp.float32) + swap(send, "tp", 1).astype(jnp.float32)
    bit = 1
    while bit < shards:
        count = summed.shape[0] // 2
        summed = summed[:count] + swap(summed[count:].astype(jnp.bfloat16), "cp", bit).astype(
            jnp.float32
        )
        bit *= 2
    grad_pair = rotary_back(summed[0], pair_cos, pair_sin).astype(jnp.bfloat16)

    branch_shared = share(place, grad_branch, shards)
    grad_w_out = weight_grad(place, branch_shared, attn, shards).T
    grad_w_query = weight_grad(place, normed1_shared, grad_query, shards)
    grad_w_pair = weight_grad(place, normed1_shared, grad_pair, shards)

    pairs_all = gather_tp(grad_pair, 1)
    grad_normed1 = contract_cols(gather_tp(grad_query, 1), w_query_all)
    for i, far in enumerate(TP_ORDER):
        grad_normed1 = grad_normed1 + contract_cols(
            pairs_all[:, i * HD : (i + 1) * HD], pair_weight(lane ^ far)
        )
    return finish(
        output, grad_middle, grad_normed1, grad_query, grad_pair, gain2_part,
        grad_w_query, grad_w_pair, grad_w_out, grad_w_gate, grad_w_up, grad_w_down,
    )


def solution(mesh):
    return jax.shard_map(
        on_device,
        mesh=mesh,
        in_specs=(
            P("cp", None),
            P(),
            P(None, "tp"),
            P("tp"),
            P(),
            P(),
            P(),
            P(),
            P("tp", None),
            P(),
            P(None, "tp"),
            P(None, "tp"),
            P("tp", None),
            P(),
            P(),
            P("cp", None),
        ),
        out_specs=(
            P("cp", None),
            P("cp", None),
            P(),
            P("cp", "tp"),
            P("tp"),
            P("cp", None),
            P(),
            P("cp", None),
            P(),
            P("tp", "cp"),
            P(),
            P("cp", "tp"),
            P("cp", "tp"),
            P("tp", "cp"),
        ),
        check_vma=False,
    )
```

```python
import functools
import math

import jax
import jax.numpy as jnp
from jax import lax
from jax.experimental import pallas as pl
from jax.experimental.pallas import tpu as pltpu
from jax.sharding import PartitionSpec as P

H = 12
HD = 128
HALF = 128
EPSILON = 1e-06
ROPE_BASE = 10000.0
MASKED = -1e30
LOG2E = 1.4426950408889634
TILE = 256
CHUNK_TILES = 3
VMEM_LIMIT = 56 * 1024 * 1024
TP_ORDER = (0, 2, 1, 3)


def matmul(left, right):
    return jnp.dot(left, right, preferred_element_type=jnp.float32)


def contract_rows(left, right):
    return lax.dot_general(
        left, right, (((0,), (0,)), ((), ())), preferred_element_type=jnp.float32
    )


def contract_cols(left, right):
    return lax.dot_general(
        left, right, (((1,), (1,)), ((), ())), preferred_element_type=jnp.float32
    )


def rope_tables(tok_pos, width):
    half = width // 2
    freq = ROPE_BASE ** (-(jnp.arange(half, dtype=jnp.float32) * 2.0 / width))
    angle = tok_pos.astype(jnp.float32)[:, None] * freq[None, :]
    cosine = jnp.concatenate([jnp.cos(angle), jnp.cos(angle)], -1)
    sine = jnp.concatenate([jnp.sin(angle), jnp.sin(angle)], -1)
    return (cosine, sine)


def rotary(values, cosine, sine):
    half = values.shape[-1] // 2
    return values * cosine + jnp.concatenate([-values[..., half:], values[..., :half]], -1) * sine


def rotary_back(grads, cosine, sine):
    half = grads.shape[-1] // 2
    scaled = grads * sine
    return grads * cosine + jnp.concatenate([scaled[..., half:], -scaled[..., :half]], -1)


def swap(value, axis, bit):
    size = lax.axis_size(axis)
    return lax.ppermute(value, axis, [(i, i ^ bit) for i in range(size)])


def after(value, *earlier):
    return lax.optimization_barrier((value, *earlier))[0]


def bits_of(size):
    return size.bit_length() - 1


def reverse_bits(index, bits):
    out = 0
    for i in range(bits):
        out = out | (((index >> i) & 1) << (bits - 1 - i))
    return out


def params(**more):
    return pltpu.CompilerParams(vmem_limit_bytes=VMEM_LIMIT, **more)


SMEM = pl.BlockSpec(memory_space=pltpu.SMEM)
VMEM = pl.BlockSpec(memory_space=pltpu.VMEM)


def spread_kernel(shards, place_ref, rows_ref, own_ref, send_ref, turned):
    me, core = place_ref[0], place_ref[1]
    turned[...] = rows_ref[...].T
    width = turned.shape[0] // shards
    bits = bits_of(shards)
    for i in range(shards // 2):
        far = reverse_bits(i, bits)
        block = pl.multiple_of((me ^ far) * width, 16)
        own_ref[i * width : (i + 1) * width, :] = turned[pl.ds(block, width), :]
    for i in range(shards // 4):
        far = reverse_bits(core * (shards // 4) + i, bits) | 1
        block = pl.multiple_of((me ^ far) * width, 16)
        send_ref[i * width : (i + 1) * width, :] = turned[pl.ds(block, width), :]


def spread(place, rows, shards):
    count, width = rows.shape
    return pl.pallas_call(
        functools.partial(spread_kernel, shards),
        out_shape=(
            jax.ShapeDtypeStruct((width // 2, count), rows.dtype),
            jax.ShapeDtypeStruct((width // 4, count), rows.dtype),
        ),
        in_specs=[SMEM, VMEM],
        out_specs=(VMEM, VMEM),
        scratch_shapes=[pltpu.VMEM((width, count), rows.dtype)],
        compiler_params=params(),
        cost_estimate=pl.CostEstimate(flops=0, bytes_accessed=4 * rows.size, transcendentals=0),
    )(place, rows)


def share(place, rows, shards):
    own, send = spread(place, rows, shards)
    near = swap(send, "cp", 1)
    return own, near, swap(near, "tp", 1)


def weigh_kernel(place_ref, own_ref, near_ref, far_ref, mine_ref, theirs_ref, send_ref, keep_ref, joined):
    core = place_ref[1]

    @pl.when(pl.program_id(0) == 0)
    def _():
        joined[core] = near_ref[...]
        joined[1 - core] = far_ref[...]

    half = send_ref.shape[0]
    mine, theirs = mine_ref[...], theirs_ref[...]
    send_ref[...] = (
        matmul(own_ref[half:, :], mine) + matmul(joined[1], theirs)
    ).astype(send_ref.dtype)
    keep_ref[...] = (
        matmul(own_ref[:half, :], mine) + matmul(joined[0], theirs)
    ).astype(keep_ref.dtype)


def weigh(place, shared, mine, theirs):
    own, near, far = shared
    half, count = near.shape
    width = mine.shape[1]
    tile = min(width, 512)
    whole = lambda j: (0, 0)
    column = lambda j: (0, j)
    return pl.pallas_call(
        weigh_kernel,
        grid=(pl.cdiv(width, tile),),
        out_shape=(jax.ShapeDtypeStruct((half, width), jnp.bfloat16),) * 2,
        in_specs=[
            SMEM,
            pl.BlockSpec((2 * half, count), whole),
            pl.BlockSpec((half, count), whole),
            pl.BlockSpec((half, count), whole),
            pl.BlockSpec((count, tile), column),
            pl.BlockSpec((count, tile), column),
        ],
        out_specs=(pl.BlockSpec((half, tile), column),) * 2,
        scratch_shapes=[pltpu.VMEM((2, half, count), jnp.bfloat16)],
        compiler_params=params(),
        cost_estimate=pl.CostEstimate(
            flops=8 * half * count * width,
            bytes_accessed=4 * (2 * half * count + count * width + half * width),
            transcendentals=0,
        ),
    )(place, own, near, far, mine, theirs)


def weight_grad(place, shared, mine, shards):
    theirs = swap(mine, "cp", 1)
    send, keep = weigh(place, shared, mine, theirs)
    terms = [keep]
    bit = 2
    while bit < shards:
        terms.append(swap(send, "cp", bit))
        bit *= 2
        if bit < shards:
            rows = terms[0].shape[0] // 2
            send = sum(t[rows:].astype(jnp.float32) for t in terms).astype(jnp.bfloat16)
            terms = [t[:rows] for t in terms]
    return sum(t.astype(jnp.float32) for t in terms)


def hidden_kernel(first, last, offset, units, *refs):
    place_ref, rows_ref, cot_ref, gate_ref, up_ref, down_ref = refs[:6]
    refs = refs[6:]
    if not first:
        before_ref, refs = refs[0], refs[1:]
    hidden_ref, grads_ref, sum_ref, total = refs
    step = pl.program_id(0)

    @pl.when(step == 0)
    def _():
        total[...] = jnp.zeros_like(total) if first else before_ref[...]

    rows = rows_ref[...]
    w_gate, w_up, w_down = gate_ref[...], up_ref[...], down_ref[...]
    if last:
        left = units - (offset + step) * TILE
        inside = lax.broadcasted_iota(jnp.int32, w_gate.shape, 1) < left
        w_gate = jnp.where(inside, w_gate, 0)
        w_up = jnp.where(inside, w_up, 0)
        inside = lax.broadcasted_iota(jnp.int32, w_down.shape, 0) < left
        w_down = jnp.where(inside, w_down, 0)
    gate = matmul(rows, w_gate)
    up_part = matmul(rows, w_up)
    grad_hidden = contract_cols(cot_ref[...], w_down)
    sigma = jax.nn.sigmoid(gate)
    swish = gate * sigma
    hidden_ref[...] = (swish * up_part).astype(jnp.bfloat16)
    grad_gate = (grad_hidden * up_part * sigma * (1.0 + gate * (1.0 - sigma))).astype(jnp.bfloat16)
    grad_up = (grad_hidden * swish).astype(jnp.bfloat16)
    grads_ref[:, :TILE] = grad_gate
    grads_ref[:, TILE:] = grad_up
    total[...] += contract_cols(grad_gate, w_gate) + contract_cols(grad_up, w_up)

    @pl.when(step == pl.num_programs(0) - 1)
    def _():
        if last:
            part = total.shape[0] // len(TP_ORDER)
            for i, far in enumerate(TP_ORDER):
                block = pl.multiple_of((place_ref[2] ^ far) * part, part)
                sum_ref[i * part : (i + 1) * part, :] = total[pl.ds(block, part), :].astype(
                    sum_ref.dtype
                )
        else:
            sum_ref[...] = total[...]


def hidden_chunk(place, rows, cotangent, w_gate, w_up, w_down, before, index):
    count, width = rows.shape
    units = w_gate.shape[1]
    tiles = pl.cdiv(units, TILE)
    offset = index * CHUNK_TILES
    steps = min(CHUNK_TILES, tiles - offset)
    first, last = index == 0, offset + steps == tiles
    inner = min(steps * TILE, units - offset * TILE)
    outer = (steps - 1) * 2 * TILE + TILE + inner - (steps - 1) * TILE
    whole = lambda j: (0, 0)
    column = lambda j: (0, j)
    in_specs = [
        SMEM,
        pl.BlockSpec((count, width), whole),
        pl.BlockSpec((count, width), whole),
        pl.BlockSpec((width, TILE), lambda j: (0, offset + j)),
        pl.BlockSpec((width, TILE), lambda j: (0, offset + j)),
        pl.BlockSpec((TILE, width), lambda j: (offset + j, 0)),
    ]
    operands = [place, rows, cotangent, w_gate, w_up, w_down]
    if not first:
        in_specs.append(pl.BlockSpec((count, width), whole))
        operands.append(before)
    return pl.pallas_call(
        functools.partial(hidden_kernel, first, last, offset, units),
        grid=(steps,),
        out_shape=(
            jax.ShapeDtypeStruct((count, inner), jnp.bfloat16),
            jax.ShapeDtypeStruct((count, outer), jnp.bfloat16),
            jax.ShapeDtypeStruct((count, width), jnp.bfloat16 if last else jnp.float32),
        ),
        in_specs=in_specs,
        out_specs=(
            pl.BlockSpec((count, TILE), column),
            pl.BlockSpec((count, 2 * TILE), column),
            pl.BlockSpec((count, width), whole),
        ),
        scratch_shapes=[pltpu.VMEM((count, width), jnp.float32)],
        compiler_params=params(),
        cost_estimate=pl.CostEstimate(
            flops=10 * count * width * inner,
            bytes_accessed=6 * width * inner + 12 * count * width,
            transcendentals=count * inner,
        ),
    )(*operands)


def region_rows(ref, start, count):
    return ref[:, start : start + count, :].reshape(-1, HD)


def triangle(rows, keys):
    row = lax.broadcasted_iota(jnp.int32, (rows, keys), 0) & (keys - 1)
    return row >= lax.broadcasted_iota(jnp.int32, (rows, keys), 1)


def regions(place_ref, shards, tok_rows):
    me, start = place_ref[0], place_ref[3]
    bits = bits_of(shards)

    def of_first(block):
        low = block < shards
        device = jnp.where(low, block, 2 * shards - 1 - block)
        return reverse_bits(device ^ me, bits), jnp.where(low, 0, tok_rows - HALF)

    def of_middle(block):
        return reverse_bits((start + block) ^ me, bits), HALF

    return (
        (0, HALF, me, of_first),
        (tok_rows - HALF, HALF, 2 * shards - 1 - me, of_first),
        (HALF, tok_rows - 2 * HALF, me - start, of_middle),
    )


def attend_kernel(shards, place_ref, q_ref, mine_ref, other_ref, low_ref, full_ref, log_ref, pair):
    core = place_ref[1]
    pair[core] = mine_ref[...]
    pair[1 - core] = other_ref[...]
    heads, tok_rows = q_ref.shape[0], q_ref.shape[1]
    factor = HD**-0.5 * LOG2E
    for begin, count, blocks, locate in regions(place_ref, shards, tok_rows):
        query = region_rows(q_ref, begin, count)
        rows = heads * count

        def read(which, block):
            slot, offset = locate(block)
            return pair[which, slot, pl.ds(pl.multiple_of(offset, HALF), count), :]

        mask = triangle(rows, count)
        last = jnp.where(mask, contract_cols(query, read(0, blocks)), MASKED)
        peak = lax.fori_loop(
            0, blocks, lambda t, top: jnp.maximum(top, contract_cols(query, read(0, t))), last
        )
        peak = jnp.max(peak, axis=1, keepdims=True) * factor

        def add(block, carry, scores):
            total, accum = carry
            weights = jnp.exp2(scores * factor - peak)
            return total + weights, accum + matmul(weights.astype(jnp.bfloat16), read(1, block))

        carry = add(blocks, (jnp.zeros((rows, count), jnp.float32), jnp.zeros((rows, HD), jnp.float32)), last)
        total, accum = lax.fori_loop(
            0, blocks, lambda t, held: add(t, held, contract_cols(query, read(0, t))), carry
        )
        total = jnp.sum(total, axis=1, keepdims=True)
        full = accum / total
        log_total = jnp.broadcast_to(peak + jnp.log2(total), (rows, HD))
        for head in range(heads):
            part = slice(head * count, (head + 1) * count)
            lanes = slice(head * HD, (head + 1) * HD)
            low_ref[begin : begin + count, lanes] = full[part].astype(jnp.bfloat16)
            full_ref[head, begin : begin + count, :] = full[part]
            log_ref[head, begin : begin + count, :] = log_total[part]


def attend(place, query, mine, other):
    heads, tok_rows, _ = query.shape
    shards = mine.shape[0]
    pairs = heads * tok_rows * tok_rows * shards // 4
    return pl.pallas_call(
        functools.partial(attend_kernel, shards),
        out_shape=(
            jax.ShapeDtypeStruct((tok_rows, heads * HD), jnp.bfloat16),
            jax.ShapeDtypeStruct((heads, tok_rows, HD), jnp.float32),
            jax.ShapeDtypeStruct((heads, tok_rows, HD), jnp.float32),
            jax.ShapeDtypeStruct((2,) + mine.shape, jnp.bfloat16),
        ),
        in_specs=[SMEM, VMEM, VMEM, VMEM],
        out_specs=(VMEM, VMEM, VMEM, VMEM),
        compiler_params=params(),
        cost_estimate=pl.CostEstimate(
            flops=6 * pairs * HD, bytes_accessed=4 * mine.size, transcendentals=pairs
        ),
    )(place, query, mine, other)


def attend_back_kernel(
    shards, place_ref, q_ref, pair, low_ref, full_ref, log_ref, cos_ref, sin_ref,
    query_ref, keep_ref, send_ref, grads,
):
    core = place_ref[1]
    grads[...] = jnp.zeros_like(grads)
    heads, tok_rows = q_ref.shape[0], q_ref.shape[1]
    scale = HD**-0.5
    factor = scale * LOG2E
    sign = jnp.where(lax.broadcasted_iota(jnp.int32, (1, HD), 1) < HD // 2, 1.0, -1.0)
    for begin, count, blocks, locate in regions(place_ref, shards, tok_rows):
        query = region_rows(q_ref, begin, count)
        rows = heads * count
        incoming = jnp.concatenate(
            [low_ref[begin : begin + count, h * HD : (h + 1) * HD] for h in range(heads)], 0
        )
        full = region_rows(full_ref, begin, count)
        log_total = region_rows(log_ref, begin, count)[:, :1]
        delta = jnp.sum(incoming.astype(jnp.float32) * full, axis=1, keepdims=True)

        def add(block, grad_query, mask=None):
            slot, offset = locate(block)
            place = pl.ds(pl.multiple_of(offset, HALF), count)
            keys, values = pair[0, slot, place, :], pair[1, slot, place, :]
            probs = jnp.exp2(contract_cols(query, keys) * factor - log_total)
            if mask is not None:
                probs = jnp.where(mask, probs, 0.0)
            grad_scores = (probs * (contract_cols(incoming, values) - delta)).astype(jnp.bfloat16)
            grads[0, slot, place, :] += contract_rows(grad_scores, query)
            grads[1, slot, place, :] += contract_rows(probs.astype(jnp.bfloat16), incoming)
            return grad_query + matmul(grad_scores, keys)

        grad_query = add(blocks, jnp.zeros((rows, HD), jnp.float32), triangle(rows, count))
        grad_query = lax.fori_loop(0, blocks, add, grad_query) * scale
        cosine, sine = cos_ref[begin : begin + count, :], sin_ref[begin : begin + count, :]
        for head in range(heads):
            part = grad_query[head * count : (head + 1) * count]
            turned = part * cosine + pltpu.roll(part * sine, HD // 2, 1) * sign
            query_ref[begin : begin + count, head * HD : (head + 1) * HD] = turned.astype(
                jnp.bfloat16
            )
    is_key = core == 0
    keep_ref[...] = (grads[core] * jnp.where(is_key, scale, 1.0)).astype(jnp.bfloat16)
    send_ref[...] = (grads[1 - core] * jnp.where(is_key, 1.0, scale)).astype(jnp.bfloat16)


def attend_back(place, query, pair, low, full, log_total, cosine, sine):
    heads, tok_rows, _ = query.shape
    shards = pair.shape[1]
    pairs = heads * tok_rows * tok_rows * shards // 4
    return pl.pallas_call(
        functools.partial(attend_back_kernel, shards),
        out_shape=(
            jax.ShapeDtypeStruct((tok_rows, heads * HD), jnp.bfloat16),
            jax.ShapeDtypeStruct(pair.shape[1:], jnp.bfloat16),
            jax.ShapeDtypeStruct(pair.shape[1:], jnp.bfloat16),
        ),
        in_specs=[SMEM] + [VMEM] * 7,
        out_specs=(VMEM, VMEM, VMEM),
        scratch_shapes=[pltpu.VMEM(pair.shape, jnp.float32)],
        compiler_params=params(),
        cost_estimate=pl.CostEstimate(
            flops=10 * pairs * HD, bytes_accessed=4 * pair.size, transcendentals=pairs
        ),
    )(place, query, pair, low, full, log_total, cosine, sine)


def gather_tp(value, axis):
    value = jnp.concatenate([value, swap(value, "tp", 2)], axis)
    return jnp.concatenate([value, swap(value, "tp", 1)], axis)


def scatter_tp(value):
    half, part = value.shape[0] // 2, value.shape[0] // 4
    other = swap(value[half:], "tp", 1)
    send = (value[part:half].astype(jnp.float32) + other[part:].astype(jnp.float32)).astype(
        jnp.bfloat16
    )
    last = swap(send, "tp", 2)
    return (
        value[:part].astype(jnp.float32)
        + other[:part].astype(jnp.float32)
        + last.astype(jnp.float32)
    )


def in_order(value, me):
    part = value.shape[0] // 4
    return jnp.concatenate(
        [
            lax.dynamic_slice_in_dim(value, reverse_bits(me ^ i, 2) * part, part, 0)
            for i in range(4)
        ],
        0,
    )


UNITS = 256
TOK = 512


def back_kernel(width, units, *refs):
    (
        docs_ref, pos_ref, freq_ref, gain1_ref, gain2_ref, bq_ref, bk_ref, bv_ref, x_hbm, cot_hbm, wq_hbm, wk_hbm, wv_hbm, wo_hbm,
        wg_hbm, wu_hbm, wd_hbm,
        tiles_out, wo_out, wq_out, wkv_out, sums_out, output_out, input_out,
        middle_hbm, pair_hbm, own_hbm, near_hbm, wo_all, wq_turned_hbm, all_hbm, n1_hbm, via_hbm,
        out_core_hbm, out_lane_hbm,
        cosine, sine, gains, w_pair_grad, query, pair, full, log_total, sums, sums_in,
        attn_all, attn_far, query_far, pair_far, middle, acc, turned,
        own_a, far_a, part_s, part_k, near1, part_s2, near2, sent_tile,
        rel, core_in, lane_send, lane_in, grad_full,
        held_query, kv_send, kv_in, grad_query, grad_pair, small_s, small_in, small_s2, small_in2, pair_terms,
        send_sem, recv_sem, local_sem, weight_sem,
    ) = refs
    me = lax.axis_index("cp")
    lane = lax.axis_index("tp")
    b0, b1, b2 = me % 2, (me // 2) % 2, me // 4
    core, high = lane % 2, lane // 2
    x_to = {"cp": me + 1 - 2 * b0}
    z1_to = {"cp": me + 2 - 4 * b1}
    z2_to = {"cp": me + 4 - 8 * b2}
    z3_to = {"cp": me + 6 - 4 * b1 - 8 * b2}
    inner = (b1 + b2) % 2
    peers = [
        me + (r % 2) * (1 - 2 * b0) + (r // 2 % 2) * (2 - 4 * b1) + (r // 4) * (4 - 8 * b2)
        for r in range(8)
    ]
    c_to = {"tp": lane + 1 - 2 * core}
    y_to = {"tp": lane + 2 - 4 * high}
    lane_c, lane_y = lane + 1 - 2 * core, lane + 2 - 4 * high
    lane_cy = 3 - lane
    cy_to = {"tp": lane_cy}
    tiles = pl.cdiv(units, UNITS)
    rest = units - (tiles - 1) * UNITS
    block = width // 8
    half = width // 4
    quarter = TOK // 4
    scale = HD**-0.5
    factor = scale * LOG2E
    used = {"remote": 0, "local": 0}

    def remote(src, dst, to, count=1):
        index = used["remote"]
        used["remote"] += 1
        return pltpu.make_async_remote_copy(
            src_ref=src, dst_ref=dst, send_sem=send_sem.at[index], recv_sem=recv_sem.at[index],
            device_id=to, device_id_type=pl.DeviceIdType.MESH,
        )

    def local(src, dst):
        index = used["local"]
        used["local"] += 1
        return pltpu.make_async_copy(src, dst, local_sem.at[index])

    def started(*copies):
        for copy in copies:
            copy.start()
        return copies[0] if len(copies) == 1 else copies

    def row_block(side, h, i):
        mine = (b0 + side) % 2 + 2 * ((b1 + h) % 2) + 4 * ((b2 + i) % 2)
        return pl.ds(pl.multiple_of(mine * block, 16), block)

    def rows_of_block(index):
        return pl.ds(pl.multiple_of(index * block, 16), block)

    def rows_of(index):
        return pl.ds(pl.multiple_of(index * quarter, quarter), quarter)

    z1_tile = remote(part_s, near1, z1_to)
    z2_tile = remote(part_s2, near2, z2_to)

    spread_base = used["remote"]
    used["remote"] += 2 * 20
    wide_half, wide_quarter = width // 2, width // 4

    def block_of(j, side):
        z = (b1 + 2 * b2, 1 - b1 + 2 * b2, 2 - b2, 3 - 3 * b2)[j]
        return 2 * z + (b0 + side) % 2

    def spread_part(k, j, side, c, y=None):
        rows = half_of(c, y)
        return all_hbm.at[k, block_of(j, side), rows]

    def half_of(c, y=None):
        if y is None:
            return pl.ds(pl.multiple_of(c * wide_half, wide_half), wide_half)
        return pl.ds(pl.multiple_of(c * wide_half + y * wide_quarter, wide_quarter), wide_quarter)

    def spread_copy(k, part, send, recv, to, source=None):
        index = spread_base + 20 * k
        return pltpu.make_async_remote_copy(
            src_ref=part if source is None else source, dst_ref=part,
            send_sem=send_sem.at[index + send],
            recv_sem=recv_sem.at[index + recv], device_id=to, device_id_type=pl.DeviceIdType.MESH,
        )

    def z_copy(k, m):
        j, recv, to = ((0, 1, z1_to), (0, 2, z3_to), (1, 3, z3_to), (2, 2, z1_to), (3, 3, z1_to))[m]
        own = turned.at[half_of(core)] if (k, j) == (1, 0) else None
        return spread_copy(k, spread_part(k, j, 0, core), m, recv, to, own)

    def z_arrival(k, j):
        return spread_copy(k, spread_part(k, j, 0, core), 0, j, z1_to)

    def c_copy(k, j, c=None):
        return spread_copy(k, spread_part(k, j, 0, core if c is None else c), 4 + j, 4 + j, c_to)

    def x_copy(k, j, side=0):
        y = None if (k, j) in WHOLE_HALVES else high
        own = turned.at[half_of(core, y)] if (k, j, side) == (1, 0, 0) else None
        return spread_copy(k, spread_part(k, j, side, core, y), 8 + j, 8 + j, x_to, own)

    def y_copy(k, j, y=None):
        return spread_copy(
            k, spread_part(k, j, 1, core, high if y is None else y), 12 + j, 12 + j, y_to
        )

    def d_copy(k, j, c=None):
        return spread_copy(k, spread_part(k, j, 1, core if c is None else c), 16 + j, 16 + j, c_to)

    def when(condition):
        return pl.when(condition == 1)

    def begin_spread(k):
        z_copy(k, 0).start()

        @when(inner)
        def _():
            z_copy(k, 1).start()

    def arrive(k, j):
        z_arrival(k, j).wait_recv()

        @when(inner)
        def _():
            z_copy(k, j + 1).start()

        started(c_copy(k, j), x_copy(k, j))

    def arrive_inner(k, j):
        @when(inner)
        def _():
            arrive(k, j)

    def arrive_outer(k, j):
        @when(1 - inner)
        def _():
            arrive(k, j)

    def pass_y(k, j):
        assert (k, j) not in WHOLE_HALVES
        x_copy(k, j, 1).wait_recv()
        y_copy(k, j).start()

    def pass_core(k, j):
        if (k, j) in WHOLE_HALVES:
            x_copy(k, j, 1).wait_recv()
        else:
            y_copy(k, j, 1 - high).wait_recv()
        d_copy(k, j).start()

    barrier = pltpu.get_barrier_semaphore()
    for to in (*({"cp": peer} for peer in peers[1:]), c_to, y_to, cy_to):
        pl.semaphore_signal(barrier, inc=1, device_id=to, device_id_type=pl.DeviceIdType.MESH)

    def share(source, index):
        return [
            remote(
                source.at[row_block(1, core, i)],
                far_a.at[index, core, pl.ds(i * block, block)],
                x_to,
            )
            for i in range(2)
        ]

    def forward(index):
        return remote(far_a.at[index, core], far_a.at[index, core], c_to)

    COT, N2, GB, N1 = range(4)
    own_blocks = [local(turned, all_hbm.at[k, me]) for k in range(2)]
    wo_y = remote(wo_hbm, wo_all.at[1], y_to)
    wo_c = remote(wo_hbm, wo_all.at[2], c_to)
    wo_cy = remote(wo_all.at[1], wo_all.at[3], c_to)
    attn_y, attn_c, attn_cy = [
        [
            remote(
                attn_all.at[src, pl.ds(begin, count)], attn_all.at[dst, pl.ds(begin, count)], to
            )
            for begin, count in ((0, HALF), (TOK - HALF, HALF), (HALF, TOK - 2 * HALF))
        ]
        for src, dst, to in ((0, 1, y_to), (0, 2, c_to), (1, 3, c_to))
    ]
    attn_x = remote(attn_all.at[0], attn_far, x_to)
    n1_x = share(n1_hbm, N1)
    n1_keep = local(turned, n1_hbm)
    pair_1 = remote(pair.at[core, 0], pair.at[core, 2], z1_to)
    pair_2 = remote(pair.at[core, 0], pair.at[core, 1], z2_to)
    pair_3 = remote(pair.at[core, 0], pair.at[core, 3], z3_to)
    pair_near = [remote(pair.at[core, i], pair.at[core, 4 + i], x_to) for i in range(4)]
    pair_core = [remote(pair.at[core, i], pair.at[core, i], c_to) for i in range(8)]
    def norm_scale(rows):
        return lax.rsqrt(jnp.mean(rows * rows, axis=-1, keepdims=True) + EPSILON)

    sign = jnp.where(lax.broadcasted_iota(jnp.int32, (1, HD), 1) < HD // 2, 1.0, -1.0)
    is_key = jnp.where(core == 0, 1.0, 0.0)

    def turn(rows, cosines, sines):
        return rows * cosines + pltpu.roll(rows * sign, HD // 2, 1) * sines

    def turn_back(rows, cosines, sines):
        return rows * cosines + pltpu.roll(rows * sines, HD // 2, 1) * sign

    def opening(x_rows, cot_rows, normed, w_query, w_pair, w_turned):
        loads = [
            local(x_hbm, x_rows),
            local(wq_hbm, w_query),
            local(cot_hbm, cot_rows),
        ]
        started(*loads)
        index = used["local"]
        used["local"] += 1
        columns = pl.ds(pl.multiple_of(high * HD, HD), HD)
        key_load = pltpu.make_async_copy(wk_hbm.at[:, columns], w_pair, local_sem.at[index])
        value_load = pltpu.make_async_copy(wv_hbm.at[:, columns], w_pair, local_sem.at[index])

        @pl.when(core == 0)
        def _():
            key_load.start()

        @pl.when(core == 1)
        def _():
            value_load.start()

        lanes_of = [slice(i * HD, (i + 1) * HD) for i in range(width // HD)]
        for i, lanes in enumerate(lanes_of):
            gains[0:1, lanes] = gain1_ref[i : i + 1, :]
            gains[1:2, lanes] = gain2_ref[i : i + 1, :]
        places = pos_ref[pl.ds(me * 4, 4), :].astype(jnp.float32)
        places = jnp.concatenate([places, places], 0).T
        for i in range(4):
            angle = places[:, i : i + 1] * freq_ref[...]
            cosine[i * HD : (i + 1) * HD, :] = jnp.cos(angle)
            sine[i * HD : (i + 1) * HD, :] = jnp.sin(angle)
        loads[0].wait()

        def norm(a, carry):
            rows = x_rows[rows_of(a), :].astype(jnp.float32)
            normed[rows_of(a), :] = (rows * norm_scale(rows) * gains[0:1, :]).astype(
                jnp.bfloat16
            )
            return carry

        lax.fori_loop(0, 4, norm, 0)
        key_load.wait()
        rows = (
            matmul(normed[...], w_pair[...])
            + bk_ref[pl.ds(high, 1), :] * is_key
            + bv_ref[pl.ds(high, 1), :] * (1.0 - is_key)
        )
        pair[core, 0] = turn(
            rows, cosine[...] * is_key + (1.0 - is_key), sine[...] * is_key
        ).astype(jnp.bfloat16)
        pl.semaphore_wait(barrier, 10)
        started(pair_1, pair_2, pair_3, pair_near[0], pair_core[0], wo_y, wo_c)
        loads[2].wait()

        def flip_cot(a, carry):
            turned[:, rows_of(a)] = cot_rows[rows_of(a), :].T
            return carry

        lax.fori_loop(0, 4, flip_cot, 0)
        own_blocks[0].start()
        loads[1].wait()
        rows = matmul(normed[...], w_query[...])
        for h in range(3):
            query[h] = turn(
                rows[:, h * HD : (h + 1) * HD] + bq_ref[h : h + 1, :], cosine[...], sine[...]
            ).astype(jnp.bfloat16)
        own_blocks[0].wait()
        begin_spread(0)
        w_turned[...] = w_query[...].T
        turned_copy = started(local(w_turned, wq_turned_hbm))
        for copy, i in ((pair_1, 2), (pair_2, 1), (pair_3, 3)):
            copy.wait_recv()
            started(pair_near[i], pair_core[i])

        def flip(a, carry):
            turned[:, rows_of(a)] = normed[rows_of(a), :].T
            return carry

        lax.fori_loop(0, 4, flip, 0)
        for p in range(4):
            own_a[N1, p * block : (p + 1) * block, :] = turned[row_block(0, p // 2, p % 2), :]
        for i in (0, 2, 1, 3):
            pair_near[i].wait_recv()
            pair_core[4 + i].start()
        x_copy(0, 0).start()
        n1_keep.start()
        for copy in pair_core:
            copy.wait_recv()
        turned_copy.wait()

    pl.run_scoped(
        opening,
        pltpu.VMEM((TOK, width), jnp.bfloat16),
        pltpu.VMEM((TOK, width), jnp.bfloat16),
        pltpu.VMEM((TOK, width), jnp.bfloat16),
        pltpu.VMEM((width, 3 * HD), jnp.bfloat16),
        pltpu.VMEM((width, HD), jnp.bfloat16),
        pltpu.VMEM((3 * HD, width), jnp.bfloat16),
    )

    def of_first(t):
        t = t - t // 16
        late = t // 8
        device = t * (1 - late) + (15 - t) * late
        return device, late * (TOK - HALF)

    def same_document(device):
        ids = [docs_ref[pl.ds(4 * at + 1, 1), :] for at in (device, me)]
        return jnp.concatenate([ids[0], ids[0]], 1) == jnp.concatenate([ids[1], ids[1]], 1)

    def slot_of(device):
        return (
            4 * ((device % 2 + b0) % 2)
            + 2 * (((device // 2) % 2 + b1) % 2)
            + (device // 4 + b2) % 2
        )

    def places_of(step, wide):
        if wide:
            return [(slot_of(step), pl.ds(HALF, TOK - 2 * HALF))]
        places = []
        for block in (2 * step, 2 * step + 1):
            device, offset = of_first(block)
            places.append((slot_of(device), pl.ds(pl.multiple_of(offset, HALF), HALF)))
        return places

    def keys_of(which, step, wide):
        parts = [pair[which, slot, rows, :] for slot, rows in places_of(step, wide)]
        return parts[0] if wide else jnp.concatenate(parts, 0)

    def seen(begin, count, blocks, wide):
        shape = (3 * count, 2 * HALF)
        row = lax.broadcasted_iota(jnp.int32, shape, 0) & (count - 1)
        if not wide:
            row = row + blocks % 2 * HALF
        return row >= lax.broadcasted_iota(jnp.int32, shape, 1)

    def regions():
        return (
            (0, HALF, me, False, me // 2),
            (TOK - HALF, HALF, 15 - me, False, (15 - me) // 2),
            (HALF, TOK - 2 * HALF, me, True, me),
        )

    def attend_region(begin, count, blocks, wide, steps):
        rows = 3 * count
        q_rows = region_rows(query, begin, count)

        def score(step):
            scores = contract_cols(q_rows, keys_of(0, step, wide))
            return jnp.where(same_document(step), scores, MASKED) if wide else scores

        def add(step, carry, scores):
            total, accum = carry
            weights = jnp.exp2(scores * factor - peak)
            return total + weights, accum + matmul(
                weights.astype(jnp.bfloat16), keys_of(1, step, wide)
            )

        last = jnp.where(
            seen(begin, count, blocks, wide),
            contract_cols(q_rows, keys_of(0, steps, wide)),
            MASKED,
        )
        peak = lax.fori_loop(0, steps, lambda t, top: jnp.maximum(top, score(t)), last)
        peak = jnp.max(peak, axis=1, keepdims=True) * factor
        carry = add(
            steps,
            (jnp.zeros((rows, 2 * HALF), jnp.float32), jnp.zeros((rows, HD), jnp.float32)),
            last,
        )
        total, accum = lax.fori_loop(0, steps, lambda t, held: add(t, held, score(t)), carry)
        total = jnp.sum(total, axis=1, keepdims=True)
        result = accum / total
        logs = jnp.broadcast_to(peak + jnp.log2(total), (rows, HD))
        for h in range(3):
            part = slice(h * count, (h + 1) * count)
            attn_all[0, begin : begin + count, h * HD : (h + 1) * HD] = result[part].astype(
                jnp.bfloat16
            )
            full[h, begin : begin + count, :] = result[part]
            log_total[h, begin : begin + count, :] = logs[part]

    def front(weights, ring, wo, x_rows, cot_turned):
        def fetch(t, slot, rows):
            return [
                pltpu.make_async_copy(
                    source.at[pl.ds(t * UNITS, rows)],
                    weights.at[slot, k, pl.ds(0, rows)],
                    weight_sem.at[slot, k],
                )
                for k, source in enumerate((wg_hbm, wu_hbm, wd_hbm))
            ]

        loads = [
            local(wo_hbm, wo.at[0]),
            local(x_hbm, x_rows),
            local(wo_all.at[2], wo.at[2]),
            local(wo_all.at[1], wo.at[1]),
            local(wo_all.at[3], wo.at[3]),
            local(all_hbm.at[0, me], cot_turned),
        ]
        wo_c.wait_recv()
        started(*loads[:3], loads[5])
        started(*fetch(0, 0, UNITS))
        attend_region(*regions()[0])
        attend_region(*regions()[1])
        started(*attn_y[:2], *attn_c[:2])
        n1_keep.wait()
        started(*n1_x)
        arrive(0, 1)
        arrive_inner(0, 2)
        attend_region(*regions()[2])
        started(attn_y[2], attn_c[2])
        wo_y.wait_recv()
        wo_cy.start()
        loads[3].start()
        pass_y(0, 0)
        for load in loads[:3]:
            load.wait()
        for copy in (pair_1, pair_2, pair_3, *pair_near, *pair_core):
            copy.wait_send()
        def add_part(p, first=False):
            def body(n, carry):
                cols = pl.ds(pl.multiple_of(n * 512, 512), 512)
                held = x_rows[:, cols].astype(jnp.float32) if first else middle[:, cols]
                middle[:, cols] = held + matmul(attn_all[p], wo[p, :, cols])
                return carry

            lax.fori_loop(0, width // 512, body, 0)

        add_part(0, True)
        for copy in attn_c:
            copy.wait_recv()
        add_part(2)
        for copy, forward_copy in zip(attn_y, attn_cy):
            copy.wait_recv()
            forward_copy.start()
        loads[3].wait()
        wo_cy.wait_recv()
        loads[4].start()
        add_part(1)
        for copy in attn_cy:
            copy.wait_recv()
        loads[4].wait()
        add_part(3)

        def norm(a, carry):
            rows = middle[rows_of(a), :]
            turned[:, rows_of(a)] = (rows * norm_scale(rows) * gains[1:2, :]).astype(jnp.bfloat16).T
            return carry

        lax.fori_loop(0, 4, norm, 0)
        begin_spread(1)
        x_copy(1, 0).start()
        own_blocks[1].start()
        loads[5].wait()
        acc[...] = jnp.zeros_like(acc)

        def keep_tile(t):
            return pltpu.make_async_copy(ring.at[t % 2], own_hbm.at[t], weight_sem.at[2, t % 2])

        def tile(t, carry):
            slot = t % 2

            @pl.when(t < tiles - 1)
            def _():
                for copy in fetch(t, slot, UNITS):
                    copy.wait()

            @pl.when(t == tiles - 1)
            def _():
                for copy in fetch(t, slot, rest):
                    copy.wait()

            @pl.when(t + 1 < tiles - 1)
            def _():
                started(*fetch(t + 1, 1 - slot, UNITS))

            @pl.when(t + 1 == tiles - 1)
            def _():
                weights[1 - slot, :, rest:, :] = jnp.zeros(
                    (3, UNITS - rest, width), weights.dtype
                )
                started(*fetch(t + 1, 1 - slot, rest))

            for part in (slice(0, TOK // 2), slice(TOK // 2, TOK)):
                gate = matmul(weights[slot, 0], turned[:, part])
                up_part = matmul(weights[slot, 1], turned[:, part])
                grad_hidden = matmul(weights[slot, 2], cot_turned[:, part])
                sigma = jax.nn.sigmoid(gate)
                swish = gate * sigma
                ring[slot, part, :UNITS] = (swish * up_part).astype(jnp.bfloat16).T
                ring[slot, part, UNITS : 2 * UNITS] = (
                    (grad_hidden * up_part * sigma * (1.0 + gate * (1.0 - sigma)))
                    .astype(jnp.bfloat16)
                    .T
                )
                ring[slot, part, 2 * UNITS :] = (grad_hidden * swish).astype(jnp.bfloat16).T
            for part in (slice(0, TOK // 2), slice(TOK // 2, TOK)):
                acc[part, :] += matmul(
                    ring[slot, part, UNITS:], weights[slot, 0:2].reshape(2 * UNITS, width)
                )

            @pl.when(t > 0)
            def _():
                keep_tile(t - 1).wait()

            @pl.when(t == 3)
            def _():
                arrive_outer(0, 2)
                arrive_inner(0, 3)
                pass_core(0, 0)
                pass_y(0, 1)

            @pl.when(t == 6)
            def _():
                pass_y(1, 0)

            @pl.when(t == 7)
            def _():
                arrive(1, 1)
                arrive_inner(1, 2)

            keep_tile(t).start()
            return carry

        lax.fori_loop(0, tiles, tile, 0)
        keep_tile(tiles - 1).wait()
        own_blocks[1].wait()

    pl.run_scoped(
        front,
        pltpu.VMEM((2, 3, UNITS, width), jnp.bfloat16),
        pltpu.VMEM((2, TOK, 3 * UNITS), jnp.bfloat16),
        pltpu.VMEM((4, width // 4, width), jnp.bfloat16),
        pltpu.VMEM((TOK, width), jnp.bfloat16),
        pltpu.VMEM((width, TOK), jnp.bfloat16),
    )

    def reduce_copies():
        return (
            remote(rel.at[rows_of(lane_c)], core_in.at[0], c_to),
            remote(rel.at[rows_of(lane_cy)], core_in.at[1], c_to),
            remote(lane_send, lane_in, y_to),
        )

    def reduce_start(copies):
        rel[...] = acc[...].astype(jnp.bfloat16)
        started(*copies[:2])

    def reduce_middle(copies):
        copies[0].wait()
        copies[1].wait()
        lane_send[...] = (
            acc[rows_of(lane_y), :] + core_in[1].astype(jnp.float32)
        ).astype(jnp.bfloat16)
        copies[2].start()

    def reduce_end(copies, held):
        copies[2].wait()
        return held + core_in[0].astype(jnp.float32) + lane_in[...].astype(jnp.float32)

    def spread_copies(full):
        mine, theirs = full.at[rows_of(lane)], full.at[rows_of(lane_y)]
        return [
            remote(mine, mine, y_to),
            remote(mine, mine, c_to),
            remote(theirs, theirs, c_to),
        ]

    def spread_end(copies):
        copies[0].wait_recv()
        copies[2].start()
        copies[0].wait_send()
        copies[1].wait()
        copies[2].wait()

    near_base = used["remote"]
    used["remote"] += 4

    def near_copy(r):
        index = near_base + r
        return pltpu.make_async_remote_copy(
            src_ref=sent_tile.at[rows_of_block(peers[r] - 4 * b2)],
            dst_ref=via_hbm if r == 3 else near_hbm.at[r],
            send_sem=send_sem.at[index], recv_sem=recv_sem.at[index],
            device_id={"cp": peers[1 if r == 3 else r]}, device_id_type=pl.DeviceIdType.MESH,
        )

    via_copy = remote(via_hbm, near_hbm.at[3], z1_to)

    final_base = used["local"]
    used["local"] += 24

    SMALL = {"out": (0, 384, GB), "query": (384, 384, N1), "pair": (768, 128, N1)}
    small_base = used["remote"]
    used["remote"] += 6
    pair_hops = [
        remote(
            small_s.at[pl.ds(p * block, block), pl.ds(768, HD)], pair_terms.at[p - 1], to
        )
        for p, to in ((1, z2_to), (2, z1_to), (3, z3_to))
    ]

    def small_copy(name, second):
        begin, wide, _ = SMALL[name]
        index = small_base + 2 * list(SMALL).index(name) + second
        cols = pl.ds(begin, wide)
        if second:
            src, dst, to = small_s2.at[:, cols], small_in2.at[:, cols], z2_to
        else:
            src, dst, to = small_s.at[pl.ds(half, half), cols], small_in.at[:, cols], z1_to
        return pltpu.make_async_remote_copy(
            src_ref=src, dst_ref=dst, send_sem=send_sem.at[index], recv_sem=recv_sem.at[index],
            device_id=to, device_id_type=pl.DeviceIdType.MESH,
        )

    def small_first(name, b_own, b_far):
        begin, wide, index = SMALL[name]
        cols = slice(begin, begin + wide)
        small_s[half:, cols] = (
            matmul(own_a[index, half:, :], b_own) + matmul(far_a[index, 1], b_far)
        ).astype(jnp.bfloat16)
        if name != "pair":
            small_copy(name, 0).start()
        small_s[:half, cols] = (
            matmul(own_a[index, :half, :], b_own) + matmul(far_a[index, 0], b_far)
        ).astype(jnp.bfloat16)
        if name == "pair":
            started(*pair_hops)

    def small_second(name):
        begin, wide, _ = SMALL[name]
        cols = slice(begin, begin + wide)
        small_copy(name, 0).wait_recv()
        small_s2[:, cols] = (
            small_s[block:half, cols].astype(jnp.float32)
            + small_in[block:, cols].astype(jnp.float32)
        ).astype(jnp.bfloat16)
        small_copy(name, 1).start()
        small_copy(name, 0).wait_send()

    def small_third(name, out_ref):
        begin, wide, _ = SMALL[name]
        cols = slice(begin, begin + wide)
        small_copy(name, 1).wait()
        out_ref[...] = (
            small_s[:block, cols].astype(jnp.float32)
            + small_in[:block, cols].astype(jnp.float32)
            + small_in2[:, cols].astype(jnp.float32)
        )

    query_x = remote(grad_query, query_far, x_to)
    pair_x = remote(grad_pair, pair_far, x_to)
    pair_y = remote(grad_pair, pair_hbm.at[1], y_to)
    pair_c = remote(grad_pair, pair_hbm.at[2], c_to)
    pair_cy = remote(pair_hbm.at[1], pair_hbm.at[3], c_to)
    pair_own = local(grad_pair, pair_hbm.at[0])
    here = output_out.at[rows_of(lane)]
    there = output_out.at[rows_of(lane_y)]
    out_spread = [
        remote(lane_send, here, y_to),
        remote(lane_send, here, c_to),
        remote(there, there, c_to),
    ]
    out_own = local(lane_send, here)

    query_reduction = reduce_copies()

    def rest_of(grads, wo_own, second, cots, weights, w_last, ring, total_tile):
        mine = [b0 + 2 * b1 + 4 * i for i in range(2)]
        weight_loads = [
            local(
                source.at[pl.ds(pl.multiple_of(tile * UNITS, UNITS), UNITS)],
                weights.at[k, pl.ds(i * UNITS, UNITS)],
            )
            for i, tile in enumerate(mine)
            for k, source in enumerate((wg_hbm, wu_hbm, wd_hbm))
        ]
        wo_load = local(wo_hbm, wo_own)
        own_tiles = [
            local(
                own_hbm.at[tile, :, pl.ds(k * UNITS, UNITS)],
                ring.at[:, pl.ds((2 * k + i) * UNITS, UNITS)],
            )
            for i, tile in enumerate(mine)
            for k in range(3)
        ]
        block_base = used["local"]
        used["local"] += 3
        own_rows = pl.ds(pl.multiple_of(b2 * wide_half, wide_half), wide_half)
        order = ((0, 0), (1, 0), (0, 1), (1, 1), (2, 0), (3, 0), (2, 1), (3, 1))

        def load_second(j, side):
            slot = order.index((j, side)) % 2
            return pltpu.make_async_copy(
                all_hbm.at[1, block_of(j, side)], second.at[slot], local_sem.at[block_base + slot]
            )

        def load_cots(j, side):
            return pltpu.make_async_copy(
                all_hbm.at[0, block_of(j, side)], cots, local_sem.at[block_base + 2]
            )

        def prefetch(j, side):
            if side:
                d_copy(0, j, 1 - core).wait_recv()
                d_copy(1, j, 1 - core).wait_recv()
            elif j:
                c_copy(0, j, 1 - core).wait_recv()
                c_copy(1, j, 1 - core).wait_recv()
            load_second(j, side).start()

        def product(q):
            slot = q % 2
            pltpu.make_async_copy(
                all_hbm.at[1, 0], second.at[slot], local_sem.at[block_base + slot]
            ).wait()
            cots_load = pltpu.make_async_copy(
                all_hbm.at[0, 0], cots, local_sem.at[block_base + 2]
            )

            @pl.when(q == 0)
            def _():
                for load in own_tiles:
                    load.wait()
                cots_load.wait()

            @pl.when(q > 0)
            def _():
                for part in (slice(0, TOK // 2), slice(TOK // 2, TOK)):
                    gate = matmul(weights[0], second[slot, :, part])
                    up_part = matmul(weights[1], second[slot, :, part])
                    sigma = jax.nn.sigmoid(gate)
                    swish = gate * sigma
                    ring[part, : 2 * UNITS] = (swish * up_part).astype(jnp.bfloat16).T
                    if part.start == 0:
                        cots_load.wait()
                    grad_hidden = matmul(weights[2], cots[:, part])
                    ring[part, 2 * UNITS : 4 * UNITS] = (
                        (grad_hidden * up_part * sigma * (1.0 + gate * (1.0 - sigma)))
                        .astype(jnp.bfloat16)
                        .T
                    )
                    ring[part, 4 * UNITS :] = (grad_hidden * swish).astype(jnp.bfloat16).T

            for n in range(3):
                cols = slice(2 * n * UNITS, 2 * (n + 1) * UNITS)
                rows = second[slot, own_rows, :] if n else cots[own_rows, :]
                total_tile[:, cols] += matmul(rows, ring[:, cols])

        far_loads = [
            local(
                all_hbm.at[k, block_of(0, side), row_block(0, p // 2, p % 2)],
                (
                    far_a.at[k, p // 2, pl.ds((p % 2) * block, block)]
                    if side
                    else own_a.at[k, pl.ds(p * block, block)]
                ),
            )
            for k in range(2)
            for side in range(2)
            for p in range(4)
        ]
        last_loads = [local(own_hbm.at[tiles - 1], sent_tile.at[:TOK, : 3 * UNITS])]
        last_weights = [
            local(source.at[pl.ds((tiles - 1) * UNITS, rest)], w_last.at[k])
            for k, source in enumerate((wg_hbm, wu_hbm, wd_hbm))
        ]

        def last_far():
            slot = order.index((0, 1)) % 2
            for load in last_weights:
                load.wait()
            padding = jnp.zeros((TOK, UNITS - rest), jnp.bfloat16)
            gate = matmul(w_last[0], second[slot])
            up_part = matmul(w_last[1], second[slot])
            grad_hidden = matmul(w_last[2], cots[...])
            sigma = jax.nn.sigmoid(gate)
            swish = gate * sigma
            parts = (
                swish * up_part,
                grad_hidden * up_part * sigma * (1.0 + gate * (1.0 - sigma)),
                grad_hidden * swish,
            )
            for k, part in enumerate(parts):
                begin = (3 + k) * UNITS
                sent_tile[:TOK, begin : begin + UNITS] = jnp.concatenate(
                    [part.astype(jnp.bfloat16).T, padding], 1
                )

        def last_first():
            for load in (*far_loads, *last_loads):
                load.wait()

            def body(n, h):
                cols = pl.ds(pl.multiple_of(n * UNITS, UNITS), UNITS)
                far_cols = pl.ds(pl.multiple_of((3 + n) * UNITS, UNITS), UNITS)
                index = (n + 1) // 2
                return cols, matmul(
                    own_a[index, h * half : (h + 1) * half, :], sent_tile[:TOK, cols]
                ) + matmul(far_a[index, h], sent_tile[:TOK, far_cols])

            def sent(n, carry):
                cols, value = body(n, 1)
                part_s[:, cols] = value.astype(jnp.bfloat16)
                return carry

            def kept(n, carry):
                cols, value = body(n, 0)
                part_k[:, cols] = value.astype(jnp.bfloat16)
                return carry

            lax.fori_loop(0, 3, sent, 0)
            z1_tile.start()
            lax.fori_loop(0, 3, kept, 0)

        reduction = reduce_copies()
        wq_load = local(wq_turned_hbm, wo_own)
        spread = spread_copies(grad_full)
        cot_load = local(cot_hbm, rel)
        kv_c = remote(kv_send.at[pl.ds(0, 8)], kv_in.at[pl.ds(0, 8)], c_to)
        kv_x = remote(kv_send.at[pl.ds(0, 4)], kv_in.at[pl.ds(8, 4)], x_to)
        kv_1 = remote(kv_send.at[pl.ds(4, 2)], kv_in.at[pl.ds(12, 2)], z1_to)
        kv_2 = remote(kv_send.at[pl.ds(6, 1)], kv_in.at[pl.ds(14, 1)], z2_to)
        keep_by = is_key * scale + (1.0 - is_key)
        send_by = (1.0 - is_key) * scale + is_key

        def middle_back(a, total):
            grad = grad_full[rows_of(a), :].astype(jnp.float32)
            rows = middle[rows_of(a), :]
            factor2 = norm_scale(rows)
            weighted = grad * gains[1:2, :]
            result = (
                rel[rows_of(a), :].astype(jnp.float32)
                + factor2 * weighted
                - rows * factor2**3 * jnp.mean(weighted * rows, axis=-1, keepdims=True)
            )
            acc[rows_of(a), :] = result
            turned[:, rows_of(a)] = result.astype(jnp.bfloat16).T
            return total + jnp.sum(grad * rows * factor2, axis=0, keepdims=True)

        def region(begin, count, blocks, wide, steps):
            heads = query.shape[0]
            rows = heads * count
            q_rows = region_rows(query, begin, count)
            grad_rows = jnp.concatenate(
                [attn_all[1, begin : begin + count, h * HD : (h + 1) * HD] for h in range(heads)], 0
            )
            logs = region_rows(log_total, begin, count)[:, :1]
            delta = jnp.sum(
                grad_rows.astype(jnp.float32) * region_rows(full, begin, count),
                axis=1,
                keepdims=True,
            )

            def add(step, carry, last=False):
                keys, values = keys_of(0, step, wide), keys_of(1, step, wide)
                probs = jnp.exp2(contract_cols(q_rows, keys) * factor - logs)
                if last:
                    probs = jnp.where(seen(begin, count, blocks, wide), probs, 0.0)
                elif wide:
                    probs = jnp.where(same_document(step), probs, 0.0)
                grad_scores = (probs * (contract_cols(grad_rows, values) - delta)).astype(
                    jnp.bfloat16
                )
                key_part = contract_rows(grad_scores, q_rows)
                value_part = contract_rows(probs.astype(jnp.bfloat16), grad_rows)
                for i, (slot, place) in enumerate(places_of(step, wide)):
                    part = slice(None) if wide else slice(i * HALF, (i + 1) * HALF)
                    grads[0, slot, place, :] += key_part[part]
                    grads[1, slot, place, :] += value_part[part]
                return carry + matmul(grad_scores, keys)

            total = add(steps, jnp.zeros((rows, HD), jnp.float32), True)
            total = lax.fori_loop(0, steps, add, total) * scale
            cosines, sines = cosine[begin : begin + count, :], sine[begin : begin + count, :]
            for h in range(heads):
                part = total[h * count : (h + 1) * count]
                grad_query[begin : begin + count, h * HD : (h + 1) * HD] = (
                    turn_back(part, cosines, sines)
                ).astype(jnp.bfloat16)

        def to_core(s, carry):
            kv_send[s] = (grads[1 - core, s] * send_by).astype(jnp.bfloat16)
            return carry

        def from_core(s, carry):
            grads[core, s] = grads[core, s] * keep_by + kv_in[s].astype(jnp.float32)
            return carry

        def pass_on(copy, first, count):
            def cast(s, carry):
                kv_send[first - 8 + s] = grads[core, count + s].astype(jnp.bfloat16)
                return carry

            lax.fori_loop(0, count, cast, 0)
            copy.start()

        def take(copy, first, count):
            copy.wait()

            def add(s, carry):
                grads[core, s] += kv_in[first + s].astype(jnp.float32)
                return carry

            lax.fori_loop(0, count, add, 0)

        def stage_0():
            reduce_start(reduction)
            total_tile[...] = jnp.zeros_like(total_tile)
            reduce_middle(reduction)
            prefetch(1, 0)
            started(*weight_loads, wo_load)
            pass_core(1, 0)

        def stage_1():
            started(*last_weights, attn_x)
            for load in weight_loads:
                load.wait()

        def stage_2():
            arrive_inner(1, 3)
            prefetch(0, 1)
            grads[...] = jnp.zeros_like(grads)
            grad_full[rows_of(lane), :] = reduce_end(reduction, acc[rows_of(lane), :]).astype(
                jnp.bfloat16
            )
            started(*spread[:2])
            cot_load.start()
            pass_core(0, 1)

        def stage_3():
            last_far()
            spread_end(spread)
            pass_y(1, 1)
            cot_load.wait()
            wo_load.wait()
            z_copy(1, 0).wait_send()
            x_copy(1, 0).wait_send()

            @when(inner)
            def _():
                z_copy(1, 1).wait_send()

            sums[...] = jnp.zeros_like(sums)
            gain2_part = lax.fori_loop(0, 4, middle_back, jnp.zeros((1, width), jnp.float32))
            for i in range(width // HD):
                sums[12 + i : 13 + i, :] = gain2_part[:, i * HD : (i + 1) * HD]
            middle_copy.start()
            for copy in attn_cy:
                copy.wait_send()
            attn_all[1] = matmul(wo_own[...], turned[...]).astype(jnp.bfloat16).T
            wq_load.start()
            arrive_outer(1, 2)
            arrive_outer(0, 3)
            region(*regions()[0])
            pass_y(0, 2)
            region(*regions()[1])
            pass_core(1, 1)
            region(*regions()[2])
            lax.fori_loop(0, 8, to_core, 0)
            kv_c.start()
            prefetch(1, 1)
            arrive_outer(1, 3)
            prefetch(2, 0)

        def stage_4():
            started(*far_loads, *last_loads)
            kv_c.wait()
            lax.fori_loop(0, 8, from_core, 0)
            pass_on(kv_x, 8, 4)
            pass_y(1, 2)
            pass_y(0, 3)
            pass_core(0, 2)
            wq_load.wait()
            middle_copy.wait()
            acc[...] = matmul(grad_query[...], wo_own[...])
            reduce_start(query_reduction)

        def stage_5():
            prefetch(3, 0)
            last_first()
            started(*branch_x)
            pass_core(1, 2)

        def stage_6():
            prefetch(2, 1)
            take(kv_x, 8, 4)
            pass_on(kv_1, 12, 2)
            started(query_x)
            pass_y(1, 3)
            pass_core(0, 3)
            for p in range(4):
                own_a[GB, p * block : (p + 1) * block, :] = turned[
                    row_block(0, p // 2, p % 2), :
                ]
            for copy in n1_x:
                copy.wait()
            n1_forward.start()
            z1_tile.wait_recv()
            part_s2[...] = (
                part_k[block:, :].astype(jnp.float32) + near1[block:, :].astype(jnp.float32)
            ).astype(jnp.bfloat16)
            z2_tile.start()

        def stage_7():
            for copy in branch_x:
                copy.wait()
            branch_forward.start()
            reduce_middle(query_reduction)
            held_query[...] = acc[rows_of(lane), :].astype(jnp.bfloat16)
            take(kv_1, 12, 2)
            pass_on(kv_2, 14, 1)
            pass_core(1, 3)
            branch_forward.wait()
            attn_x.wait()
            small_first("out", attn_all[0], attn_far[...])
            n1_forward.wait()
            prefetch(3, 1)

        stages = (stage_0, stage_1, stage_2, stage_3, stage_4, stage_5, stage_6, stage_7)

        def body(q, carry):
            for at, (stage, of) in enumerate(zip(stages, order)):

                @pl.when(q == at)
                def _(stage=stage, of=of):
                    stage()
                    if of != order[0]:
                        load_cots(*of).start()

            product(q)
            return carry

        prefetch(0, 0)
        load_cots(0, 0).start()
        started(*own_tiles)
        lax.fori_loop(0, len(order), body, 0)
        sent_tile[...] = total_tile[...].astype(jnp.bfloat16)
        near_copy(2).start()
        query_x.wait()
        small_first("query", grad_query[...], query_far[...])
        kv_2.wait()
        f_cos = cosine[...] * is_key + (1.0 - is_key)
        f_sin = sine[...] * is_key
        total = grads[core, 0] + kv_in[14].astype(jnp.float32)
        grad_pair[...] = turn_back(total, f_cos, f_sin).astype(jnp.bfloat16)
        started(pair_x, pair_y, pair_c, pair_own)
        near_copy(3).start()

    n1_forward = forward(N1)
    branch_x = share(turned, GB)
    branch_forward = forward(GB)
    middle_copy = local(acc, middle_hbm)
    pl.run_scoped(
        rest_of,
        pltpu.VMEM((2, 8, TOK, HD), jnp.float32),
        pltpu.VMEM((width // 4, width), jnp.bfloat16),
        pltpu.VMEM((2, width, TOK), jnp.bfloat16),
        pltpu.VMEM((width, TOK), jnp.bfloat16),
        pltpu.VMEM((3, 2 * UNITS, width), jnp.bfloat16),
        pltpu.VMEM((3, rest, width), jnp.bfloat16),
        pltpu.VMEM((TOK, 6 * UNITS), jnp.bfloat16),
        pltpu.VMEM((width // 2, 6 * UNITS), jnp.float32),
    )

    def closing(
        x_rows, pres, w_pres, w_down, hidden, near_low, final, held
    ):
        gathered_pair = []
        loads = [local(x_hbm, x_rows)]
        pairs_load = [
            local(pair_hbm.at[p], pres.at[:, pl.ds(p * HD, HD)]) for p in range(4)
        ]
        for p, far in enumerate(TP_ORDER):
            head = (high + far // 2) % 2
            lanes = pl.ds(pl.multiple_of(head * HD, HD), HD)
            index = used["local"]
            used["local"] += 1
            key_load, value_load = [
                pltpu.make_async_copy(
                    source.at[:, lanes],
                    w_pres.at[:, pl.ds(p * HD, HD)],
                    local_sem.at[index],
                )
                for source in (wk_hbm, wv_hbm)
            ]
            kind = (core + far % 2) % 2

            @pl.when(kind == 0)
            def _(key_load=key_load):
                key_load.start()

            @pl.when(kind == 1)
            def _(value_load=value_load):
                value_load.start()

            gathered_pair.append(key_load)
        middle_load = local(middle_hbm, middle)
        wide_unit = 2 * UNITS
        steps = [
            (t, min(wide_unit, units - t * wide_unit)) for t in range(pl.cdiv(units, wide_unit))
        ]

        def fetch(t, rows):
            slot = t % 2
            copies = [
                pltpu.make_async_copy(
                    wd_hbm.at[pl.ds(t * wide_unit, rows)],
                    w_down.at[slot, pl.ds(0, rows)],
                    weight_sem.at[slot, 0],
                )
            ]
            for i in range(pl.cdiv(rows, UNITS)):
                copies.append(
                    pltpu.make_async_copy(
                        own_hbm.at[2 * t + i, :, pl.ds(0, UNITS)],
                        hidden.at[slot, :, pl.ds(i * UNITS, UNITS)],
                        weight_sem.at[slot, 1 + i],
                    )
                )
            return copies

        started(*fetch(*steps[0]), *loads)
        for t, rows in steps:
            slot = t % 2
            if t + 1 < len(steps):
                more = steps[t + 1][1]
                if more < wide_unit:
                    end = pl.cdiv(more, UNITS) * UNITS
                    w_down[1 - slot, more:end, :] = jnp.zeros((end - more, width), w_down.dtype)
                started(*fetch(*steps[t + 1]))
            for copy in fetch(t, rows):
                copy.wait()
            depth = pl.cdiv(rows, UNITS) * UNITS

            for part in (slice(0, TOK // 2), slice(TOK // 2, TOK)):
                value = matmul(hidden[slot, part, :depth], w_down[slot, :depth, :])
                if t == 0:
                    acc[part, :] = value
                else:
                    acc[part, :] += value
            if t == 0:
                pair_y.wait_recv()
                pair_cy.start()
                pair_c.wait_recv()
                pair_own.wait()
            if t == 1:
                pair_cy.wait_recv()
                started(*pairs_load)
                pair_x.wait()
                small_first("pair", grad_pair[...], pair_far[...])
                for load in (*pairs_load, *gathered_pair):
                    load.wait()
                grad_full[rows_of(lane), :] = (
                    reduce_end(query_reduction, held_query[...].astype(jnp.float32))
                    + contract_cols(pres[rows_of(lane), :], w_pres[...])
                ).astype(jnp.bfloat16)
                started(*normed_spread[:2])
        acc[rows_of(lane), :] += middle[rows_of(lane), :]
        middle_load.start()
        reduce_start(out_reduction)
        for copy in out_reduction[:2]:
            copy.wait()
        out_core_load.start()
        out_core_load.wait()
        lane_send[...] = (
            acc[rows_of(lane_y), :] + core_in[1].astype(jnp.float32)
        ).astype(jnp.bfloat16)
        out_reduction[2].start()
        held[...] = acc[rows_of(lane), :] + core_in[0].astype(jnp.float32)
        near_copy(3).wait_recv()
        via_copy.start()
        near_copy(1).start()
        spread_end(normed_spread)
        for load in (*loads, middle_load):
            load.wait()

        def last(a, total):
            grad = grad_full[rows_of(a), :].astype(jnp.float32)
            rows = x_rows[rows_of(a), :].astype(jnp.float32)
            scale1 = norm_scale(rows)
            weighted = grad * gains[0:1, :]
            rel[rows_of(a), :] = (
                middle[rows_of(a), :]
                + scale1 * weighted
                - rows * scale1**3 * jnp.mean(weighted * rows, axis=-1, keepdims=True)
            ).astype(jnp.bfloat16)
            return total + jnp.sum(grad * rows * scale1, axis=0, keepdims=True)

        gain1_part = lax.fori_loop(0, 4, last, jnp.zeros((1, width), jnp.float32))
        input_copy = started(local(rel, input_out))
        for i in range(width // HD):
            sums[i : i + 1, :] = gain1_part[:, i * HD : (i + 1) * HD]
        bias_part = jnp.sum(grad_query[...].astype(jnp.float32), axis=0, keepdims=True)
        for h in range(3):
            sums[24 + h : 25 + h, :] = bias_part[:, h * HD : (h + 1) * HD]
        for p, far in enumerate(TP_ORDER):
            row = 27 + 2 * ((core + far % 2) % 2) + (high + far // 2) % 2
            lanes = slice(p * HD, (p + 1) * HD)
            sums[pl.ds(row, 1), :] = jnp.sum(
                pres[:, lanes].astype(jnp.float32), axis=0, keepdims=True
            )
        started(*sums_copies)
        small_second("out")
        small_second("query")
        out_reduction[2].wait()
        out_lane_load.start()
        out_lane_load.wait()
        lane_send[...] = (held[...] + lane_in[...].astype(jnp.float32)).astype(jnp.bfloat16)
        started(out_spread[0], out_spread[1], out_own)
        for copy in pair_hops:
            copy.wait()
        w_pair_grad[...] = small_s[:block, 768 : 768 + HD].astype(jnp.float32) + sum(
            pair_terms[i].astype(jnp.float32) for i in range(3)
        )
        started(*w_pair_copies)

        mine_rows = rows_of_block(me - 4 * b2)

        def tile_copies(r):
            tile = peers[r] - 4 * b2
            return [
                pltpu.make_async_copy(
                    (near_low.at[r - 1] if r else sent_tile.at[mine_rows]).at[
                        :, pl.ds((2 * k + i) * UNITS, UNITS)
                    ],
                    tiles_out.at[
                        k, :, pl.ds(pl.multiple_of((tile + 4 * i) * UNITS, UNITS), UNITS)
                    ],
                    local_sem.at[final_base + 6 * r + 2 * k + i],
                )
                for k in range(3)
                for i in range(2)
            ]

        started(*tile_copies(0))
        near_loads = [None] + [local(near_hbm.at[r], near_low.at[r - 1]) for r in (1, 2, 3)]
        for r in (2, 1, 3):
            if r == 3:
                via_copy.wait_recv()
            else:
                near_copy(r).wait_recv()
            near_loads[r].start()
            near_loads[r].wait()
            started(*tile_copies(r))
        out_spread[0].wait_recv()
        out_spread[2].start()
        z2_tile.wait_recv()
        final[...] = (
            part_k[:block, :].astype(jnp.float32)
            + near1[:block, :].astype(jnp.float32)
            + near2[...].astype(jnp.float32)
        ).astype(jnp.bfloat16)
        last_copies = [
            local(
                final.at[:, pl.ds(k * UNITS, UNITS)],
                tiles_out.at[k, :, pl.ds((tiles - 1) * UNITS, UNITS)],
            )
            for k in range(3)
        ]
        started(*last_copies)
        small_third("out", wo_out)
        small_third("query", wq_out)
        input_copy.wait()
        for r in range(4):
            for copy in tile_copies(r):
                copy.wait()
        for copy in last_copies:
            copy.wait()

    out_reduction = (
        remote(rel.at[rows_of(lane_c)], out_core_hbm.at[0], c_to),
        remote(rel.at[rows_of(lane_cy)], out_core_hbm.at[1], c_to),
        remote(lane_send, out_lane_hbm, y_to),
    )
    out_core_load = local(out_core_hbm, core_in)
    out_lane_load = local(out_lane_hbm, lane_in)
    normed_spread = spread_copies(grad_full)
    sums_copies = [
        remote(sums, sums_in.at[r], {"cp": peers[r]}) for r in range(1, 8)
    ]
    w_pair_place = wkv_out.at[core, :, pl.ds(pl.multiple_of(high * HD, HD), HD)]
    w_pair_copies = [remote(w_pair_grad, w_pair_place, to) for to in (y_to, c_to, cy_to)]
    w_pair_copies.append(local(w_pair_grad, w_pair_place))
    pl.run_scoped(
        closing,
        pltpu.VMEM((TOK, width), jnp.bfloat16),
        pltpu.VMEM((TOK, 4 * HD), jnp.bfloat16),
        pltpu.VMEM((width, 4 * HD), jnp.bfloat16),
        pltpu.VMEM((2, 2 * UNITS, width), jnp.bfloat16),
        pltpu.VMEM((2, TOK, 2 * UNITS), jnp.bfloat16),
        pltpu.VMEM((3, block, 6 * UNITS), jnp.bfloat16),
        pltpu.VMEM((block, 3 * UNITS), jnp.bfloat16),
        pltpu.VMEM((quarter, width), jnp.float32),
    )
    for copy in sums_copies:
        copy.wait()
    sums_out[...] = sums[...] + sum(sums_in[r] for r in range(1, 8))
    for copy in w_pair_copies:
        copy.wait()
    z1_tile.wait_send()
    z2_tile.wait_send()
    for r in (1, 2, 3):
        near_copy(r).wait_send()
    via_copy.wait_send()
    z_copy(0, 0).wait_send()
    x_copy(0, 0).wait_send()

    @when(inner)
    def _():
        z_copy(0, 1).wait_send()
        for k in range(2):
            for m in (2, 3, 4):
                z_copy(k, m).wait_send()

    for k in range(2):
        for j in range(4):
            if j:
                c_copy(k, j).wait_send()
                x_copy(k, j).wait_send()
            if (k, j) not in WHOLE_HALVES:
                y_copy(k, j).wait_send()
            d_copy(k, j).wait_send()
    for copy in (
        *attn_y, *attn_c, pair_y, pair_c, pair_cy, out_spread[0], wo_y, wo_c, wo_cy,
    ):
        copy.wait_send()
    for copy in (out_spread[1], out_spread[2]):
        copy.wait()
    out_own.wait()
    assert used["remote"] <= REMOTE and used["local"] <= LOCAL, used


WHOLE_HALVES = ()
REMOTE = 134
LOCAL = 150


def whole_layer(
    docs, places, freq, gain1, gain2, b_query, b_key, b_value,
    x, cot, w_query, w_key, w_value, w_out, w_gate, w_up, w_down,
):
    tok_rows, width = x.shape
    units = w_gate.shape[0]
    tiles = pl.cdiv(units, UNITS)
    half, block, quarter = width // 4, width // 8, tok_rows // 4
    low, wide = jnp.bfloat16, jnp.float32
    shape = jax.ShapeDtypeStruct
    any_ = pl.BlockSpec(memory_space=pl.ANY)
    outs = (
        shape((3, block, tiles * UNITS), low),
        shape((block, 384), wide),
        shape((block, 384), wide),
        shape((2, block, 2 * HD), wide),
        shape((32, HD), wide),
        shape((tok_rows, width), low),
        shape((tok_rows, width), low),
        shape((tok_rows, width), wide),
        shape((4, tok_rows, HD), low),
        shape((tiles, tok_rows, 3 * UNITS), low),
        shape((4, block, 6 * UNITS), low),
        shape((4,) + w_out.shape, low),
        shape(w_query.shape[::-1], low),
        shape((2, 8, width, tok_rows), low),
        shape((width, tok_rows), low),
        shape((block, 6 * UNITS), low),
        shape((2, quarter, width), low),
        shape((quarter, width), low),
    )
    vmem = pltpu.VMEM
    scratch = [
        vmem((tok_rows, HD), wide),
        vmem((tok_rows, HD), wide),
        vmem((2, width), wide),
        vmem((block, HD), wide),
        vmem((3, tok_rows, HD), low),
        vmem((2, 8, tok_rows, HD), low),
        vmem((3, tok_rows, HD), wide),
        vmem((3, tok_rows, HD), wide),
        vmem((32, HD), wide),
        vmem((8, 32, HD), wide),
        vmem((4, tok_rows, 384), low),
        vmem((tok_rows, 384), low),
        vmem((tok_rows, 384), low),
        vmem((tok_rows, HD), low),
        vmem((tok_rows, width), wide),
        vmem((tok_rows, width), wide),
        vmem((width, tok_rows), low),
        vmem((4, width // 2, tok_rows), low),
        vmem((4, 2, half, tok_rows), low),
        vmem((half, 3 * UNITS), low),
        vmem((half, 3 * UNITS), low),
        vmem((half, 3 * UNITS), low),
        vmem((block, 3 * UNITS), low),
        vmem((block, 3 * UNITS), low),
        vmem((width // 2, 6 * UNITS), low),
        vmem((tok_rows, width), low),
        vmem((2, quarter, width), low),
        vmem((quarter, width), low),
        vmem((quarter, width), low),
        vmem((tok_rows, width), low),
        vmem((quarter, width), low),
        vmem((8, tok_rows, HD), low),
        vmem((15, tok_rows, HD), low),
        vmem((tok_rows, 384), low),
        vmem((tok_rows, HD), low),
        vmem((2 * half, 896), low),
        vmem((half, 896), low),
        vmem((block, 896), low),
        vmem((block, 896), low),
        vmem((3, block, HD), low),
        pltpu.SemaphoreType.DMA((REMOTE,)),
        pltpu.SemaphoreType.DMA((REMOTE,)),
        pltpu.SemaphoreType.DMA((LOCAL,)),
        pltpu.SemaphoreType.DMA((3, 3)),
    ]
    return pl.pallas_call(
        functools.partial(back_kernel, width, units),
        out_shape=outs,
        in_specs=[VMEM] * 8 + [any_] * 9,
        out_specs=(any_, VMEM, VMEM, any_, VMEM) + (any_,) * 13,
        scratch_shapes=scratch,
        compiler_params=pltpu.CompilerParams(
            vmem_limit_bytes=64 * 1024 * 1024, collective_id=0, has_side_effects=True
        ),
        cost_estimate=pl.CostEstimate(
            flops=20 * tok_rows * width * units, bytes_accessed=10 * width * units, transcendentals=0
        ),
    )(
        docs, places, freq, gain1, gain2, b_query, b_key, b_value,
        x, cot, w_query, w_key, w_value, w_out, w_gate, w_up, w_down,
    )


def on_device(
    layer_input,
    norm1_gain,
    w_query,
    b_query,
    w_key,
    b_key,
    w_value,
    b_value,
    w_out,
    norm2_gain,
    w_gate,
    w_up,
    w_down,
    doc_ids,
    positions,
    cotangent,
):
    tok_rows, width = layer_input.shape
    shards = lax.axis_size("cp")
    heads = w_query.shape[1] // HD
    kv_heads = w_key.shape[1] // HD
    me = lax.axis_index("cp")
    lane = lax.axis_index("tp")
    core = lane % 2
    kv_index = lane * heads // (H // kv_heads)
    is_key = core == 0

    if shards == 8 and tok_rows == TOK:
        half = HD // 2
        freq = ROPE_BASE ** (-(jnp.arange(half, dtype=jnp.float32) * 2.0 / HD))
        tiles, grad_w_out, grad_w_query, grad_w_pairs, sums, output, grad_input, *_ = whole_layer(
            doc_ids.reshape(-1, HD), positions.reshape(-1, HD),
            jnp.concatenate([freq, freq])[None],
            norm1_gain.reshape(-1, HD), norm2_gain.reshape(-1, HD),
            b_query.reshape(-1, HD), b_key.reshape(-1, HD), b_value.reshape(-1, HD),
            layer_input, cotangent, w_query, w_key, w_value, w_out,
            w_gate.T, w_up.T, w_down,
        )
        units = w_gate.shape[1]
        wide = width // HD
        return (
            output,
            grad_input,
            sums[:wide].reshape(-1),
            grad_w_query,
            sums[24 : 24 + heads].reshape(-1),
            grad_w_pairs[0],
            sums[27:29].reshape(-1),
            grad_w_pairs[1],
            sums[29:31].reshape(-1),
            grad_w_out.T,
            sums[wide : 2 * wide].reshape(-1),
            tiles[1, :, :units].astype(jnp.float32),
            tiles[2, :, :units].astype(jnp.float32),
            tiles[0, :, :units].astype(jnp.float32).T,
        )

    def assemble(parts, axis):
        at = lambda index: lax.dynamic_index_in_dim(parts, reverse_bits(lane ^ index, 2), 0, keepdims=False)
        return (
            jnp.concatenate([at(0), at(2)], axis),
            jnp.concatenate([at(1), at(3)], axis),
        )

    def finish(
        output, grad_middle, grad_normed1, grad_query, grad_pair, gain2_part,
        grad_w_query, grad_w_pair, grad_w_out, grad_w_gate, grad_w_up, grad_w_down,
    ):
        weighted1 = grad_normed1 * norm1_gain
        gain1_part = jnp.sum(grad_normed1 * inputs * scale1, axis=0)
        grad_input = (
            grad_middle
            + scale1 * weighted1
            - inputs * scale1**3 * jnp.mean(weighted1 * inputs, axis=-1, keepdims=True)
        ).astype(jnp.bfloat16)

        small = jnp.concatenate(
            [
                gain1_part,
                gain2_part,
                jnp.sum(grad_query.astype(jnp.float32), axis=0),
                jnp.sum(grad_pair.astype(jnp.float32), axis=0),
            ]
        ).reshape(-1, HD)
        bit = 1
        while bit < shards:
            small = small + swap(small, "cp", bit)
            bit *= 2
        wide = width // HD
        gain1_sum = small[:wide].reshape(-1)
        gain2_sum = small[wide : 2 * wide].reshape(-1)
        bias_query = small[2 * wide : 2 * wide + heads].reshape(-1)

        bias_key, bias_value = assemble(gather_tp(small[None, 2 * wide + heads], 0), 0)
        grad_w_key, grad_w_value = assemble(gather_tp(grad_w_pair[None], 0), 1)
        return (
            output,
            grad_input,
            gain1_sum,
            grad_w_query,
            bias_query,
            grad_w_key,
            bias_key,
            grad_w_value,
            bias_value,
            grad_w_out,
            gain2_sum,
            grad_w_gate,
            grad_w_up,
            grad_w_down,
        )

    middle_docs = doc_ids.reshape(shards, tok_rows)[:, HALF]
    my_doc = middle_docs[me]
    start = jnp.sum((middle_docs < my_doc).astype(jnp.int32))
    place = jnp.stack([me, core, lane, start]).astype(jnp.int32)
    my_pos = lax.dynamic_slice_in_dim(positions, me * tok_rows, tok_rows)
    cosine, sine = rope_tables(my_pos, HD)

    pair_bias = lax.dynamic_slice_in_dim(jnp.where(is_key, b_key, b_value), kv_index * HD, HD)

    inputs = layer_input.astype(jnp.float32)
    scale1 = lax.rsqrt(jnp.mean(inputs * inputs, axis=-1, keepdims=True) + EPSILON)
    normed1 = (inputs * scale1 * norm1_gain).astype(jnp.bfloat16)

    def pair_weight(index):
        head = index * heads // (H // kv_heads)
        source = jnp.where(index % 2 == 0, w_key, w_value)
        return lax.dynamic_slice_in_dim(source, head * HD, HD, 1)

    pair_cos = jnp.where(is_key, cosine, 1.0)
    pair_sin = jnp.where(is_key, sine, 0.0)
    pair_pre = matmul(normed1, pair_weight(lane)) + pair_bias
    pair = rotary(pair_pre, pair_cos, pair_sin).astype(jnp.bfloat16)[None]
    bit = shards // 2
    while bit:
        pair = jnp.concatenate([pair, swap(pair, "cp", bit)], 0)
        bit //= 2
    other = swap(pair, "tp", 1)

    q_pre = matmul(normed1, w_query) + b_query
    query = rotary(
        q_pre.reshape(tok_rows, heads, HD), cosine[:, None, :], sine[:, None, :]
    ).astype(jnp.bfloat16)
    query = query.transpose(1, 0, 2)

    attn, attn_full, log_total, pair = attend(place, query, pair, other)
    w_out_all = gather_tp(w_out, 0)
    w_query_all = gather_tp(w_query, 1)
    cot_shared = share(place, cotangent, shards)
    normed1_shared = share(place, normed1, shards)

    middle = inputs + matmul(gather_tp(attn, 1), w_out_all)
    scale2 = lax.rsqrt(jnp.mean(middle * middle, axis=-1, keepdims=True) + EPSILON)
    normed2 = (middle * scale2 * norm2_gain).astype(jnp.bfloat16)

    units = w_gate.shape[1]
    chunks = pl.cdiv(pl.cdiv(units, TILE), CHUNK_TILES)
    hiddens, grads, total = [], [], None
    for index in range(chunks):
        hidden, grad, total = hidden_chunk(
            place, normed2, cotangent, w_gate, w_up, w_down, total, index
        )
        hiddens.append(hidden)
        grads.append(grad)
    normed2_shared = share(place, normed2, shards)

    downs, gates, ups = [], [], []
    for hidden, grad in zip(hiddens, grads):
        downs.append(weight_grad(place, cot_shared, hidden, shards).T)
        both = weight_grad(place, normed2_shared, grad, shards)
        span = hidden.shape[1]
        for at in range(0, span, TILE):
            size = min(TILE, span - at)
            gates.append(both[:, 2 * at : 2 * at + size])
            ups.append(both[:, 2 * at + TILE : 2 * at + TILE + size])
    grad_w_down = jnp.concatenate(downs, 0)
    grad_w_gate = jnp.concatenate(gates, 1)
    grad_w_up = jnp.concatenate(ups, 1)

    grad_normed2 = in_order(gather_tp(scatter_tp(total).astype(jnp.bfloat16), 0), lane).astype(
        jnp.float32
    )
    weighted2 = grad_normed2 * norm2_gain
    gain2_part = jnp.sum(grad_normed2 * middle * scale2, axis=0)
    grad_middle = (
        cotangent.astype(jnp.float32)
        + scale2 * weighted2
        - middle * scale2**3 * jnp.mean(weighted2 * middle, axis=-1, keepdims=True)
    )
    grad_branch = grad_middle.astype(jnp.bfloat16)
    grad_attn = contract_cols(grad_branch, w_out).astype(jnp.bfloat16)
    grad_query, keep, send = attend_back(
        place, query, pair, grad_attn, attn_full, log_total, cosine, sine
    )

    part = tok_rows // 4
    ffn = sum(matmul(h, lax.slice_in_dim(w_down, i * CHUNK_TILES * TILE, i * CHUNK_TILES * TILE + h.shape[1])) for i, h in enumerate(hiddens))
    ffn = after(ffn.astype(jnp.bfloat16), grad_middle)
    ffn_rel = jnp.concatenate(
        [lax.dynamic_slice_in_dim(ffn, (lane ^ far) * part, part, 0) for far in TP_ORDER], 0
    )
    out_part = scatter_tp(ffn_rel) + lax.dynamic_slice_in_dim(middle, lane * part, part, 0)
    output = in_order(gather_tp(out_part.astype(jnp.bfloat16), 0), lane)

    summed = keep.astype(jnp.float32) + swap(send, "tp", 1).astype(jnp.float32)
    bit = 1
    while bit < shards:
        count = summed.shape[0] // 2
        summed = summed[:count] + swap(summed[count:].astype(jnp.bfloat16), "cp", bit).astype(
            jnp.float32
        )
        bit *= 2
    grad_pair = rotary_back(summed[0], pair_cos, pair_sin).astype(jnp.bfloat16)

    branch_shared = share(place, grad_branch, shards)
    grad_w_out = weight_grad(place, branch_shared, attn, shards).T
    grad_w_query = weight_grad(place, normed1_shared, grad_query, shards)
    grad_w_pair = weight_grad(place, normed1_shared, grad_pair, shards)

    pairs_all = gather_tp(grad_pair, 1)
    grad_normed1 = contract_cols(gather_tp(grad_query, 1), w_query_all)
    for i, far in enumerate(TP_ORDER):
        grad_normed1 = grad_normed1 + contract_cols(
            pairs_all[:, i * HD : (i + 1) * HD], pair_weight(lane ^ far)
        )
    return finish(
        output, grad_middle, grad_normed1, grad_query, grad_pair, gain2_part,
        grad_w_query, grad_w_pair, grad_w_out, grad_w_gate, grad_w_up, grad_w_down,
    )


def solution(mesh):
    return jax.shard_map(
        on_device,
        mesh=mesh,
        in_specs=(
            P("cp", None),
            P(),
            P(None, "tp"),
            P("tp"),
            P(),
            P(),
            P(),
            P(),
            P("tp", None),
            P(),
            P(None, "tp"),
            P(None, "tp"),
            P("tp", None),
            P(),
            P(),
            P("cp", None),
        ),
        out_specs=(
            P("cp", None),
            P("cp", None),
            P(),
            P("cp", "tp"),
            P("tp"),
            P("cp", None),
            P(),
            P("cp", None),
            P(),
            P("tp", "cp"),
            P(),
            P("cp", "tp"),
            P("cp", "tp"),
            P("tp", "cp"),
        ),
        check_vma=False,
    )
```

```python
import functools
import math

import jax
import jax.numpy as jnp
from jax import lax
from jax.experimental import pallas as pl
from jax.experimental.pallas import tpu as pltpu
from jax.sharding import PartitionSpec as P

H = 12
HD = 128
HALF = 128
EPSILON = 1e-06
ROPE_BASE = 10000.0
MASKED = -1e30
LOG2E = 1.4426950408889634
TILE = 256
CHUNK_TILES = 3
VMEM_LIMIT = 56 * 1024 * 1024
TP_ORDER = (0, 2, 1, 3)


def matmul(left, right):
    return jnp.dot(left, right, preferred_element_type=jnp.float32)


def contract_rows(left, right):
    return lax.dot_general(
        left, right, (((0,), (0,)), ((), ())), preferred_element_type=jnp.float32
    )


def contract_cols(left, right):
    return lax.dot_general(
        left, right, (((1,), (1,)), ((), ())), preferred_element_type=jnp.float32
    )


def rope_tables(tok_pos, width):
    half = width // 2
    freq = ROPE_BASE ** (-(jnp.arange(half, dtype=jnp.float32) * 2.0 / width))
    angle = tok_pos.astype(jnp.float32)[:, None] * freq[None, :]
    cosine = jnp.concatenate([jnp.cos(angle), jnp.cos(angle)], -1)
    sine = jnp.concatenate([jnp.sin(angle), jnp.sin(angle)], -1)
    return (cosine, sine)


def rotary(values, cosine, sine):
    half = values.shape[-1] // 2
    return values * cosine + jnp.concatenate([-values[..., half:], values[..., :half]], -1) * sine


def rotary_back(grads, cosine, sine):
    half = grads.shape[-1] // 2
    scaled = grads * sine
    return grads * cosine + jnp.concatenate([scaled[..., half:], -scaled[..., :half]], -1)


def swap(value, axis, bit):
    size = lax.axis_size(axis)
    return lax.ppermute(value, axis, [(i, i ^ bit) for i in range(size)])


def after(value, *earlier):
    return lax.optimization_barrier((value, *earlier))[0]


def bits_of(size):
    return size.bit_length() - 1


def reverse_bits(index, bits):
    out = 0
    for i in range(bits):
        out = out | (((index >> i) & 1) << (bits - 1 - i))
    return out


def params(**more):
    return pltpu.CompilerParams(vmem_limit_bytes=VMEM_LIMIT, **more)


SMEM = pl.BlockSpec(memory_space=pltpu.SMEM)
VMEM = pl.BlockSpec(memory_space=pltpu.VMEM)


def spread_kernel(shards, place_ref, rows_ref, own_ref, send_ref, turned):
    me, core = place_ref[0], place_ref[1]
    turned[...] = rows_ref[...].T
    width = turned.shape[0] // shards
    bits = bits_of(shards)
    for i in range(shards // 2):
        far = reverse_bits(i, bits)
        block = pl.multiple_of((me ^ far) * width, 16)
        own_ref[i * width : (i + 1) * width, :] = turned[pl.ds(block, width), :]
    for i in range(shards // 4):
        far = reverse_bits(core * (shards // 4) + i, bits) | 1
        block = pl.multiple_of((me ^ far) * width, 16)
        send_ref[i * width : (i + 1) * width, :] = turned[pl.ds(block, width), :]


def spread(place, rows, shards):
    count, width = rows.shape
    return pl.pallas_call(
        functools.partial(spread_kernel, shards),
        out_shape=(
            jax.ShapeDtypeStruct((width // 2, count), rows.dtype),
            jax.ShapeDtypeStruct((width // 4, count), rows.dtype),
        ),
        in_specs=[SMEM, VMEM],
        out_specs=(VMEM, VMEM),
        scratch_shapes=[pltpu.VMEM((width, count), rows.dtype)],
        compiler_params=params(),
        cost_estimate=pl.CostEstimate(flops=0, bytes_accessed=4 * rows.size, transcendentals=0),
    )(place, rows)


def share(place, rows, shards):
    own, send = spread(place, rows, shards)
    near = swap(send, "cp", 1)
    return own, near, swap(near, "tp", 1)


def weigh_kernel(place_ref, own_ref, near_ref, far_ref, mine_ref, theirs_ref, send_ref, keep_ref, joined):
    core = place_ref[1]

    @pl.when(pl.program_id(0) == 0)
    def _():
        joined[core] = near_ref[...]
        joined[1 - core] = far_ref[...]

    half = send_ref.shape[0]
    mine, theirs = mine_ref[...], theirs_ref[...]
    send_ref[...] = (
        matmul(own_ref[half:, :], mine) + matmul(joined[1], theirs)
    ).astype(send_ref.dtype)
    keep_ref[...] = (
        matmul(own_ref[:half, :], mine) + matmul(joined[0], theirs)
    ).astype(keep_ref.dtype)


def weigh(place, shared, mine, theirs):
    own, near, far = shared
    half, count = near.shape
    width = mine.shape[1]
    tile = min(width, 512)
    whole = lambda j: (0, 0)
    column = lambda j: (0, j)
    return pl.pallas_call(
        weigh_kernel,
        grid=(pl.cdiv(width, tile),),
        out_shape=(jax.ShapeDtypeStruct((half, width), jnp.bfloat16),) * 2,
        in_specs=[
            SMEM,
            pl.BlockSpec((2 * half, count), whole),
            pl.BlockSpec((half, count), whole),
            pl.BlockSpec((half, count), whole),
            pl.BlockSpec((count, tile), column),
            pl.BlockSpec((count, tile), column),
        ],
        out_specs=(pl.BlockSpec((half, tile), column),) * 2,
        scratch_shapes=[pltpu.VMEM((2, half, count), jnp.bfloat16)],
        compiler_params=params(),
        cost_estimate=pl.CostEstimate(
            flops=8 * half * count * width,
            bytes_accessed=4 * (2 * half * count + count * width + half * width),
            transcendentals=0,
        ),
    )(place, own, near, far, mine, theirs)


def weight_grad(place, shared, mine, shards):
    theirs = swap(mine, "cp", 1)
    send, keep = weigh(place, shared, mine, theirs)
    terms = [keep]
    bit = 2
    while bit < shards:
        terms.append(swap(send, "cp", bit))
        bit *= 2
        if bit < shards:
            rows = terms[0].shape[0] // 2
            send = sum(t[rows:].astype(jnp.float32) for t in terms).astype(jnp.bfloat16)
            terms = [t[:rows] for t in terms]
    return sum(t.astype(jnp.float32) for t in terms)


def hidden_kernel(first, last, offset, units, *refs):
    place_ref, rows_ref, cot_ref, gate_ref, up_ref, down_ref = refs[:6]
    refs = refs[6:]
    if not first:
        before_ref, refs = refs[0], refs[1:]
    hidden_ref, grads_ref, sum_ref, total = refs
    step = pl.program_id(0)

    @pl.when(step == 0)
    def _():
        total[...] = jnp.zeros_like(total) if first else before_ref[...]

    rows = rows_ref[...]
    w_gate, w_up, w_down = gate_ref[...], up_ref[...], down_ref[...]
    if last:
        left = units - (offset + step) * TILE
        inside = lax.broadcasted_iota(jnp.int32, w_gate.shape, 1) < left
        w_gate = jnp.where(inside, w_gate, 0)
        w_up = jnp.where(inside, w_up, 0)
        inside = lax.broadcasted_iota(jnp.int32, w_down.shape, 0) < left
        w_down = jnp.where(inside, w_down, 0)
    gate = matmul(rows, w_gate)
    up_part = matmul(rows, w_up)
    grad_hidden = contract_cols(cot_ref[...], w_down)
    sigma = jax.nn.sigmoid(gate)
    swish = gate * sigma
    hidden_ref[...] = (swish * up_part).astype(jnp.bfloat16)
    grad_gate = (grad_hidden * up_part * sigma * (1.0 + gate * (1.0 - sigma))).astype(jnp.bfloat16)
    grad_up = (grad_hidden * swish).astype(jnp.bfloat16)
    grads_ref[:, :TILE] = grad_gate
    grads_ref[:, TILE:] = grad_up
    total[...] += contract_cols(grad_gate, w_gate) + contract_cols(grad_up, w_up)

    @pl.when(step == pl.num_programs(0) - 1)
    def _():
        if last:
            part = total.shape[0] // len(TP_ORDER)
            for i, far in enumerate(TP_ORDER):
                block = pl.multiple_of((place_ref[2] ^ far) * part, part)
                sum_ref[i * part : (i + 1) * part, :] = total[pl.ds(block, part), :].astype(
                    sum_ref.dtype
                )
        else:
            sum_ref[...] = total[...]


def hidden_chunk(place, rows, cotangent, w_gate, w_up, w_down, before, index):
    count, width = rows.shape
    units = w_gate.shape[1]
    tiles = pl.cdiv(units, TILE)
    offset = index * CHUNK_TILES
    steps = min(CHUNK_TILES, tiles - offset)
    first, last = index == 0, offset + steps == tiles
    inner = min(steps * TILE, units - offset * TILE)
    outer = (steps - 1) * 2 * TILE + TILE + inner - (steps - 1) * TILE
    whole = lambda j: (0, 0)
    column = lambda j: (0, j)
    in_specs = [
        SMEM,
        pl.BlockSpec((count, width), whole),
        pl.BlockSpec((count, width), whole),
        pl.BlockSpec((width, TILE), lambda j: (0, offset + j)),
        pl.BlockSpec((width, TILE), lambda j: (0, offset + j)),
        pl.BlockSpec((TILE, width), lambda j: (offset + j, 0)),
    ]
    operands = [place, rows, cotangent, w_gate, w_up, w_down]
    if not first:
        in_specs.append(pl.BlockSpec((count, width), whole))
        operands.append(before)
    return pl.pallas_call(
        functools.partial(hidden_kernel, first, last, offset, units),
        grid=(steps,),
        out_shape=(
            jax.ShapeDtypeStruct((count, inner), jnp.bfloat16),
            jax.ShapeDtypeStruct((count, outer), jnp.bfloat16),
            jax.ShapeDtypeStruct((count, width), jnp.bfloat16 if last else jnp.float32),
        ),
        in_specs=in_specs,
        out_specs=(
            pl.BlockSpec((count, TILE), column),
            pl.BlockSpec((count, 2 * TILE), column),
            pl.BlockSpec((count, width), whole),
        ),
        scratch_shapes=[pltpu.VMEM((count, width), jnp.float32)],
        compiler_params=params(),
        cost_estimate=pl.CostEstimate(
            flops=10 * count * width * inner,
            bytes_accessed=6 * width * inner + 12 * count * width,
            transcendentals=count * inner,
        ),
    )(*operands)


def region_rows(ref, start, count):
    return ref[:, start : start + count, :].reshape(-1, HD)


def triangle(rows, keys):
    row = lax.broadcasted_iota(jnp.int32, (rows, keys), 0) & (keys - 1)
    return row >= lax.broadcasted_iota(jnp.int32, (rows, keys), 1)


def regions(place_ref, shards, tok_rows):
    me, start = place_ref[0], place_ref[3]
    bits = bits_of(shards)

    def of_first(block):
        low = block < shards
        device = jnp.where(low, block, 2 * shards - 1 - block)
        return reverse_bits(device ^ me, bits), jnp.where(low, 0, tok_rows - HALF)

    def of_middle(block):
        return reverse_bits((start + block) ^ me, bits), HALF

    return (
        (0, HALF, me, of_first),
        (tok_rows - HALF, HALF, 2 * shards - 1 - me, of_first),
        (HALF, tok_rows - 2 * HALF, me - start, of_middle),
    )


def attend_kernel(shards, place_ref, q_ref, mine_ref, other_ref, low_ref, full_ref, log_ref, pair):
    core = place_ref[1]
    pair[core] = mine_ref[...]
    pair[1 - core] = other_ref[...]
    heads, tok_rows = q_ref.shape[0], q_ref.shape[1]
    factor = HD**-0.5 * LOG2E
    for begin, count, blocks, locate in regions(place_ref, shards, tok_rows):
        query = region_rows(q_ref, begin, count)
        rows = heads * count

        def read(which, block):
            slot, offset = locate(block)
            return pair[which, slot, pl.ds(pl.multiple_of(offset, HALF), count), :]

        mask = triangle(rows, count)
        last = jnp.where(mask, contract_cols(query, read(0, blocks)), MASKED)
        peak = lax.fori_loop(
            0, blocks, lambda t, top: jnp.maximum(top, contract_cols(query, read(0, t))), last
        )
        peak = jnp.max(peak, axis=1, keepdims=True) * factor

        def add(block, carry, scores):
            total, accum = carry
            weights = jnp.exp2(scores * factor - peak)
            return total + weights, accum + matmul(weights.astype(jnp.bfloat16), read(1, block))

        carry = add(blocks, (jnp.zeros((rows, count), jnp.float32), jnp.zeros((rows, HD), jnp.float32)), last)
        total, accum = lax.fori_loop(
            0, blocks, lambda t, held: add(t, held, contract_cols(query, read(0, t))), carry
        )
        total = jnp.sum(total, axis=1, keepdims=True)
        full = accum / total
        log_total = jnp.broadcast_to(peak + jnp.log2(total), (rows, HD))
        for head in range(heads):
            part = slice(head * count, (head + 1) * count)
            lanes = slice(head * HD, (head + 1) * HD)
            low_ref[begin : begin + count, lanes] = full[part].astype(jnp.bfloat16)
            full_ref[head, begin : begin + count, :] = full[part]
            log_ref[head, begin : begin + count, :] = log_total[part]


def attend(place, query, mine, other):
    heads, tok_rows, _ = query.shape
    shards = mine.shape[0]
    pairs = heads * tok_rows * tok_rows * shards // 4
    return pl.pallas_call(
        functools.partial(attend_kernel, shards),
        out_shape=(
            jax.ShapeDtypeStruct((tok_rows, heads * HD), jnp.bfloat16),
            jax.ShapeDtypeStruct((heads, tok_rows, HD), jnp.float32),
            jax.ShapeDtypeStruct((heads, tok_rows, HD), jnp.float32),
            jax.ShapeDtypeStruct((2,) + mine.shape, jnp.bfloat16),
        ),
        in_specs=[SMEM, VMEM, VMEM, VMEM],
        out_specs=(VMEM, VMEM, VMEM, VMEM),
        compiler_params=params(),
        cost_estimate=pl.CostEstimate(
            flops=6 * pairs * HD, bytes_accessed=4 * mine.size, transcendentals=pairs
        ),
    )(place, query, mine, other)


def attend_back_kernel(
    shards, place_ref, q_ref, pair, low_ref, full_ref, log_ref, cos_ref, sin_ref,
    query_ref, keep_ref, send_ref, grads,
):
    core = place_ref[1]
    grads[...] = jnp.zeros_like(grads)
    heads, tok_rows = q_ref.shape[0], q_ref.shape[1]
    scale = HD**-0.5
    factor = scale * LOG2E
    sign = jnp.where(lax.broadcasted_iota(jnp.int32, (1, HD), 1) < HD // 2, 1.0, -1.0)
    for begin, count, blocks, locate in regions(place_ref, shards, tok_rows):
        query = region_rows(q_ref, begin, count)
        rows = heads * count
        incoming = jnp.concatenate(
            [low_ref[begin : begin + count, h * HD : (h + 1) * HD] for h in range(heads)], 0
        )
        full = region_rows(full_ref, begin, count)
        log_total = region_rows(log_ref, begin, count)[:, :1]
        delta = jnp.sum(incoming.astype(jnp.float32) * full, axis=1, keepdims=True)

        def add(block, grad_query, mask=None):
            slot, offset = locate(block)
            place = pl.ds(pl.multiple_of(offset, HALF), count)
            keys, values = pair[0, slot, place, :], pair[1, slot, place, :]
            probs = jnp.exp2(contract_cols(query, keys) * factor - log_total)
            if mask is not None:
                probs = jnp.where(mask, probs, 0.0)
            grad_scores = (probs * (contract_cols(incoming, values) - delta)).astype(jnp.bfloat16)
            grads[0, slot, place, :] += contract_rows(grad_scores, query)
            grads[1, slot, place, :] += contract_rows(probs.astype(jnp.bfloat16), incoming)
            return grad_query + matmul(grad_scores, keys)

        grad_query = add(blocks, jnp.zeros((rows, HD), jnp.float32), triangle(rows, count))
        grad_query = lax.fori_loop(0, blocks, add, grad_query) * scale
        cosine, sine = cos_ref[begin : begin + count, :], sin_ref[begin : begin + count, :]
        for head in range(heads):
            part = grad_query[head * count : (head + 1) * count]
            turned = part * cosine + pltpu.roll(part * sine, HD // 2, 1) * sign
            query_ref[begin : begin + count, head * HD : (head + 1) * HD] = turned.astype(
                jnp.bfloat16
            )
    is_key = core == 0
    keep_ref[...] = (grads[core] * jnp.where(is_key, scale, 1.0)).astype(jnp.bfloat16)
    send_ref[...] = (grads[1 - core] * jnp.where(is_key, 1.0, scale)).astype(jnp.bfloat16)


def attend_back(place, query, pair, low, full, log_total, cosine, sine):
    heads, tok_rows, _ = query.shape
    shards = pair.shape[1]
    pairs = heads * tok_rows * tok_rows * shards // 4
    return pl.pallas_call(
        functools.partial(attend_back_kernel, shards),
        out_shape=(
            jax.ShapeDtypeStruct((tok_rows, heads * HD), jnp.bfloat16),
            jax.ShapeDtypeStruct(pair.shape[1:], jnp.bfloat16),
            jax.ShapeDtypeStruct(pair.shape[1:], jnp.bfloat16),
        ),
        in_specs=[SMEM] + [VMEM] * 7,
        out_specs=(VMEM, VMEM, VMEM),
        scratch_shapes=[pltpu.VMEM(pair.shape, jnp.float32)],
        compiler_params=params(),
        cost_estimate=pl.CostEstimate(
            flops=10 * pairs * HD, bytes_accessed=4 * pair.size, transcendentals=pairs
        ),
    )(place, query, pair, low, full, log_total, cosine, sine)


def gather_tp(value, axis):
    value = jnp.concatenate([value, swap(value, "tp", 2)], axis)
    return jnp.concatenate([value, swap(value, "tp", 1)], axis)


def scatter_tp(value):
    half, part = value.shape[0] // 2, value.shape[0] // 4
    other = swap(value[half:], "tp", 1)
    send = (value[part:half].astype(jnp.float32) + other[part:].astype(jnp.float32)).astype(
        jnp.bfloat16
    )
    last = swap(send, "tp", 2)
    return (
        value[:part].astype(jnp.float32)
        + other[:part].astype(jnp.float32)
        + last.astype(jnp.float32)
    )


def in_order(value, me):
    part = value.shape[0] // 4
    return jnp.concatenate(
        [
            lax.dynamic_slice_in_dim(value, reverse_bits(me ^ i, 2) * part, part, 0)
            for i in range(4)
        ],
        0,
    )


UNITS = 256
TOK = 512


def back_kernel(width, units, *refs):
    (
        docs_ref, pos_ref, freq_ref, gain1_ref, gain2_ref, bq_ref, bk_ref, bv_ref, x_hbm, cot_hbm, wq_hbm, wk_hbm, wv_hbm, wo_hbm,
        wg_hbm, wu_hbm, wd_hbm,
        tiles_out, wo_out, wq_out, wkv_out, sums_out, output_out, input_out,
        middle_hbm, pair_hbm, own_hbm, near_hbm, wo_all, wq_turned_hbm, all_hbm, n1_hbm, via_hbm,
        out_core_hbm, out_lane_hbm,
        cosine, sine, gains, w_pair_grad, query, pair, full, log_total, sums, sums_in,
        attn_all, attn_far, query_far, pair_far, middle, acc, turned,
        own_a, far_a, part_s, part_k, near1, part_s2, near2, sent_tile,
        rel, core_in, lane_send, lane_in, grad_full,
        held_query, kv_send, kv_in, grad_query, grad_pair, small_s, small_in, small_s2, small_in2, pair_terms,
        send_sem, recv_sem, local_sem, weight_sem,
    ) = refs
    me = lax.axis_index("cp")
    lane = lax.axis_index("tp")
    b0, b1, b2 = me % 2, (me // 2) % 2, me // 4
    core, high = lane % 2, lane // 2
    x_to = {"cp": me + 1 - 2 * b0}
    z1_to = {"cp": me + 2 - 4 * b1}
    z2_to = {"cp": me + 4 - 8 * b2}
    z3_to = {"cp": me + 6 - 4 * b1 - 8 * b2}
    inner = (b1 + b2) % 2
    peers = [
        me + (r % 2) * (1 - 2 * b0) + (r // 2 % 2) * (2 - 4 * b1) + (r // 4) * (4 - 8 * b2)
        for r in range(8)
    ]
    c_to = {"tp": lane + 1 - 2 * core}
    y_to = {"tp": lane + 2 - 4 * high}
    lane_c, lane_y = lane + 1 - 2 * core, lane + 2 - 4 * high
    lane_cy = 3 - lane
    cy_to = {"tp": lane_cy}
    tiles = pl.cdiv(units, UNITS)
    rest = units - (tiles - 1) * UNITS
    block = width // 8
    half = width // 4
    quarter = TOK // 4
    scale = HD**-0.5
    factor = scale * LOG2E
    used = {"remote": 0, "local": 0}

    def remote(src, dst, to, count=1):
        index = used["remote"]
        used["remote"] += 1
        return pltpu.make_async_remote_copy(
            src_ref=src, dst_ref=dst, send_sem=send_sem.at[index], recv_sem=recv_sem.at[index],
            device_id=to, device_id_type=pl.DeviceIdType.MESH,
        )

    def local(src, dst):
        index = used["local"]
        used["local"] += 1
        return pltpu.make_async_copy(src, dst, local_sem.at[index])

    def started(*copies):
        for copy in copies:
            copy.start()
        return copies[0] if len(copies) == 1 else copies

    def row_block(side, h, i):
        mine = (b0 + side) % 2 + 2 * ((b1 + h) % 2) + 4 * ((b2 + i) % 2)
        return pl.ds(pl.multiple_of(mine * block, 16), block)

    def rows_of_block(index):
        return pl.ds(pl.multiple_of(index * block, 16), block)

    def rows_of(index):
        return pl.ds(pl.multiple_of(index * quarter, quarter), quarter)

    z1_tile = remote(part_s, near1, z1_to)
    z2_tile = remote(part_s2, near2, z2_to)

    spread_base = used["remote"]
    used["remote"] += 2 * 20
    wide_half, wide_quarter = width // 2, width // 4

    def block_of(j, side):
        z = (b1 + 2 * b2, 1 - b1 + 2 * b2, 2 - b2, 3 - 3 * b2)[j]
        return 2 * z + (b0 + side) % 2

    def spread_part(k, j, side, c, y=None):
        rows = half_of(c, y)
        return all_hbm.at[k, block_of(j, side), rows]

    def half_of(c, y=None):
        if y is None:
            return pl.ds(pl.multiple_of(c * wide_half, wide_half), wide_half)
        return pl.ds(pl.multiple_of(c * wide_half + y * wide_quarter, wide_quarter), wide_quarter)

    def spread_copy(k, part, send, recv, to, source=None):
        index = spread_base + 20 * k
        return pltpu.make_async_remote_copy(
            src_ref=part if source is None else source, dst_ref=part,
            send_sem=send_sem.at[index + send],
            recv_sem=recv_sem.at[index + recv], device_id=to, device_id_type=pl.DeviceIdType.MESH,
        )

    def z_copy(k, m):
        j, recv, to = ((0, 1, z1_to), (0, 2, z3_to), (1, 3, z3_to), (2, 2, z1_to), (3, 3, z1_to))[m]
        own = turned.at[half_of(core)] if (k, j) == (1, 0) else None
        return spread_copy(k, spread_part(k, j, 0, core), m, recv, to, own)

    def z_arrival(k, j):
        return spread_copy(k, spread_part(k, j, 0, core), 0, j, z1_to)

    def c_copy(k, j, c=None):
        return spread_copy(k, spread_part(k, j, 0, core if c is None else c), 4 + j, 4 + j, c_to)

    def x_copy(k, j, side=0):
        y = None if (k, j) in WHOLE_HALVES else high
        own = turned.at[half_of(core, y)] if (k, j, side) == (1, 0, 0) else None
        return spread_copy(k, spread_part(k, j, side, core, y), 8 + j, 8 + j, x_to, own)

    def y_copy(k, j, y=None):
        return spread_copy(
            k, spread_part(k, j, 1, core, high if y is None else y), 12 + j, 12 + j, y_to
        )

    def d_copy(k, j, c=None):
        return spread_copy(k, spread_part(k, j, 1, core if c is None else c), 16 + j, 16 + j, c_to)

    def when(condition):
        return pl.when(condition == 1)

    def begin_spread(k):
        z_copy(k, 0).start()

        @when(inner)
        def _():
            z_copy(k, 1).start()

    def arrive(k, j):
        z_arrival(k, j).wait_recv()

        @when(inner)
        def _():
            z_copy(k, j + 1).start()

        started(c_copy(k, j), x_copy(k, j))

    def arrive_inner(k, j):
        @when(inner)
        def _():
            arrive(k, j)

    def arrive_outer(k, j):
        @when(1 - inner)
        def _():
            arrive(k, j)

    def pass_y(k, j):
        assert (k, j) not in WHOLE_HALVES
        x_copy(k, j, 1).wait_recv()
        y_copy(k, j).start()

    def pass_core(k, j):
        if (k, j) in WHOLE_HALVES:
            x_copy(k, j, 1).wait_recv()
        else:
            y_copy(k, j, 1 - high).wait_recv()
        d_copy(k, j).start()

    barrier = pltpu.get_barrier_semaphore()
    for to in (*({"cp": peer} for peer in peers[1:]), c_to, y_to, cy_to):
        pl.semaphore_signal(barrier, inc=1, device_id=to, device_id_type=pl.DeviceIdType.MESH)

    def share(source, index):
        return [
            remote(
                source.at[row_block(1, core, i)],
                far_a.at[index, core, pl.ds(i * block, block)],
                x_to,
            )
            for i in range(2)
        ]

    def forward(index):
        return remote(far_a.at[index, core], far_a.at[index, core], c_to)

    COT, N2, GB, N1 = range(4)
    own_blocks = [local(turned, all_hbm.at[k, me]) for k in range(2)]
    wo_y = remote(wo_hbm, wo_all.at[1], y_to)
    wo_c = remote(wo_hbm, wo_all.at[2], c_to)
    wo_cy = remote(wo_all.at[1], wo_all.at[3], c_to)
    attn_y, attn_c, attn_cy = [
        [
            remote(
                attn_all.at[src, pl.ds(begin, count)], attn_all.at[dst, pl.ds(begin, count)], to
            )
            for begin, count in ((0, HALF), (TOK - HALF, HALF), (HALF, TOK - 2 * HALF))
        ]
        for src, dst, to in ((0, 1, y_to), (0, 2, c_to), (1, 3, c_to))
    ]
    attn_x = remote(attn_all.at[0], attn_far, x_to)
    n1_x = share(n1_hbm, N1)
    n1_keep = local(turned, n1_hbm)
    pair_1 = remote(pair.at[core, 0], pair.at[core, 2], z1_to)
    pair_2 = remote(pair.at[core, 0], pair.at[core, 1], z2_to)
    pair_3 = remote(pair.at[core, 0], pair.at[core, 3], z3_to)
    pair_near = [remote(pair.at[core, i], pair.at[core, 4 + i], x_to) for i in range(4)]
    pair_core = [remote(pair.at[core, i], pair.at[core, i], c_to) for i in range(8)]
    def norm_scale(rows):
        return lax.rsqrt(jnp.mean(rows * rows, axis=-1, keepdims=True) + EPSILON)

    sign = jnp.where(lax.broadcasted_iota(jnp.int32, (1, HD), 1) < HD // 2, 1.0, -1.0)
    is_key = jnp.where(core == 0, 1.0, 0.0)

    def turn(rows, cosines, sines):
        return rows * cosines + pltpu.roll(rows * sign, HD // 2, 1) * sines

    def turn_back(rows, cosines, sines):
        return rows * cosines + pltpu.roll(rows * sines, HD // 2, 1) * sign

    def opening(x_rows, cot_rows, normed, w_query, w_pair, w_turned):
        loads = [
            local(x_hbm, x_rows),
            local(wq_hbm, w_query),
            local(cot_hbm, cot_rows),
        ]
        started(*loads)
        index = used["local"]
        used["local"] += 1
        columns = pl.ds(pl.multiple_of(high * HD, HD), HD)
        key_load = pltpu.make_async_copy(wk_hbm.at[:, columns], w_pair, local_sem.at[index])
        value_load = pltpu.make_async_copy(wv_hbm.at[:, columns], w_pair, local_sem.at[index])

        @pl.when(core == 0)
        def _():
            key_load.start()

        @pl.when(core == 1)
        def _():
            value_load.start()

        lanes_of = [slice(i * HD, (i + 1) * HD) for i in range(width // HD)]
        for i, lanes in enumerate(lanes_of):
            gains[0:1, lanes] = gain1_ref[i : i + 1, :]
            gains[1:2, lanes] = gain2_ref[i : i + 1, :]
        places = pos_ref[pl.ds(me * 4, 4), :].astype(jnp.float32)
        places = jnp.concatenate([places, places], 0).T
        for i in range(4):
            angle = places[:, i : i + 1] * freq_ref[...]
            cosine[i * HD : (i + 1) * HD, :] = jnp.cos(angle)
            sine[i * HD : (i + 1) * HD, :] = jnp.sin(angle)
        loads[0].wait()

        def norm(a, carry):
            rows = x_rows[rows_of(a), :].astype(jnp.float32)
            normed[rows_of(a), :] = (rows * norm_scale(rows) * gains[0:1, :]).astype(
                jnp.bfloat16
            )
            return carry

        lax.fori_loop(0, 4, norm, 0)
        key_load.wait()
        rows = (
            matmul(normed[...], w_pair[...])
            + bk_ref[pl.ds(high, 1), :] * is_key
            + bv_ref[pl.ds(high, 1), :] * (1.0 - is_key)
        )
        pair[core, 0] = turn(
            rows, cosine[...] * is_key + (1.0 - is_key), sine[...] * is_key
        ).astype(jnp.bfloat16)
        pl.semaphore_wait(barrier, 10)
        started(pair_1, pair_2, pair_3, pair_near[0], pair_core[0], wo_y, wo_c)
        loads[2].wait()

        def flip_cot(a, carry):
            turned[:, rows_of(a)] = cot_rows[rows_of(a), :].T
            return carry

        lax.fori_loop(0, 4, flip_cot, 0)
        own_blocks[0].start()
        loads[1].wait()
        rows = matmul(normed[...], w_query[...])
        for h in range(3):
            query[h] = turn(
                rows[:, h * HD : (h + 1) * HD] + bq_ref[h : h + 1, :], cosine[...], sine[...]
            ).astype(jnp.bfloat16)
        own_blocks[0].wait()
        begin_spread(0)
        w_turned[...] = w_query[...].T
        turned_copy = started(local(w_turned, wq_turned_hbm))
        for copy, i in ((pair_1, 2), (pair_2, 1), (pair_3, 3)):
            copy.wait_recv()
            started(pair_near[i], pair_core[i])

        def flip(a, carry):
            turned[:, rows_of(a)] = normed[rows_of(a), :].T
            return carry

        lax.fori_loop(0, 4, flip, 0)
        for p in range(4):
            own_a[N1, p * block : (p + 1) * block, :] = turned[row_block(0, p // 2, p % 2), :]
        for i in (0, 2, 1, 3):
            pair_near[i].wait_recv()
            pair_core[4 + i].start()
        x_copy(0, 0).start()
        n1_keep.start()
        for copy in pair_core:
            copy.wait_recv()
        turned_copy.wait()

    pl.run_scoped(
        opening,
        pltpu.VMEM((TOK, width), jnp.bfloat16),
        pltpu.VMEM((TOK, width), jnp.bfloat16),
        pltpu.VMEM((TOK, width), jnp.bfloat16),
        pltpu.VMEM((width, 3 * HD), jnp.bfloat16),
        pltpu.VMEM((width, HD), jnp.bfloat16),
        pltpu.VMEM((3 * HD, width), jnp.bfloat16),
    )

    def of_first(t):
        t = t - t // 16
        late = t // 8
        device = t * (1 - late) + (15 - t) * late
        return device, late * (TOK - HALF)

    def same_document(device):
        ids = [docs_ref[pl.ds(4 * at + 1, 1), :] for at in (device, me)]
        return jnp.concatenate([ids[0], ids[0]], 1) == jnp.concatenate([ids[1], ids[1]], 1)

    def slot_of(device):
        return (
            4 * ((device % 2 + b0) % 2)
            + 2 * (((device // 2) % 2 + b1) % 2)
            + (device // 4 + b2) % 2
        )

    def places_of(step, wide):
        if wide:
            return [(slot_of(step), pl.ds(HALF, TOK - 2 * HALF))]
        places = []
        for block in (2 * step, 2 * step + 1):
            device, offset = of_first(block)
            places.append((slot_of(device), pl.ds(pl.multiple_of(offset, HALF), HALF)))
        return places

    def keys_of(which, step, wide):
        parts = [pair[which, slot, rows, :] for slot, rows in places_of(step, wide)]
        return parts[0] if wide else jnp.concatenate(parts, 0)

    def seen(begin, count, blocks, wide):
        shape = (3 * count, 2 * HALF)
        row = lax.broadcasted_iota(jnp.int32, shape, 0) & (count - 1)
        if not wide:
            row = row + blocks % 2 * HALF
        return row >= lax.broadcasted_iota(jnp.int32, shape, 1)

    def regions():
        return (
            (0, HALF, me, False, me // 2),
            (TOK - HALF, HALF, 15 - me, False, (15 - me) // 2),
            (HALF, TOK - 2 * HALF, me, True, me),
        )

    def attend_region(begin, count, blocks, wide, steps):
        rows = 3 * count
        q_rows = region_rows(query, begin, count)

        def score(step):
            scores = contract_cols(q_rows, keys_of(0, step, wide))
            return jnp.where(same_document(step), scores, MASKED) if wide else scores

        def add(step, carry, scores):
            total, accum = carry
            weights = jnp.exp2(scores * factor - peak)
            return total + weights, accum + matmul(
                weights.astype(jnp.bfloat16), keys_of(1, step, wide)
            )

        last = jnp.where(
            seen(begin, count, blocks, wide),
            contract_cols(q_rows, keys_of(0, steps, wide)),
            MASKED,
        )
        peak = lax.fori_loop(0, steps, lambda t, top: jnp.maximum(top, score(t)), last)
        peak = jnp.max(peak, axis=1, keepdims=True) * factor
        carry = add(
            steps,
            (jnp.zeros((rows, 2 * HALF), jnp.float32), jnp.zeros((rows, HD), jnp.float32)),
            last,
        )
        total, accum = lax.fori_loop(0, steps, lambda t, held: add(t, held, score(t)), carry)
        total = jnp.sum(total, axis=1, keepdims=True)
        result = accum / total
        logs = jnp.broadcast_to(peak + jnp.log2(total), (rows, HD))
        for h in range(3):
            part = slice(h * count, (h + 1) * count)
            attn_all[0, begin : begin + count, h * HD : (h + 1) * HD] = result[part].astype(
                jnp.bfloat16
            )
            full[h, begin : begin + count, :] = result[part]
            log_total[h, begin : begin + count, :] = logs[part]

    def front(weights, ring, wo, x_rows, cot_turned):
        def fetch(t, slot, rows):
            return [
                pltpu.make_async_copy(
                    source.at[pl.ds(t * UNITS, rows)],
                    weights.at[slot, k, pl.ds(0, rows)],
                    weight_sem.at[slot, k],
                )
                for k, source in enumerate((wg_hbm, wu_hbm, wd_hbm))
            ]

        loads = [
            local(wo_hbm, wo.at[0]),
            local(x_hbm, x_rows),
            local(wo_all.at[2], wo.at[2]),
            local(wo_all.at[1], wo.at[1]),
            local(wo_all.at[3], wo.at[3]),
            local(all_hbm.at[0, me], cot_turned),
        ]
        wo_c.wait_recv()
        started(*loads[:3], loads[5])
        started(*fetch(0, 0, UNITS))
        attend_region(*regions()[0])
        attend_region(*regions()[1])
        started(*attn_y[:2], *attn_c[:2])
        n1_keep.wait()
        started(*n1_x)
        arrive(0, 1)
        arrive_inner(0, 2)
        attend_region(*regions()[2])
        started(attn_y[2], attn_c[2])
        wo_y.wait_recv()
        wo_cy.start()
        loads[3].start()
        pass_y(0, 0)
        for load in loads[:3]:
            load.wait()
        for copy in (pair_1, pair_2, pair_3, *pair_near, *pair_core):
            copy.wait_send()
        def add_part(p, first=False):
            def body(n, carry):
                cols = pl.ds(pl.multiple_of(n * 512, 512), 512)
                held = x_rows[:, cols].astype(jnp.float32) if first else middle[:, cols]
                middle[:, cols] = held + matmul(attn_all[p], wo[p, :, cols])
                return carry

            lax.fori_loop(0, width // 512, body, 0)

        add_part(0, True)
        for copy in attn_c:
            copy.wait_recv()
        add_part(2)
        for copy, forward_copy in zip(attn_y, attn_cy):
            copy.wait_recv()
            forward_copy.start()
        loads[3].wait()
        wo_cy.wait_recv()
        loads[4].start()
        add_part(1)
        for copy in attn_cy:
            copy.wait_recv()
        loads[4].wait()
        add_part(3)

        def norm(a, carry):
            rows = middle[rows_of(a), :]
            turned[:, rows_of(a)] = (rows * norm_scale(rows) * gains[1:2, :]).astype(jnp.bfloat16).T
            return carry

        lax.fori_loop(0, 4, norm, 0)
        begin_spread(1)
        x_copy(1, 0).start()
        own_blocks[1].start()
        loads[5].wait()
        acc[...] = jnp.zeros_like(acc)

        def keep_tile(t):
            return pltpu.make_async_copy(ring.at[t % 2], own_hbm.at[t], weight_sem.at[2, t % 2])

        def tile(t, carry):
            slot = t % 2

            @pl.when(t < tiles - 1)
            def _():
                for copy in fetch(t, slot, UNITS):
                    copy.wait()

            @pl.when(t == tiles - 1)
            def _():
                for copy in fetch(t, slot, rest):
                    copy.wait()

            @pl.when(t + 1 < tiles - 1)
            def _():
                started(*fetch(t + 1, 1 - slot, UNITS))

            @pl.when(t + 1 == tiles - 1)
            def _():
                weights[1 - slot, :, rest:, :] = jnp.zeros(
                    (3, UNITS - rest, width), weights.dtype
                )
                started(*fetch(t + 1, 1 - slot, rest))

            for part in (slice(0, TOK // 2), slice(TOK // 2, TOK)):
                gate = matmul(weights[slot, 0], turned[:, part])
                up_part = matmul(weights[slot, 1], turned[:, part])
                grad_hidden = matmul(weights[slot, 2], cot_turned[:, part])
                sigma = jax.nn.sigmoid(gate)
                swish = gate * sigma
                ring[slot, part, :UNITS] = (swish * up_part).astype(jnp.bfloat16).T
                ring[slot, part, UNITS : 2 * UNITS] = (
                    (grad_hidden * up_part * sigma * (1.0 + gate * (1.0 - sigma)))
                    .astype(jnp.bfloat16)
                    .T
                )
                ring[slot, part, 2 * UNITS :] = (grad_hidden * swish).astype(jnp.bfloat16).T
            for part in (slice(0, TOK // 2), slice(TOK // 2, TOK)):
                acc[part, :] += matmul(
                    ring[slot, part, UNITS:], weights[slot, 0:2].reshape(2 * UNITS, width)
                )

            @pl.when(t > 0)
            def _():
                keep_tile(t - 1).wait()

            @pl.when(t == 3)
            def _():
                arrive_outer(0, 2)
                arrive_inner(0, 3)
                pass_core(0, 0)
                pass_y(0, 1)

            @pl.when(t == 6)
            def _():
                pass_y(1, 0)

            @pl.when(t == 7)
            def _():
                arrive(1, 1)
                arrive_inner(1, 2)

            keep_tile(t).start()
            return carry

        lax.fori_loop(0, tiles, tile, 0)
        keep_tile(tiles - 1).wait()
        own_blocks[1].wait()

    pl.run_scoped(
        front,
        pltpu.VMEM((2, 3, UNITS, width), jnp.bfloat16),
        pltpu.VMEM((2, TOK, 3 * UNITS), jnp.bfloat16),
        pltpu.VMEM((4, width // 4, width), jnp.bfloat16),
        pltpu.VMEM((TOK, width), jnp.bfloat16),
        pltpu.VMEM((width, TOK), jnp.bfloat16),
    )

    def reduce_copies():
        return (
            remote(rel.at[rows_of(lane_c)], core_in.at[0], c_to),
            remote(rel.at[rows_of(lane_cy)], core_in.at[1], c_to),
            remote(lane_send, lane_in, y_to),
        )

    def reduce_start(copies):
        rel[...] = acc[...].astype(jnp.bfloat16)
        started(*copies[:2])

    def reduce_middle(copies):
        copies[0].wait()
        copies[1].wait()
        lane_send[...] = (
            acc[rows_of(lane_y), :] + core_in[1].astype(jnp.float32)
        ).astype(jnp.bfloat16)
        copies[2].start()

    def reduce_end(copies, held):
        copies[2].wait()
        return held + core_in[0].astype(jnp.float32) + lane_in[...].astype(jnp.float32)

    def spread_copies(full):
        mine, theirs = full.at[rows_of(lane)], full.at[rows_of(lane_y)]
        return [
            remote(mine, mine, y_to),
            remote(mine, mine, c_to),
            remote(theirs, theirs, c_to),
        ]

    def spread_end(copies):
        copies[0].wait_recv()
        copies[2].start()
        copies[0].wait_send()
        copies[1].wait()
        copies[2].wait()

    near_base = used["remote"]
    used["remote"] += 4

    def near_copy(r):
        index = near_base + r
        return pltpu.make_async_remote_copy(
            src_ref=sent_tile.at[rows_of_block(peers[r] - 4 * b2)],
            dst_ref=via_hbm if r == 3 else near_hbm.at[r],
            send_sem=send_sem.at[index], recv_sem=recv_sem.at[index],
            device_id={"cp": peers[1 if r == 3 else r]}, device_id_type=pl.DeviceIdType.MESH,
        )

    via_copy = remote(via_hbm, near_hbm.at[3], z1_to)

    final_base = used["local"]
    used["local"] += 24

    SMALL = {"out": (0, 384, GB), "query": (384, 384, N1), "pair": (768, 128, N1)}
    small_base = used["remote"]
    used["remote"] += 6
    pair_hops = [
        remote(
            small_s.at[pl.ds(p * block, block), pl.ds(768, HD)], pair_terms.at[p - 1], to
        )
        for p, to in ((1, z2_to), (2, z1_to), (3, z3_to))
    ]

    def small_copy(name, second):
        begin, wide, _ = SMALL[name]
        index = small_base + 2 * list(SMALL).index(name) + second
        cols = pl.ds(begin, wide)
        if second:
            src, dst, to = small_s2.at[:, cols], small_in2.at[:, cols], z2_to
        else:
            src, dst, to = small_s.at[pl.ds(half, half), cols], small_in.at[:, cols], z1_to
        return pltpu.make_async_remote_copy(
            src_ref=src, dst_ref=dst, send_sem=send_sem.at[index], recv_sem=recv_sem.at[index],
            device_id=to, device_id_type=pl.DeviceIdType.MESH,
        )

    def small_first(name, b_own, b_far):
        begin, wide, index = SMALL[name]
        cols = slice(begin, begin + wide)
        small_s[half:, cols] = (
            matmul(own_a[index, half:, :], b_own) + matmul(far_a[index, 1], b_far)
        ).astype(jnp.bfloat16)
        if name != "pair":
            small_copy(name, 0).start()
        small_s[:half, cols] = (
            matmul(own_a[index, :half, :], b_own) + matmul(far_a[index, 0], b_far)
        ).astype(jnp.bfloat16)
        if name == "pair":
            started(*pair_hops)

    def small_second(name):
        begin, wide, _ = SMALL[name]
        cols = slice(begin, begin + wide)
        small_copy(name, 0).wait_recv()
        small_s2[:, cols] = (
            small_s[block:half, cols].astype(jnp.float32)
            + small_in[block:, cols].astype(jnp.float32)
        ).astype(jnp.bfloat16)
        small_copy(name, 1).start()
        small_copy(name, 0).wait_send()

    def small_third(name, out_ref):
        begin, wide, _ = SMALL[name]
        cols = slice(begin, begin + wide)
        small_copy(name, 1).wait()
        out_ref[...] = (
            small_s[:block, cols].astype(jnp.float32)
            + small_in[:block, cols].astype(jnp.float32)
            + small_in2[:, cols].astype(jnp.float32)
        )

    query_x = remote(grad_query, query_far, x_to)
    pair_x = remote(grad_pair, pair_far, x_to)
    pair_y = remote(grad_pair, pair_hbm.at[1], y_to)
    pair_c = remote(grad_pair, pair_hbm.at[2], c_to)
    pair_cy = remote(pair_hbm.at[1], pair_hbm.at[3], c_to)
    pair_own = local(grad_pair, pair_hbm.at[0])
    here = output_out.at[rows_of(lane)]
    there = output_out.at[rows_of(lane_y)]
    out_spread = [
        remote(lane_send, here, y_to),
        remote(lane_send, here, c_to),
        remote(there, there, c_to),
    ]
    out_own = local(lane_send, here)

    query_reduction = reduce_copies()

    def rest_of(grads, wo_own, second, cots, weights, w_last, ring, total_tile):
        mine = [b0 + 2 * b1 + 4 * i for i in range(2)]
        weight_loads = [
            local(
                source.at[pl.ds(pl.multiple_of(tile * UNITS, UNITS), UNITS)],
                weights.at[k, pl.ds(i * UNITS, UNITS)],
            )
            for i, tile in enumerate(mine)
            for k, source in enumerate((wg_hbm, wu_hbm, wd_hbm))
        ]
        wo_load = local(wo_hbm, wo_own)
        own_tiles = [
            local(
                own_hbm.at[tile, :, pl.ds(k * UNITS, UNITS)],
                ring.at[:, pl.ds((2 * k + i) * UNITS, UNITS)],
            )
            for i, tile in enumerate(mine)
            for k in range(3)
        ]
        block_base = used["local"]
        used["local"] += 3
        own_rows = pl.ds(pl.multiple_of(b2 * wide_half, wide_half), wide_half)
        order = ((0, 0), (1, 0), (0, 1), (1, 1), (2, 0), (3, 0), (2, 1), (3, 1))

        def load_second(j, side):
            slot = order.index((j, side)) % 2
            return pltpu.make_async_copy(
                all_hbm.at[1, block_of(j, side)], second.at[slot], local_sem.at[block_base + slot]
            )

        def load_cots(j, side):
            return pltpu.make_async_copy(
                all_hbm.at[0, block_of(j, side)], cots, local_sem.at[block_base + 2]
            )

        def prefetch(j, side):
            if side:
                d_copy(0, j, 1 - core).wait_recv()
                d_copy(1, j, 1 - core).wait_recv()
            elif j:
                c_copy(0, j, 1 - core).wait_recv()
                c_copy(1, j, 1 - core).wait_recv()
            load_second(j, side).start()

        def product(q):
            slot = q % 2
            pltpu.make_async_copy(
                all_hbm.at[1, 0], second.at[slot], local_sem.at[block_base + slot]
            ).wait()
            cots_load = pltpu.make_async_copy(
                all_hbm.at[0, 0], cots, local_sem.at[block_base + 2]
            )

            @pl.when(q == 0)
            def _():
                for load in own_tiles:
                    load.wait()
                cots_load.wait()

            @pl.when(q > 0)
            def _():
                for part in (slice(0, TOK // 2), slice(TOK // 2, TOK)):
                    gate = matmul(weights[0], second[slot, :, part])
                    up_part = matmul(weights[1], second[slot, :, part])
                    sigma = jax.nn.sigmoid(gate)
                    swish = gate * sigma
                    ring[part, : 2 * UNITS] = (swish * up_part).astype(jnp.bfloat16).T
                    if part.start == 0:
                        cots_load.wait()
                    grad_hidden = matmul(weights[2], cots[:, part])
                    ring[part, 2 * UNITS : 4 * UNITS] = (
                        (grad_hidden * up_part * sigma * (1.0 + gate * (1.0 - sigma)))
                        .astype(jnp.bfloat16)
                        .T
                    )
                    ring[part, 4 * UNITS :] = (grad_hidden * swish).astype(jnp.bfloat16).T

            for n in range(3):
                cols = slice(2 * n * UNITS, 2 * (n + 1) * UNITS)
                rows = second[slot, own_rows, :] if n else cots[own_rows, :]
                total_tile[:, cols] += matmul(rows, ring[:, cols])

        far_loads = [
            local(
                all_hbm.at[k, block_of(0, side), row_block(0, p // 2, p % 2)],
                (
                    far_a.at[k, p // 2, pl.ds((p % 2) * block, block)]
                    if side
                    else own_a.at[k, pl.ds(p * block, block)]
                ),
            )
            for k in range(2)
            for side in range(2)
            for p in range(4)
        ]
        last_loads = [local(own_hbm.at[tiles - 1], sent_tile.at[:TOK, : 3 * UNITS])]
        last_weights = [
            local(source.at[pl.ds((tiles - 1) * UNITS, rest)], w_last.at[k])
            for k, source in enumerate((wg_hbm, wu_hbm, wd_hbm))
        ]

        def last_far():
            slot = order.index((0, 1)) % 2
            for load in last_weights:
                load.wait()
            padding = jnp.zeros((TOK, UNITS - rest), jnp.bfloat16)
            gate = matmul(w_last[0], second[slot])
            up_part = matmul(w_last[1], second[slot])
            grad_hidden = matmul(w_last[2], cots[...])
            sigma = jax.nn.sigmoid(gate)
            swish = gate * sigma
            parts = (
                swish * up_part,
                grad_hidden * up_part * sigma * (1.0 + gate * (1.0 - sigma)),
                grad_hidden * swish,
            )
            for k, part in enumerate(parts):
                begin = (3 + k) * UNITS
                sent_tile[:TOK, begin : begin + UNITS] = jnp.concatenate(
                    [part.astype(jnp.bfloat16).T, padding], 1
                )

        def last_first():
            for load in (*far_loads, *last_loads):
                load.wait()

            def body(n, h):
                cols = pl.ds(pl.multiple_of(n * UNITS, UNITS), UNITS)
                far_cols = pl.ds(pl.multiple_of((3 + n) * UNITS, UNITS), UNITS)
                index = (n + 1) // 2
                return cols, matmul(
                    own_a[index, h * half : (h + 1) * half, :], sent_tile[:TOK, cols]
                ) + matmul(far_a[index, h], sent_tile[:TOK, far_cols])

            def sent(n, carry):
                cols, value = body(n, 1)
                part_s[:, cols] = value.astype(jnp.bfloat16)
                return carry

            def kept(n, carry):
                cols, value = body(n, 0)
                part_k[:, cols] = value.astype(jnp.bfloat16)
                return carry

            lax.fori_loop(0, 3, sent, 0)
            z1_tile.start()
            lax.fori_loop(0, 3, kept, 0)

        reduction = reduce_copies()
        wq_load = local(wq_turned_hbm, wo_own)
        spread = spread_copies(grad_full)
        cot_load = local(cot_hbm, rel)
        kv_c = remote(kv_send.at[pl.ds(0, 8)], kv_in.at[pl.ds(0, 8)], c_to)
        kv_x = remote(kv_send.at[pl.ds(0, 4)], kv_in.at[pl.ds(8, 4)], x_to)
        kv_1 = remote(kv_send.at[pl.ds(4, 2)], kv_in.at[pl.ds(12, 2)], z1_to)
        kv_2 = remote(kv_send.at[pl.ds(6, 1)], kv_in.at[pl.ds(14, 1)], z2_to)
        keep_by = is_key * scale + (1.0 - is_key)
        send_by = (1.0 - is_key) * scale + is_key

        def middle_back(a, total):
            grad = grad_full[rows_of(a), :].astype(jnp.float32)
            rows = middle[rows_of(a), :]
            factor2 = norm_scale(rows)
            weighted = grad * gains[1:2, :]
            result = (
                rel[rows_of(a), :].astype(jnp.float32)
                + factor2 * weighted
                - rows * factor2**3 * jnp.mean(weighted * rows, axis=-1, keepdims=True)
            )
            acc[rows_of(a), :] = result
            turned[:, rows_of(a)] = result.astype(jnp.bfloat16).T
            return total + jnp.sum(grad * rows * factor2, axis=0, keepdims=True)

        def region(begin, count, blocks, wide, steps):
            heads = query.shape[0]
            rows = heads * count
            q_rows = region_rows(query, begin, count)
            grad_rows = jnp.concatenate(
                [attn_all[1, begin : begin + count, h * HD : (h + 1) * HD] for h in range(heads)], 0
            )
            logs = region_rows(log_total, begin, count)[:, :1]
            delta = jnp.sum(
                grad_rows.astype(jnp.float32) * region_rows(full, begin, count),
                axis=1,
                keepdims=True,
            )

            def add(step, carry, last=False):
                keys, values = keys_of(0, step, wide), keys_of(1, step, wide)
                probs = jnp.exp2(contract_cols(q_rows, keys) * factor - logs)
                if last:
                    probs = jnp.where(seen(begin, count, blocks, wide), probs, 0.0)
                elif wide:
                    probs = jnp.where(same_document(step), probs, 0.0)
                grad_scores = (probs * (contract_cols(grad_rows, values) - delta)).astype(
                    jnp.bfloat16
                )
                key_part = contract_rows(grad_scores, q_rows)
                value_part = contract_rows(probs.astype(jnp.bfloat16), grad_rows)
                for i, (slot, place) in enumerate(places_of(step, wide)):
                    part = slice(None) if wide else slice(i * HALF, (i + 1) * HALF)
                    grads[0, slot, place, :] += key_part[part]
                    grads[1, slot, place, :] += value_part[part]
                return carry + matmul(grad_scores, keys)

            total = add(steps, jnp.zeros((rows, HD), jnp.float32), True)
            total = lax.fori_loop(0, steps, add, total) * scale
            cosines, sines = cosine[begin : begin + count, :], sine[begin : begin + count, :]
            for h in range(heads):
                part = total[h * count : (h + 1) * count]
                grad_query[begin : begin + count, h * HD : (h + 1) * HD] = (
                    turn_back(part, cosines, sines)
                ).astype(jnp.bfloat16)

        def to_core(s, carry):
            kv_send[s] = (grads[1 - core, s] * send_by).astype(jnp.bfloat16)
            return carry

        def from_core(s, carry):
            grads[core, s] = grads[core, s] * keep_by + kv_in[s].astype(jnp.float32)
            return carry

        def pass_on(copy, first, count):
            def cast(s, carry):
                kv_send[first - 8 + s] = grads[core, count + s].astype(jnp.bfloat16)
                return carry

            lax.fori_loop(0, count, cast, 0)
            copy.start()

        def take(copy, first, count):
            copy.wait()

            def add(s, carry):
                grads[core, s] += kv_in[first + s].astype(jnp.float32)
                return carry

            lax.fori_loop(0, count, add, 0)

        def stage_0():
            reduce_start(reduction)
            total_tile[...] = jnp.zeros_like(total_tile)
            reduce_middle(reduction)
            prefetch(1, 0)
            started(*weight_loads, wo_load)
            pass_core(1, 0)

        def stage_1():
            started(*last_weights, attn_x)
            for load in weight_loads:
                load.wait()

        def stage_2():
            arrive_inner(1, 3)
            prefetch(0, 1)
            grads[...] = jnp.zeros_like(grads)
            grad_full[rows_of(lane), :] = reduce_end(reduction, acc[rows_of(lane), :]).astype(
                jnp.bfloat16
            )
            started(*spread[:2])
            cot_load.start()
            pass_core(0, 1)

        def stage_3():
            last_far()
            spread_end(spread)
            pass_y(1, 1)
            cot_load.wait()
            wo_load.wait()
            z_copy(1, 0).wait_send()
            x_copy(1, 0).wait_send()

            @when(inner)
            def _():
                z_copy(1, 1).wait_send()

            sums[...] = jnp.zeros_like(sums)
            gain2_part = lax.fori_loop(0, 4, middle_back, jnp.zeros((1, width), jnp.float32))
            for i in range(width // HD):
                sums[12 + i : 13 + i, :] = gain2_part[:, i * HD : (i + 1) * HD]
            middle_copy.start()
            for copy in attn_cy:
                copy.wait_send()
            attn_all[1] = matmul(wo_own[...], turned[...]).astype(jnp.bfloat16).T
            wq_load.start()
            arrive_outer(1, 2)
            arrive_outer(0, 3)
            region(*regions()[0])
            pass_y(0, 2)
            region(*regions()[1])
            pass_core(1, 1)
            region(*regions()[2])
            lax.fori_loop(0, 8, to_core, 0)
            kv_c.start()
            prefetch(1, 1)
            arrive_outer(1, 3)
            prefetch(2, 0)

        def stage_4():
            started(*far_loads, *last_loads)
            kv_c.wait()
            lax.fori_loop(0, 8, from_core, 0)
            pass_on(kv_x, 8, 4)
            pass_y(1, 2)
            pass_y(0, 3)
            pass_core(0, 2)
            wq_load.wait()
            middle_copy.wait()
            acc[...] = matmul(grad_query[...], wo_own[...])
            reduce_start(query_reduction)

        def stage_5():
            prefetch(3, 0)
            last_first()
            started(*branch_x)
            pass_core(1, 2)

        def stage_6():
            prefetch(2, 1)
            take(kv_x, 8, 4)
            pass_on(kv_1, 12, 2)
            started(query_x)
            pass_y(1, 3)
            pass_core(0, 3)
            for p in range(4):
                own_a[GB, p * block : (p + 1) * block, :] = turned[
                    row_block(0, p // 2, p % 2), :
                ]
            for copy in n1_x:
                copy.wait()
            n1_forward.start()
            z1_tile.wait_recv()
            part_s2[...] = (
                part_k[block:, :].astype(jnp.float32) + near1[block:, :].astype(jnp.float32)
            ).astype(jnp.bfloat16)
            z2_tile.start()

        def stage_7():
            for copy in branch_x:
                copy.wait()
            branch_forward.start()
            reduce_middle(query_reduction)
            held_query[...] = acc[rows_of(lane), :].astype(jnp.bfloat16)
            take(kv_1, 12, 2)
            pass_on(kv_2, 14, 1)
            pass_core(1, 3)
            branch_forward.wait()
            attn_x.wait()
            small_first("out", attn_all[0], attn_far[...])
            n1_forward.wait()
            prefetch(3, 1)

        stages = (stage_0, stage_1, stage_2, stage_3, stage_4, stage_5, stage_6, stage_7)

        def body(q, carry):
            for at, (stage, of) in enumerate(zip(stages, order)):

                @pl.when(q == at)
                def _(stage=stage, of=of):
                    stage()
                    if of != order[0]:
                        load_cots(*of).start()

            product(q)
            return carry

        prefetch(0, 0)
        load_cots(0, 0).start()
        started(*own_tiles)
        lax.fori_loop(0, len(order), body, 0)
        sent_tile[...] = total_tile[...].astype(jnp.bfloat16)
        near_copy(2).start()
        query_x.wait()
        small_first("query", grad_query[...], query_far[...])
        kv_2.wait()
        f_cos = cosine[...] * is_key + (1.0 - is_key)
        f_sin = sine[...] * is_key
        total = grads[core, 0] + kv_in[14].astype(jnp.float32)
        grad_pair[...] = turn_back(total, f_cos, f_sin).astype(jnp.bfloat16)
        started(pair_x, pair_y, pair_c, pair_own)
        near_copy(3).start()

    n1_forward = forward(N1)
    branch_x = share(turned, GB)
    branch_forward = forward(GB)
    middle_copy = local(acc, middle_hbm)
    pl.run_scoped(
        rest_of,
        pltpu.VMEM((2, 8, TOK, HD), jnp.float32),
        pltpu.VMEM((width // 4, width), jnp.bfloat16),
        pltpu.VMEM((2, width, TOK), jnp.bfloat16),
        pltpu.VMEM((width, TOK), jnp.bfloat16),
        pltpu.VMEM((3, 2 * UNITS, width), jnp.bfloat16),
        pltpu.VMEM((3, rest, width), jnp.bfloat16),
        pltpu.VMEM((TOK, 6 * UNITS), jnp.bfloat16),
        pltpu.VMEM((width // 2, 6 * UNITS), jnp.float32),
    )

    def closing(
        x_rows, pres, w_pres, w_down, hidden, near_low, final, held
    ):
        gathered_pair = []
        loads = [local(x_hbm, x_rows)]
        pairs_load = [
            local(pair_hbm.at[p], pres.at[:, pl.ds(p * HD, HD)]) for p in range(4)
        ]
        for p, far in enumerate(TP_ORDER):
            head = (high + far // 2) % 2
            lanes = pl.ds(pl.multiple_of(head * HD, HD), HD)
            index = used["local"]
            used["local"] += 1
            key_load, value_load = [
                pltpu.make_async_copy(
                    source.at[:, lanes],
                    w_pres.at[:, pl.ds(p * HD, HD)],
                    local_sem.at[index],
                )
                for source in (wk_hbm, wv_hbm)
            ]
            kind = (core + far % 2) % 2

            @pl.when(kind == 0)
            def _(key_load=key_load):
                key_load.start()

            @pl.when(kind == 1)
            def _(value_load=value_load):
                value_load.start()

            gathered_pair.append(key_load)
        middle_load = local(middle_hbm, middle)
        wide_unit = 2 * UNITS
        steps = [
            (t, min(wide_unit, units - t * wide_unit)) for t in range(pl.cdiv(units, wide_unit))
        ]

        def fetch(t, rows):
            slot = t % 2
            copies = [
                pltpu.make_async_copy(
                    wd_hbm.at[pl.ds(t * wide_unit, rows)],
                    w_down.at[slot, pl.ds(0, rows)],
                    weight_sem.at[slot, 0],
                )
            ]
            for i in range(pl.cdiv(rows, UNITS)):
                copies.append(
                    pltpu.make_async_copy(
                        own_hbm.at[2 * t + i, :, pl.ds(0, UNITS)],
                        hidden.at[slot, :, pl.ds(i * UNITS, UNITS)],
                        weight_sem.at[slot, 1 + i],
                    )
                )
            return copies

        started(*fetch(*steps[0]), *loads)
        for t, rows in steps:
            slot = t % 2
            if t + 1 < len(steps):
                more = steps[t + 1][1]
                if more < wide_unit:
                    end = pl.cdiv(more, UNITS) * UNITS
                    w_down[1 - slot, more:end, :] = jnp.zeros((end - more, width), w_down.dtype)
                started(*fetch(*steps[t + 1]))
            for copy in fetch(t, rows):
                copy.wait()
            depth = pl.cdiv(rows, UNITS) * UNITS

            for part in (slice(0, TOK // 2), slice(TOK // 2, TOK)):
                value = matmul(hidden[slot, part, :depth], w_down[slot, :depth, :])
                if t == 0:
                    acc[part, :] = value
                else:
                    acc[part, :] += value
            if t == 0:
                pair_y.wait_recv()
                pair_cy.start()
                pair_c.wait_recv()
                pair_own.wait()
            if t == 1:
                pair_cy.wait_recv()
                started(*pairs_load)
                pair_x.wait()
                small_first("pair", grad_pair[...], pair_far[...])
                for load in (*pairs_load, *gathered_pair):
                    load.wait()
                grad_full[rows_of(lane), :] = (
                    reduce_end(query_reduction, held_query[...].astype(jnp.float32))
                    + contract_cols(pres[rows_of(lane), :], w_pres[...])
                ).astype(jnp.bfloat16)
                started(*normed_spread[:2])
            if t == 3:
                small_second("out")
        acc[rows_of(lane), :] += middle[rows_of(lane), :]
        middle_load.start()
        reduce_start(out_reduction)
        for copy in out_reduction[:2]:
            copy.wait()
        out_core_load.start()
        out_core_load.wait()
        lane_send[...] = (
            acc[rows_of(lane_y), :] + core_in[1].astype(jnp.float32)
        ).astype(jnp.bfloat16)
        out_reduction[2].start()
        held[...] = acc[rows_of(lane), :] + core_in[0].astype(jnp.float32)
        near_copy(3).wait_recv()
        via_copy.start()
        near_copy(1).start()
        small_second("query")
        spread_end(normed_spread)
        for load in (*loads, middle_load):
            load.wait()

        def last(a, total):
            grad = grad_full[rows_of(a), :].astype(jnp.float32)
            rows = x_rows[rows_of(a), :].astype(jnp.float32)
            scale1 = norm_scale(rows)
            weighted = grad * gains[0:1, :]
            rel[rows_of(a), :] = (
                middle[rows_of(a), :]
                + scale1 * weighted
                - rows * scale1**3 * jnp.mean(weighted * rows, axis=-1, keepdims=True)
            ).astype(jnp.bfloat16)
            return total + jnp.sum(grad * rows * scale1, axis=0, keepdims=True)

        gain1_part = lax.fori_loop(0, 4, last, jnp.zeros((1, width), jnp.float32))
        input_copy = started(local(rel, input_out))
        for i in range(width // HD):
            sums[i : i + 1, :] = gain1_part[:, i * HD : (i + 1) * HD]
        bias_part = jnp.sum(grad_query[...].astype(jnp.float32), axis=0, keepdims=True)
        for h in range(3):
            sums[24 + h : 25 + h, :] = bias_part[:, h * HD : (h + 1) * HD]
        for p, far in enumerate(TP_ORDER):
            row = 27 + 2 * ((core + far % 2) % 2) + (high + far // 2) % 2
            lanes = slice(p * HD, (p + 1) * HD)
            sums[pl.ds(row, 1), :] = jnp.sum(
                pres[:, lanes].astype(jnp.float32), axis=0, keepdims=True
            )
        started(*sums_copies)
        out_reduction[2].wait()
        out_lane_load.start()
        out_lane_load.wait()
        lane_send[...] = (held[...] + lane_in[...].astype(jnp.float32)).astype(jnp.bfloat16)
        started(out_spread[0], out_spread[1], out_own)
        for copy in pair_hops:
            copy.wait()
        w_pair_grad[...] = small_s[:block, 768 : 768 + HD].astype(jnp.float32) + sum(
            pair_terms[i].astype(jnp.float32) for i in range(3)
        )
        started(*w_pair_copies)

        mine_rows = rows_of_block(me - 4 * b2)

        def tile_copies(r):
            tile = peers[r] - 4 * b2
            return [
                pltpu.make_async_copy(
                    (near_low.at[r - 1] if r else sent_tile.at[mine_rows]).at[
                        :, pl.ds((2 * k + i) * UNITS, UNITS)
                    ],
                    tiles_out.at[
                        k, :, pl.ds(pl.multiple_of((tile + 4 * i) * UNITS, UNITS), UNITS)
                    ],
                    local_sem.at[final_base + 6 * r + 2 * k + i],
                )
                for k in range(3)
                for i in range(2)
            ]

        started(*tile_copies(0))
        near_loads = [None] + [local(near_hbm.at[r], near_low.at[r - 1]) for r in (1, 2, 3)]
        for r in (2, 1, 3):
            if r == 3:
                via_copy.wait_recv()
            else:
                near_copy(r).wait_recv()
            near_loads[r].start()
            near_loads[r].wait()
            started(*tile_copies(r))
        out_spread[0].wait_recv()
        out_spread[2].start()
        z2_tile.wait_recv()
        final[...] = (
            part_k[:block, :].astype(jnp.float32)
            + near1[:block, :].astype(jnp.float32)
            + near2[...].astype(jnp.float32)
        ).astype(jnp.bfloat16)
        last_copies = [
            local(
                final.at[:, pl.ds(k * UNITS, UNITS)],
                tiles_out.at[k, :, pl.ds((tiles - 1) * UNITS, UNITS)],
            )
            for k in range(3)
        ]
        started(*last_copies)
        small_third("out", wo_out)
        small_third("query", wq_out)
        input_copy.wait()
        for r in range(4):
            for copy in tile_copies(r):
                copy.wait()
        for copy in last_copies:
            copy.wait()

    out_reduction = (
        remote(rel.at[rows_of(lane_c)], out_core_hbm.at[0], c_to),
        remote(rel.at[rows_of(lane_cy)], out_core_hbm.at[1], c_to),
        remote(lane_send, out_lane_hbm, y_to),
    )
    out_core_load = local(out_core_hbm, core_in)
    out_lane_load = local(out_lane_hbm, lane_in)
    normed_spread = spread_copies(grad_full)
    sums_copies = [
        remote(sums, sums_in.at[r], {"cp": peers[r]}) for r in range(1, 8)
    ]
    w_pair_place = wkv_out.at[core, :, pl.ds(pl.multiple_of(high * HD, HD), HD)]
    w_pair_copies = [remote(w_pair_grad, w_pair_place, to) for to in (y_to, c_to, cy_to)]
    w_pair_copies.append(local(w_pair_grad, w_pair_place))
    pl.run_scoped(
        closing,
        pltpu.VMEM((TOK, width), jnp.bfloat16),
        pltpu.VMEM((TOK, 4 * HD), jnp.bfloat16),
        pltpu.VMEM((width, 4 * HD), jnp.bfloat16),
        pltpu.VMEM((2, 2 * UNITS, width), jnp.bfloat16),
        pltpu.VMEM((2, TOK, 2 * UNITS), jnp.bfloat16),
        pltpu.VMEM((3, block, 6 * UNITS), jnp.bfloat16),
        pltpu.VMEM((block, 3 * UNITS), jnp.bfloat16),
        pltpu.VMEM((quarter, width), jnp.float32),
    )
    for copy in sums_copies:
        copy.wait()
    sums_out[...] = sums[...] + sum(sums_in[r] for r in range(1, 8))
    for copy in w_pair_copies:
        copy.wait()
    z1_tile.wait_send()
    z2_tile.wait_send()
    for r in (1, 2, 3):
        near_copy(r).wait_send()
    via_copy.wait_send()
    z_copy(0, 0).wait_send()
    x_copy(0, 0).wait_send()

    @when(inner)
    def _():
        z_copy(0, 1).wait_send()
        for k in range(2):
            for m in (2, 3, 4):
                z_copy(k, m).wait_send()

    for k in range(2):
        for j in range(4):
            if j:
                c_copy(k, j).wait_send()
                x_copy(k, j).wait_send()
            if (k, j) not in WHOLE_HALVES:
                y_copy(k, j).wait_send()
            d_copy(k, j).wait_send()
    for copy in (
        *attn_y, *attn_c, pair_y, pair_c, pair_cy, out_spread[0], wo_y, wo_c, wo_cy,
    ):
        copy.wait_send()
    for copy in (out_spread[1], out_spread[2]):
        copy.wait()
    out_own.wait()
    assert used["remote"] <= REMOTE and used["local"] <= LOCAL, used


WHOLE_HALVES = ()
REMOTE = 134
LOCAL = 150


def whole_layer(
    docs, places, freq, gain1, gain2, b_query, b_key, b_value,
    x, cot, w_query, w_key, w_value, w_out, w_gate, w_up, w_down,
):
    tok_rows, width = x.shape
    units = w_gate.shape[0]
    tiles = pl.cdiv(units, UNITS)
    half, block, quarter = width // 4, width // 8, tok_rows // 4
    low, wide = jnp.bfloat16, jnp.float32
    shape = jax.ShapeDtypeStruct
    any_ = pl.BlockSpec(memory_space=pl.ANY)
    outs = (
        shape((3, block, tiles * UNITS), low),
        shape((block, 384), wide),
        shape((block, 384), wide),
        shape((2, block, 2 * HD), wide),
        shape((32, HD), wide),
        shape((tok_rows, width), low),
        shape((tok_rows, width), low),
        shape((tok_rows, width), wide),
        shape((4, tok_rows, HD), low),
        shape((tiles, tok_rows, 3 * UNITS), low),
        shape((4, block, 6 * UNITS), low),
        shape((4,) + w_out.shape, low),
        shape(w_query.shape[::-1], low),
        shape((2, 8, width, tok_rows), low),
        shape((width, tok_rows), low),
        shape((block, 6 * UNITS), low),
        shape((2, quarter, width), low),
        shape((quarter, width), low),
    )
    vmem = pltpu.VMEM
    scratch = [
        vmem((tok_rows, HD), wide),
        vmem((tok_rows, HD), wide),
        vmem((2, width), wide),
        vmem((block, HD), wide),
        vmem((3, tok_rows, HD), low),
        vmem((2, 8, tok_rows, HD), low),
        vmem((3, tok_rows, HD), wide),
        vmem((3, tok_rows, HD), wide),
        vmem((32, HD), wide),
        vmem((8, 32, HD), wide),
        vmem((4, tok_rows, 384), low),
        vmem((tok_rows, 384), low),
        vmem((tok_rows, 384), low),
        vmem((tok_rows, HD), low),
        vmem((tok_rows, width), wide),
        vmem((tok_rows, width), wide),
        vmem((width, tok_rows), low),
        vmem((4, width // 2, tok_rows), low),
        vmem((4, 2, half, tok_rows), low),
        vmem((half, 3 * UNITS), low),
        vmem((half, 3 * UNITS), low),
        vmem((half, 3 * UNITS), low),
        vmem((block, 3 * UNITS), low),
        vmem((block, 3 * UNITS), low),
        vmem((width // 2, 6 * UNITS), low),
        vmem((tok_rows, width), low),
        vmem((2, quarter, width), low),
        vmem((quarter, width), low),
        vmem((quarter, width), low),
        vmem((tok_rows, width), low),
        vmem((quarter, width), low),
        vmem((8, tok_rows, HD), low),
        vmem((15, tok_rows, HD), low),
        vmem((tok_rows, 384), low),
        vmem((tok_rows, HD), low),
        vmem((2 * half, 896), low),
        vmem((half, 896), low),
        vmem((block, 896), low),
        vmem((block, 896), low),
        vmem((3, block, HD), low),
        pltpu.SemaphoreType.DMA((REMOTE,)),
        pltpu.SemaphoreType.DMA((REMOTE,)),
        pltpu.SemaphoreType.DMA((LOCAL,)),
        pltpu.SemaphoreType.DMA((3, 3)),
    ]
    return pl.pallas_call(
        functools.partial(back_kernel, width, units),
        out_shape=outs,
        in_specs=[VMEM] * 8 + [any_] * 9,
        out_specs=(any_, VMEM, VMEM, any_, VMEM) + (any_,) * 13,
        scratch_shapes=scratch,
        compiler_params=pltpu.CompilerParams(
            vmem_limit_bytes=64 * 1024 * 1024, collective_id=0, has_side_effects=True
        ),
        cost_estimate=pl.CostEstimate(
            flops=20 * tok_rows * width * units, bytes_accessed=10 * width * units, transcendentals=0
        ),
    )(
        docs, places, freq, gain1, gain2, b_query, b_key, b_value,
        x, cot, w_query, w_key, w_value, w_out, w_gate, w_up, w_down,
    )


def on_device(
    layer_input,
    norm1_gain,
    w_query,
    b_query,
    w_key,
    b_key,
    w_value,
    b_value,
    w_out,
    norm2_gain,
    w_gate,
    w_up,
    w_down,
    doc_ids,
    positions,
    cotangent,
):
    tok_rows, width = layer_input.shape
    shards = lax.axis_size("cp")
    heads = w_query.shape[1] // HD
    kv_heads = w_key.shape[1] // HD
    me = lax.axis_index("cp")
    lane = lax.axis_index("tp")
    core = lane % 2
    kv_index = lane * heads // (H // kv_heads)
    is_key = core == 0

    if shards == 8 and tok_rows == TOK:
        half = HD // 2
        freq = ROPE_BASE ** (-(jnp.arange(half, dtype=jnp.float32) * 2.0 / HD))
        tiles, grad_w_out, grad_w_query, grad_w_pairs, sums, output, grad_input, *_ = whole_layer(
            doc_ids.reshape(-1, HD), positions.reshape(-1, HD),
            jnp.concatenate([freq, freq])[None],
            norm1_gain.reshape(-1, HD), norm2_gain.reshape(-1, HD),
            b_query.reshape(-1, HD), b_key.reshape(-1, HD), b_value.reshape(-1, HD),
            layer_input, cotangent, w_query, w_key, w_value, w_out,
            w_gate.T, w_up.T, w_down,
        )
        units = w_gate.shape[1]
        wide = width // HD
        return (
            output,
            grad_input,
            sums[:wide].reshape(-1),
            grad_w_query,
            sums[24 : 24 + heads].reshape(-1),
            grad_w_pairs[0],
            sums[27:29].reshape(-1),
            grad_w_pairs[1],
            sums[29:31].reshape(-1),
            grad_w_out.T,
            sums[wide : 2 * wide].reshape(-1),
            tiles[1, :, :units].astype(jnp.float32),
            tiles[2, :, :units].astype(jnp.float32),
            tiles[0, :, :units].astype(jnp.float32).T,
        )

    def assemble(parts, axis):
        at = lambda index: lax.dynamic_index_in_dim(parts, reverse_bits(lane ^ index, 2), 0, keepdims=False)
        return (
            jnp.concatenate([at(0), at(2)], axis),
            jnp.concatenate([at(1), at(3)], axis),
        )

    def finish(
        output, grad_middle, grad_normed1, grad_query, grad_pair, gain2_part,
        grad_w_query, grad_w_pair, grad_w_out, grad_w_gate, grad_w_up, grad_w_down,
    ):
        weighted1 = grad_normed1 * norm1_gain
        gain1_part = jnp.sum(grad_normed1 * inputs * scale1, axis=0)
        grad_input = (
            grad_middle
            + scale1 * weighted1
            - inputs * scale1**3 * jnp.mean(weighted1 * inputs, axis=-1, keepdims=True)
        ).astype(jnp.bfloat16)

        small = jnp.concatenate(
            [
                gain1_part,
                gain2_part,
                jnp.sum(grad_query.astype(jnp.float32), axis=0),
                jnp.sum(grad_pair.astype(jnp.float32), axis=0),
            ]
        ).reshape(-1, HD)
        bit = 1
        while bit < shards:
            small = small + swap(small, "cp", bit)
            bit *= 2
        wide = width // HD
        gain1_sum = small[:wide].reshape(-1)
        gain2_sum = small[wide : 2 * wide].reshape(-1)
        bias_query = small[2 * wide : 2 * wide + heads].reshape(-1)

        bias_key, bias_value = assemble(gather_tp(small[None, 2 * wide + heads], 0), 0)
        grad_w_key, grad_w_value = assemble(gather_tp(grad_w_pair[None], 0), 1)
        return (
            output,
            grad_input,
            gain1_sum,
            grad_w_query,
            bias_query,
            grad_w_key,
            bias_key,
            grad_w_value,
            bias_value,
            grad_w_out,
            gain2_sum,
            grad_w_gate,
            grad_w_up,
            grad_w_down,
        )

    middle_docs = doc_ids.reshape(shards, tok_rows)[:, HALF]
    my_doc = middle_docs[me]
    start = jnp.sum((middle_docs < my_doc).astype(jnp.int32))
    place = jnp.stack([me, core, lane, start]).astype(jnp.int32)
    my_pos = lax.dynamic_slice_in_dim(positions, me * tok_rows, tok_rows)
    cosine, sine = rope_tables(my_pos, HD)

    pair_bias = lax.dynamic_slice_in_dim(jnp.where(is_key, b_key, b_value), kv_index * HD, HD)

    inputs = layer_input.astype(jnp.float32)
    scale1 = lax.rsqrt(jnp.mean(inputs * inputs, axis=-1, keepdims=True) + EPSILON)
    normed1 = (inputs * scale1 * norm1_gain).astype(jnp.bfloat16)

    def pair_weight(index):
        head = index * heads // (H // kv_heads)
        source = jnp.where(index % 2 == 0, w_key, w_value)
        return lax.dynamic_slice_in_dim(source, head * HD, HD, 1)

    pair_cos = jnp.where(is_key, cosine, 1.0)
    pair_sin = jnp.where(is_key, sine, 0.0)
    pair_pre = matmul(normed1, pair_weight(lane)) + pair_bias
    pair = rotary(pair_pre, pair_cos, pair_sin).astype(jnp.bfloat16)[None]
    bit = shards // 2
    while bit:
        pair = jnp.concatenate([pair, swap(pair, "cp", bit)], 0)
        bit //= 2
    other = swap(pair, "tp", 1)

    q_pre = matmul(normed1, w_query) + b_query
    query = rotary(
        q_pre.reshape(tok_rows, heads, HD), cosine[:, None, :], sine[:, None, :]
    ).astype(jnp.bfloat16)
    query = query.transpose(1, 0, 2)

    attn, attn_full, log_total, pair = attend(place, query, pair, other)
    w_out_all = gather_tp(w_out, 0)
    w_query_all = gather_tp(w_query, 1)
    cot_shared = share(place, cotangent, shards)
    normed1_shared = share(place, normed1, shards)

    middle = inputs + matmul(gather_tp(attn, 1), w_out_all)
    scale2 = lax.rsqrt(jnp.mean(middle * middle, axis=-1, keepdims=True) + EPSILON)
    normed2 = (middle * scale2 * norm2_gain).astype(jnp.bfloat16)

    units = w_gate.shape[1]
    chunks = pl.cdiv(pl.cdiv(units, TILE), CHUNK_TILES)
    hiddens, grads, total = [], [], None
    for index in range(chunks):
        hidden, grad, total = hidden_chunk(
            place, normed2, cotangent, w_gate, w_up, w_down, total, index
        )
        hiddens.append(hidden)
        grads.append(grad)
    normed2_shared = share(place, normed2, shards)

    downs, gates, ups = [], [], []
    for hidden, grad in zip(hiddens, grads):
        downs.append(weight_grad(place, cot_shared, hidden, shards).T)
        both = weight_grad(place, normed2_shared, grad, shards)
        span = hidden.shape[1]
        for at in range(0, span, TILE):
            size = min(TILE, span - at)
            gates.append(both[:, 2 * at : 2 * at + size])
            ups.append(both[:, 2 * at + TILE : 2 * at + TILE + size])
    grad_w_down = jnp.concatenate(downs, 0)
    grad_w_gate = jnp.concatenate(gates, 1)
    grad_w_up = jnp.concatenate(ups, 1)

    grad_normed2 = in_order(gather_tp(scatter_tp(total).astype(jnp.bfloat16), 0), lane).astype(
        jnp.float32
    )
    weighted2 = grad_normed2 * norm2_gain
    gain2_part = jnp.sum(grad_normed2 * middle * scale2, axis=0)
    grad_middle = (
        cotangent.astype(jnp.float32)
        + scale2 * weighted2
        - middle * scale2**3 * jnp.mean(weighted2 * middle, axis=-1, keepdims=True)
    )
    grad_branch = grad_middle.astype(jnp.bfloat16)
    grad_attn = contract_cols(grad_branch, w_out).astype(jnp.bfloat16)
    grad_query, keep, send = attend_back(
        place, query, pair, grad_attn, attn_full, log_total, cosine, sine
    )

    part = tok_rows // 4
    ffn = sum(matmul(h, lax.slice_in_dim(w_down, i * CHUNK_TILES * TILE, i * CHUNK_TILES * TILE + h.shape[1])) for i, h in enumerate(hiddens))
    ffn = after(ffn.astype(jnp.bfloat16), grad_middle)
    ffn_rel = jnp.concatenate(
        [lax.dynamic_slice_in_dim(ffn, (lane ^ far) * part, part, 0) for far in TP_ORDER], 0
    )
    out_part = scatter_tp(ffn_rel) + lax.dynamic_slice_in_dim(middle, lane * part, part, 0)
    output = in_order(gather_tp(out_part.astype(jnp.bfloat16), 0), lane)

    summed = keep.astype(jnp.float32) + swap(send, "tp", 1).astype(jnp.float32)
    bit = 1
    while bit < shards:
        count = summed.shape[0] // 2
        summed = summed[:count] + swap(summed[count:].astype(jnp.bfloat16), "cp", bit).astype(
            jnp.float32
        )
        bit *= 2
    grad_pair = rotary_back(summed[0], pair_cos, pair_sin).astype(jnp.bfloat16)

    branch_shared = share(place, grad_branch, shards)
    grad_w_out = weight_grad(place, branch_shared, attn, shards).T
    grad_w_query = weight_grad(place, normed1_shared, grad_query, shards)
    grad_w_pair = weight_grad(place, normed1_shared, grad_pair, shards)

    pairs_all = gather_tp(grad_pair, 1)
    grad_normed1 = contract_cols(gather_tp(grad_query, 1), w_query_all)
    for i, far in enumerate(TP_ORDER):
        grad_normed1 = grad_normed1 + contract_cols(
            pairs_all[:, i * HD : (i + 1) * HD], pair_weight(lane ^ far)
        )
    return finish(
        output, grad_middle, grad_normed1, grad_query, grad_pair, gain2_part,
        grad_w_query, grad_w_pair, grad_w_out, grad_w_gate, grad_w_up, grad_w_down,
    )


def solution(mesh):
    return jax.shard_map(
        on_device,
        mesh=mesh,
        in_specs=(
            P("cp", None),
            P(),
            P(None, "tp"),
            P("tp"),
            P(),
            P(),
            P(),
            P(),
            P("tp", None),
            P(),
            P(None, "tp"),
            P(None, "tp"),
            P("tp", None),
            P(),
            P(),
            P("cp", None),
        ),
        out_specs=(
            P("cp", None),
            P("cp", None),
            P(),
            P("cp", "tp"),
            P("tp"),
            P("cp", None),
            P(),
            P("cp", None),
            P(),
            P("tp", "cp"),
            P(),
            P("cp", "tp"),
            P("cp", "tp"),
            P("tp", "cp"),
        ),
        check_vma=False,
    )
```
